32 devices in a mesh: groups: 2 (over y), patch: 16 (over z, x, core).
Axes of the slice: x: 2, y: 2, z: 4, core: 2. Of those that a mesh axis runs over, the one named last changes fastest.
Arguments:
- nodes: bfloat16 [8192, 512], P(('groups', 'patch')), parts along dimension 0, may hold values from -6 to 6
- fine_edges: bfloat16 [16384, 512], P(('groups', 'patch')), parts along dimension 0, may hold values from -6 to 6
- coarse_edges: bfloat16 [4096, 512], P(('groups', 'patch')), parts along dimension 0, may hold values from -6 to 6
- fine_send: int32 [16384], P(('groups', 'patch')), parts along dimension 0, may hold values from 0 to 767
- fine_recv: int32 [16384], P(('groups', 'patch')), parts along dimension 0, may hold values from 0 to 255
- coarse_send: int32 [4096], P(('groups', 'patch')), parts along dimension 0, may hold values from 0 to 127
- coarse_recv: int32 [4096], P(('groups', 'patch')), parts along dimension 0, may hold values from 0 to 127
- halo_rows: int32 [32, 4, 128], P(('groups', 'patch')), parts along dimension 0, may hold values from 0 to 255
- edge_count: int32 [32], P(('groups', 'patch')), parts along dimension 0, may hold values from 1 to 512, 4915 in all
- edge_w1: bfloat16 [1536, 512], replicated, may hold values from -0.15625 to 0.15625
- edge_w2: bfloat16 [512, 512], replicated, may hold values from -0.25 to 0.25
- edge_gain: float32 [512], replicated, may hold values from 0.1 to 1.9
- node_w1: bfloat16 [1024, 512], replicated, may hold values from -0.1875 to 0.1875
- node_w2: bfloat16 [512, 512], replicated, may hold values from -0.25 to 0.25
- node_gain: float32 [512], replicated, may hold values from 0.1 to 1.9
- d_nodes: bfloat16 [8192, 512], P(('groups', 'patch')), parts along dimension 0, may hold values from -6 to 6
- d_fine: bfloat16 [16384, 512], P(('groups', 'patch')), parts along dimension 0, may hold values from -6 to 6
- d_coarse: bfloat16 [4096, 512], P(('groups', 'patch')), parts along dimension 0, may hold values from -6 to 6
Outputs:
- new_nodes: bfloat16 [8192, 512], P(('groups', 'patch')), parts along dimension 0
- new_fine: bfloat16 [16384, 512], P(('groups', 'patch')), parts along dimension 0
- new_coarse: bfloat16 [4096, 512], P(('groups', 'patch')), parts along dimension 0
- g_nodes: bfloat16 [8192, 512], P(('groups', 'patch')), parts along dimension 0
- g_fine: bfloat16 [16384, 512], P(('groups', 'patch')), parts along dimension 0
- g_coarse: bfloat16 [4096, 512], P(('groups', 'patch')), parts along dimension 0
- g_edge_w1: float32 [3072, 512], P(('groups', 'patch')), parts along dimension 0
- g_edge_w2: float32 [1024, 512], P(('groups', 'patch')), parts along dimension 0
- g_node_w1: float32 [2048, 512], P(('groups', 'patch')), parts along dimension 0
- g_node_w2: float32 [1024, 512], P(('groups', 'patch')), parts along dimension 0
The draws below stay inside these ranges and needn't reach their ends.
There are 2 independent parts, one for each index of `groups`. The reference program is written for one: setup_inputs(seed, part) draws one part's arguments, and reference() takes and returns one part's arrays. A program takes and returns all parts, laid end to end along the dimension named above; an argument that names none is the same for every part. Nothing has to cross between parts.
Inputs may be any that keep to these rules, and one draw needn't show every extreme that they name: `halo_rows`: local node rows of the sending patch, for the slot order of the steps. `fine_send`: rows below 256 are the patch's own nodes; the others index the received tiles in slot order. `coarse_send`: coarse node c is row c mod 8 of patch c // 8. The live fine edges of a patch are its first edge_count slots; in every draw some patch has all 512 slots live.
All inputs are finite; a program needn't handle non-finite values. No bound on the sum of `edge_count` on one device may be relied on, other than what follows from the above.
Results may differ from the reference program's by a relative error of at most 0.007.
Values may be sent and summed in bfloat16 or wider, within the bound.
No kernel may reach another device: no remote copies, remote signals or barrier semaphores. Data moves between devices by JAX's collectives and lax.ppermute only.
A program may use at most 128 MiB of HBM per device.

```python
import math
import jax
import jax.numpy as jnp
import numpy as np
from jax import lax

D = 512
NODES_DEV = 256
EDGES_DEV = 512
CEDGES_DEV = 128
COARSE_DEV = 8
TILE = 128
HOPS = 2
NODES = 4096
FINE_EDGES = 8192
COARSE_EDGES = 2048
COARSE = 128
N_PATCH = 16


def touch_ends(entries, key, least, largest):
    longest = entries.shape.index(max(entries.shape))
    spots = []
    for shift in (0, 1):
        where = [jax.random.randint(jax.random.fold_in(key, axis), (), 0, length) for axis, length in enumerate(entries.shape)]
        where[longest] = (where[longest] + shift) % entries.shape[longest]
        spots.append(tuple(where))
    return entries.at[spots[0]].set(least).at[spots[1]].set(largest)


def levels(key, dims, cuts, low, high):
    def one(position, shards_of):
        steps = jax.random.uniform(jax.random.fold_in(jax.random.fold_in(key, 6), position), (shards_of,), jnp.float32, low / len(cuts), high / len(cuts))
        return jnp.repeat(jnp.exp(steps), dims[position] // shards_of).reshape((-1,) + (1,) * (len(dims) - position - 1))

    level = one(*cuts[0])
    for cut in cuts[1:]:
        level = level * one(*cut)
    return level


def profile(number_of, total, bound, skew):
    weights = [(1 << 20) // math.isqrt(standing ** skew) + 1 for standing in range(2, number_of + 1)]
    rest, given = total - bound - (number_of - 1), [1] * (number_of - 1)
    while rest > 0:
        candidates = [i for i in range(number_of - 1) if given[i] < bound]
        mass, remaining = sum([weights[i] for i in candidates]), rest
        for i in candidates:
            extra = min(bound - given[i], max(1, remaining * weights[i] // mass), rest)
            given[i] = given[i] + extra
            rest = rest - extra
    return np.array([bound] + given)


def ragged(rng, amount, total, bound, skew):
    if amount == 2:
        one = jax.random.randint(rng, (), max(1, total - bound), min(bound, total - 1) + 1)
        return jnp.stack([one, total - one])
    sizes = jnp.asarray(profile(amount, total, bound, skew), jnp.int32)
    couples = (amount - 1) // 2
    donor, receiver = sizes[1:1 + 2 * couples:2], sizes[2:2 + 2 * couples:2]
    margin = jnp.minimum(donor - 1, bound - receiver)
    shifted = jax.random.randint(jax.random.fold_in(rng, 1), (couples,), 0, 1 << 20) % (margin + 1)
    sizes = sizes.at[1:1 + 2 * couples:2].set(donor - shifted).at[2:2 + 2 * couples:2].set(receiver + shifted)
    return sizes[jax.random.permutation(jax.random.fold_in(rng, 2), amount)]


def noise(rng, extent, spread, reach, cuts=(), held_as=jnp.bfloat16):
    level = levels(rng, extent, cuts, -0.22, 0.18) if cuts else 1.0
    entries = jax.random.normal(rng, extent, jnp.float32) * spread * level
    return jnp.minimum(jnp.maximum(entries, -reach), reach).astype(held_as)


def setup_inputs(seed: int = 0, part: int = 0) -> dict:
    arg_keys = jax.random.split(jax.random.key(seed), 19)
    part_keys = jax.random.split(jax.random.fold_in(arg_keys[18], part), 19)
    nodes = noise(part_keys[0], (NODES, D), 1.0, 6.0, ((0, 16),))
    fine_edges = noise(part_keys[1], (FINE_EDGES, D), 1.0, 6.0, ((0, 16),))
    coarse_edges = noise(part_keys[2], (COARSE_EDGES, D), 1.0, 6.0, ((0, 16),))
    fine_send = touch_ends(jax.random.randint(part_keys[3], (FINE_EDGES,), 0, NODES_DEV + 2 * HOPS * TILE), jax.random.fold_in(part_keys[3], 1), 0, (NODES_DEV + 2 * HOPS * TILE) - 1).astype(jnp.int32)
    fine_recv = touch_ends(jax.random.randint(part_keys[4], (FINE_EDGES,), 0, NODES_DEV), jax.random.fold_in(part_keys[4], 1), 0, NODES_DEV - 1).astype(jnp.int32)
    coarse_send = touch_ends(jax.random.randint(part_keys[5], (COARSE_EDGES,), 0, COARSE), jax.random.fold_in(part_keys[5], 1), 0, COARSE - 1).astype(jnp.int32)
    coarse_recv = touch_ends(jax.random.randint(part_keys[6], (COARSE_EDGES,), 0, COARSE), jax.random.fold_in(part_keys[6], 1), 0, COARSE - 1).astype(jnp.int32)
    halo_rows = touch_ends(jax.random.randint(part_keys[7], (N_PATCH, 2 * HOPS, TILE), 0, NODES_DEV), jax.random.fold_in(part_keys[7], 1), 0, NODES_DEV - 1).astype(jnp.int32)
    edge_count = ragged(part_keys[8], N_PATCH, N_PATCH * EDGES_DEV * 3 // 5, EDGES_DEV, 2).astype(jnp.int32)
    edge_w1 = noise(arg_keys[9], (3 * D, D), (3 * D) ** -0.5, 0.15625)
    edge_w2 = noise(arg_keys[10], (D, D), D ** -0.5, 0.25)
    edge_gain = jnp.clip(1.0 + 0.18 * jax.random.normal(arg_keys[11], (D,), jnp.float32), 0.1, 1.9)
    node_w1 = noise(arg_keys[12], (2 * D, D), (2 * D) ** -0.5, 0.1875)
    node_w2 = noise(arg_keys[13], (D, D), D ** -0.5, 0.25)
    node_gain = jnp.clip(1.0 + 0.18 * jax.random.normal(arg_keys[14], (D,), jnp.float32), 0.1, 1.9)
    d_nodes = noise(part_keys[15], (NODES, D), 1.0, 6.0, ((0, 16),))
    d_fine = noise(part_keys[16], (FINE_EDGES, D), 1.0, 6.0, ((0, 16),))
    d_coarse = noise(part_keys[17], (COARSE_EDGES, D), 1.0, 6.0, ((0, 16),))
    return dict(nodes=nodes, fine_edges=fine_edges, coarse_edges=coarse_edges, fine_send=fine_send, fine_recv=fine_recv, coarse_send=coarse_send, coarse_recv=coarse_recv, halo_rows=halo_rows, edge_count=edge_count, edge_w1=edge_w1, edge_w2=edge_w2, edge_gain=edge_gain, node_w1=node_w1, node_w2=node_w2, node_gain=node_gain, d_nodes=d_nodes, d_fine=d_fine, d_coarse=d_coarse)


EPSILON = 1e-05

def swish_and_slope(pre_act):
    sigmoid = jax.nn.sigmoid(pre_act)
    return (pre_act * sigmoid, sigmoid * (1.0 + pre_act * (1.0 - sigmoid)))

def mlp_forward(inputs, first_w, second_w, gain):
    pre_act = jnp.dot(inputs, first_w, preferred_element_type=jnp.float32)
    activ, slope = swish_and_slope(pre_act)
    hidden = activ.astype(jnp.bfloat16)
    output = jnp.dot(hidden, second_w, preferred_element_type=jnp.float32)
    centred = output - lax.optimization_barrier(jnp.mean(output, axis=-1, keepdims=True))
    inv_std = lax.rsqrt(lax.optimization_barrier(jnp.mean(centred * centred, axis=-1, keepdims=True)) + EPSILON)
    normed = centred * inv_std
    return (normed * gain.astype(jnp.float32), (hidden, slope, normed, inv_std))

def mlp_backward(inputs, first_w, second_w, gain, saved, cotan):
    hidden, slope, normed, inv_std = saved
    scaled = cotan * gain.astype(jnp.float32)
    back_out = inv_std * (scaled - lax.optimization_barrier(jnp.mean(scaled, axis=-1, keepdims=True)) - normed * lax.optimization_barrier(jnp.mean(scaled * normed, axis=-1, keepdims=True)))
    back_out = back_out.astype(jnp.bfloat16)
    grad_second = lax.dot_general(hidden, back_out, (((0,), (0,)), ((), ())), preferred_element_type=jnp.float32)
    back_hidden = lax.dot_general(back_out, second_w, (((1,), (1,)), ((), ())), preferred_element_type=jnp.float32)
    back_pre = (back_hidden * slope).astype(jnp.bfloat16)
    grad_first = lax.dot_general(inputs, back_pre, (((0,), (0,)), ((), ())), preferred_element_type=jnp.float32)
    back_in = lax.dot_general(back_pre, first_w, (((1,), (1,)), ((), ())), preferred_element_type=jnp.float32)
    return (grad_first, grad_second, back_in)

def peer_offsets(hops):
    return list(range(1, hops + 1)) + [-step_k for step_k in range(1, hops + 1)]

def reference(nodes, fine_edges, coarse_edges, fine_send, fine_recv, coarse_send, coarse_recv, halo_rows, edge_count, edge_w1, edge_w2, edge_gain, node_w1, node_w2, node_gain, d_nodes, d_fine, d_coarse):
    patches = N_PATCH
    offsets = peer_offsets(HOPS)
    nodes_blocks = nodes.reshape(patches, NODES_DEV, D)
    fine_blocks = fine_edges.reshape(patches, EDGES_DEV, D)
    coarse_blocks = coarse_edges.reshape(patches, CEDGES_DEV, D)
    send_blocks = fine_send.reshape(patches, EDGES_DEV)
    recv_blocks = fine_recv.reshape(patches, EDGES_DEV)
    csend_blocks = coarse_send.reshape(patches, CEDGES_DEV)
    crecv_blocks = coarse_recv.reshape(patches, CEDGES_DEV)
    dfine_blocks = d_fine.reshape(patches, EDGES_DEV, D)
    dcoarse_blocks = d_coarse.reshape(patches, CEDGES_DEV, D)
    coarse_all = nodes_blocks[:, :COARSE_DEV].reshape(COARSE, D)
    space_rows = NODES_DEV + 2 * HOPS * TILE

    def edge_inputs(device):
        pieces = [nodes_blocks[device]]
        for slot, offset in enumerate(offsets):
            source = (device - offset) % patches
            pieces.append(nodes_blocks[source][halo_rows[source, slot]])
        space = jnp.concatenate(pieces, 0)
        own = nodes_blocks[device]
        fine_in = jnp.concatenate([fine_blocks[device], space[send_blocks[device]], own[recv_blocks[device]]], 1)
        coarse_in = jnp.concatenate([coarse_blocks[device], coarse_all[csend_blocks[device]], coarse_all[crecv_blocks[device]]], 1)
        alive = (jnp.arange(EDGES_DEV) < edge_count[device]).astype(jnp.float32)[:, None]
        return (jnp.concatenate([fine_in, coarse_in], 0), alive)

    def forward_step(carry, device):
        inputs, alive = edge_inputs(device)
        message, saved = mlp_forward(inputs, edge_w1, edge_w2, edge_gain)
        fine_msg = message[:EDGES_DEV] * alive
        coarse_msg = message[EDGES_DEV:]
        fine_agg = jax.ops.segment_sum(fine_msg, recv_blocks[device], num_segments=NODES_DEV)
        carry = carry + jax.ops.segment_sum(coarse_msg, crecv_blocks[device], num_segments=COARSE)
        new_f = (fine_blocks[device].astype(jnp.float32) + fine_msg).astype(jnp.bfloat16)
        new_c = (coarse_blocks[device].astype(jnp.float32) + coarse_msg).astype(jnp.bfloat16)
        return (carry, (fine_agg, new_f, new_c))
    device_ids = jnp.arange(patches, dtype=jnp.int32)
    coarse_agg, (agg_blocks, new_fine, new_coarse) = lax.scan(forward_step, jnp.zeros((COARSE, D), jnp.float32), device_ids)
    agg_blocks = agg_blocks.at[:, :COARSE_DEV].add(coarse_agg.reshape(patches, COARSE_DEV, D))
    node_inputs = jnp.concatenate([nodes, agg_blocks.reshape(NODES, D).astype(jnp.bfloat16)], 1)
    update, node_saved = mlp_forward(node_inputs, node_w1, node_w2, node_gain)
    new_nodes = (nodes.astype(jnp.float32) + update).astype(jnp.bfloat16)
    node_cot = d_nodes.astype(jnp.float32)
    grad_nw1, grad_nw2, node_dz = mlp_backward(node_inputs, node_w1, node_w2, node_gain, node_saved, node_cot)
    grad_blocks = (node_cot + node_dz[:, :D]).reshape(patches, NODES_DEV, D)
    dagg_blocks = node_dz[:, D:].reshape(patches, NODES_DEV, D)
    dagg_coarse = dagg_blocks[:, :COARSE_DEV].reshape(COARSE, D)

    def backward_step(carry, device):
        grad_acc, coarse_grad, acc_w1, acc_w2 = carry
        inputs, alive = edge_inputs(device)
        message, saved = mlp_forward(inputs, edge_w1, edge_w2, edge_gain)
        cot_fine = alive * (dfine_blocks[device].astype(jnp.float32) + dagg_blocks[device][recv_blocks[device]])
        cot_coarse = dcoarse_blocks[device].astype(jnp.float32) + dagg_coarse[crecv_blocks[device]]
        grad_first, grad_second, back_in = mlp_backward(inputs, edge_w1, edge_w2, edge_gain, saved, jnp.concatenate([cot_fine, cot_coarse], 0))
        fine_dz = back_in[:EDGES_DEV]
        coarse_dz = back_in[EDGES_DEV:]
        grad_f = (dfine_blocks[device].astype(jnp.float32) + fine_dz[:, :D]).astype(jnp.bfloat16)
        grad_c = (dcoarse_blocks[device].astype(jnp.float32) + coarse_dz[:, :D]).astype(jnp.bfloat16)
        space_grad = jax.ops.segment_sum(fine_dz[:, D:2 * D], send_blocks[device], num_segments=space_rows)
        local = space_grad[:NODES_DEV] + jax.ops.segment_sum(fine_dz[:, 2 * D:], recv_blocks[device], num_segments=NODES_DEV)
        grad_acc = grad_acc.at[device].add(local)
        for slot, offset in enumerate(offsets):
            source = (device - offset) % patches
            piece = space_grad[NODES_DEV + slot * TILE:NODES_DEV + (slot + 1) * TILE]
            grad_acc = grad_acc.at[source, halo_rows[source, slot]].add(piece)
        coarse_grad = coarse_grad + jax.ops.segment_sum(coarse_dz[:, D:2 * D], csend_blocks[device], num_segments=COARSE)
        coarse_grad = coarse_grad + jax.ops.segment_sum(coarse_dz[:, 2 * D:], crecv_blocks[device], num_segments=COARSE)
        return ((grad_acc, coarse_grad, acc_w1 + grad_first, acc_w2 + grad_second), (grad_f, grad_c))
    start = (grad_blocks, jnp.zeros((COARSE, D), jnp.float32), jnp.zeros((3 * D, D), jnp.float32), jnp.zeros((D, D), jnp.float32))
    (grad_blocks, coarse_grad, grad_ew1, grad_ew2), (g_fine, g_coarse) = lax.scan(backward_step, start, device_ids)
    grad_blocks = grad_blocks.at[:, :COARSE_DEV].add(coarse_grad.reshape(patches, COARSE_DEV, D))
    g_nodes = grad_blocks.reshape(NODES, D).astype(jnp.bfloat16)
    return (new_nodes, new_fine.reshape(FINE_EDGES, D), new_coarse.reshape(COARSE_EDGES, D), g_nodes, g_fine.reshape(FINE_EDGES, D), g_coarse.reshape(COARSE_EDGES, D), grad_ew1, grad_ew2, grad_nw1, grad_nw2)
```

```python
import jax
import jax.numpy as jnp
from jax import lax
from jax.sharding import PartitionSpec as P

COARSE_DEV = 8


EPSILON = 1e-05


def passed_along(block, axis, distance):
    devices = range(lax.axis_size(axis))
    route = [((i - distance) % len(devices), i) for i in devices]
    return lax.ppermute(block, axis, route)


def from_all(rows, axis):
    count = lax.axis_size(axis)
    spread = jnp.broadcast_to(rows[None], (count,) + rows.shape)
    return lax.all_to_all(spread, axis, 0, 0).reshape((count * rows.shape[0],) + rows.shape[1:])


def summed_to_owner(whole, axis):
    count = lax.axis_size(axis)
    blocks = whole.reshape((count, whole.shape[0] // count) + whole.shape[1:])
    return jnp.sum(lax.all_to_all(blocks, axis, 0, 0).astype(jnp.float32), 0)


def halved_to_owner(whole, axis):
    count = lax.axis_size(axis)
    blocks = whole.reshape((count, whole.shape[0] // count) + whole.shape[1:])
    me = lax.axis_index(axis)
    distance = 1
    while distance < count:
        side = (me // distance) % 2
        pairs = blocks.reshape((blocks.shape[0] // 2, 2) + blocks.shape[1:])
        kept = lax.dynamic_index_in_dim(pairs, side, 1, keepdims=False)
        given = lax.dynamic_index_in_dim(pairs, 1 - side, 1, keepdims=False)
        route = [(i, i ^ distance) for i in range(count)]
        taken = lax.ppermute(given.astype(jnp.bfloat16), axis, route)
        blocks = kept + taken.astype(jnp.float32)
        distance *= 2
    return blocks[0]


def swish_and_slope(pre_act):
    sigmoid = jax.nn.sigmoid(pre_act)
    return (pre_act * sigmoid, sigmoid * (1.0 + pre_act * (1.0 - sigmoid)))


def mlp_forward(inputs, first_w, second_w, gain):
    pre_act = jnp.dot(inputs, first_w, preferred_element_type=jnp.float32)
    activ, slope = swish_and_slope(pre_act)
    hidden = activ.astype(jnp.bfloat16)
    output = jnp.dot(hidden, second_w, preferred_element_type=jnp.float32)
    centred = output - jnp.mean(output, axis=-1, keepdims=True)
    inv_std = lax.rsqrt(jnp.mean(centred * centred, axis=-1, keepdims=True) + EPSILON)
    normed = centred * inv_std
    return (normed * gain, (hidden, slope, normed, inv_std))


def mlp_backward(inputs, first_w, second_w, gain, saved, cotan):
    hidden, slope, normed, inv_std = saved
    scaled = cotan * gain
    back_out = inv_std * (
        scaled
        - jnp.mean(scaled, axis=-1, keepdims=True)
        - normed * jnp.mean(scaled * normed, axis=-1, keepdims=True)
    )
    back_out = back_out.astype(jnp.bfloat16)
    grad_second = lax.dot_general(
        hidden, back_out, (((0,), (0,)), ((), ())), preferred_element_type=jnp.float32
    )
    back_hidden = lax.dot_general(
        back_out, second_w, (((1,), (1,)), ((), ())), preferred_element_type=jnp.float32
    )
    back_pre = (back_hidden * slope).astype(jnp.bfloat16)
    grad_first = lax.dot_general(
        inputs, back_pre, (((0,), (0,)), ((), ())), preferred_element_type=jnp.float32
    )
    back_in = lax.dot_general(
        back_pre, first_w, (((1,), (1,)), ((), ())), preferred_element_type=jnp.float32
    )
    return (grad_first, grad_second, back_in)


def peer_offsets(hops):
    return list(range(1, hops + 1)) + [-step_k for step_k in range(1, hops + 1)]


def local(
    nodes,
    fine_edges,
    coarse_edges,
    fine_send,
    fine_recv,
    coarse_send,
    coarse_recv,
    halo_rows,
    edge_count,
    edge_w1,
    edge_w2,
    edge_gain,
    node_w1,
    node_w2,
    node_gain,
    d_nodes,
    d_fine,
    d_coarse,
):
    count_nodes = nodes.shape[0]
    width = nodes.shape[1]
    count_edges = fine_edges.shape[0]
    tile_rows = halo_rows[0]
    hops = tile_rows.shape[0] // 2
    tile_size = tile_rows.shape[1]
    offsets = peer_offsets(hops)
    tiles = nodes[tile_rows.reshape(-1)].reshape(2 * hops, tile_size, width)
    received = []
    for slot, offset in enumerate(offsets):
        received.append(passed_along(tiles[slot], "patch", offset))
    space = jnp.concatenate([nodes] + received, 0)
    coarse_all = from_all(nodes[:COARSE_DEV], "patch")
    total_coarse = coarse_all.shape[0]
    fine_in = jnp.concatenate([fine_edges, space[fine_send], nodes[fine_recv]], 1)
    coarse_in = jnp.concatenate([coarse_edges, coarse_all[coarse_send], coarse_all[coarse_recv]], 1)
    inputs = jnp.concatenate([fine_in, coarse_in], 0)
    alive = (jnp.arange(count_edges) < edge_count[0]).astype(jnp.float32)[:, None]
    message, saved = mlp_forward(inputs, edge_w1, edge_w2, edge_gain)
    fine_msg = message[:count_edges] * alive
    coarse_msg = message[count_edges:]
    new_fine = (fine_edges.astype(jnp.float32) + fine_msg).astype(jnp.bfloat16)
    new_coarse = (coarse_edges.astype(jnp.float32) + coarse_msg).astype(jnp.bfloat16)
    fine_agg = jax.ops.segment_sum(fine_msg, fine_recv, num_segments=count_nodes)
    partial_agg = jax.ops.segment_sum(coarse_msg, coarse_recv, num_segments=total_coarse)
    share = summed_to_owner(partial_agg, "patch")
    aggregate = fine_agg.at[:COARSE_DEV].add(share)
    node_inputs = jnp.concatenate([nodes, aggregate.astype(jnp.bfloat16)], 1)
    update, node_saved = mlp_forward(node_inputs, node_w1, node_w2, node_gain)
    new_nodes = (nodes.astype(jnp.float32) + update).astype(jnp.bfloat16)
    node_cot = d_nodes.astype(jnp.float32)
    grad_nw1, grad_nw2, node_dz = mlp_backward(
        node_inputs, node_w1, node_w2, node_gain, node_saved, node_cot
    )
    d_aggregate = node_dz[:, width:]
    dagg_coarse = from_all(d_aggregate[:COARSE_DEV], "patch")
    cot_fine = alive * (d_fine.astype(jnp.float32) + d_aggregate[fine_recv])
    cot_coarse = d_coarse.astype(jnp.float32) + dagg_coarse[coarse_recv]
    grad_ew1, grad_ew2, back_in = mlp_backward(
        inputs, edge_w1, edge_w2, edge_gain, saved, jnp.concatenate([cot_fine, cot_coarse], 0)
    )
    fine_dz = back_in[:count_edges]
    coarse_dz = back_in[count_edges:]
    g_fine = (d_fine.astype(jnp.float32) + fine_dz[:, :width]).astype(jnp.bfloat16)
    g_coarse = (d_coarse.astype(jnp.float32) + coarse_dz[:, :width]).astype(jnp.bfloat16)
    space_grad = jax.ops.segment_sum(
        fine_dz[:, width : 2 * width], fine_send, num_segments=count_nodes + 2 * hops * tile_size
    )
    grad_nodes = node_cot + node_dz[:, :width] + space_grad[:count_nodes]
    grad_nodes = grad_nodes + jax.ops.segment_sum(
        fine_dz[:, 2 * width :], fine_recv, num_segments=count_nodes
    )
    for slot, offset in enumerate(offsets):
        piece = space_grad[count_nodes + slot * tile_size : count_nodes + (slot + 1) * tile_size]
        returned = passed_along(piece.astype(jnp.bfloat16), "patch", -offset).astype(piece.dtype)
        grad_nodes = grad_nodes.at[tile_rows[slot]].add(returned)
    coarse_part = jax.ops.segment_sum(
        coarse_dz[:, width : 2 * width], coarse_send, num_segments=total_coarse
    )
    coarse_part = coarse_part + jax.ops.segment_sum(
        coarse_dz[:, 2 * width :], coarse_recv, num_segments=total_coarse
    )
    grad_nodes = grad_nodes.at[:COARSE_DEV].add(
        summed_to_owner(coarse_part, "patch")
    )
    g_nodes = grad_nodes.astype(jnp.bfloat16)
    weight_parts = (
        halved_to_owner(grad_ew1, "patch"),
        halved_to_owner(grad_ew2, "patch"),
        summed_to_owner(grad_nw1.astype(jnp.bfloat16), "patch"),
        summed_to_owner(grad_nw2.astype(jnp.bfloat16), "patch"),
    )
    return (
        new_nodes,
        new_fine,
        new_coarse,
        g_nodes,
        g_fine,
        g_coarse,
        weight_parts[0],
        weight_parts[1],
        weight_parts[2],
        weight_parts[3],
    )


def solution(mesh):
    placed = (
        P(("groups", "patch"), None),
        P(("groups", "patch"), None),
        P(("groups", "patch"), None),
        P(("groups", "patch")),
        P(("groups", "patch")),
        P(("groups", "patch")),
        P(("groups", "patch")),
        P(("groups", "patch"), None, None),
        P(("groups", "patch")),
        P(),
        P(),
        P(),
        P(),
        P(),
        P(),
        P(("groups", "patch"), None),
        P(("groups", "patch"), None),
        P(("groups", "patch"), None),
    )
    return jax.shard_map(
        local,
        mesh=mesh,
        in_specs=placed,
        out_specs=(
            P(("groups", "patch"), None),
            P(("groups", "patch"), None),
            P(("groups", "patch"), None),
            P(("groups", "patch"), None),
            P(("groups", "patch"), None),
            P(("groups", "patch"), None),
            P(("groups", "patch"), None),
            P(("groups", "patch"), None),
            P(("groups", "patch"), None),
            P(("groups", "patch"), None),
        ),
        check_vma=False,
    )
```

```python
import functools

import jax
import jax.numpy as jnp
from jax import lax
from jax.experimental import pallas as pl
from jax.experimental.pallas import tpu as pltpu
from jax.sharding import PartitionSpec as P

COARSE_DEV = 8
EPSILON = 1e-05
F32 = jnp.float32
BF16 = jnp.bfloat16
VMEM_LIMIT = 44 * 1024 * 1024


def mm(a, b):
    return lax.dot_general(a, b, (((1,), (0,)), ((), ())), preferred_element_type=F32)


def mm_nt(a, b):
    return lax.dot_general(a, b, (((1,), (1,)), ((), ())), preferred_element_type=F32)


def mm_tn(a, b):
    return lax.dot_general(a, b, (((0,), (0,)), ((), ())), preferred_element_type=F32)


def halves(value):
    high = value.astype(BF16)
    low = (value - high.astype(F32)).astype(BF16)
    return high, low


def one_hot(index, rows):
    row = lax.broadcasted_iota(jnp.int32, (rows, index.shape[1]), 0)
    return jnp.where(row == index, 1.0, 0.0).astype(BF16)


def pick(hot, table):
    return mm_tn(hot, table)


def pick_wide(hot, table):
    high, low = halves(table)
    return mm_tn(hot, high) + mm_tn(hot, low)


def put_wide(hot, rows):
    high, low = halves(rows)
    return mm(hot, high) + mm(hot, low)


def row_mean(value):
    return jnp.mean(value, axis=-1, keepdims=True)


def tail_of_forward(pre, second_w, gain):
    sigmoid = jax.nn.sigmoid(pre)
    hidden = (pre * sigmoid).astype(BF16)
    slope = sigmoid * (1.0 + pre * (1.0 - sigmoid))
    output = mm(hidden, second_w)
    centred = output - row_mean(output)
    inv_std = lax.rsqrt(row_mean(centred * centred) + EPSILON)
    normed = centred * inv_std
    return normed * gain, hidden, slope, normed, inv_std


def head_of_backward(cotan, second_w, gain, slope, normed, inv_std):
    scaled = cotan * gain
    back_out = inv_std * (scaled - row_mean(scaled) - normed * row_mean(scaled * normed))
    back_out = back_out.astype(BF16)
    back_pre = (mm_nt(back_out, second_w) * slope).astype(BF16)
    return back_out, back_pre


def tiles_kernel(nodes_ref, halo_ref, *outs):
    spread_ref = outs[-1]
    nodes = nodes_ref[...]
    for slot, out in enumerate(outs[:-1]):
        hot = one_hot(halo_ref[slot : slot + 1, :], nodes.shape[0])
        out[...] = pick(hot, nodes).astype(BF16)
    rows = nodes_ref[0:16, :].astype(F32)[:COARSE_DEV].astype(BF16)
    for peer in range(spread_ref.shape[0]):
        spread_ref[peer] = rows


def gathered(ref):
    value = ref[...].astype(F32)
    return value.reshape(value.shape[0] * value.shape[1], value.shape[2])


def coarse_forward_kernel(
    all_ref, edges_ref, send_ref, recv_ref, w1_ref, w2_ref, gain_ref,
    new_ref, part_ref, zs_ref, zr_ref, hidden_ref, slope_ref, normed_ref, std_ref,
):
    width = edges_ref.shape[1]
    table = gathered(all_ref).astype(BF16)
    hot_s = one_hot(send_ref[...], table.shape[0])
    hot_r = one_hot(recv_ref[...], table.shape[0])
    edges = edges_ref[...]
    zs = pick(hot_s, table).astype(BF16)
    zr = pick(hot_r, table).astype(BF16)
    pre = (
        mm(edges, w1_ref[0:width, :])
        + mm(zs, w1_ref[width : 2 * width, :])
        + mm(zr, w1_ref[2 * width : 3 * width, :])
    )
    message, hidden, slope, normed, inv_std = tail_of_forward(pre, w2_ref[...], gain_ref[...])
    total = put_wide(hot_r, message)
    part_ref[...] = total.reshape(part_ref.shape).astype(BF16)
    new_ref[...] = (edges.astype(F32) + message).astype(BF16)
    zs_ref[...] = zs
    zr_ref[...] = zr
    hidden_ref[...] = hidden
    slope_ref[...] = slope
    normed_ref[...] = normed
    std_ref[...] = jnp.broadcast_to(inv_std, std_ref.shape)


def fine_forward_kernel(
    count_ref, nodes_ref, *refs, slots,
):
    tile_refs = refs[:slots]
    (
        edges_ref, send_ref, recv_ref, w1_ref, w2_ref, gain_ref,
        new_ref, agg_ref, zs_ref, zr_ref, hidden_ref, slope_ref, normed_ref, std_ref, space_ref,
    ) = refs[slots:]
    step = pl.program_id(0)
    rows, width = edges_ref.shape
    own = nodes_ref.shape[0]
    tile = tile_refs[0].shape[0]

    @pl.when(step == 0)
    def _():
        space_ref[0:own, :] = nodes_ref[...]
        for slot in range(slots):
            space_ref[own + slot * tile : own + (slot + 1) * tile, :] = tile_refs[slot][...]
        agg_ref[...] = jnp.zeros_like(agg_ref)

    edges = edges_ref[...]
    hot_s = one_hot(send_ref[...], space_ref.shape[0])
    hot_r = one_hot(recv_ref[...], own)
    zs = pick(hot_s, space_ref[...]).astype(BF16)
    zr = pick(hot_r, nodes_ref[...]).astype(BF16)
    pre = (
        mm(edges, w1_ref[0:width, :])
        + mm(zs, w1_ref[width : 2 * width, :])
        + mm(zr, w1_ref[2 * width : 3 * width, :])
    )
    message, hidden, slope, normed, inv_std = tail_of_forward(pre, w2_ref[...], gain_ref[...])
    place = step * rows + lax.broadcasted_iota(jnp.int32, (rows, 1), 0)
    message = jnp.where(place < count_ref[0], message, 0.0)
    agg_ref[...] += put_wide(hot_r, message)
    new_ref[...] = (edges.astype(F32) + message).astype(BF16)
    zs_ref[...] = zs
    zr_ref[...] = zr
    hidden_ref[...] = hidden
    slope_ref[...] = slope
    normed_ref[...] = normed
    std_ref[...] = jnp.broadcast_to(inv_std, std_ref.shape)


def by_distance(me, peers, firsts, seconds, kept_ref, given_ref):
    rows1 = firsts.shape[0] // peers
    rows2 = seconds.shape[0] // peers
    for r in range(peers):
        to = jnp.bitwise_xor(me, r)
        first = firsts[pl.ds(pl.multiple_of(to * rows1, 16), rows1), :]
        second = seconds[pl.ds(pl.multiple_of(to * rows2, 16), rows2), :]
        out = given_ref if r % 2 else kept_ref
        out[r // 2, 0:rows1, :] = first.astype(out.dtype)
        out[r // 2, rows1 : rows1 + rows2, :] = second.astype(out.dtype)


def node_kernel(
    me_ref, nodes_ref, agg_ref, share_ref, d_ref, w1_ref, w2_ref, gain_ref,
    new_ref, base_ref, dagg_ref, spread_ref, *rest, ordered,
):
    if ordered:
        kept_ref, given_ref, total_ref, g1_ref, g2_ref = rest
    else:
        g1_ref, g2_ref, total_ref = rest
    width = nodes_ref.shape[1]
    total_ref[...] = agg_ref[...]
    total_ref[0:COARSE_DEV, :] += jnp.sum(share_ref[...].astype(F32), 0)
    nodes = nodes_ref[...]
    agg = total_ref[...].astype(BF16)
    pre = mm(nodes, w1_ref[0:width, :]) + mm(agg, w1_ref[width : 2 * width, :])
    update, hidden, slope, normed, inv_std = tail_of_forward(pre, w2_ref[...], gain_ref[...])
    new_ref[...] = (nodes.astype(F32) + update).astype(BF16)
    cotan = d_ref[...].astype(F32)
    back_out, back_pre = head_of_backward(cotan, w2_ref[...], gain_ref[...], slope, normed, inv_std)
    dagg = mm_nt(back_pre, w1_ref[width : 2 * width, :])
    dagg_ref[...] = dagg
    rows = dagg[:COARSE_DEV].astype(BF16)
    for peer in range(spread_ref.shape[0]):
        spread_ref[peer] = rows
    base_ref[...] = cotan + mm_nt(back_pre, w1_ref[0:width, :])
    g1_ref[0:width, :] = mm_tn(nodes, back_pre)
    g1_ref[width : 2 * width, :] = mm_tn(agg, back_pre)
    g2_ref[...] = mm_tn(hidden, back_out)
    if ordered:
        by_distance(me_ref[0], spread_ref.shape[0], g1_ref, g2_ref, kept_ref, given_ref)


def fine_backward_kernel(
    count_ref, edges_ref, d_ref, send_ref, recv_ref, w1_ref, w2_ref, gain_ref, dagg_ref, base_ref,
    zs_ref, zr_ref, hidden_ref, slope_ref, normed_ref, std_ref,
    g_ref, g1_ref, g2_ref, own_ref, *rest,
):
    piece_refs, space_ref, received_ref = rest[:-2], rest[-2], rest[-1]
    step = pl.program_id(0)
    rows, width = edges_ref.shape
    own = base_ref.shape[0]

    @pl.when(step == 0)
    def _():
        g1_ref[...] = jnp.zeros_like(g1_ref)
        g2_ref[...] = jnp.zeros_like(g2_ref)
        space_ref[...] = jnp.zeros_like(space_ref)
        received_ref[...] = jnp.zeros_like(received_ref)

    hot_r = one_hot(recv_ref[...], own)
    d_edges = d_ref[...].astype(F32)
    place = step * rows + lax.broadcasted_iota(jnp.int32, (rows, 1), 0)
    cotan = jnp.where(place < count_ref[0], d_edges + pick_wide(hot_r, dagg_ref[...]), 0.0)
    back_out, back_pre = head_of_backward(
        cotan, w2_ref[...], gain_ref[...], slope_ref[...], normed_ref[...], std_ref[:, 0:1]
    )
    g2_ref[...] += mm_tn(hidden_ref[...], back_out)
    g1_ref[0:width, :] += mm_tn(edges_ref[...], back_pre)
    g1_ref[width : 2 * width, :] += mm_tn(zs_ref[...], back_pre)
    g1_ref[2 * width : 3 * width, :] += mm_tn(zr_ref[...], back_pre)
    g_ref[...] = (d_edges + mm_nt(back_pre, w1_ref[0:width, :])).astype(BF16)
    hot_s = one_hot(send_ref[...], space_ref.shape[0])
    space_ref[...] += put_wide(hot_s, mm_nt(back_pre, w1_ref[width : 2 * width, :]))
    received_ref[...] += put_wide(hot_r, mm_nt(back_pre, w1_ref[2 * width : 3 * width, :]))

    @pl.when(step == pl.num_programs(0) - 1)
    def _():
        own_ref[...] = base_ref[...] + received_ref[...] + space_ref[0:own, :]
        tile = piece_refs[0].shape[0]
        for slot, piece in enumerate(piece_refs):
            piece[...] = space_ref[own + slot * tile : own + (slot + 1) * tile, :].astype(BF16)


def coarse_backward_kernel(
    me_ref, all_ref, edges_ref, d_ref, send_ref, recv_ref, w1_ref, w2_ref, gain_ref,
    zs_ref, zr_ref, hidden_ref, slope_ref, normed_ref, std_ref, f1_ref, f2_ref,
    g_ref, part_ref, *rest, ordered,
):
    if ordered:
        kept_ref, given_ref, g1_ref, g2_ref = rest
    else:
        g1_ref, g2_ref = rest
    width = edges_ref.shape[1]
    table = gathered(all_ref).astype(BF16)
    hot_r = one_hot(recv_ref[...], table.shape[0])
    d_edges = d_ref[...].astype(F32)
    cotan = d_edges + pick(hot_r, table)
    back_out, back_pre = head_of_backward(
        cotan, w2_ref[...], gain_ref[...], slope_ref[...], normed_ref[...], std_ref[:, 0:1]
    )
    g2_ref[...] = f2_ref[...] + mm_tn(hidden_ref[...], back_out)
    g1_ref[0:width, :] = f1_ref[0:width, :] + mm_tn(edges_ref[...], back_pre)
    g1_ref[width : 2 * width, :] = f1_ref[width : 2 * width, :] + mm_tn(zs_ref[...], back_pre)
    g1_ref[2 * width : 3 * width, :] = f1_ref[2 * width : 3 * width, :] + mm_tn(zr_ref[...], back_pre)
    if ordered:
        by_distance(me_ref[0], part_ref.shape[0], g1_ref, g2_ref, kept_ref, given_ref)
    g_ref[...] = (d_edges + mm_nt(back_pre, w1_ref[0:width, :])).astype(BF16)
    hot_s = one_hot(send_ref[...], table.shape[0])
    total = put_wide(hot_s, mm_nt(back_pre, w1_ref[width : 2 * width, :]))
    total = total + put_wide(hot_r, mm_nt(back_pre, w1_ref[2 * width : 3 * width, :]))
    part_ref[...] = total.reshape(part_ref.shape).astype(BF16)


def node_gradient_kernel(own_ref, halo_ref, share_ref, *refs):
    piece_refs, g_ref, total_ref = refs[:-2], refs[-2], refs[-1]
    arrived = None
    for slot, piece in enumerate(piece_refs):
        hot = one_hot(halo_ref[slot : slot + 1, :], own_ref.shape[0])
        part = mm(hot, piece[...])
        arrived = part if arrived is None else arrived + part
    total_ref[...] = own_ref[...] + arrived
    total_ref[0:COARSE_DEV, :] += jnp.sum(share_ref[...].astype(F32), 0)
    g_ref[...] = total_ref[...].astype(BF16)


VM = pl.BlockSpec(memory_space=pltpu.VMEM)
SM = pl.BlockSpec(memory_space=pltpu.SMEM)


def shape(dims, dtype):
    return jax.ShapeDtypeStruct(tuple(dims), dtype)


def call(kernel, name, ins, in_specs, outs, out_specs=None, scratch=(), grid=(), flops=0):
    moved = sum(a.size * a.dtype.itemsize for a in list(ins) + list(outs))
    return pl.pallas_call(
        kernel,
        out_shape=tuple(outs),
        grid=grid,
        in_specs=in_specs,
        out_specs=tuple([VM] * len(outs) if out_specs is None else out_specs),
        scratch_shapes=list(scratch),
        name=name,
        cost_estimate=pl.CostEstimate(flops=flops, bytes_accessed=moved, transcendentals=0),
        compiler_params=pltpu.CompilerParams(vmem_limit_bytes=VMEM_LIMIT),
    )(*ins)


def passed_along(block, axis, distance):
    count = lax.axis_size(axis)
    route = [((i - distance) % count, i) for i in range(count)]
    return lax.ppermute(block, axis, route)


def exchanged(block, axis, distance):
    return lax.ppermute(block, axis, [(i, i ^ distance) for i in range(lax.axis_size(axis))])


def exchanged_with_all(blocks, axis):
    return lax.all_to_all(blocks, axis, 0, 0)


def owners_sum(kept, given, axis):
    total = kept + exchanged(given, axis, 1).astype(F32)
    pairs = total.reshape((total.shape[0] // 2, 2) + total.shape[1:])
    total = pairs[:, 0] + exchanged(pairs[:, 1].astype(BF16), axis, 2).astype(F32)
    result = total[0]
    taken = [exchanged(total[k].astype(BF16), axis, 4 * k) for k in range(1, total.shape[0])]
    for block in taken:
        result = result + block.astype(F32)
    return result


def local(
    nodes,
    fine_edges,
    coarse_edges,
    fine_send,
    fine_recv,
    coarse_send,
    coarse_recv,
    halo_rows,
    edge_count,
    edge_w1,
    edge_w2,
    edge_gain,
    node_w1,
    node_w2,
    node_gain,
    d_nodes,
    d_fine,
    d_coarse,
):
    axis = "patch"
    peers = lax.axis_size(axis)
    own, width = nodes.shape
    fine = fine_edges.shape[0]
    coarse = coarse_edges.shape[0]
    halo = halo_rows[0]
    slots, tile = halo.shape
    hops = slots // 2
    offsets = list(range(1, hops + 1)) + [-k for k in range(1, hops + 1)]
    ordered = peers == 16 and all(
        w.shape[0] % (16 * peers) == 0 for w in (edge_w1, edge_w2, node_w1, node_w2)
    )
    me = lax.axis_index(axis).astype(jnp.int32).reshape(1)
    fs, fr = fine_send.reshape(1, fine), fine_recv.reshape(1, fine)
    cs, cr = coarse_send.reshape(1, coarse), coarse_recv.reshape(1, coarse)
    eg, ng = edge_gain.reshape(1, width), node_gain.reshape(1, width)
    every = shape((peers, COARSE_DEV, width), BF16)

    made = call(
        tiles_kernel, "tiles", (nodes, halo), [VM, VM],
        [shape((tile, width), BF16)] * slots + [every],
    )
    received = [passed_along(made[slot], axis, offset) for slot, offset in enumerate(offsets)]
    coarse_all = exchanged_with_all(made[-1], axis)

    def saved_shapes(rows):
        return [
            shape((rows, width), BF16), shape((rows, width), BF16), shape((rows, width), BF16),
            shape((rows, width), F32), shape((rows, width), F32), shape((rows, 128), F32),
        ]

    new_coarse, coarse_part, *coarse_saved = call(
        coarse_forward_kernel, "coarse_forward",
        (coarse_all, coarse_edges, cs, cr, edge_w1, edge_w2, eg), [VM] * 7,
        [shape((coarse, width), BF16), every] + saved_shapes(coarse),
        flops=2 * coarse * width * width * 4,
    )
    share = exchanged_with_all(coarse_part, axis)

    rows = 256 if fine % 256 == 0 else fine
    grid = (fine // rows,)

    def whole(dims):
        return pl.BlockSpec(dims, lambda i: (0,) * len(dims))

    by_rows = pl.BlockSpec((rows, width), lambda i: (i, 0))
    by_lanes = pl.BlockSpec((1, rows), lambda i: (0, i))
    std_rows = pl.BlockSpec((rows, 128), lambda i: (i, 0))
    saved_specs = [by_rows] * 5 + [std_rows]
    weight_specs = [whole(edge_w1.shape), whole(edge_w2.shape), whole(eg.shape)]
    space_rows = own + slots * tile
    new_fine, fine_agg, *fine_saved = call(
        functools.partial(fine_forward_kernel, slots=slots), "fine_forward",
        (edge_count, nodes, *received, fine_edges, fs, fr, edge_w1, edge_w2, eg),
        [SM, whole(nodes.shape)] + [whole((tile, width))] * slots + [by_rows, by_lanes, by_lanes] + weight_specs,
        [shape((fine, width), BF16), shape((own, width), F32)] + saved_shapes(fine),
        [by_rows, whole((own, width))] + saved_specs,
        scratch=[pltpu.VMEM((space_rows, width), BF16)],
        grid=grid,
        flops=2 * fine * width * (4 * width + space_rows + 3 * own),
    )

    def weight_shapes(w1, w2):
        if not ordered:
            return [shape(w1.shape, F32), shape(w2.shape, F32)], []
        block = (w1.shape[0] + w2.shape[0]) // peers
        outs = [shape((peers // 2, block, width), F32), shape((peers // 2, block, width), BF16)]
        return outs, [pltpu.VMEM(w1.shape, F32), pltpu.VMEM(w2.shape, F32)]

    def weight_sums(parts, w1, w2):
        if not ordered:
            return [lax.psum_scatter(g, axis, scatter_dimension=0, tiled=True) for g in parts]
        block = owners_sum(parts[0], parts[1], axis)
        cut = w1.shape[0] // peers
        return [block[:cut], block[cut:]]

    sum_shapes, sum_scratch = weight_shapes(node_w1, node_w2)
    new_nodes, base, dagg, dagg_spread, *node_parts = call(
        functools.partial(node_kernel, ordered=ordered), "node_both",
        (me, nodes, fine_agg, share, d_nodes, node_w1, node_w2, ng), [SM] + [VM] * 7,
        [shape((own, width), BF16), shape((own, width), F32), shape((own, width), F32), every] + sum_shapes,
        scratch=[pltpu.VMEM((own, width), F32)] + sum_scratch,
        flops=2 * own * width * width * 9,
    )
    dagg_all = exchanged_with_all(dagg_spread, axis)

    g_fine, fine_g1, fine_g2, own_grad, *pieces = call(
        fine_backward_kernel, "fine_backward",
        (edge_count, fine_edges, d_fine, fs, fr, edge_w1, edge_w2, eg, dagg, base, *fine_saved),
        [SM, by_rows, by_rows, by_lanes, by_lanes] + weight_specs
        + [whole((own, width))] * 2 + saved_specs,
        [shape((fine, width), BF16), shape(edge_w1.shape, F32), shape(edge_w2.shape, F32), shape((own, width), F32)]
        + [shape((tile, width), BF16)] * slots,
        [by_rows, whole(edge_w1.shape), whole(edge_w2.shape), whole((own, width))] + [whole((tile, width))] * slots,
        scratch=[pltpu.VMEM((space_rows, width), F32), pltpu.VMEM((own, width), F32)],
        grid=grid,
        flops=2 * fine * width * (8 * width + 2 * space_rows + 4 * own),
    )
    returned = [passed_along(pieces[slot], axis, -offset) for slot, offset in enumerate(offsets)]

    sum_shapes, sum_scratch = weight_shapes(edge_w1, edge_w2)
    g_coarse, coarse_part, *edge_parts = call(
        functools.partial(coarse_backward_kernel, ordered=ordered), "coarse_backward",
        (me, dagg_all, coarse_edges, d_coarse, cs, cr, edge_w1, edge_w2, eg, *coarse_saved, fine_g1, fine_g2),
        [SM] + [VM] * 16,
        [shape((coarse, width), BF16), every] + sum_shapes,
        scratch=sum_scratch,
        flops=2 * coarse * width * width * 8,
    )
    g_ew1, g_ew2 = weight_sums(edge_parts, edge_w1, edge_w2)
    g_nw1, g_nw2 = weight_sums(node_parts, node_w1, node_w2)
    coarse_share = exchanged_with_all(coarse_part, axis)
    (g_nodes,) = call(
        node_gradient_kernel, "node_gradient",
        (own_grad, halo, coarse_share, *returned), [VM] * (3 + slots),
        [shape((own, width), BF16)],
        scratch=[pltpu.VMEM((own, width), F32)],
        flops=2 * own * width * slots * tile,
    )
    return (new_nodes, new_fine, new_coarse, g_nodes, g_fine, g_coarse, g_ew1, g_ew2, g_nw1, g_nw2)


def solution(mesh):
    split = P(("groups", "patch"))
    rows = P(("groups", "patch"), None)
    return jax.shard_map(
        local,
        mesh=mesh,
        in_specs=(
            rows, rows, rows, split, split, split, split, P(("groups", "patch"), None, None), split,
            P(), P(), P(), P(), P(), P(), rows, rows, rows,
        ),
        out_specs=(rows,) * 10,
        check_vma=False,
    )
```

```python
import functools

import jax
import jax.numpy as jnp
from jax import lax
from jax.experimental import pallas as pl
from jax.experimental.pallas import tpu as pltpu
from jax.sharding import PartitionSpec as P

COARSE_DEV = 8
EPSILON = 1e-05
F32 = jnp.float32
BF16 = jnp.bfloat16
VMEM_LIMIT = 16 * 1024 * 1024


def mm(a, b):
    return lax.dot_general(a, b, (((1,), (0,)), ((), ())), preferred_element_type=F32)


def mm_nt(a, b):
    return lax.dot_general(a, b, (((1,), (1,)), ((), ())), preferred_element_type=F32)


def mm_tn(a, b):
    return lax.dot_general(a, b, (((0,), (0,)), ((), ())), preferred_element_type=F32)


def halves(value):
    high = value.astype(BF16)
    low = (value - high.astype(F32)).astype(BF16)
    return high, low


def one_hot(index, rows):
    row = lax.broadcasted_iota(jnp.int32, (rows, index.shape[1]), 0)
    return jnp.where(row == index, 1.0, 0.0).astype(BF16)


def pick(hot, table):
    return mm_tn(hot, table)


def pick_wide(hot, table):
    high, low = halves(table)
    return mm_tn(hot, high) + mm_tn(hot, low)


def put_wide(hot, rows):
    high, low = halves(rows)
    return mm(hot, high) + mm(hot, low)


def row_mean(value):
    return jnp.mean(value, axis=-1, keepdims=True)


def tail_of_forward(pre, second_w, gain):
    sigmoid = jax.nn.sigmoid(pre)
    hidden = (pre * sigmoid).astype(BF16)
    slope = sigmoid * (1.0 + pre * (1.0 - sigmoid))
    output = mm(hidden, second_w)
    centred = output - row_mean(output)
    inv_std = lax.rsqrt(row_mean(centred * centred) + EPSILON)
    normed = centred * inv_std
    return normed * gain, hidden, slope, normed, inv_std


def head_of_backward(cotan, second_w, gain, slope, normed, inv_std):
    scaled = cotan * gain
    back_out = inv_std * (scaled - row_mean(scaled) - normed * row_mean(scaled * normed))
    back_out = back_out.astype(BF16)
    back_pre = (mm_nt(back_out, second_w) * slope).astype(BF16)
    return back_out, back_pre


def tiles_kernel(nodes_ref, halo_ref, *outs):
    spread_ref = outs[-1]
    nodes = nodes_ref[...]
    for slot, out in enumerate(outs[:-1]):
        hot = one_hot(halo_ref[slot : slot + 1, :], nodes.shape[0])
        out[...] = pick(hot, nodes).astype(BF16)
    rows = nodes_ref[0:16, :].astype(F32)[:COARSE_DEV].astype(BF16)
    for peer in range(spread_ref.shape[0]):
        spread_ref[peer] = rows


def gathered(ref):
    value = ref[...].astype(F32)
    return value.reshape(value.shape[0] * value.shape[1], value.shape[2])


def coarse_forward_kernel(
    all_ref, edges_ref, send_ref, recv_ref, w1_ref, w2_ref, gain_ref,
    new_ref, part_ref, zs_ref, zr_ref, hidden_ref, slope_ref, normed_ref, std_ref,
):
    width = edges_ref.shape[1]
    table = gathered(all_ref).astype(BF16)
    hot_s = one_hot(send_ref[...], table.shape[0])
    hot_r = one_hot(recv_ref[...], table.shape[0])
    edges = edges_ref[...]
    zs = pick(hot_s, table).astype(BF16)
    zr = pick(hot_r, table).astype(BF16)
    pre = (
        mm(edges, w1_ref[0:width, :])
        + mm(zs, w1_ref[width : 2 * width, :])
        + mm(zr, w1_ref[2 * width : 3 * width, :])
    )
    message, hidden, slope, normed, inv_std = tail_of_forward(pre, w2_ref[...], gain_ref[...])
    total = put_wide(hot_r, message)
    part_ref[...] = total.reshape(part_ref.shape).astype(BF16)
    new_ref[...] = (edges.astype(F32) + message).astype(BF16)
    zs_ref[...] = zs
    zr_ref[...] = zr
    hidden_ref[...] = hidden
    slope_ref[...] = slope
    normed_ref[...] = normed
    std_ref[...] = jnp.broadcast_to(inv_std, std_ref.shape)


def fine_forward_kernel(count_ref, nodes_ref, *refs, slots, block):
    tile_refs = refs[:slots]
    (
        edges_ref, send_ref, recv_ref, w1_ref, w2_ref, gain_ref,
        new_ref, agg_ref, zs_ref, zr_ref, hidden_ref, slope_ref, normed_ref, std_ref, space_ref,
    ) = refs[slots:]
    count, width = edges_ref.shape
    own = nodes_ref.shape[0]
    tile = tile_refs[0].shape[0]
    space_ref[0:own, :] = nodes_ref[...]
    for slot in range(slots):
        space_ref[own + slot * tile : own + (slot + 1) * tile, :] = tile_refs[slot][...]
    for start in range(0, count, block):
        rows = slice(start, start + block)
        edges = edges_ref[rows, :]
        hot_s = one_hot(send_ref[:, rows], space_ref.shape[0])
        hot_r = one_hot(recv_ref[:, rows], own)
        zs = pick(hot_s, space_ref[...]).astype(BF16)
        zr = pick(hot_r, nodes_ref[...]).astype(BF16)
        pre = (
            mm(edges, w1_ref[0:width, :])
            + mm(zs, w1_ref[width : 2 * width, :])
            + mm(zr, w1_ref[2 * width : 3 * width, :])
        )
        message, hidden, slope, normed, inv_std = tail_of_forward(pre, w2_ref[...], gain_ref[...])
        place = start + lax.broadcasted_iota(jnp.int32, (block, 1), 0)
        message = jnp.where(place < count_ref[0], message, 0.0)
        arrived = put_wide(hot_r, message)
        agg_ref[...] = arrived if start == 0 else agg_ref[...] + arrived
        new_ref[rows, :] = (edges.astype(F32) + message).astype(BF16)
        zs_ref[rows, :] = zs
        zr_ref[rows, :] = zr
        hidden_ref[rows, :] = hidden
        slope_ref[rows, :] = slope
        normed_ref[rows, :] = normed
        std_ref[rows, :] = jnp.broadcast_to(inv_std, (block, std_ref.shape[1]))


def by_distance(me, peers, firsts, seconds, kept_ref, given_ref):
    rows1 = firsts.shape[0] // peers
    rows2 = seconds.shape[0] // peers
    for r in range(peers):
        to = jnp.bitwise_xor(me, r)
        first = firsts[pl.ds(pl.multiple_of(to * rows1, 16), rows1), :]
        second = seconds[pl.ds(pl.multiple_of(to * rows2, 16), rows2), :]
        out = given_ref if r % 2 else kept_ref
        out[r // 2, 0:rows1, :] = first.astype(out.dtype)
        out[r // 2, rows1 : rows1 + rows2, :] = second.astype(out.dtype)


def node_kernel(
    me_ref, nodes_ref, agg_ref, share_ref, d_ref, w1_ref, w2_ref, gain_ref,
    new_ref, base_ref, dagg_ref, spread_ref, *rest, ordered,
):
    if ordered:
        kept_ref, given_ref, total_ref, g1_ref, g2_ref = rest
    else:
        g1_ref, g2_ref, total_ref = rest
    width = nodes_ref.shape[1]
    total_ref[...] = agg_ref[...]
    total_ref[0:COARSE_DEV, :] += jnp.sum(share_ref[...].astype(F32), 0)
    nodes = nodes_ref[...]
    agg = total_ref[...].astype(BF16)
    pre = mm(nodes, w1_ref[0:width, :]) + mm(agg, w1_ref[width : 2 * width, :])
    update, hidden, slope, normed, inv_std = tail_of_forward(pre, w2_ref[...], gain_ref[...])
    new_ref[...] = (nodes.astype(F32) + update).astype(BF16)
    cotan = d_ref[...].astype(F32)
    back_out, back_pre = head_of_backward(cotan, w2_ref[...], gain_ref[...], slope, normed, inv_std)
    dagg = mm_nt(back_pre, w1_ref[width : 2 * width, :])
    dagg_ref[...] = dagg
    rows = dagg[:COARSE_DEV].astype(BF16)
    for peer in range(spread_ref.shape[0]):
        spread_ref[peer] = rows
    base_ref[...] = cotan + mm_nt(back_pre, w1_ref[0:width, :])
    g1_ref[0:width, :] = mm_tn(nodes, back_pre)
    g1_ref[width : 2 * width, :] = mm_tn(agg, back_pre)
    g2_ref[...] = mm_tn(hidden, back_out)
    if ordered:
        by_distance(me_ref[0], spread_ref.shape[0], g1_ref, g2_ref, kept_ref, given_ref)


def fine_backward_kernel(
    count_ref, edges_ref, d_ref, send_ref, recv_ref, w1_ref, w2_ref, gain_ref, dagg_ref, base_ref,
    zs_ref, zr_ref, hidden_ref, slope_ref, normed_ref, std_ref,
    g_ref, g1_ref, g2_ref, own_ref, *rest, block,
):
    piece_refs = rest[:-4]
    space_ref, received_ref, out_ref, pre_ref = rest[-4:]
    count, width = edges_ref.shape
    own = base_ref.shape[0]
    for start in range(0, count, block):
        rows = slice(start, start + block)
        hot_r = one_hot(recv_ref[:, rows], own)
        hot_s = one_hot(send_ref[:, rows], space_ref.shape[0])
        d_edges = d_ref[rows, :].astype(F32)
        place = start + lax.broadcasted_iota(jnp.int32, (block, 1), 0)
        cotan = jnp.where(place < count_ref[0], d_edges + pick_wide(hot_r, dagg_ref[...]), 0.0)
        back_out, back_pre = head_of_backward(
            cotan, w2_ref[...], gain_ref[...],
            slope_ref[rows, :], normed_ref[rows, :], std_ref[rows, 0:1],
        )
        out_ref[rows, :] = back_out
        pre_ref[rows, :] = back_pre
        g_ref[rows, :] = (d_edges + mm_nt(back_pre, w1_ref[0:width, :])).astype(BF16)
        sent = mm(hot_s, mm_nt(back_pre, w1_ref[width : 2 * width, :]).astype(BF16))
        received = mm(hot_r, mm_nt(back_pre, w1_ref[2 * width : 3 * width, :]).astype(BF16))
        space_ref[...] = sent if start == 0 else space_ref[...] + sent
        received_ref[...] = received if start == 0 else received_ref[...] + received
    own_ref[...] = base_ref[...] + received_ref[...] + space_ref[0:own, :]
    for slot, piece in enumerate(piece_refs):
        tile = piece.shape[0]
        piece[...] = space_ref[own + slot * tile : own + (slot + 1) * tile, :].astype(BF16)
    g2_ref[...] = mm_tn(hidden_ref[...], out_ref[...])
    g1_ref[0:width, :] = mm_tn(edges_ref[...], pre_ref[...])
    g1_ref[width : 2 * width, :] = mm_tn(zs_ref[...], pre_ref[...])
    g1_ref[2 * width : 3 * width, :] = mm_tn(zr_ref[...], pre_ref[...])


def coarse_backward_kernel(
    me_ref, all_ref, edges_ref, d_ref, send_ref, recv_ref, w1_ref, w2_ref, gain_ref,
    zs_ref, zr_ref, hidden_ref, slope_ref, normed_ref, std_ref, f1_ref, f2_ref,
    g_ref, part_ref, *rest, ordered,
):
    if ordered:
        kept_ref, given_ref, g1_ref, g2_ref = rest
    else:
        g1_ref, g2_ref = rest
    width = edges_ref.shape[1]
    table = gathered(all_ref).astype(BF16)
    hot_r = one_hot(recv_ref[...], table.shape[0])
    d_edges = d_ref[...].astype(F32)
    cotan = d_edges + pick(hot_r, table)
    back_out, back_pre = head_of_backward(
        cotan, w2_ref[...], gain_ref[...], slope_ref[...], normed_ref[...], std_ref[:, 0:1]
    )
    g2_ref[...] = f2_ref[...] + mm_tn(hidden_ref[...], back_out)
    g1_ref[0:width, :] = f1_ref[0:width, :] + mm_tn(edges_ref[...], back_pre)
    g1_ref[width : 2 * width, :] = f1_ref[width : 2 * width, :] + mm_tn(zs_ref[...], back_pre)
    g1_ref[2 * width : 3 * width, :] = f1_ref[2 * width : 3 * width, :] + mm_tn(zr_ref[...], back_pre)
    if ordered:
        by_distance(me_ref[0], part_ref.shape[0], g1_ref, g2_ref, kept_ref, given_ref)
    g_ref[...] = (d_edges + mm_nt(back_pre, w1_ref[0:width, :])).astype(BF16)
    hot_s = one_hot(send_ref[...], table.shape[0])
    total = put_wide(hot_s, mm_nt(back_pre, w1_ref[width : 2 * width, :]))
    total = total + put_wide(hot_r, mm_nt(back_pre, w1_ref[2 * width : 3 * width, :]))
    part_ref[...] = total.reshape(part_ref.shape).astype(BF16)


def node_gradient_kernel(own_ref, halo_ref, share_ref, *refs):
    piece_refs, g_ref, total_ref = refs[:-2], refs[-2], refs[-1]
    arrived = None
    for slot, piece in enumerate(piece_refs):
        hot = one_hot(halo_ref[slot : slot + 1, :], own_ref.shape[0])
        part = mm(hot, piece[...])
        arrived = part if arrived is None else arrived + part
    total_ref[...] = own_ref[...] + arrived
    total_ref[0:COARSE_DEV, :] += jnp.sum(share_ref[...].astype(F32), 0)
    g_ref[...] = total_ref[...].astype(BF16)


def first_halving_kernel(kept_ref, taken_ref, *refs):
    keep_ref, give_ref = refs if len(refs) == 2 else refs[1:3]
    for j in range(kept_ref.shape[0]):
        total = kept_ref[j] + taken_ref[j].astype(F32)
        if j % 2:
            give_ref[j // 2] = total.astype(BF16)
        else:
            keep_ref[j // 2] = total


def second_halving_kernel(kept_ref, taken_ref, keep_ref, *give_refs):
    for j in range(kept_ref.shape[0]):
        total = kept_ref[j] + taken_ref[j].astype(F32)
        if j:
            give_refs[j - 1][...] = total.astype(BF16)
        else:
            keep_ref[...] = total


def last_sum_kernel(kept_ref, *refs):
    taken, (first_ref, second_ref) = refs[:-2], refs[-2:]
    cut = first_ref.shape[0]
    total = kept_ref[...]
    for ref in taken:
        total = total + ref[...].astype(F32)
    first_ref[...] = total[:cut]
    second_ref[...] = total[cut:]


VM = pl.BlockSpec(memory_space=pltpu.VMEM)
SM = pl.BlockSpec(memory_space=pltpu.SMEM)
ANY = pl.BlockSpec(memory_space=pl.ANY)


def shape(dims, dtype):
    return jax.ShapeDtypeStruct(tuple(dims), dtype)


def call(kernel, name, ins, in_specs, outs, out_specs=None, scratch=(), aliases=None, flops=0):
    moved = sum(a.size * a.dtype.itemsize for a in list(ins) + list(outs))
    return pl.pallas_call(
        kernel,
        out_shape=tuple(outs),
        input_output_aliases=aliases or {},
        in_specs=in_specs,
        out_specs=tuple([VM] * len(outs) if out_specs is None else out_specs),
        scratch_shapes=list(scratch),
        name=name,
        cost_estimate=pl.CostEstimate(flops=flops, bytes_accessed=moved, transcendentals=0),
        compiler_params=pltpu.CompilerParams(vmem_limit_bytes=VMEM_LIMIT),
    )(*ins)


def passed_along(block, axis, distance):
    count = lax.axis_size(axis)
    route = [((i - distance) % count, i) for i in range(count)]
    return lax.ppermute(block, axis, route)


def exchanged(block, axis, distance):
    return lax.ppermute(block, axis, [(i, i ^ distance) for i in range(lax.axis_size(axis))])


def exchanged_with_all(blocks, axis):
    return lax.all_to_all(blocks, axis, 0, 0)


def first_halving(kept, taken, passing=None):
    half = (kept.shape[0] // 2,) + kept.shape[1:]
    outs = [shape(half, F32), shape(half, BF16)]
    if passing is None:
        return call(first_halving_kernel, "first_halving", (kept, taken), [VM, VM], outs)
    outs.append(shape(passing.shape, passing.dtype))
    return call(
        first_halving_kernel, "first_halving", (kept, taken, passing), [VM, VM, ANY],
        outs, [VM, VM, ANY], aliases={2: 2},
    )


def second_halving(kept, taken):
    block = kept.shape[1:]
    outs = [shape(block, F32)] + [shape(block, BF16)] * (kept.shape[0] - 1)
    return call(second_halving_kernel, "second_halving", (kept, taken), [VM, VM], outs)


def last_sum(kept, taken, first_rows):
    rows, width = kept.shape
    outs = [shape((first_rows, width), F32), shape((rows - first_rows, width), F32)]
    return call(last_sum_kernel, "last_sum", (kept, *taken), [VM] * (1 + len(taken)), outs)


def local(
    nodes,
    fine_edges,
    coarse_edges,
    fine_send,
    fine_recv,
    coarse_send,
    coarse_recv,
    halo_rows,
    edge_count,
    edge_w1,
    edge_w2,
    edge_gain,
    node_w1,
    node_w2,
    node_gain,
    d_nodes,
    d_fine,
    d_coarse,
):
    axis = "patch"
    peers = lax.axis_size(axis)
    own, width = nodes.shape
    fine = fine_edges.shape[0]
    coarse = coarse_edges.shape[0]
    halo = halo_rows[0]
    slots, tile = halo.shape
    hops = slots // 2
    offsets = list(range(1, hops + 1)) + [-k for k in range(1, hops + 1)]
    ordered = peers == 16 and all(
        w.shape[0] % (16 * peers) == 0 for w in (edge_w1, edge_w2, node_w1, node_w2)
    )
    me = lax.axis_index(axis).astype(jnp.int32).reshape(1)
    fs, fr = fine_send.reshape(1, fine), fine_recv.reshape(1, fine)
    cs, cr = coarse_send.reshape(1, coarse), coarse_recv.reshape(1, coarse)
    eg, ng = edge_gain.reshape(1, width), node_gain.reshape(1, width)
    every = shape((peers, COARSE_DEV, width), BF16)

    made = call(
        tiles_kernel, "tiles", (nodes, halo), [VM, VM],
        [shape((tile, width), BF16)] * slots + [every],
    )
    received = [passed_along(made[slot], axis, offset) for slot, offset in enumerate(offsets)]
    coarse_all = exchanged_with_all(made[-1], axis)

    def saved_shapes(rows):
        return [
            shape((rows, width), BF16), shape((rows, width), BF16), shape((rows, width), BF16),
            shape((rows, width), F32), shape((rows, width), F32), shape((rows, 128), F32),
        ]

    new_coarse, coarse_part, *coarse_saved = call(
        coarse_forward_kernel, "coarse_forward",
        (coarse_all, coarse_edges, cs, cr, edge_w1, edge_w2, eg), [VM] * 7,
        [shape((coarse, width), BF16), every] + saved_shapes(coarse),
        flops=2 * coarse * width * width * 4,
    )
    share = exchanged_with_all(coarse_part, axis)

    block = 256 if fine % 256 == 0 else fine
    space_rows = own + slots * tile
    new_fine, fine_agg, *fine_saved = call(
        functools.partial(fine_forward_kernel, slots=slots, block=block), "fine_forward",
        (edge_count, nodes, *received, fine_edges, fs, fr, edge_w1, edge_w2, eg),
        [SM] + [VM] * (slots + 7),
        [shape((fine, width), BF16), shape((own, width), F32)] + saved_shapes(fine),
        scratch=[pltpu.VMEM((space_rows, width), BF16)],
        flops=2 * fine * width * (4 * width + space_rows + 3 * own),
    )

    def weight_shapes(w1, w2):
        if not ordered:
            return [shape(w1.shape, F32), shape(w2.shape, F32)], []
        rows = (w1.shape[0] + w2.shape[0]) // peers
        outs = [shape((peers // 2, rows, width), F32), shape((peers // 2, rows, width), BF16)]
        return outs, [pltpu.VMEM(w1.shape, F32), pltpu.VMEM(w2.shape, F32)]

    sum_shapes, sum_scratch = weight_shapes(node_w1, node_w2)
    new_nodes, base, dagg, dagg_spread, *node_parts = call(
        functools.partial(node_kernel, ordered=ordered), "node_both",
        (me, nodes, fine_agg, share, d_nodes, node_w1, node_w2, ng), [SM] + [VM] * 7,
        [shape((own, width), BF16), shape((own, width), F32), shape((own, width), F32), every] + sum_shapes,
        scratch=[pltpu.VMEM((own, width), F32)] + sum_scratch,
        flops=2 * own * width * width * 9,
    )
    dagg_all = exchanged_with_all(dagg_spread, axis)
    if ordered:
        node_taken = exchanged(node_parts[1], axis, 1)

    g_fine, fine_g1, fine_g2, own_grad, *pieces = call(
        functools.partial(fine_backward_kernel, block=block), "fine_backward",
        (edge_count, fine_edges, d_fine, fs, fr, edge_w1, edge_w2, eg, dagg, base, *fine_saved),
        [SM] + [VM] * 15,
        [shape((fine, width), BF16), shape(edge_w1.shape, F32), shape(edge_w2.shape, F32), shape((own, width), F32)]
        + [shape((tile, width), BF16)] * slots,
        scratch=[
            pltpu.VMEM((space_rows, width), F32), pltpu.VMEM((own, width), F32),
            pltpu.VMEM((fine, width), BF16), pltpu.VMEM((fine, width), BF16),
        ],
        flops=2 * fine * width * (8 * width + 2 * space_rows + 4 * own),
    )
    if ordered:
        node_kept, node_given, fine_g2 = first_halving(node_parts[0], node_taken, fine_g2)
        node_taken = exchanged(node_given, axis, 2)
    returned = [passed_along(pieces[slot], axis, -offset) for slot, offset in enumerate(offsets)]

    sum_shapes, sum_scratch = weight_shapes(edge_w1, edge_w2)
    g_coarse, coarse_part, *edge_parts = call(
        functools.partial(coarse_backward_kernel, ordered=ordered), "coarse_backward",
        (me, dagg_all, coarse_edges, d_coarse, cs, cr, edge_w1, edge_w2, eg, *coarse_saved, fine_g1, fine_g2),
        [SM] + [VM] * 16,
        [shape((coarse, width), BF16), every] + sum_shapes,
        scratch=sum_scratch,
        flops=2 * coarse * width * width * 8,
    )
    if ordered:
        edge_taken = exchanged(edge_parts[1], axis, 1)
        edge_kept, edge_given, coarse_part = first_halving(edge_parts[0], edge_taken, coarse_part)
        edge_taken = exchanged(edge_given, axis, 2)
        node_kept, *given = second_halving(node_kept, node_taken)
        node_taken = [exchanged(part, axis, 4 * (k + 1)) for k, part in enumerate(given)]
        g_nw1, g_nw2 = last_sum(node_kept, node_taken, node_w1.shape[0] // peers)
        edge_kept, *given = second_halving(edge_kept, edge_taken)
        edge_taken = [exchanged(part, axis, 4 * (k + 1)) for k, part in enumerate(given)]
        g_ew1, g_ew2 = last_sum(edge_kept, edge_taken, edge_w1.shape[0] // peers)
    else:
        g_nw1, g_nw2, g_ew1, g_ew2 = [
            lax.psum_scatter(g, axis, scatter_dimension=0, tiled=True) for g in node_parts + edge_parts
        ]
    coarse_share = exchanged_with_all(coarse_part, axis)
    (g_nodes,) = call(
        node_gradient_kernel, "node_gradient",
        (own_grad, halo, coarse_share, *returned), [VM] * (3 + slots),
        [shape((own, width), BF16)],
        scratch=[pltpu.VMEM((own, width), F32)],
        flops=2 * own * width * slots * tile,
    )
    return (new_nodes, new_fine, new_coarse, g_nodes, g_fine, g_coarse, g_ew1, g_ew2, g_nw1, g_nw2)


def solution(mesh):
    split = P(("groups", "patch"))
    rows = P(("groups", "patch"), None)
    return jax.shard_map(
        local,
        mesh=mesh,
        in_specs=(
            rows, rows, rows, split, split, split, split, P(("groups", "patch"), None, None), split,
            P(), P(), P(), P(), P(), P(), rows, rows, rows,
        ),
        out_specs=(rows,) * 10,
        check_vma=False,
    )
```

```python
import functools

import jax
import jax.numpy as jnp
from jax import lax
from jax.experimental import pallas as pl
from jax.experimental.pallas import tpu as pltpu
from jax.sharding import PartitionSpec as P

COARSE_DEV = 8
EPSILON = 1e-05
F32 = jnp.float32
BF16 = jnp.bfloat16
VMEM_LIMIT = 60 * 1024 * 1024


def mm(a, b):
    return lax.dot_general(a, b, (((1,), (0,)), ((), ())), preferred_element_type=F32)


def mm_nt(a, b):
    return lax.dot_general(a, b, (((1,), (1,)), ((), ())), preferred_element_type=F32)


def mm_tn(a, b):
    return lax.dot_general(a, b, (((0,), (0,)), ((), ())), preferred_element_type=F32)


def halves(value):
    high = value.astype(BF16)
    low = (value - high.astype(F32)).astype(BF16)
    return high, low


def one_hot(index, rows):
    row = lax.broadcasted_iota(jnp.int32, (rows, index.shape[1]), 0)
    return jnp.where(row == index, 1.0, 0.0).astype(BF16)


def pick(hot, table):
    return mm_tn(hot, table)


def pick_wide(hot, table):
    high, low = halves(table)
    return mm_tn(hot, high) + mm_tn(hot, low)


def put_wide(hot, rows):
    high, low = halves(rows)
    return mm(hot, high) + mm(hot, low)


def row_mean(value):
    return jnp.mean(value, axis=-1, keepdims=True)


def tail_of_forward(pre, second_w, gain):
    sigmoid = jax.nn.sigmoid(pre)
    hidden = (pre * sigmoid).astype(BF16)
    slope = sigmoid * (1.0 + pre * (1.0 - sigmoid))
    output = mm(hidden, second_w)
    centred = output - row_mean(output)
    inv_std = lax.rsqrt(row_mean(centred * centred) + EPSILON)
    normed = centred * inv_std
    return normed * gain, hidden, slope, normed, inv_std


def head_of_backward(cotan, second_w, gain, slope, normed, inv_std):
    scaled = cotan * gain
    back_out = inv_std * (scaled - row_mean(scaled) - normed * row_mean(scaled * normed))
    back_out = back_out.astype(BF16)
    back_pre = (mm_nt(back_out, second_w) * slope).astype(BF16)
    return back_out, back_pre


def tiles_kernel(nodes_ref, halo_ref, *outs):
    spread_ref = outs[-1]
    nodes = nodes_ref[...]
    for slot, out in enumerate(outs[:-1]):
        hot = one_hot(halo_ref[slot : slot + 1, :], nodes.shape[0])
        out[...] = pick(hot, nodes).astype(BF16)
        out.done()
    rows = nodes_ref[0:16, :].astype(F32)[:COARSE_DEV].astype(BF16)
    for peer in range(spread_ref.shape[0]):
        spread_ref[peer] = rows


def gathered(ref):
    value = ref[...].astype(F32)
    return value.reshape(value.shape[0] * value.shape[1], value.shape[2])


def coarse_forward_kernel(
    all_ref, edges_ref, send_ref, recv_ref, w1_ref, w2_ref, gain_ref,
    new_ref, part_ref, zs_ref, zr_ref, hidden_ref, slope_ref, normed_ref, std_ref,
):
    width = edges_ref.shape[1]
    table = gathered(all_ref).astype(BF16)
    hot_s = one_hot(send_ref[...], table.shape[0])
    hot_r = one_hot(recv_ref[...], table.shape[0])
    edges = edges_ref[...]
    zs = pick(hot_s, table).astype(BF16)
    zr = pick(hot_r, table).astype(BF16)
    pre = (
        mm(edges, w1_ref[0:width, :])
        + mm(zs, w1_ref[width : 2 * width, :])
        + mm(zr, w1_ref[2 * width : 3 * width, :])
    )
    message, hidden, slope, normed, inv_std = tail_of_forward(pre, w2_ref[...], gain_ref[...])
    total = put_wide(hot_r, message)
    part_ref[...] = total.reshape(part_ref.shape).astype(BF16)
    part_ref.done()
    new_ref[...] = (edges.astype(F32) + message).astype(BF16)
    zs_ref[...] = zs
    zr_ref[...] = zr
    hidden_ref[...] = hidden
    slope_ref[...] = slope
    normed_ref[...] = normed
    std_ref[...] = jnp.broadcast_to(inv_std, std_ref.shape)


def fine_forward_kernel(count_ref, nodes_ref, *refs, slots, block):
    tile_refs = refs[:slots]
    (
        edges_ref, send_ref, recv_ref, w1_ref, w2_ref, gain_ref,
        new_ref, agg_ref, zs_ref, zr_ref, hidden_ref, slope_ref, normed_ref, std_ref, space_ref,
    ) = refs[slots:]
    count, width = edges_ref.shape
    own = nodes_ref.shape[0]
    tile = tile_refs[0].shape[0]
    space_ref[0:own, :] = nodes_ref[...]
    for slot in range(slots):
        space_ref[own + slot * tile : own + (slot + 1) * tile, :] = tile_refs[slot][...]
    for start in range(0, count, block):
        rows = slice(start, start + block)
        edges = edges_ref[rows, :]
        hot_s = one_hot(send_ref[:, rows], space_ref.shape[0])
        hot_r = one_hot(recv_ref[:, rows], own)
        zs = pick(hot_s, space_ref[...]).astype(BF16)
        zr = pick(hot_r, nodes_ref[...]).astype(BF16)
        pre = (
            mm(edges, w1_ref[0:width, :])
            + mm(zs, w1_ref[width : 2 * width, :])
            + mm(zr, w1_ref[2 * width : 3 * width, :])
        )
        message, hidden, slope, normed, inv_std = tail_of_forward(pre, w2_ref[...], gain_ref[...])
        place = start + lax.broadcasted_iota(jnp.int32, (block, 1), 0)
        message = jnp.where(place < count_ref[0], message, 0.0)
        arrived = put_wide(hot_r, message)
        agg_ref[...] = arrived if start == 0 else agg_ref[...] + arrived
        new_ref[rows, :] = (edges.astype(F32) + message).astype(BF16)
        zs_ref[rows, :] = zs
        zr_ref[rows, :] = zr
        hidden_ref[rows, :] = hidden
        slope_ref[rows, :] = slope
        normed_ref[rows, :] = normed
        std_ref[rows, :] = jnp.broadcast_to(inv_std, (block, std_ref.shape[1]))


def by_distance(me, peers, firsts, seconds, kept_ref, given_ref):
    rows1 = firsts.shape[0] // peers
    rows2 = seconds.shape[0] // peers
    for r in list(range(1, peers, 2)) + list(range(0, peers, 2)):
        if r == 0:
            given_ref.done()
        to = jnp.bitwise_xor(me, r)
        first = firsts[pl.ds(pl.multiple_of(to * rows1, 16), rows1), :]
        second = seconds[pl.ds(pl.multiple_of(to * rows2, 16), rows2), :]
        out = given_ref if r % 2 else kept_ref
        out[r // 2, 0:rows1, :] = first.astype(out.dtype)
        out[r // 2, rows1 : rows1 + rows2, :] = second.astype(out.dtype)


def node_kernel(
    me_ref, nodes_ref, agg_ref, share_ref, d_ref, w1_ref, w2_ref, gain_ref,
    new_ref, base_ref, dagg_ref, spread_ref, *rest, ordered,
):
    if ordered:
        kept_ref, given_ref, total_ref, g1_ref, g2_ref = rest
    else:
        g1_ref, g2_ref, total_ref = rest
    width = nodes_ref.shape[1]
    total_ref[...] = agg_ref[...]
    total_ref[0:COARSE_DEV, :] += jnp.sum(share_ref[...].astype(F32), 0)
    nodes = nodes_ref[...]
    agg = total_ref[...].astype(BF16)
    pre = mm(nodes, w1_ref[0:width, :]) + mm(agg, w1_ref[width : 2 * width, :])
    update, hidden, slope, normed, inv_std = tail_of_forward(pre, w2_ref[...], gain_ref[...])
    new_ref[...] = (nodes.astype(F32) + update).astype(BF16)
    cotan = d_ref[...].astype(F32)
    back_out, back_pre = head_of_backward(cotan, w2_ref[...], gain_ref[...], slope, normed, inv_std)
    dagg = mm_nt(back_pre, w1_ref[width : 2 * width, :])
    dagg_ref[...] = dagg
    rows = dagg[:COARSE_DEV].astype(BF16)
    for peer in range(spread_ref.shape[0]):
        spread_ref[peer] = rows
    base_ref[...] = cotan + mm_nt(back_pre, w1_ref[0:width, :])
    g1_ref[0:width, :] = mm_tn(nodes, back_pre)
    g1_ref[width : 2 * width, :] = mm_tn(agg, back_pre)
    g2_ref[...] = mm_tn(hidden, back_out)
    if ordered:
        by_distance(me_ref[0], spread_ref.shape[0], g1_ref, g2_ref, kept_ref, given_ref)


def fine_backward_kernel(
    count_ref, edges_ref, d_ref, send_ref, recv_ref, w1_ref, w2_ref, gain_ref, dagg_ref, base_ref,
    zs_ref, zr_ref, hidden_ref, slope_ref, normed_ref, std_ref,
    g_ref, g1_ref, g2_ref, own_ref, *rest, block,
):
    piece_refs = rest[:-4]
    space_ref, received_ref, out_ref, pre_ref = rest[-4:]
    count, width = edges_ref.shape
    own = base_ref.shape[0]
    for start in range(0, count, block):
        rows = slice(start, start + block)
        hot_r = one_hot(recv_ref[:, rows], own)
        hot_s = one_hot(send_ref[:, rows], space_ref.shape[0])
        d_edges = d_ref[rows, :].astype(F32)
        place = start + lax.broadcasted_iota(jnp.int32, (block, 1), 0)
        cotan = jnp.where(place < count_ref[0], d_edges + pick_wide(hot_r, dagg_ref[...]), 0.0)
        back_out, back_pre = head_of_backward(
            cotan, w2_ref[...], gain_ref[...],
            slope_ref[rows, :], normed_ref[rows, :], std_ref[rows, 0:1],
        )
        out_ref[rows, :] = back_out
        pre_ref[rows, :] = back_pre
        g_ref[rows, :] = (d_edges + mm_nt(back_pre, w1_ref[0:width, :])).astype(BF16)
        sent = mm(hot_s, mm_nt(back_pre, w1_ref[width : 2 * width, :]).astype(BF16))
        received = mm(hot_r, mm_nt(back_pre, w1_ref[2 * width : 3 * width, :]).astype(BF16))
        space_ref[...] = sent if start == 0 else space_ref[...] + sent
        received_ref[...] = received if start == 0 else received_ref[...] + received
    g_ref.done()
    own_ref[...] = base_ref[...] + received_ref[...] + space_ref[0:own, :]
    own_ref.done()
    for slot, piece in enumerate(piece_refs):
        tile = piece.shape[0]
        piece[...] = space_ref[own + slot * tile : own + (slot + 1) * tile, :].astype(BF16)
        piece.done()
    g2_ref[...] = mm_tn(hidden_ref[...], out_ref[...])
    g2_ref.done()
    g1_ref[0:width, :] = mm_tn(edges_ref[...], pre_ref[...])
    g1_ref[width : 2 * width, :] = mm_tn(zs_ref[...], pre_ref[...])
    g1_ref[2 * width : 3 * width, :] = mm_tn(zr_ref[...], pre_ref[...])


def coarse_backward_kernel(
    me_ref, all_ref, edges_ref, d_ref, send_ref, recv_ref, w1_ref, w2_ref, gain_ref,
    zs_ref, zr_ref, hidden_ref, slope_ref, normed_ref, std_ref, f1_ref, f2_ref,
    g_ref, part_ref, *rest, ordered,
):
    if ordered:
        kept_ref, given_ref, g1_ref, g2_ref = rest
    else:
        g1_ref, g2_ref = rest
    width = edges_ref.shape[1]
    table = gathered(all_ref).astype(BF16)
    hot_r = one_hot(recv_ref[...], table.shape[0])
    d_edges = d_ref[...].astype(F32)
    cotan = d_edges + pick(hot_r, table)
    back_out, back_pre = head_of_backward(
        cotan, w2_ref[...], gain_ref[...], slope_ref[...], normed_ref[...], std_ref[:, 0:1]
    )
    g2_ref[...] = f2_ref[...] + mm_tn(hidden_ref[...], back_out)
    g1_ref[0:width, :] = f1_ref[0:width, :] + mm_tn(edges_ref[...], back_pre)
    g1_ref[width : 2 * width, :] = f1_ref[width : 2 * width, :] + mm_tn(zs_ref[...], back_pre)
    g1_ref[2 * width : 3 * width, :] = f1_ref[2 * width : 3 * width, :] + mm_tn(zr_ref[...], back_pre)
    if ordered:
        by_distance(me_ref[0], part_ref.shape[0], g1_ref, g2_ref, kept_ref, given_ref)
    g_ref[...] = (d_edges + mm_nt(back_pre, w1_ref[0:width, :])).astype(BF16)
    hot_s = one_hot(send_ref[...], table.shape[0])
    total = put_wide(hot_s, mm_nt(back_pre, w1_ref[width : 2 * width, :]))
    total = total + put_wide(hot_r, mm_nt(back_pre, w1_ref[2 * width : 3 * width, :]))
    part_ref[...] = total.reshape(part_ref.shape).astype(BF16)


def node_gradient_kernel(own_ref, halo_ref, share_ref, *refs):
    piece_refs, g_ref, total_ref = refs[:-2], refs[-2], refs[-1]
    arrived = None
    for slot, piece in enumerate(piece_refs):
        hot = one_hot(halo_ref[slot : slot + 1, :], own_ref.shape[0])
        part = mm(hot, piece[...])
        arrived = part if arrived is None else arrived + part
    total_ref[...] = own_ref[...] + arrived
    total_ref[0:COARSE_DEV, :] += jnp.sum(share_ref[...].astype(F32), 0)
    g_ref[...] = total_ref[...].astype(BF16)


def first_halving_kernel(kept_ref, taken_ref, *refs):
    keep_ref, give_ref = refs
    for j in range(kept_ref.shape[0]):
        total = kept_ref[j] + taken_ref[j].astype(F32)
        if j % 2:
            give_ref[j // 2] = total.astype(BF16)
        else:
            keep_ref[j // 2] = total


def second_halving_kernel(kept_ref, taken_ref, keep_ref, *give_refs):
    for j in range(kept_ref.shape[0]):
        total = kept_ref[j] + taken_ref[j].astype(F32)
        if j:
            give_refs[j - 1][...] = total.astype(BF16)
        else:
            keep_ref[...] = total


def last_sum_kernel(kept_ref, *refs):
    taken, (first_ref, second_ref) = refs[:-2], refs[-2:]
    cut = first_ref.shape[0]
    total = kept_ref[...]
    for ref in taken:
        total = total + ref[...].astype(F32)
    first_ref[...] = total[:cut]
    second_ref[...] = total[cut:]


VM = pl.BlockSpec(memory_space=pltpu.VMEM)
SM = pl.BlockSpec(memory_space=pltpu.SMEM)
ANY = pl.BlockSpec(memory_space=pl.ANY)


def shape(dims, dtype):
    return jax.ShapeDtypeStruct(tuple(dims), dtype)


class Fetched:
    def __init__(self, source, buffer, semaphore):
        self.buffer = buffer
        self.shape = buffer.shape
        self.copy = pltpu.make_async_copy(source, buffer, semaphore)
        self.copy.start()
        self.waiting = True

    def ready(self):
        if self.waiting:
            self.copy.wait()
            self.waiting = False

    def __getitem__(self, index):
        self.ready()
        return self.buffer[index]


class Stored:
    def __init__(self, target, buffer, semaphore):
        self.buffer = buffer
        self.shape = buffer.shape
        self.dtype = buffer.dtype
        self.copy = pltpu.make_async_copy(buffer, target, semaphore)
        self.started = False

    def __getitem__(self, index):
        return self.buffer[index]

    def __setitem__(self, index, value):
        self.buffer[index] = value

    def done(self):
        if not self.started:
            self.copy.start()
            self.started = True


def staged_kernel(body, in_specs, out_specs, *refs):
    ins, outs = refs[: len(in_specs)], refs[len(in_specs) : len(in_specs) + len(out_specs)]
    rest = refs[len(in_specs) + len(out_specs) :]
    fetched, stored, taken = [], [], 0
    semaphores, buffers = rest[0], rest[1:]
    for ref, spec in zip(ins, in_specs):
        if spec is VM:
            fetched.append(Fetched(ref, buffers[taken], semaphores.at[taken]))
            taken += 1
        elif spec is SM:
            fetched.append(ref)
    for ref, spec in zip(outs, out_specs):
        if spec is VM:
            stored.append(Stored(ref, buffers[taken], semaphores.at[taken]))
            taken += 1
    body(*fetched, *stored, *buffers[taken:])
    for ref in fetched:
        if isinstance(ref, Fetched):
            ref.ready()
    for ref in stored:
        ref.done()
    for ref in stored:
        ref.copy.wait()


def call(kernel, name, ins, in_specs, outs, out_specs=None, scratch=(), aliases=None, flops=0):
    out_specs = [VM] * len(outs) if out_specs is None else out_specs
    moved = sum(a.size * a.dtype.itemsize for a in list(ins) + list(outs))
    staged = [a for a, spec in zip(list(ins) + list(outs), list(in_specs) + list(out_specs)) if spec is VM]
    buffers = [pltpu.VMEM(a.shape, a.dtype) for a in staged]
    return pl.pallas_call(
        functools.partial(staged_kernel, kernel, in_specs, out_specs),
        out_shape=tuple(outs),
        input_output_aliases=aliases or {},
        in_specs=[SM if spec is SM else ANY for spec in in_specs],
        out_specs=tuple([ANY] * len(outs)),
        scratch_shapes=[pltpu.SemaphoreType.DMA((len(buffers),))] + buffers + list(scratch),
        name=name,
        cost_estimate=pl.CostEstimate(flops=flops, bytes_accessed=moved, transcendentals=0),
        compiler_params=pltpu.CompilerParams(vmem_limit_bytes=VMEM_LIMIT),
    )(*ins)


def passed_along(block, axis, distance):
    count = lax.axis_size(axis)
    route = [((i - distance) % count, i) for i in range(count)]
    return lax.ppermute(block, axis, route)


def exchanged(block, axis, distance):
    return lax.ppermute(block, axis, [(i, i ^ distance) for i in range(lax.axis_size(axis))])


def exchanged_with_all(blocks, axis):
    return lax.all_to_all(blocks, axis, 0, 0)


def first_halving(kept, taken, passing=None):
    half = (kept.shape[0] // 2,) + kept.shape[1:]
    outs = [shape(half, F32), shape(half, BF16)]
    if passing is None:
        return call(first_halving_kernel, "first_halving", (kept, taken), [VM, VM], outs)
    outs.append(shape(passing.shape, passing.dtype))
    return call(
        first_halving_kernel, "first_halving", (kept, taken, passing), [VM, VM, ANY],
        outs, [VM, VM, ANY], aliases={2: 2},
    )


def second_halving(kept, taken):
    block = kept.shape[1:]
    outs = [shape(block, F32)] + [shape(block, BF16)] * (kept.shape[0] - 1)
    return call(second_halving_kernel, "second_halving", (kept, taken), [VM, VM], outs)


def last_sum(kept, taken, first_rows):
    rows, width = kept.shape
    outs = [shape((first_rows, width), F32), shape((rows - first_rows, width), F32)]
    return call(last_sum_kernel, "last_sum", (kept, *taken), [VM] * (1 + len(taken)), outs)


def local(
    nodes,
    fine_edges,
    coarse_edges,
    fine_send,
    fine_recv,
    coarse_send,
    coarse_recv,
    halo_rows,
    edge_count,
    edge_w1,
    edge_w2,
    edge_gain,
    node_w1,
    node_w2,
    node_gain,
    d_nodes,
    d_fine,
    d_coarse,
):
    axis = "patch"
    peers = lax.axis_size(axis)
    own, width = nodes.shape
    fine = fine_edges.shape[0]
    coarse = coarse_edges.shape[0]
    halo = halo_rows[0]
    slots, tile = halo.shape
    hops = slots // 2
    offsets = list(range(1, hops + 1)) + [-k for k in range(1, hops + 1)]
    ordered = peers == 16 and all(
        w.shape[0] % (16 * peers) == 0 for w in (edge_w1, edge_w2, node_w1, node_w2)
    )
    me = lax.axis_index(axis).astype(jnp.int32).reshape(1)
    fs, fr = fine_send.reshape(1, fine), fine_recv.reshape(1, fine)
    cs, cr = coarse_send.reshape(1, coarse), coarse_recv.reshape(1, coarse)
    eg, ng = edge_gain.reshape(1, width), node_gain.reshape(1, width)
    every = shape((peers, COARSE_DEV, width), BF16)

    made = call(
        tiles_kernel, "tiles", (nodes, halo), [VM, VM],
        [shape((tile, width), BF16)] * slots + [every],
    )
    received = [passed_along(made[slot], axis, offset) for slot, offset in enumerate(offsets)]
    coarse_all = exchanged_with_all(made[-1], axis)

    def saved_shapes(rows):
        return [
            shape((rows, width), BF16), shape((rows, width), BF16), shape((rows, width), BF16),
            shape((rows, width), F32), shape((rows, width), F32), shape((rows, 128), F32),
        ]

    new_coarse, coarse_part, *coarse_saved = call(
        coarse_forward_kernel, "coarse_forward",
        (coarse_all, coarse_edges, cs, cr, edge_w1, edge_w2, eg), [VM] * 7,
        [shape((coarse, width), BF16), every] + saved_shapes(coarse),
        flops=2 * coarse * width * width * 4,
    )
    share = exchanged_with_all(coarse_part, axis)

    block = 256 if fine % 256 == 0 else fine
    space_rows = own + slots * tile
    new_fine, fine_agg, *fine_saved = call(
        functools.partial(fine_forward_kernel, slots=slots, block=block), "fine_forward",
        (edge_count, nodes, *received, fine_edges, fs, fr, edge_w1, edge_w2, eg),
        [SM] + [VM] * (slots + 7),
        [shape((fine, width), BF16), shape((own, width), F32)] + saved_shapes(fine),
        scratch=[pltpu.VMEM((space_rows, width), BF16)],
        flops=2 * fine * width * (4 * width + space_rows + 3 * own),
    )

    def weight_shapes(w1, w2):
        if not ordered:
            return [shape(w1.shape, F32), shape(w2.shape, F32)], []
        rows = (w1.shape[0] + w2.shape[0]) // peers
        outs = [shape((peers // 2, rows, width), F32), shape((peers // 2, rows, width), BF16)]
        return outs, [pltpu.VMEM(w1.shape, F32), pltpu.VMEM(w2.shape, F32)]

    sum_shapes, sum_scratch = weight_shapes(node_w1, node_w2)
    new_nodes, base, dagg, dagg_spread, *node_parts = call(
        functools.partial(node_kernel, ordered=ordered), "node_both",
        (me, nodes, fine_agg, share, d_nodes, node_w1, node_w2, ng), [SM] + [VM] * 7,
        [shape((own, width), BF16), shape((own, width), F32), shape((own, width), F32), every] + sum_shapes,
        scratch=[pltpu.VMEM((own, width), F32)] + sum_scratch,
        flops=2 * own * width * width * 9,
    )
    dagg_all = exchanged_with_all(dagg_spread, axis)
    if ordered:
        node_taken = exchanged(node_parts[1], axis, 1)
        node_kept, node_given, base = first_halving(node_parts[0], node_taken, base)
        node_taken = exchanged(node_given, axis, 2)

    g_fine, fine_g1, fine_g2, own_grad, *pieces = call(
        functools.partial(fine_backward_kernel, block=block), "fine_backward",
        (edge_count, fine_edges, d_fine, fs, fr, edge_w1, edge_w2, eg, dagg, base, *fine_saved),
        [SM] + [VM] * 15,
        [shape((fine, width), BF16), shape(edge_w1.shape, F32), shape(edge_w2.shape, F32), shape((own, width), F32)]
        + [shape((tile, width), BF16)] * slots,
        scratch=[
            pltpu.VMEM((space_rows, width), F32), pltpu.VMEM((own, width), F32),
            pltpu.VMEM((fine, width), BF16), pltpu.VMEM((fine, width), BF16),
        ],
        flops=2 * fine * width * (8 * width + 2 * space_rows + 4 * own),
    )
    returned = [passed_along(pieces[slot], axis, -offset) for slot, offset in enumerate(offsets)]

    sum_shapes, sum_scratch = weight_shapes(edge_w1, edge_w2)
    g_coarse, coarse_part, *edge_parts = call(
        functools.partial(coarse_backward_kernel, ordered=ordered), "coarse_backward",
        (me, dagg_all, coarse_edges, d_coarse, cs, cr, edge_w1, edge_w2, eg, *coarse_saved, fine_g1, fine_g2),
        [SM] + [VM] * 16,
        [shape((coarse, width), BF16), every] + sum_shapes,
        scratch=sum_scratch,
        flops=2 * coarse * width * width * 8,
    )
    if ordered:
        edge_taken = exchanged(edge_parts[1], axis, 1)
        edge_kept, edge_given, coarse_part = first_halving(edge_parts[0], edge_taken, coarse_part)
        edge_taken = exchanged(edge_given, axis, 2)
        node_kept, *given = second_halving(node_kept, node_taken)
        node_taken = [exchanged(part, axis, 4 * (k + 1)) for k, part in enumerate(given)]
        g_nw1, g_nw2 = last_sum(node_kept, node_taken, node_w1.shape[0] // peers)
        edge_kept, *given = second_halving(edge_kept, edge_taken)
        edge_taken = [exchanged(part, axis, 4 * (k + 1)) for k, part in enumerate(given)]
        g_ew1, g_ew2 = last_sum(edge_kept, edge_taken, edge_w1.shape[0] // peers)
    else:
        g_nw1, g_nw2, g_ew1, g_ew2 = [
            lax.psum_scatter(g, axis, scatter_dimension=0, tiled=True) for g in node_parts + edge_parts
        ]
    coarse_share = exchanged_with_all(coarse_part, axis)
    (g_nodes,) = call(
        node_gradient_kernel, "node_gradient",
        (own_grad, halo, coarse_share, *returned), [VM] * (3 + slots),
        [shape((own, width), BF16)],
        scratch=[pltpu.VMEM((own, width), F32)],
        flops=2 * own * width * slots * tile,
    )
    return (new_nodes, new_fine, new_coarse, g_nodes, g_fine, g_coarse, g_ew1, g_ew2, g_nw1, g_nw2)


def solution(mesh):
    split = P(("groups", "patch"))
    rows = P(("groups", "patch"), None)
    return jax.shard_map(
        local,
        mesh=mesh,
        in_specs=(
            rows, rows, rows, split, split, split, split, P(("groups", "patch"), None, None), split,
            P(), P(), P(), P(), P(), P(), rows, rows, rows,
        ),
        out_specs=(rows,) * 10,
        check_vma=False,
    )
```

```python
import functools

import jax
import jax.numpy as jnp
from jax import lax
from jax.experimental import pallas as pl
from jax.experimental.pallas import tpu as pltpu
from jax.sharding import PartitionSpec as P

COARSE_DEV = 8
EPSILON = 1e-05
F32 = jnp.float32
BF16 = jnp.bfloat16
VMEM_LIMIT = 60 * 1024 * 1024
SMALL_LIMIT = 16 * 1024 * 1024


def mm(a, b):
    return lax.dot_general(a, b, (((1,), (0,)), ((), ())), preferred_element_type=F32)


def mm_nt(a, b):
    return lax.dot_general(a, b, (((1,), (1,)), ((), ())), preferred_element_type=F32)


def mm_tn(a, b):
    return lax.dot_general(a, b, (((0,), (0,)), ((), ())), preferred_element_type=F32)


def halves(value):
    high = value.astype(BF16)
    low = (value - high.astype(F32)).astype(BF16)
    return high, low


def one_hot(index, rows):
    row = lax.broadcasted_iota(jnp.int32, (rows, index.shape[1]), 0)
    return jnp.where(row == index, 1.0, 0.0).astype(BF16)


def pick(hot, table):
    return mm_tn(hot, table)


def pick_wide(hot, table):
    high, low = halves(table)
    return mm_tn(hot, high) + mm_tn(hot, low)


def put_wide(hot, rows):
    high, low = halves(rows)
    return mm(hot, high) + mm(hot, low)


def row_mean(value):
    return jnp.mean(value, axis=-1, keepdims=True)


def tail_of_forward(pre, second_w, gain):
    sigmoid = jax.nn.sigmoid(pre)
    hidden = (pre * sigmoid).astype(BF16)
    slope = sigmoid * (1.0 + pre * (1.0 - sigmoid))
    output = mm(hidden, second_w)
    centred = output - row_mean(output)
    inv_std = lax.rsqrt(row_mean(centred * centred) + EPSILON)
    normed = centred * inv_std
    return normed * gain, hidden, slope, normed, inv_std


def head_of_backward(cotan, second_w, gain, slope, normed, inv_std):
    scaled = cotan * gain
    back_out = inv_std * (scaled - row_mean(scaled) - normed * row_mean(scaled * normed))
    back_out = back_out.astype(BF16)
    back_pre = (mm_nt(back_out, second_w) * slope).astype(BF16)
    return back_out, back_pre


def tiles_kernel(nodes_ref, halo_ref, *outs):
    spread_ref = outs[-1]
    nodes = nodes_ref[...]
    for slot, out in enumerate(outs[:-1]):
        hot = one_hot(halo_ref[slot : slot + 1, :], nodes.shape[0])
        out[...] = pick(hot, nodes).astype(BF16)
        out.done()
    rows = nodes_ref[0:16, :].astype(F32)[:COARSE_DEV].astype(BF16)
    for peer in range(spread_ref.shape[0]):
        spread_ref[peer] = rows


def gathered(ref):
    value = ref[...].astype(F32)
    return value.reshape(value.shape[0] * value.shape[1], value.shape[2])


def coarse_forward_kernel(
    all_ref, edges_ref, send_ref, recv_ref, w1_ref, w2_ref, gain_ref,
    new_ref, part_ref, zs_ref, zr_ref, hidden_ref, slope_ref, normed_ref, std_ref,
):
    width = edges_ref.shape[1]
    table = gathered(all_ref).astype(BF16)
    hot_s = one_hot(send_ref[...], table.shape[0])
    hot_r = one_hot(recv_ref[...], table.shape[0])
    edges = edges_ref[...]
    zs = pick(hot_s, table).astype(BF16)
    zr = pick(hot_r, table).astype(BF16)
    pre = (
        mm(edges, w1_ref[0:width, :])
        + mm(zs, w1_ref[width : 2 * width, :])
        + mm(zr, w1_ref[2 * width : 3 * width, :])
    )
    message, hidden, slope, normed, inv_std = tail_of_forward(pre, w2_ref[...], gain_ref[...])
    total = put_wide(hot_r, message)
    part_ref[...] = total.reshape(part_ref.shape).astype(BF16)
    part_ref.done()
    new_ref[...] = (edges.astype(F32) + message).astype(BF16)
    zs_ref[...] = zs
    zr_ref[...] = zr
    hidden_ref[...] = hidden
    slope_ref[...] = slope.astype(BF16)
    normed_ref[...] = normed.astype(BF16)
    std_ref[...] = jnp.broadcast_to(inv_std, std_ref.shape)


def fine_forward_kernel(count_ref, nodes_ref, *refs, slots, block):
    tile_refs = refs[:slots]
    (
        edges_ref, send_ref, recv_ref, w1_ref, w2_ref, gain_ref,
        new_ref, agg_ref, zs_ref, zr_ref, hidden_ref, slope_ref, normed_ref, std_ref, space_ref,
    ) = refs[slots:]
    count, width = edges_ref.shape
    own = nodes_ref.shape[0]
    tile = tile_refs[0].shape[0]
    space_ref[0:own, :] = nodes_ref[...]
    for slot in range(slots):
        space_ref[own + slot * tile : own + (slot + 1) * tile, :] = tile_refs[slot][...]
    for start in range(0, count, block):
        rows = slice(start, start + block)
        edges = edges_ref[rows, :]
        hot_s = one_hot(send_ref[:, rows], space_ref.shape[0])
        hot_r = one_hot(recv_ref[:, rows], own)
        zs = pick(hot_s, space_ref[...]).astype(BF16)
        zr = pick(hot_r, nodes_ref[...]).astype(BF16)
        pre = (
            mm(edges, w1_ref[0:width, :])
            + mm(zs, w1_ref[width : 2 * width, :])
            + mm(zr, w1_ref[2 * width : 3 * width, :])
        )
        message, hidden, slope, normed, inv_std = tail_of_forward(pre, w2_ref[...], gain_ref[...])
        place = start + lax.broadcasted_iota(jnp.int32, (block, 1), 0)
        message = jnp.where(place < count_ref[0], message, 0.0)
        arrived = put_wide(hot_r, message)
        agg_ref[...] = arrived if start == 0 else agg_ref[...] + arrived
        new_ref[rows, :] = (edges.astype(F32) + message).astype(BF16)
        zs_ref[rows, :] = zs
        zr_ref[rows, :] = zr
        hidden_ref[rows, :] = hidden
        slope_ref[rows, :] = slope.astype(BF16)
        normed_ref[rows, :] = normed.astype(BF16)
        std_ref[rows, :] = jnp.broadcast_to(inv_std, (block, std_ref.shape[1]))
        for ref in (new_ref, zs_ref, zr_ref, hidden_ref, slope_ref, normed_ref, std_ref):
            ref.done(rows)


def by_distance(me, peers, sums, kept_ref, given_ref):
    for r in list(range(1, peers, 2)) + list(range(0, peers, 2)):
        if r == 0:
            given_ref.done()
        to = jnp.bitwise_xor(me, r)
        out = given_ref if r % 2 else kept_ref
        place = 0
        for total in sums:
            rows = total.shape[0] // peers
            part = total[pl.ds(pl.multiple_of(to * rows, 8), rows), :]
            if rows % 16:
                part = jnp.concatenate([part, jnp.zeros((-rows % 16, part.shape[1]), F32)], 0)
            out[r // 2, place : place + part.shape[0], :] = part.astype(BF16)
            place += part.shape[0]


def node_kernel(
    me_ref, nodes_ref, agg_ref, share_ref, d_ref, w1_ref, w2_ref, gain_ref,
    new_ref, base_ref, dagg_ref, spread_ref, *rest, ordered,
):
    if ordered:
        kept_ref, given_ref, total_ref, g1_ref, g2_ref = rest
    else:
        g1_ref, g2_ref, total_ref = rest
    width = nodes_ref.shape[1]
    total_ref[...] = agg_ref[...]
    total_ref[0:COARSE_DEV, :] += jnp.sum(share_ref[...].astype(F32), 0)
    nodes = nodes_ref[...]
    agg = total_ref[...].astype(BF16)
    pre = mm(nodes, w1_ref[0:width, :]) + mm(agg, w1_ref[width : 2 * width, :])
    update, hidden, slope, normed, inv_std = tail_of_forward(pre, w2_ref[...], gain_ref[...])
    new_ref[...] = (nodes.astype(F32) + update).astype(BF16)
    cotan = d_ref[...].astype(F32)
    back_out, back_pre = head_of_backward(cotan, w2_ref[...], gain_ref[...], slope, normed, inv_std)
    dagg = mm_nt(back_pre, w1_ref[width : 2 * width, :])
    dagg_ref[...] = dagg.astype(BF16)
    rows = dagg[:COARSE_DEV].astype(BF16)
    for peer in range(spread_ref.shape[0]):
        spread_ref[peer] = rows
    base_ref[...] = cotan + mm_nt(back_pre, w1_ref[0:width, :])
    g1_ref[0:width, :] = mm_tn(nodes, back_pre)
    g1_ref[width : 2 * width, :] = mm_tn(agg, back_pre)
    g2_ref[...] = mm_tn(hidden, back_out)
    if ordered:
        by_distance(me_ref[0], spread_ref.shape[0], (g1_ref, g2_ref), kept_ref, given_ref)


def fine_backward_kernel(
    count_ref, recv_ref, dagg_ref, d_ref, gain_ref, std_ref, normed_ref, w2_ref, slope_ref,
    w1_ref, send_ref, base_ref,
    out_ref, pre_ref, g_ref, own_ref, *rest, block,
):
    piece_refs, space_ref = rest[:-1], rest[-1]
    count, width = d_ref.shape
    own = base_ref.shape[0]
    received = None
    for start in range(0, count, block):
        rows = slice(start, start + block)
        hot_r = one_hot(recv_ref[:, rows], own)
        d_edges = d_ref[rows, :].astype(F32)
        place = start + lax.broadcasted_iota(jnp.int32, (block, 1), 0)
        cotan = jnp.where(place < count_ref[0], d_edges + pick(hot_r, dagg_ref[...]), 0.0)
        back_out, back_pre = head_of_backward(
            cotan, w2_ref[...], gain_ref[...], slope_ref[rows, :].astype(F32),
            normed_ref[rows, :].astype(F32), std_ref[rows, 0:1],
        )
        out_ref[rows, :] = back_out
        pre_ref[rows, :] = back_pre
        out_ref.done(rows)
        pre_ref.done(rows)
        g_ref[rows, :] = (d_edges + mm_nt(back_pre, w1_ref[0:width, :])).astype(BF16)
        g_ref.done(rows)
        dz_send = mm_nt(back_pre, w1_ref[width : 2 * width, :]).astype(BF16)
        dz_recv = mm_nt(back_pre, w1_ref[2 * width : 3 * width, :]).astype(BF16)
        sent = mm(one_hot(send_ref[:, rows], space_ref.shape[0]), dz_send)
        space_ref[...] = sent if start == 0 else space_ref[...] + sent
        arrived = mm(hot_r, dz_recv)
        received = arrived if received is None else received + arrived
    for slot, piece in enumerate(piece_refs):
        tile = piece.shape[0]
        piece[...] = space_ref[own + slot * tile : own + (slot + 1) * tile, :].astype(BF16)
        piece.done()
    own_ref[...] = base_ref[...] + received + space_ref[0:own, :]


def coarse_backward_kernel(
    me_ref, recv_ref, all_ref, d_ref, gain_ref, std_ref, normed_ref, w2_ref, slope_ref,
    hidden_ref, out_ref, pre_ref, edges_ref, zs_ref, zr_ref, w1_ref, send_ref,
    g_ref, *rest, ordered,
):
    if ordered:
        kept_ref, given_ref, part_ref, g1_ref, g2_ref = rest
    else:
        part_ref, g1_ref, g2_ref = rest
    width = d_ref.shape[1]
    count = hidden_ref.shape[0]
    rows = slice(count - d_ref.shape[0], count)
    table = gathered(all_ref).astype(BF16)
    hot_r = one_hot(recv_ref[...], table.shape[0])
    d_edges = d_ref[...].astype(F32)
    cotan = d_edges + pick(hot_r, table)
    back_out, back_pre = head_of_backward(
        cotan, w2_ref[...], gain_ref[...], slope_ref[...].astype(F32), normed_ref[...].astype(F32), std_ref[:, 0:1]
    )
    out_ref[rows, :] = back_out
    pre_ref[rows, :] = back_pre
    g2_ref[...] = mm_tn(hidden_ref[...], out_ref[...])
    g1_ref[0:width, :] = mm_tn(edges_ref[...], pre_ref[...])
    g1_ref[width : 2 * width, :] = mm_tn(zs_ref[...], pre_ref[...])
    g1_ref[2 * width : 3 * width, :] = mm_tn(zr_ref[...], pre_ref[...])
    dz_send = mm_nt(back_pre, w1_ref[width : 2 * width, :]).astype(BF16)
    dz_recv = mm_nt(back_pre, w1_ref[2 * width : 3 * width, :]).astype(BF16)
    total = mm(one_hot(send_ref[...], table.shape[0]), dz_send) + mm(hot_r, dz_recv)
    if ordered:
        part_ref[...] = total
        by_distance(me_ref[0], 2 * kept_ref.shape[0], (g1_ref, g2_ref, part_ref), kept_ref, given_ref)
        kept_ref.done()
    else:
        part_ref[...] = total.reshape(part_ref.shape).astype(BF16)
    g_ref[...] = (d_edges + mm_nt(back_pre, w1_ref[0:width, :])).astype(BF16)


def node_gradient_kernel(own_ref, halo_ref, *refs, slots):
    piece_refs, out_ref = refs[:slots], refs[len(refs) - 1 - (len(refs) - 1 - slots) // 2]
    arrived = None
    for slot, piece in enumerate(piece_refs):
        part = mm(one_hot(halo_ref[slot : slot + 1, :], own_ref.shape[0]), piece[...])
        arrived = part if arrived is None else arrived + part
    out_ref[...] = own_ref[...] + arrived


def coarse_gradient_kernel(total_ref, share_ref, g_ref):
    share = jnp.sum(share_ref[...].astype(F32), 0)
    first = total_ref[0:16, :] + jnp.concatenate([share, jnp.zeros_like(share)], 0)
    g_ref[...] = total_ref[...].astype(BF16)
    g_ref[0:16, :] = first.astype(BF16)


def first_halving_kernel(kept_ref, taken_ref, *refs):
    passing = (len(refs) - 2) // 2
    keep_ref, give_ref = refs[passing : passing + 2]
    for j in range(kept_ref.shape[0]):
        total = (kept_ref[j].astype(F32) + taken_ref[j].astype(F32)).astype(BF16)
        out = give_ref if j % 2 else keep_ref
        out[j // 2] = total


def second_halving_kernel(kept_ref, taken_ref, *refs, passing):
    keep_ref, give_refs = refs[passing], refs[passing + 1 : len(refs) - passing]
    for j in range(kept_ref.shape[0]):
        total = kept_ref[j].astype(F32) + taken_ref[j].astype(F32)
        if j:
            give_refs[j - 1][...] = total.astype(BF16)
        else:
            keep_ref[...] = total


def last_sum_kernel(kept_ref, *refs, taken, with_nodes, passing):
    total = kept_ref[...]
    for ref in refs[:taken]:
        total = total + ref[...].astype(F32)
    if with_nodes:
        nodes_ref, first_ref, second_ref, g_ref = refs[taken:]
    else:
        first_ref, second_ref = refs[taken + passing : len(refs) - passing]
    cut = first_ref.shape[0]
    end = cut + second_ref.shape[0]
    first_ref[...] = total[:cut]
    second_ref[...] = total[cut:end]
    if with_nodes:
        g_ref[...] = nodes_ref[...].astype(BF16)
        g_ref[0:16, :] = (nodes_ref[0:16, :] + total[end : end + 16]).astype(BF16)


VM = pl.BlockSpec(memory_space=pltpu.VMEM)
SM = pl.BlockSpec(memory_space=pltpu.SMEM)
ANY = pl.BlockSpec(memory_space=pl.ANY)


def shape(dims, dtype):
    return jax.ShapeDtypeStruct(tuple(dims), dtype)


class Rows:
    def __init__(self, parts=1, joined=1, extra=0):
        self.parts = parts
        self.joined = joined
        self.extra = extra


class Fetched:
    def __init__(self, sources, buffer, semaphores, parts):
        self.buffer = buffer
        self.shape = buffer.shape
        self.waiting = []
        place = 0
        for source in sources:
            rows = source.shape[0] // parts
            for part in range(parts):
                if source.shape == buffer.shape and parts == 1:
                    copy = pltpu.make_async_copy(source, buffer, next(semaphores))
                else:
                    copy = pltpu.make_async_copy(
                        source.at[pl.ds(part * rows, rows)], buffer.at[pl.ds(place, rows)], next(semaphores)
                    )
                copy.start()
                self.waiting.append((place, place + rows, copy))
                place += rows

    def ready(self, low=0, high=None):
        left = []
        for first, last, copy in self.waiting:
            if high is None or (first < high and low < last):
                copy.wait()
            else:
                left.append((first, last, copy))
        self.waiting = left

    def __getitem__(self, index):
        rows = index[0] if isinstance(index, tuple) else None
        if isinstance(rows, slice) and rows.start is not None:
            self.ready(rows.start, rows.stop)
        else:
            self.ready()
        return self.buffer[index]

    def __setitem__(self, index, value):
        self.buffer[index] = value


class Stored:
    def __init__(self, target, buffer, semaphores):
        self.target = target
        self.buffer = buffer
        self.shape = buffer.shape
        self.dtype = buffer.dtype
        self.semaphores = semaphores
        self.copies = []

    def __getitem__(self, index):
        return self.buffer[index]

    def __setitem__(self, index, value):
        self.buffer[index] = value

    def done(self, rows=None):
        if rows is None:
            copy = pltpu.make_async_copy(self.buffer, self.target, next(self.semaphores))
        else:
            part = pl.ds(rows.start, rows.stop - rows.start)
            copy = pltpu.make_async_copy(self.buffer.at[part], self.target.at[part], next(self.semaphores))
        copy.start()
        self.copies.append(copy)


SEMAPHORES = 64


def staged_kernel(body, in_specs, out_specs, *refs):
    ins, outs = refs[: len(in_specs)], refs[len(in_specs) : len(in_specs) + len(out_specs)]
    rest = refs[len(in_specs) + len(out_specs) :]
    semaphores = iter([rest[0].at[i] for i in range(SEMAPHORES)])
    buffers = iter(rest[1:])
    fetched, stored = [], []
    for place, (ref, spec) in enumerate(zip(ins, in_specs)):
        if spec is VM:
            fetched.append(Fetched([ref], next(buffers), semaphores, 1))
        elif spec is SM:
            fetched.append(ref)
        elif isinstance(spec, Rows):
            fetched.append(Fetched(ins[place : place + spec.joined], next(buffers), semaphores, spec.parts))
    for ref, spec in zip(outs, out_specs):
        stored.append(Stored(ref, next(buffers), semaphores))
    body(*fetched, *stored, *buffers)
    for ref in fetched:
        if isinstance(ref, Fetched):
            ref.ready()
    for ref in stored:
        if not ref.copies:
            ref.done()
    for ref in stored:
        for copy in ref.copies:
            copy.wait()


def cost(ins, outs, flops):
    moved = sum(a.size * a.dtype.itemsize for a in list(ins) + list(outs))
    return pl.CostEstimate(flops=flops, bytes_accessed=moved, transcendentals=0)


def call(kernel, name, ins, in_specs, outs, scratch=(), flops=0):
    out_specs = [VM] * len(outs)
    buffers = []
    for place, spec in enumerate(in_specs):
        if spec is VM:
            buffers.append(pltpu.VMEM(ins[place].shape, ins[place].dtype))
        elif isinstance(spec, Rows):
            joined = ins[place : place + spec.joined]
            rows = sum(a.shape[0] for a in joined) + spec.extra
            buffers.append(pltpu.VMEM((rows,) + joined[0].shape[1:], joined[0].dtype))
    buffers += [pltpu.VMEM(a.shape, a.dtype) for a in outs]
    return pl.pallas_call(
        functools.partial(staged_kernel, kernel, in_specs, out_specs),
        out_shape=tuple(outs),
        in_specs=[SM if spec is SM else ANY for spec in in_specs],
        out_specs=tuple([ANY] * len(outs)),
        scratch_shapes=[pltpu.SemaphoreType.DMA((SEMAPHORES,))] + buffers + list(scratch),
        name=name,
        cost_estimate=cost(ins, outs, flops),
        compiler_params=pltpu.CompilerParams(vmem_limit_bytes=VMEM_LIMIT),
    )(*ins)


def small_call(kernel, name, ins, outs, passing=()):
    first = len(ins)
    last = len(outs)
    outs = list(outs) + [shape(a.shape, a.dtype) for a in passing]
    return pl.pallas_call(
        kernel,
        out_shape=tuple(outs),
        input_output_aliases={first + i: last + i for i in range(len(passing))},
        in_specs=[VM] * first + [ANY] * len(passing),
        out_specs=tuple([VM] * last + [ANY] * len(passing)),
        name=name,
        cost_estimate=cost(ins, outs, 0),
        compiler_params=pltpu.CompilerParams(vmem_limit_bytes=SMALL_LIMIT),
    )(*ins, *passing)


def passed_along(block, axis, distance):
    count = lax.axis_size(axis)
    route = [((i - distance) % count, i) for i in range(count)]
    return lax.ppermute(block, axis, route)


def exchanged(block, axis, distance):
    return lax.ppermute(block, axis, [(i, i ^ distance) for i in range(lax.axis_size(axis))])


def exchanged_with_all(blocks, axis):
    return lax.all_to_all(blocks, axis, 0, 0)


def first_halving(kept, taken, passing=()):
    half = shape((kept.shape[0] // 2,) + kept.shape[1:], BF16)
    return small_call(first_halving_kernel, "first_halving", (kept, taken), [half, half], passing)


def second_halving(kept, taken, passing=()):
    block = kept.shape[1:]
    outs = [shape(block, F32)] + [shape(block, BF16)] * (kept.shape[0] - 1)
    kernel = functools.partial(second_halving_kernel, passing=len(passing))
    return small_call(kernel, "second_halving", (kept, taken), outs, passing)


def last_sum(kept, taken, first_rows, second_rows, nodes=None, passing=()):
    width = kept.shape[1]
    outs = [shape((first_rows, width), F32), shape((second_rows, width), F32)]
    ins = (kept, *taken)
    if nodes is not None:
        outs.append(shape(nodes.shape, BF16))
        ins += (nodes,)
    kernel = functools.partial(
        last_sum_kernel, taken=len(taken), with_nodes=nodes is not None, passing=len(passing)
    )
    return small_call(kernel, "last_sum", ins, outs, passing)


def local(
    nodes,
    fine_edges,
    coarse_edges,
    fine_send,
    fine_recv,
    coarse_send,
    coarse_recv,
    halo_rows,
    edge_count,
    edge_w1,
    edge_w2,
    edge_gain,
    node_w1,
    node_w2,
    node_gain,
    d_nodes,
    d_fine,
    d_coarse,
):
    axis = "patch"
    peers = lax.axis_size(axis)
    own, width = nodes.shape
    fine = fine_edges.shape[0]
    coarse = coarse_edges.shape[0]
    halo = halo_rows[0]
    slots, tile = halo.shape
    hops = slots // 2
    offsets = list(range(1, hops + 1)) + [-k for k in range(1, hops + 1)]
    ordered = peers == 16 and all(
        w.shape[0] % (16 * peers) == 0 for w in (edge_w1, edge_w2, node_w1, node_w2)
    )
    me = lax.axis_index(axis).astype(jnp.int32).reshape(1)
    fs, fr = fine_send.reshape(1, fine), fine_recv.reshape(1, fine)
    cs, cr = coarse_send.reshape(1, coarse), coarse_recv.reshape(1, coarse)
    eg, ng = edge_gain.reshape(1, width), node_gain.reshape(1, width)
    every = shape((peers, COARSE_DEV, width), BF16)

    made = call(
        tiles_kernel, "tiles", (nodes, halo), [VM, VM],
        [shape((tile, width), BF16)] * slots + [every],
    )
    received = [passed_along(made[slot], axis, offset) for slot, offset in enumerate(offsets)]
    coarse_all = exchanged_with_all(made[-1], axis)

    def saved_shapes(rows):
        return [
            shape((rows, width), BF16), shape((rows, width), BF16), shape((rows, width), BF16),
            shape((rows, width), BF16), shape((rows, width), BF16), shape((rows, 128), F32),
        ]

    new_coarse, coarse_part, *coarse_saved = call(
        coarse_forward_kernel, "coarse_forward",
        (coarse_all, coarse_edges, cs, cr, edge_w1, edge_w2, eg), [VM] * 4 + [Rows(3), VM, VM],
        [shape((coarse, width), BF16), every] + saved_shapes(coarse),
        flops=2 * coarse * width * width * 4,
    )
    share = exchanged_with_all(coarse_part, axis)

    block = 256 if fine % 256 == 0 else fine
    space_rows = own + slots * tile
    new_fine, fine_agg, *fine_saved = call(
        functools.partial(fine_forward_kernel, slots=slots, block=block), "fine_forward",
        (edge_count, nodes, *received, fine_edges, fs, fr, edge_w1, edge_w2, eg),
        [SM] + [VM] * (slots + 4) + [Rows(3), VM, VM],
        [shape((fine, width), BF16), shape((own, width), F32)] + saved_shapes(fine),
        scratch=[pltpu.VMEM((space_rows, width), BF16)],
        flops=2 * fine * width * (4 * width + space_rows + 3 * own),
    )

    def weight_shapes(w1, w2, more):
        if not ordered:
            return [shape(w1.shape, F32), shape(w2.shape, F32)], []
        rows = (w1.shape[0] + w2.shape[0]) // peers + more
        outs = [shape((peers // 2, rows, width), BF16)] * 2
        return outs, [pltpu.VMEM(w1.shape, F32), pltpu.VMEM(w2.shape, F32)]

    sum_shapes, sum_scratch = weight_shapes(node_w1, node_w2, 0)
    new_nodes, base, dagg, dagg_spread, *node_parts = call(
        functools.partial(node_kernel, ordered=ordered), "node_both",
        (me, nodes, fine_agg, share, d_nodes, node_w1, node_w2, ng), [SM] + [VM] * 4 + [Rows(2), VM, VM],
        [shape((own, width), BF16), shape((own, width), F32), shape((own, width), BF16), every] + sum_shapes,
        scratch=[pltpu.VMEM((own, width), F32)] + sum_scratch,
        flops=2 * own * width * width * 9,
    )
    dagg_all = exchanged_with_all(dagg_spread, axis)
    if ordered:
        node_taken = exchanged(node_parts[1], axis, 1)
        node_kept, node_given, base = first_halving(node_parts[0], node_taken, (base,))
        node_taken = exchanged(node_given, axis, 2)

    sum_shapes, sum_scratch = weight_shapes(edge_w1, edge_w2, 16)
    f_zs, f_zr, f_hidden, f_slope, f_normed, f_std = fine_saved
    c_zs, c_zr, c_hidden, c_slope, c_normed, c_std = coarse_saved
    fine_out, fine_pre, g_fine, own_grad, *pieces = call(
        functools.partial(fine_backward_kernel, block=block), "fine_backward",
        (edge_count, fr, dagg, d_fine, eg, f_std, f_normed, edge_w2, f_slope, edge_w1, fs, base),
        [SM] + [VM] * 8 + [Rows(3), VM, VM],
        [shape((fine, width), BF16)] * 3 + [shape((own, width), F32)] + [shape((tile, width), BF16)] * slots,
        scratch=[pltpu.VMEM((space_rows, width), F32)],
        flops=2 * fine * width * (4 * width + space_rows + 2 * own),
    )
    returned = [passed_along(pieces[slot], axis, -offset) for slot, offset in enumerate(offsets)]

    pair = [Rows(joined=2), None]
    more = [Rows(extra=coarse)]
    order = (node_taken,) if ordered else ()
    g_coarse, *edge_parts = call(
        functools.partial(coarse_backward_kernel, ordered=ordered), "coarse_backward",
        (
            me, cr, dagg_all, d_coarse, eg, c_std, c_normed, edge_w2, c_slope, f_hidden, c_hidden,
            fine_out, fine_pre, fine_edges, coarse_edges, f_zs, c_zs, f_zr, c_zr, edge_w1, cs, *order,
        ),
        [SM] + [VM] * 8 + pair + more * 2 + pair * 3 + [Rows(3), VM] + [None] * len(order),
        [shape((coarse, width), BF16)] + ([] if ordered else [every]) + sum_shapes,
        scratch=([pltpu.VMEM((peers * COARSE_DEV, width), F32)] if ordered else []) + sum_scratch,
        flops=2 * width * width * (4 * fine + 12 * coarse),
    )

    def rows_of(w):
        return w.shape[0] // peers

    def returned_tiles(passing=()):
        return small_call(
            functools.partial(node_gradient_kernel, slots=slots), "node_gradient",
            (own_grad, halo, *returned), [shape((own, width), F32)], passing,
        )

    if ordered:
        edge_kept, edge_given = edge_parts
        edge_taken = exchanged(edge_given, axis, 1)
        total, edge_kept = returned_tiles((edge_kept,))
        node_kept, *given, edge_kept = second_halving(node_kept, node_taken, (edge_kept,))
        node_taken = [exchanged(part, axis, 4 * (k + 1)) for k, part in enumerate(given)]
        edge_kept, edge_given = first_halving(edge_kept, edge_taken)
        edge_taken = exchanged(edge_given, axis, 2)
        g_nw1, g_nw2, edge_kept = last_sum(
            node_kept, node_taken, rows_of(node_w1), rows_of(node_w2), passing=(edge_kept,)
        )
        edge_kept, *given = second_halving(edge_kept, edge_taken)
        edge_taken = [exchanged(part, axis, 4 * (k + 1)) for k, part in enumerate(given)]
        g_ew1, g_ew2, g_nodes = last_sum(edge_kept, edge_taken, rows_of(edge_w1), rows_of(edge_w2), total)
    else:
        coarse_share = exchanged_with_all(edge_parts[0], axis)
        (g_nodes,) = small_call(
            coarse_gradient_kernel, "coarse_gradient", (*returned_tiles(), coarse_share),
            [shape((own, width), BF16)],
        )
        g_nw1, g_nw2, g_ew1, g_ew2 = [
            lax.psum_scatter(g, axis, scatter_dimension=0, tiled=True) for g in node_parts + edge_parts[1:]
        ]
    return (new_nodes, new_fine, new_coarse, g_nodes, g_fine, g_coarse, g_ew1, g_ew2, g_nw1, g_nw2)


def solution(mesh):
    split = P(("groups", "patch"))
    rows = P(("groups", "patch"), None)
    return jax.shard_map(
        local,
        mesh=mesh,
        in_specs=(
            rows, rows, rows, split, split, split, split, P(("groups", "patch"), None, None), split,
            P(), P(), P(), P(), P(), P(), rows, rows, rows,
        ),
        out_specs=(rows,) * 10,
        check_vma=False,
    )
```

```python
import functools

import jax
import jax.numpy as jnp
from jax import lax
from jax.experimental import pallas as pl
from jax.experimental.pallas import tpu as pltpu
from jax.sharding import PartitionSpec as P

COARSE_DEV = 8
EPSILON = 1e-05
F32 = jnp.float32
BF16 = jnp.bfloat16
VMEM_LIMIT = 60 * 1024 * 1024
SMALL_LIMIT = 16 * 1024 * 1024


def mm(a, b):
    return lax.dot_general(a, b, (((1,), (0,)), ((), ())), preferred_element_type=F32)


def mm_nt(a, b):
    return lax.dot_general(a, b, (((1,), (1,)), ((), ())), preferred_element_type=F32)


def mm_tn(a, b):
    return lax.dot_general(a, b, (((0,), (0,)), ((), ())), preferred_element_type=F32)


def halves(value):
    high = value.astype(BF16)
    low = (value - high.astype(F32)).astype(BF16)
    return high, low


def one_hot(index, rows):
    row = lax.broadcasted_iota(jnp.int32, (rows, index.shape[1]), 0)
    return jnp.where(row == index, 1.0, 0.0).astype(BF16)


def pick(hot, table):
    return mm_tn(hot, table)


def pick_wide(hot, table):
    high, low = halves(table)
    return mm_tn(hot, high) + mm_tn(hot, low)


def put_wide(hot, rows):
    high, low = halves(rows)
    return mm(hot, high) + mm(hot, low)


def row_mean(value):
    return jnp.mean(value, axis=-1, keepdims=True)


def tail_of_forward(pre, second_w, gain):
    sigmoid = jax.nn.sigmoid(pre)
    hidden = (pre * sigmoid).astype(BF16)
    slope = sigmoid * (1.0 + pre * (1.0 - sigmoid))
    output = mm(hidden, second_w)
    centred = output - row_mean(output)
    inv_std = lax.rsqrt(row_mean(centred * centred) + EPSILON)
    normed = centred * inv_std
    return normed * gain, hidden, slope, normed, inv_std


def head_of_backward(cotan, second_w, gain, slope, normed, inv_std):
    scaled = cotan * gain
    back_out = inv_std * (scaled - row_mean(scaled) - normed * row_mean(scaled * normed))
    back_out = back_out.astype(BF16)
    back_pre = (mm_nt(back_out, second_w) * slope).astype(BF16)
    return back_out, back_pre


def tiles_kernel(nodes_ref, halo_ref, *outs):
    spread_ref = outs[-1]
    nodes = nodes_ref[...]
    for slot, out in enumerate(outs[:-1]):
        hot = one_hot(halo_ref[slot : slot + 1, :], nodes.shape[0])
        out[...] = pick(hot, nodes).astype(BF16)
        out.done()
    rows = nodes_ref[0:16, :].astype(F32)[:COARSE_DEV].astype(BF16)
    for peer in range(spread_ref.shape[0]):
        spread_ref[peer] = rows


def gathered(ref):
    value = ref[...].astype(F32)
    return value.reshape(value.shape[0] * value.shape[1], value.shape[2])


def coarse_forward_kernel(
    all_ref, edges_ref, send_ref, recv_ref, w1_ref, w2_ref, gain_ref,
    new_ref, part_ref, zs_ref, zr_ref, hidden_ref, slope_ref, normed_ref, std_ref,
):
    width = edges_ref.shape[1]
    table = gathered(all_ref).astype(BF16)
    hot_s = one_hot(send_ref[...], table.shape[0])
    hot_r = one_hot(recv_ref[...], table.shape[0])
    edges = edges_ref[...]
    zs = pick(hot_s, table).astype(BF16)
    zr = pick(hot_r, table).astype(BF16)
    pre = (
        mm(edges, w1_ref[0:width, :])
        + mm(zs, w1_ref[width : 2 * width, :])
        + mm(zr, w1_ref[2 * width : 3 * width, :])
    )
    message, hidden, slope, normed, inv_std = tail_of_forward(pre, w2_ref[...], gain_ref[...])
    total = put_wide(hot_r, message)
    part_ref[...] = total.reshape(part_ref.shape).astype(BF16)
    part_ref.done()
    new_ref[...] = (edges.astype(F32) + message).astype(BF16)
    zs_ref[...] = zs
    zr_ref[...] = zr
    hidden_ref[...] = hidden
    slope_ref[...] = slope.astype(BF16)
    normed_ref[...] = normed.astype(BF16)
    std_ref[...] = jnp.broadcast_to(inv_std, std_ref.shape)


def fine_forward_kernel(count_ref, nodes_ref, *refs, slots, block):
    tile_refs = refs[:slots]
    (
        edges_ref, send_ref, recv_ref, w1_ref, w2_ref, gain_ref,
        new_ref, agg_ref, zs_ref, zr_ref, hidden_ref, slope_ref, normed_ref, std_ref, space_ref,
    ) = refs[slots:]
    count, width = edges_ref.shape
    own = nodes_ref.shape[0]
    tile = tile_refs[0].shape[0]
    space_ref[0:own, :] = nodes_ref[...]
    for slot in range(slots):
        space_ref[own + slot * tile : own + (slot + 1) * tile, :] = tile_refs[slot][...]
    for start in range(0, count, block):
        rows = slice(start, start + block)
        edges = edges_ref[rows, :]
        hot_s = one_hot(send_ref[:, rows], space_ref.shape[0])
        hot_r = one_hot(recv_ref[:, rows], own)
        zs = pick(hot_s, space_ref[...]).astype(BF16)
        zr = pick(hot_r, nodes_ref[...]).astype(BF16)
        pre = (
            mm(edges, w1_ref[0:width, :])
            + mm(zs, w1_ref[width : 2 * width, :])
            + mm(zr, w1_ref[2 * width : 3 * width, :])
        )
        message, hidden, slope, normed, inv_std = tail_of_forward(pre, w2_ref[...], gain_ref[...])
        place = start + lax.broadcasted_iota(jnp.int32, (block, 1), 0)
        message = jnp.where(place < count_ref[0], message, 0.0)
        arrived = put_wide(hot_r, message)
        agg_ref[...] = arrived if start == 0 else agg_ref[...] + arrived
        new_ref[rows, :] = (edges.astype(F32) + message).astype(BF16)
        zs_ref[rows, :] = zs
        zr_ref[rows, :] = zr
        hidden_ref[rows, :] = hidden
        slope_ref[rows, :] = slope.astype(BF16)
        normed_ref[rows, :] = normed.astype(BF16)
        std_ref[rows, :] = jnp.broadcast_to(inv_std, (block, std_ref.shape[1]))
        for ref in (new_ref, zs_ref, zr_ref, hidden_ref, slope_ref, normed_ref, std_ref):
            ref.done(rows)


def by_distance(me, peers, sums, kept_ref, given_ref):
    for r in list(range(1, peers, 2)) + list(range(0, peers, 2)):
        if r == 0:
            given_ref.done()
        to = jnp.bitwise_xor(me, r)
        out = given_ref if r % 2 else kept_ref
        place = 0
        for total in sums:
            rows = total.shape[0] // peers
            part = total[pl.ds(pl.multiple_of(to * rows, 8), rows), :]
            if rows % 16:
                part = jnp.concatenate([part, jnp.zeros((-rows % 16, part.shape[1]), F32)], 0)
            out[r // 2, place : place + part.shape[0], :] = part.astype(BF16)
            place += part.shape[0]


def node_kernel(
    me_ref, nodes_ref, agg_ref, share_ref, d_ref, w1_ref, w2_ref, gain_ref,
    new_ref, base_ref, dagg_ref, spread_ref, *rest, ordered,
):
    if ordered:
        kept_ref, given_ref, total_ref, g1_ref, g2_ref = rest
    else:
        g1_ref, g2_ref, total_ref = rest
    width = nodes_ref.shape[1]
    total_ref[...] = agg_ref[...]
    total_ref[0:COARSE_DEV, :] += jnp.sum(share_ref[...].astype(F32), 0)
    nodes = nodes_ref[...]
    agg = total_ref[...].astype(BF16)
    pre = mm(nodes, w1_ref[0:width, :]) + mm(agg, w1_ref[width : 2 * width, :])
    update, hidden, slope, normed, inv_std = tail_of_forward(pre, w2_ref[...], gain_ref[...])
    new_ref[...] = (nodes.astype(F32) + update).astype(BF16)
    cotan = d_ref[...].astype(F32)
    back_out, back_pre = head_of_backward(cotan, w2_ref[...], gain_ref[...], slope, normed, inv_std)
    dagg = mm_nt(back_pre, w1_ref[width : 2 * width, :])
    dagg_ref[...] = dagg.astype(BF16)
    rows = dagg[:COARSE_DEV].astype(BF16)
    for peer in range(spread_ref.shape[0]):
        spread_ref[peer] = rows
    base_ref[...] = cotan + mm_nt(back_pre, w1_ref[0:width, :])
    g1_ref[0:width, :] = mm_tn(nodes, back_pre)
    g1_ref[width : 2 * width, :] = mm_tn(agg, back_pre)
    g2_ref[...] = mm_tn(hidden, back_out)
    if ordered:
        by_distance(me_ref[0], spread_ref.shape[0], (g1_ref, g2_ref), kept_ref, given_ref)


def edge_heads_kernel(
    count_ref, recv_ref, dagg_ref, d_ref, gain_ref, std_ref, normed_ref, w2_ref, slope_ref,
    w1_ref, send_ref, crecv_ref, all_ref, csend_ref, base_ref,
    out_ref, pre_ref, g_ref, gc_ref, part_ref, own_ref, *rest, block, fine,
):
    piece_refs, space_ref = rest[:-1], rest[-1]
    count, width = d_ref.shape
    own = base_ref.shape[0]
    received = None
    for start in list(range(0, fine, block)) + [fine]:
        rows = slice(start, start + block if start < fine else count)
        d_edges = d_ref[rows, :].astype(F32)
        if start < fine:
            hot_r = one_hot(recv_ref[:, rows], own)
            hot_s = one_hot(send_ref[:, rows], space_ref.shape[0])
            place = start + lax.broadcasted_iota(jnp.int32, (block, 1), 0)
            cotan = jnp.where(place < count_ref[0], d_edges + pick(hot_r, dagg_ref[...]), 0.0)
        else:
            table = gathered(all_ref).astype(BF16)
            hot_r = one_hot(crecv_ref[...], table.shape[0])
            hot_s = one_hot(csend_ref[...], table.shape[0])
            cotan = d_edges + pick(hot_r, table)
        back_out, back_pre = head_of_backward(
            cotan, w2_ref[...], gain_ref[...], slope_ref[rows, :].astype(F32),
            normed_ref[rows, :].astype(F32), std_ref[rows, 0:1],
        )
        out_ref[rows, :] = back_out
        pre_ref[rows, :] = back_pre
        out_ref.done(rows)
        pre_ref.done(rows)
        grads = (d_edges + mm_nt(back_pre, w1_ref[0:width, :])).astype(BF16)
        sent = mm(hot_s, mm_nt(back_pre, w1_ref[width : 2 * width, :]).astype(BF16))
        arrived = mm(hot_r, mm_nt(back_pre, w1_ref[2 * width : 3 * width, :]).astype(BF16))
        if start < fine:
            g_ref[rows, :] = grads
            g_ref.done(rows)
            space_ref[...] = sent if start == 0 else space_ref[...] + sent
            received = arrived if received is None else received + arrived
        else:
            gc_ref[...] = grads
            part_ref[...] = (sent + arrived).reshape(part_ref.shape).astype(part_ref.dtype)
        if start + block == fine:
            for slot, piece in enumerate(piece_refs):
                tile = piece.shape[0]
                piece[...] = space_ref[own + slot * tile : own + (slot + 1) * tile, :].astype(BF16)
                piece.done()
            own_ref[...] = base_ref[...] + received + space_ref[0:own, :]
            own_ref.done()


def edge_weights_kernel(
    me_ref, hidden_ref, out_ref, edges_ref, pre_ref, zs_ref, zr_ref, *rest, ordered,
):
    if ordered:
        part_ref, kept_ref, given_ref, g1_ref, g2_ref = rest
    else:
        g1_ref, g2_ref = rest
    width = edges_ref.shape[1]
    g2_ref[...] = mm_tn(hidden_ref[...], out_ref[...])
    g1_ref[0:width, :] = mm_tn(edges_ref[...], pre_ref[...])
    g1_ref[width : 2 * width, :] = mm_tn(zs_ref[...], pre_ref[...])
    g1_ref[2 * width : 3 * width, :] = mm_tn(zr_ref[...], pre_ref[...])
    if ordered:
        by_distance(me_ref[0], 2 * kept_ref.shape[0], (g1_ref, g2_ref, part_ref), kept_ref, given_ref)


def node_gradient_kernel(own_ref, halo_ref, *refs):
    piece_refs, out_ref = refs[:-1], refs[-1]
    arrived = None
    for slot, piece in enumerate(piece_refs):
        part = mm(one_hot(halo_ref[slot : slot + 1, :], own_ref.shape[0]), piece[...])
        arrived = part if arrived is None else arrived + part
    out_ref[...] = own_ref[...] + arrived


def coarse_gradient_kernel(total_ref, share_ref, g_ref):
    share = jnp.sum(share_ref[...].astype(F32), 0)
    first = total_ref[0:16, :] + jnp.concatenate([share, jnp.zeros_like(share)], 0)
    g_ref[...] = total_ref[...].astype(BF16)
    g_ref[0:16, :] = first.astype(BF16)


def first_halving_kernel(kept_ref, taken_ref, *refs):
    passing = (len(refs) - 2) // 2
    keep_ref, give_ref = refs[passing : passing + 2]
    for j in range(kept_ref.shape[0]):
        total = (kept_ref[j].astype(F32) + taken_ref[j].astype(F32)).astype(BF16)
        out = give_ref if j % 2 else keep_ref
        out[j // 2] = total


def second_halving_kernel(kept_ref, taken_ref, *refs, passing):
    keep_ref, give_refs = refs[passing], refs[passing + 1 : len(refs) - passing]
    for j in range(kept_ref.shape[0]):
        total = kept_ref[j].astype(F32) + taken_ref[j].astype(F32)
        if j:
            give_refs[j - 1][...] = total.astype(BF16)
        else:
            keep_ref[...] = total


def last_sum_kernel(kept_ref, *refs, taken, with_nodes, passing):
    total = kept_ref[...]
    for ref in refs[:taken]:
        total = total + ref[...].astype(F32)
    if with_nodes:
        nodes_ref, first_ref, second_ref, g_ref = refs[taken:]
    else:
        first_ref, second_ref = refs[taken + passing : len(refs) - passing]
    cut = first_ref.shape[0]
    end = cut + second_ref.shape[0]
    first_ref[...] = total[:cut]
    second_ref[...] = total[cut:end]
    if with_nodes:
        g_ref[...] = nodes_ref[...].astype(BF16)
        g_ref[0:16, :] = (nodes_ref[0:16, :] + total[end : end + 16]).astype(BF16)


VM = pl.BlockSpec(memory_space=pltpu.VMEM)
SM = pl.BlockSpec(memory_space=pltpu.SMEM)
ANY = pl.BlockSpec(memory_space=pl.ANY)


def shape(dims, dtype):
    return jax.ShapeDtypeStruct(tuple(dims), dtype)


class Rows:
    def __init__(self, parts=1, joined=1, extra=0):
        self.parts = parts
        self.joined = joined
        self.extra = extra


class Fetched:
    def __init__(self, sources, buffer, semaphores, parts):
        self.buffer = buffer
        self.shape = buffer.shape
        self.waiting = []
        place = 0
        for source in sources:
            rows = source.shape[0] // parts
            for part in range(parts):
                if source.shape == buffer.shape and parts == 1:
                    copy = pltpu.make_async_copy(source, buffer, next(semaphores))
                else:
                    copy = pltpu.make_async_copy(
                        source.at[pl.ds(part * rows, rows)], buffer.at[pl.ds(place, rows)], next(semaphores)
                    )
                copy.start()
                self.waiting.append((place, place + rows, copy))
                place += rows

    def ready(self, low=0, high=None):
        left = []
        for first, last, copy in self.waiting:
            if high is None or (first < high and low < last):
                copy.wait()
            else:
                left.append((first, last, copy))
        self.waiting = left

    def __getitem__(self, index):
        rows = index[0] if isinstance(index, tuple) else None
        if isinstance(rows, slice) and rows.start is not None:
            self.ready(rows.start, rows.stop)
        else:
            self.ready()
        return self.buffer[index]

    def __setitem__(self, index, value):
        self.buffer[index] = value


class Stored:
    def __init__(self, target, buffer, semaphores):
        self.target = target
        self.buffer = buffer
        self.shape = buffer.shape
        self.dtype = buffer.dtype
        self.semaphores = semaphores
        self.copies = []

    def __getitem__(self, index):
        return self.buffer[index]

    def __setitem__(self, index, value):
        self.buffer[index] = value

    def done(self, rows=None):
        if rows is None:
            copy = pltpu.make_async_copy(self.buffer, self.target, next(self.semaphores))
        else:
            part = pl.ds(rows.start, rows.stop - rows.start)
            copy = pltpu.make_async_copy(self.buffer.at[part], self.target.at[part], next(self.semaphores))
        copy.start()
        self.copies.append(copy)


SEMAPHORES = 64


def staged_kernel(body, in_specs, out_specs, *refs):
    ins, outs = refs[: len(in_specs)], refs[len(in_specs) : len(in_specs) + len(out_specs)]
    rest = refs[len(in_specs) + len(out_specs) :]
    semaphores = iter([rest[0].at[i] for i in range(SEMAPHORES)])
    buffers = iter(rest[1:])
    fetched, stored = [], []
    for place, (ref, spec) in enumerate(zip(ins, in_specs)):
        if spec is VM:
            fetched.append(Fetched([ref], next(buffers), semaphores, 1))
        elif spec is SM:
            fetched.append(ref)
        elif isinstance(spec, Rows):
            fetched.append(Fetched(ins[place : place + spec.joined], next(buffers), semaphores, spec.parts))
    for ref, spec in zip(outs, out_specs):
        stored.append(Stored(ref, next(buffers), semaphores))
    body(*fetched, *stored, *buffers)
    for ref in fetched:
        if isinstance(ref, Fetched):
            ref.ready()
    for ref in stored:
        if not ref.copies:
            ref.done()
    for ref in stored:
        for copy in ref.copies:
            copy.wait()


def cost(ins, outs, flops):
    moved = sum(a.size * a.dtype.itemsize for a in list(ins) + list(outs))
    return pl.CostEstimate(flops=flops, bytes_accessed=moved, transcendentals=0)


def call(kernel, name, ins, in_specs, outs, scratch=(), flops=0):
    out_specs = [VM] * len(outs)
    buffers = []
    for place, spec in enumerate(in_specs):
        if spec is VM:
            buffers.append(pltpu.VMEM(ins[place].shape, ins[place].dtype))
        elif isinstance(spec, Rows):
            joined = ins[place : place + spec.joined]
            rows = sum(a.shape[0] for a in joined) + spec.extra
            buffers.append(pltpu.VMEM((rows,) + joined[0].shape[1:], joined[0].dtype))
    buffers += [pltpu.VMEM(a.shape, a.dtype) for a in outs]
    return pl.pallas_call(
        functools.partial(staged_kernel, kernel, in_specs, out_specs),
        out_shape=tuple(outs),
        in_specs=[SM if spec is SM else ANY for spec in in_specs],
        out_specs=tuple([ANY] * len(outs)),
        scratch_shapes=[pltpu.SemaphoreType.DMA((SEMAPHORES,))] + buffers + list(scratch),
        name=name,
        cost_estimate=cost(ins, outs, flops),
        compiler_params=pltpu.CompilerParams(vmem_limit_bytes=VMEM_LIMIT),
    )(*ins)


def small_call(kernel, name, ins, outs, passing=()):
    first = len(ins)
    last = len(outs)
    outs = list(outs) + [shape(a.shape, a.dtype) for a in passing]
    return pl.pallas_call(
        kernel,
        out_shape=tuple(outs),
        input_output_aliases={first + i: last + i for i in range(len(passing))},
        in_specs=[VM] * first + [ANY] * len(passing),
        out_specs=tuple([VM] * last + [ANY] * len(passing)),
        name=name,
        cost_estimate=cost(ins, outs, 0),
        compiler_params=pltpu.CompilerParams(vmem_limit_bytes=SMALL_LIMIT),
    )(*ins, *passing)


def passed_along(block, axis, distance):
    count = lax.axis_size(axis)
    route = [((i - distance) % count, i) for i in range(count)]
    return lax.ppermute(block, axis, route)


def exchanged(block, axis, distance):
    return lax.ppermute(block, axis, [(i, i ^ distance) for i in range(lax.axis_size(axis))])


def exchanged_with_all(blocks, axis):
    return lax.all_to_all(blocks, axis, 0, 0)


def first_halving(kept, taken, passing=()):
    half = shape((kept.shape[0] // 2,) + kept.shape[1:], BF16)
    return small_call(first_halving_kernel, "first_halving", (kept, taken), [half, half], passing)


def second_halving(kept, taken, passing=()):
    block = kept.shape[1:]
    outs = [shape(block, F32)] + [shape(block, BF16)] * (kept.shape[0] - 1)
    kernel = functools.partial(second_halving_kernel, passing=len(passing))
    return small_call(kernel, "second_halving", (kept, taken), outs, passing)


def last_sum(kept, taken, first_rows, second_rows, nodes=None, passing=()):
    width = kept.shape[1]
    outs = [shape((first_rows, width), F32), shape((second_rows, width), F32)]
    ins = (kept, *taken)
    if nodes is not None:
        outs.append(shape(nodes.shape, BF16))
        ins += (nodes,)
    kernel = functools.partial(
        last_sum_kernel, taken=len(taken), with_nodes=nodes is not None, passing=len(passing)
    )
    return small_call(kernel, "last_sum", ins, outs, passing)


def local(
    nodes,
    fine_edges,
    coarse_edges,
    fine_send,
    fine_recv,
    coarse_send,
    coarse_recv,
    halo_rows,
    edge_count,
    edge_w1,
    edge_w2,
    edge_gain,
    node_w1,
    node_w2,
    node_gain,
    d_nodes,
    d_fine,
    d_coarse,
):
    axis = "patch"
    peers = lax.axis_size(axis)
    own, width = nodes.shape
    fine = fine_edges.shape[0]
    coarse = coarse_edges.shape[0]
    halo = halo_rows[0]
    slots, tile = halo.shape
    hops = slots // 2
    offsets = list(range(1, hops + 1)) + [-k for k in range(1, hops + 1)]
    ordered = peers == 16 and all(
        w.shape[0] % (16 * peers) == 0 for w in (edge_w1, edge_w2, node_w1, node_w2)
    )
    me = lax.axis_index(axis).astype(jnp.int32).reshape(1)
    fs, fr = fine_send.reshape(1, fine), fine_recv.reshape(1, fine)
    cs, cr = coarse_send.reshape(1, coarse), coarse_recv.reshape(1, coarse)
    eg, ng = edge_gain.reshape(1, width), node_gain.reshape(1, width)
    every = shape((peers, COARSE_DEV, width), BF16)

    made = call(
        tiles_kernel, "tiles", (nodes, halo), [VM, VM],
        [shape((tile, width), BF16)] * slots + [every],
    )
    received = [passed_along(made[slot], axis, offset) for slot, offset in enumerate(offsets)]
    coarse_all = exchanged_with_all(made[-1], axis)

    def saved_shapes(rows):
        return [
            shape((rows, width), BF16), shape((rows, width), BF16), shape((rows, width), BF16),
            shape((rows, width), BF16), shape((rows, width), BF16), shape((rows, 128), F32),
        ]

    new_coarse, coarse_part, *coarse_saved = call(
        coarse_forward_kernel, "coarse_forward",
        (coarse_all, coarse_edges, cs, cr, edge_w1, edge_w2, eg), [VM] * 4 + [Rows(3), VM, VM],
        [shape((coarse, width), BF16), every] + saved_shapes(coarse),
        flops=2 * coarse * width * width * 4,
    )
    share = exchanged_with_all(coarse_part, axis)

    block = 256 if fine % 256 == 0 else fine
    space_rows = own + slots * tile
    new_fine, fine_agg, *fine_saved = call(
        functools.partial(fine_forward_kernel, slots=slots, block=block), "fine_forward",
        (edge_count, nodes, *received, fine_edges, fs, fr, edge_w1, edge_w2, eg),
        [SM] + [VM] * (slots + 4) + [Rows(3), VM, VM],
        [shape((fine, width), BF16), shape((own, width), F32)] + saved_shapes(fine),
        scratch=[pltpu.VMEM((space_rows, width), BF16)],
        flops=2 * fine * width * (4 * width + space_rows + 3 * own),
    )

    def weight_shapes(w1, w2, more):
        if not ordered:
            return [shape(w1.shape, F32), shape(w2.shape, F32)], []
        rows = (w1.shape[0] + w2.shape[0]) // peers + more
        outs = [shape((peers // 2, rows, width), BF16)] * 2
        return outs, [pltpu.VMEM(w1.shape, F32), pltpu.VMEM(w2.shape, F32)]

    sum_shapes, sum_scratch = weight_shapes(node_w1, node_w2, 0)
    new_nodes, base, dagg, dagg_spread, *node_parts = call(
        functools.partial(node_kernel, ordered=ordered), "node_both",
        (me, nodes, fine_agg, share, d_nodes, node_w1, node_w2, ng), [SM] + [VM] * 4 + [Rows(2), VM, VM],
        [shape((own, width), BF16), shape((own, width), F32), shape((own, width), BF16), every] + sum_shapes,
        scratch=[pltpu.VMEM((own, width), F32)] + sum_scratch,
        flops=2 * own * width * width * 9,
    )
    dagg_all = exchanged_with_all(dagg_spread, axis)
    if ordered:
        node_taken = exchanged(node_parts[1], axis, 1)
        half = shape((peers // 2 // 2,) + node_parts[0].shape[1:], BF16)
        node_kept, node_given = call(
            first_halving_kernel, "first_halving", (node_parts[0], node_taken, base), [VM, VM, None], [half, half]
        )

    sum_shapes, sum_scratch = weight_shapes(edge_w1, edge_w2, 16)
    f_zs, f_zr, f_hidden, f_slope, f_normed, f_std = fine_saved
    c_zs, c_zr, c_hidden, c_slope, c_normed, c_std = coarse_saved
    pair = [Rows(joined=2), None]
    edges = fine + coarse
    rows_out = shape((edges, width), BF16)
    part = shape((peers * COARSE_DEV, width), F32) if ordered else every
    out, pre, g_fine, g_coarse, coarse_part, own_grad, *pieces = call(
        functools.partial(edge_heads_kernel, block=block, fine=fine), "edge_heads",
        (
            edge_count, fr, dagg, d_fine, d_coarse, eg, f_std, c_std, f_normed, c_normed, edge_w2, f_slope, c_slope,
            edge_w1, fs, cr, dagg_all, cs, base,
        ),
        [SM, VM, VM] + pair + [VM] + pair * 2 + [VM] + pair + [Rows(3)] + [VM] * 5,
        [rows_out, rows_out, shape((fine, width), BF16), shape((coarse, width), BF16), part]
        + [shape((own, width), F32)] + [shape((tile, width), BF16)] * slots,
        scratch=[pltpu.VMEM((space_rows, width), F32)],
        flops=2 * edges * width * (4 * width + space_rows + 2 * own),
    )
    if ordered:
        node_taken = exchanged(node_given, axis, 2)
    edge_parts = call(
        functools.partial(edge_weights_kernel, ordered=ordered), "edge_weights",
        (
            me, f_hidden, c_hidden, out, fine_edges, coarse_edges, pre, f_zs, c_zs, f_zr, c_zr, coarse_part,
            *((node_taken,) if ordered else ()),
        ),
        [SM] + pair + [VM] + pair + [VM] + pair * 2 + [VM if ordered else None] + [None] * ordered,
        sum_shapes,
        scratch=sum_scratch,
        flops=2 * edges * width * width * 4,
    )

    def rows_of(w):
        return w.shape[0] // peers

    def returned_tiles(pieces):
        returned = [passed_along(pieces[slot], axis, -offset) for slot, offset in enumerate(offsets)]
        (total,) = small_call(
            node_gradient_kernel, "node_gradient", (own_grad, halo, *returned), [shape((own, width), F32)]
        )
        return total

    if ordered:
        edge_kept, edge_given = edge_parts
        edge_taken = exchanged(edge_given, axis, 1)
        edge_kept, edge_given = first_halving(edge_kept, edge_taken)
        edge_taken = exchanged(edge_given, axis, 2)
        node_kept, *given = second_halving(node_kept, node_taken)
        node_taken = [exchanged(part, axis, 4 * (k + 1)) for k, part in enumerate(given)]
        g_nw1, g_nw2, edge_kept = last_sum(
            node_kept, node_taken, rows_of(node_w1), rows_of(node_w2), passing=(edge_kept,)
        )
        edge_kept, *given = second_halving(edge_kept, edge_taken, tuple(pieces))
        given, pieces = given[:-slots], given[-slots:]
        edge_taken = [exchanged(part, axis, 4 * (k + 1)) for k, part in enumerate(given)]
        total = returned_tiles(pieces)
        g_ew1, g_ew2, g_nodes = last_sum(edge_kept, edge_taken, rows_of(edge_w1), rows_of(edge_w2), total)
    else:
        coarse_share = exchanged_with_all(coarse_part, axis)
        (g_nodes,) = small_call(
            coarse_gradient_kernel, "coarse_gradient", (returned_tiles(pieces), coarse_share),
            [shape((own, width), BF16)],
        )
        g_nw1, g_nw2, g_ew1, g_ew2 = [
            lax.psum_scatter(g, axis, scatter_dimension=0, tiled=True) for g in [*node_parts, *edge_parts]
        ]
    return (new_nodes, new_fine, new_coarse, g_nodes, g_fine, g_coarse, g_ew1, g_ew2, g_nw1, g_nw2)


def solution(mesh):
    split = P(("groups", "patch"))
    rows = P(("groups", "patch"), None)
    return jax.shard_map(
        local,
        mesh=mesh,
        in_specs=(
            rows, rows, rows, split, split, split, split, P(("groups", "patch"), None, None), split,
            P(), P(), P(), P(), P(), P(), rows, rows, rows,
        ),
        out_specs=(rows,) * 10,
        check_vma=False,
    )
```

```python
import functools

import jax
import jax.numpy as jnp
from jax import lax
from jax.experimental import pallas as pl
from jax.experimental.pallas import tpu as pltpu
from jax.sharding import PartitionSpec as P

COARSE_DEV = 8
EPSILON = 1e-05
F32 = jnp.float32
BF16 = jnp.bfloat16
VMEM_LIMIT = 60 * 1024 * 1024
SMALL_LIMIT = 16 * 1024 * 1024


def mm(a, b):
    return lax.dot_general(a, b, (((1,), (0,)), ((), ())), preferred_element_type=F32)


def mm_nt(a, b):
    return lax.dot_general(a, b, (((1,), (1,)), ((), ())), preferred_element_type=F32)


def mm_tn(a, b):
    return lax.dot_general(a, b, (((0,), (0,)), ((), ())), preferred_element_type=F32)


def halves(value):
    high = value.astype(BF16)
    low = (value - high.astype(F32)).astype(BF16)
    return high, low


def one_hot(index, rows):
    row = lax.broadcasted_iota(jnp.int32, (rows, index.shape[1]), 0)
    return jnp.where(row == index, 1.0, 0.0).astype(BF16)


def pick(index, table):
    entries = index.shape[1]
    column = jnp.transpose(jnp.broadcast_to(index, (128, entries)))
    lane = lax.broadcasted_iota(jnp.int32, (entries, 128), 1)
    parts = []
    for start in range(0, table.shape[0], 128):
        parts.append(jnp.where(column == lane + start, 1.0, 0.0).astype(BF16))
    return mm(jnp.concatenate(parts, 1), table)


def put_wide(hot, rows):
    high, low = halves(rows)
    return mm(hot, high) + mm(hot, low)


def row_mean(value):
    return jnp.mean(value, axis=-1, keepdims=True)


def tail_of_forward(pre, second_w, gain):
    sigmoid = jax.nn.sigmoid(pre)
    hidden = (pre * sigmoid).astype(BF16)
    slope = sigmoid * (1.0 + pre * (1.0 - sigmoid))
    output = mm(hidden, second_w)
    centred = output - row_mean(output)
    inv_std = lax.rsqrt(row_mean(centred * centred) + EPSILON)
    normed = centred * inv_std
    return normed * gain, hidden, slope, normed, inv_std


def head_of_backward(cotan, second_w, gain, slope, normed, inv_std):
    scaled = cotan * gain
    back_out = inv_std * (scaled - row_mean(scaled) - normed * row_mean(scaled * normed))
    back_out = back_out.astype(BF16)
    back_pre = (mm_nt(back_out, second_w) * slope).astype(BF16)
    return back_out, back_pre


def tiles_kernel(nodes_ref, halo_ref, *outs):
    nodes = nodes_ref[...]
    for slot, out in enumerate(outs):
        out[...] = pick(halo_ref[slot : slot + 1, :], nodes).astype(BF16)
        out.done()


def gathered(ref):
    value = ref[...].astype(F32)
    return value.reshape(value.shape[0] * value.shape[1], value.shape[2])


def coarse_forward_kernel(
    all_ref, edges_ref, send_ref, recv_ref, w1_ref, w2_ref, gain_ref,
    new_ref, part_ref, zs_ref, zr_ref, hidden_ref, slope_ref, normed_ref, std_ref,
):
    width = edges_ref.shape[1]
    table = gathered(all_ref).astype(BF16)
    hot_r = one_hot(recv_ref[...], table.shape[0])
    edges = edges_ref[...]
    zs = pick(send_ref[...], table).astype(BF16)
    zr = pick(recv_ref[...], table).astype(BF16)
    pre = (
        mm(edges, w1_ref[0:width, :])
        + mm(zs, w1_ref[width : 2 * width, :])
        + mm(zr, w1_ref[2 * width : 3 * width, :])
    )
    message, hidden, slope, normed, inv_std = tail_of_forward(pre, w2_ref[...], gain_ref[...])
    total = put_wide(hot_r, message)
    part_ref[...] = total.reshape(part_ref.shape).astype(BF16)
    part_ref.done()
    new_ref[...] = (edges.astype(F32) + message).astype(BF16)
    zs_ref[...] = zs
    zr_ref[...] = zr
    hidden_ref[...] = hidden
    slope_ref[...] = slope.astype(BF16)
    normed_ref[...] = normed.astype(BF16)
    std_ref[...] = jnp.broadcast_to(inv_std, std_ref.shape)


def fine_forward_kernel(count_ref, nodes_ref, *refs, slots, block):
    tile_refs = refs[:slots]
    (
        edges_ref, send_ref, recv_ref, w1_ref, w2_ref, gain_ref,
        new_ref, agg_ref, zs_ref, zr_ref, hidden_ref, slope_ref, normed_ref, std_ref, space_ref,
    ) = refs[slots:]
    count, width = edges_ref.shape
    own = nodes_ref.shape[0]
    tile = tile_refs[0].shape[0]
    space_ref[0:own, :] = nodes_ref[...]
    for slot in range(slots):
        space_ref[own + slot * tile : own + (slot + 1) * tile, :] = tile_refs[slot][...]
    for start in range(0, count, block):
        rows = slice(start, start + block)
        edges = edges_ref[rows, :]
        hot_r = one_hot(recv_ref[:, rows], own)
        zs = pick(send_ref[:, rows], space_ref[...]).astype(BF16)
        zr = pick(recv_ref[:, rows], nodes_ref[...]).astype(BF16)
        pre = (
            mm(edges, w1_ref[0:width, :])
            + mm(zs, w1_ref[width : 2 * width, :])
            + mm(zr, w1_ref[2 * width : 3 * width, :])
        )
        message, hidden, slope, normed, inv_std = tail_of_forward(pre, w2_ref[...], gain_ref[...])
        place = start + lax.broadcasted_iota(jnp.int32, (block, 1), 0)
        message = jnp.where(place < count_ref[0], message, 0.0)
        arrived = put_wide(hot_r, message)
        agg_ref[...] = arrived if start == 0 else agg_ref[...] + arrived
        new_ref[rows, :] = (edges.astype(F32) + message).astype(BF16)
        zs_ref[rows, :] = zs
        zr_ref[rows, :] = zr
        hidden_ref[rows, :] = hidden
        slope_ref[rows, :] = slope.astype(BF16)
        normed_ref[rows, :] = normed.astype(BF16)
        std_ref[rows, :] = jnp.broadcast_to(inv_std, (block, std_ref.shape[1]))
        for ref in (new_ref, zs_ref, zr_ref, hidden_ref, slope_ref, normed_ref, std_ref):
            ref.done(rows)


def by_distance(me, peers, sums, kept_ref, given_ref):
    quarter = peers // 4
    for r in list(range(1, peers, 2)) + list(range(0, peers, 2)):
        if r == 0:
            given_ref.done()
        to = jnp.bitwise_xor(me, r)
        out = given_ref if r % 2 else kept_ref
        slot = (r // 2 % 2) * quarter + r // 4
        place = 0
        for total in sums:
            rows = total.shape[0] // peers
            part = total[pl.ds(pl.multiple_of(to * rows, 8), rows), :]
            if rows % 16:
                part = jnp.concatenate([part, jnp.zeros((-rows % 16, part.shape[1]), F32)], 0)
            out[slot, place : place + part.shape[0], :] = part.astype(BF16)
            place += part.shape[0]
    kept_ref.done()


def node_kernel(
    me_ref, nodes_ref, agg_ref, share_ref, d_ref, w1_ref, w2_ref, gain_ref,
    new_ref, base_ref, dagg_ref, spread_ref, *rest, ordered,
):
    if ordered:
        kept_ref, given_ref, total_ref, g1_ref, g2_ref = rest
    else:
        g1_ref, g2_ref, total_ref = rest
    width = nodes_ref.shape[1]
    total_ref[...] = agg_ref[...]
    total_ref[0:COARSE_DEV, :] += jnp.sum(share_ref[...].astype(F32), 0)
    nodes = nodes_ref[...]
    agg = total_ref[...].astype(BF16)
    pre = mm(nodes, w1_ref[0:width, :]) + mm(agg, w1_ref[width : 2 * width, :])
    update, hidden, slope, normed, inv_std = tail_of_forward(pre, w2_ref[...], gain_ref[...])
    new_ref[...] = (nodes.astype(F32) + update).astype(BF16)
    cotan = d_ref[...].astype(F32)
    back_out, back_pre = head_of_backward(cotan, w2_ref[...], gain_ref[...], slope, normed, inv_std)
    dagg = mm_nt(back_pre, w1_ref[width : 2 * width, :])
    dagg_ref[...] = dagg.astype(BF16)
    rows = dagg[:COARSE_DEV].astype(BF16)
    for peer in range(spread_ref.shape[0]):
        spread_ref[peer] = rows
    base_ref[...] = cotan + mm_nt(back_pre, w1_ref[0:width, :])
    g1_ref[0:width, :] = mm_tn(nodes, back_pre)
    g1_ref[width : 2 * width, :] = mm_tn(agg, back_pre)
    g2_ref[...] = mm_tn(hidden, back_out)
    if ordered:
        by_distance(me_ref[0], spread_ref.shape[0], (g1_ref, g2_ref), kept_ref, given_ref)


def edge_heads_kernel(
    count_ref, recv_ref, dagg_ref, d_ref, gain_ref, std_ref, normed_ref, w2_ref, slope_ref,
    w1_ref, send_ref, crecv_ref, all_ref, csend_ref, base_ref,
    out_ref, pre_ref, g_ref, gc_ref, part_ref, own_ref, *rest, block, fine,
):
    piece_refs, space_ref = rest[:-1], rest[-1]
    count, width = d_ref.shape
    own = base_ref.shape[0]
    received = None
    for start in list(range(0, fine, block)) + [fine]:
        rows = slice(start, start + block if start < fine else count)
        d_edges = d_ref[rows, :].astype(F32)
        if start < fine:
            hot_r = one_hot(recv_ref[:, rows], own)
            hot_s = one_hot(send_ref[:, rows], space_ref.shape[0])
            place = start + lax.broadcasted_iota(jnp.int32, (block, 1), 0)
            cotan = jnp.where(place < count_ref[0], d_edges + pick(recv_ref[:, rows], dagg_ref[...]), 0.0)
        else:
            table = gathered(all_ref).astype(BF16)
            hot_r = one_hot(crecv_ref[...], table.shape[0])
            hot_s = one_hot(csend_ref[...], table.shape[0])
            cotan = d_edges + pick(crecv_ref[...], table)
        back_out, back_pre = head_of_backward(
            cotan, w2_ref[...], gain_ref[...], slope_ref[rows, :].astype(F32),
            normed_ref[rows, :].astype(F32), std_ref[rows, 0:1],
        )
        out_ref[rows, :] = back_out
        pre_ref[rows, :] = back_pre
        out_ref.done(rows)
        pre_ref.done(rows)
        grads = (d_edges + mm_nt(back_pre, w1_ref[0:width, :])).astype(BF16)
        sent = mm(hot_s, mm_nt(back_pre, w1_ref[width : 2 * width, :]).astype(BF16))
        arrived = mm(hot_r, mm_nt(back_pre, w1_ref[2 * width : 3 * width, :]).astype(BF16))
        if start < fine:
            g_ref[rows, :] = grads
            g_ref.done(rows)
            space_ref[...] = sent if start == 0 else space_ref[...] + sent
            received = arrived if received is None else received + arrived
        else:
            gc_ref[...] = grads
            part_ref[...] = (sent + arrived).reshape(part_ref.shape).astype(part_ref.dtype)
        if start + block == fine:
            for slot, piece in enumerate(piece_refs):
                tile = piece.shape[0]
                piece[...] = space_ref[own + slot * tile : own + (slot + 1) * tile, :].astype(BF16)
                piece.done()
            own_ref[...] = base_ref[...] + received + space_ref[0:own, :]
            own_ref.done()


def edge_weights_kernel(
    me_ref, edges_ref, pre_ref, zs_ref, zr_ref, hidden_ref, out_ref, *rest, ordered,
):
    if ordered:
        part_ref, kept1_ref, given1_ref, kept2_ref, given2_ref, g1_ref, g2_ref = rest
    else:
        g1_ref, g2_ref = rest
    width = edges_ref.shape[1]
    g1_ref[0:width, :] = mm_tn(edges_ref[...], pre_ref[...])
    g1_ref[width : 2 * width, :] = mm_tn(zs_ref[...], pre_ref[...])
    g1_ref[2 * width : 3 * width, :] = mm_tn(zr_ref[...], pre_ref[...])
    if ordered:
        by_distance(me_ref[0], 2 * kept1_ref.shape[0], (g1_ref,), kept1_ref, given1_ref)
    g2_ref[...] = mm_tn(hidden_ref[...], out_ref[...])
    if ordered:
        by_distance(me_ref[0], 2 * kept2_ref.shape[0], (g2_ref, part_ref), kept2_ref, given2_ref)


def node_gradient_kernel(own_ref, halo_ref, *refs):
    piece_refs, out_ref = refs[:-1], refs[-1]
    arrived = None
    for slot, piece in enumerate(piece_refs):
        part = mm(one_hot(halo_ref[slot : slot + 1, :], own_ref.shape[0]), piece[...])
        arrived = part if arrived is None else arrived + part
    out_ref[...] = own_ref[...] + arrived


def coarse_gradient_kernel(total_ref, share_ref, g_ref):
    share = jnp.sum(share_ref[...].astype(F32), 0)
    first = total_ref[0:16, :] + jnp.concatenate([share, jnp.zeros_like(share)], 0)
    g_ref[...] = total_ref[...].astype(BF16)
    g_ref[0:16, :] = first.astype(BF16)


def second_halving_kernel(kept_ref, taken_ref, *refs, passing):
    keep_ref, give_refs = refs[passing], refs[passing + 1 : len(refs) - passing]
    for j in range(kept_ref.shape[0]):
        total = kept_ref[j].astype(F32) + taken_ref[j].astype(F32)
        if j:
            give_refs[j - 1][...] = total.astype(BF16)
        else:
            keep_ref[...] = total


def last_sum_kernel(kept_ref, *refs, taken):
    total = kept_ref[...]
    for ref in refs[:taken]:
        total = total + ref[...].astype(F32)
    refs = refs[taken:]
    if refs[0].shape[0] > total.shape[0]:
        nodes_ref, first_ref, g_ref = refs
        cut = first_ref.shape[0]
        first_ref[...] = total[:cut]
        g_ref[...] = nodes_ref[...].astype(BF16)
        g_ref[0:16, :] = (nodes_ref[0:16, :] + total[cut : cut + 16]).astype(BF16)
        return
    place = 0
    for ref in refs:
        ref[...] = total[place : place + ref.shape[0]]
        place += ref.shape[0]


VM = pl.BlockSpec(memory_space=pltpu.VMEM)
SM = pl.BlockSpec(memory_space=pltpu.SMEM)
ANY = pl.BlockSpec(memory_space=pl.ANY)


def shape(dims, dtype):
    return jax.ShapeDtypeStruct(tuple(dims), dtype)


class Rows:
    def __init__(self, parts=1, joined=1, extra=0):
        self.parts = parts
        self.joined = joined
        self.extra = extra


class Fetched:
    def __init__(self, sources, buffer, semaphores, parts):
        self.buffer = buffer
        self.shape = buffer.shape
        self.waiting = []
        place = 0
        for source in sources:
            rows = source.shape[0] // parts
            for part in range(parts):
                if source.shape == buffer.shape and parts == 1:
                    copy = pltpu.make_async_copy(source, buffer, next(semaphores))
                else:
                    copy = pltpu.make_async_copy(
                        source.at[pl.ds(part * rows, rows)], buffer.at[pl.ds(place, rows)], next(semaphores)
                    )
                copy.start()
                self.waiting.append((place, place + rows, copy))
                place += rows

    def ready(self, low=0, high=None):
        left = []
        for first, last, copy in self.waiting:
            if high is None or (first < high and low < last):
                copy.wait()
            else:
                left.append((first, last, copy))
        self.waiting = left

    def __getitem__(self, index):
        rows = index[0] if isinstance(index, tuple) else None
        if isinstance(rows, slice) and rows.start is not None:
            self.ready(rows.start, rows.stop)
        else:
            self.ready()
        return self.buffer[index]

    def __setitem__(self, index, value):
        self.buffer[index] = value


class Stored:
    def __init__(self, target, buffer, semaphores):
        self.target = target
        self.buffer = buffer
        self.shape = buffer.shape
        self.dtype = buffer.dtype
        self.semaphores = semaphores
        self.copies = []

    def __getitem__(self, index):
        return self.buffer[index]

    def __setitem__(self, index, value):
        self.buffer[index] = value

    def done(self, rows=None):
        if rows is None:
            copy = pltpu.make_async_copy(self.buffer, self.target, next(self.semaphores))
        else:
            part = pl.ds(rows.start, rows.stop - rows.start)
            copy = pltpu.make_async_copy(self.buffer.at[part], self.target.at[part], next(self.semaphores))
        copy.start()
        self.copies.append(copy)


SEMAPHORES = 64


def staged_kernel(body, in_specs, out_specs, *refs):
    ins, outs = refs[: len(in_specs)], refs[len(in_specs) : len(in_specs) + len(out_specs)]
    rest = refs[len(in_specs) + len(out_specs) :]
    semaphores = iter([rest[0].at[i] for i in range(SEMAPHORES)])
    buffers = iter(rest[1:])
    fetched, stored = [], []
    for place, (ref, spec) in enumerate(zip(ins, in_specs)):
        if spec is VM:
            fetched.append(Fetched([ref], next(buffers), semaphores, 1))
        elif spec is SM:
            fetched.append(ref)
        elif isinstance(spec, Rows):
            fetched.append(Fetched(ins[place : place + spec.joined], next(buffers), semaphores, spec.parts))
    for ref, spec in zip(outs, out_specs):
        stored.append(Stored(ref, next(buffers), semaphores))
    body(*fetched, *stored, *buffers)
    for ref in fetched:
        if isinstance(ref, Fetched):
            ref.ready()
    for ref in stored:
        if not ref.copies:
            ref.done()
    for ref in stored:
        for copy in ref.copies:
            copy.wait()


def cost(ins, outs, flops):
    moved = sum(a.size * a.dtype.itemsize for a in list(ins) + list(outs))
    return pl.CostEstimate(flops=flops, bytes_accessed=moved, transcendentals=0)


def call(kernel, name, ins, in_specs, outs, scratch=(), flops=0):
    out_specs = [VM] * len(outs)
    buffers = []
    for place, spec in enumerate(in_specs):
        if spec is VM:
            buffers.append(pltpu.VMEM(ins[place].shape, ins[place].dtype))
        elif isinstance(spec, Rows):
            joined = ins[place : place + spec.joined]
            rows = sum(a.shape[0] for a in joined) + spec.extra
            buffers.append(pltpu.VMEM((rows,) + joined[0].shape[1:], joined[0].dtype))
    buffers += [pltpu.VMEM(a.shape, a.dtype) for a in outs]
    return pl.pallas_call(
        functools.partial(staged_kernel, kernel, in_specs, out_specs),
        out_shape=tuple(outs),
        in_specs=[SM if spec is SM else ANY for spec in in_specs],
        out_specs=tuple([ANY] * len(outs)),
        scratch_shapes=[pltpu.SemaphoreType.DMA((SEMAPHORES,))] + buffers + list(scratch),
        name=name,
        cost_estimate=cost(ins, outs, flops),
        compiler_params=pltpu.CompilerParams(vmem_limit_bytes=VMEM_LIMIT),
    )(*ins)


def small_call(kernel, name, ins, outs, passing=()):
    first = len(ins)
    last = len(outs)
    outs = list(outs) + [shape(a.shape, a.dtype) for a in passing]
    return pl.pallas_call(
        kernel,
        out_shape=tuple(outs),
        input_output_aliases={first + i: last + i for i in range(len(passing))},
        in_specs=[VM] * first + [ANY] * len(passing),
        out_specs=tuple([VM] * last + [ANY] * len(passing)),
        name=name,
        cost_estimate=cost(ins, outs, 0),
        compiler_params=pltpu.CompilerParams(vmem_limit_bytes=SMALL_LIMIT),
    )(*ins, *passing)


def passed_along(block, axis, distance):
    count = lax.axis_size(axis)
    route = [((i - distance) % count, i) for i in range(count)]
    return lax.ppermute(block, axis, route)


def exchanged(block, axis, distance):
    return lax.ppermute(block, axis, [(i, i ^ distance) for i in range(lax.axis_size(axis))])


def exchanged_with_all(blocks, axis):
    return lax.all_to_all(blocks, axis, 0, 0)


def first_halving(kept, taken):
    half = kept.shape[0] // 2
    give = (kept[half:].astype(F32) + taken[half:].astype(F32)).astype(BF16)
    return kept[:half].astype(F32) + taken[:half].astype(F32), give


def second_halving(kept, taken, passing=()):
    block = kept.shape[1:]
    outs = [shape(block, F32)] + [shape(block, BF16)] * (kept.shape[0] - 1)
    kernel = functools.partial(second_halving_kernel, passing=len(passing))
    return small_call(kernel, "second_halving", (kept, taken), outs, passing)


def last_sum(kept, taken, sizes, nodes=None):
    outs = [shape((rows, kept.shape[1]), F32) for rows in sizes]
    ins = (kept, *taken)
    if nodes is not None:
        outs.append(shape(nodes.shape, BF16))
        ins += (nodes,)
    return small_call(functools.partial(last_sum_kernel, taken=len(taken)), "last_sum", ins, outs)


def local(
    nodes,
    fine_edges,
    coarse_edges,
    fine_send,
    fine_recv,
    coarse_send,
    coarse_recv,
    halo_rows,
    edge_count,
    edge_w1,
    edge_w2,
    edge_gain,
    node_w1,
    node_w2,
    node_gain,
    d_nodes,
    d_fine,
    d_coarse,
):
    axis = "patch"
    peers = lax.axis_size(axis)
    own, width = nodes.shape
    fine = fine_edges.shape[0]
    coarse = coarse_edges.shape[0]
    halo = halo_rows[0]
    slots, tile = halo.shape
    hops = slots // 2
    offsets = list(range(1, hops + 1)) + [-k for k in range(1, hops + 1)]
    ordered = peers == 16 and all(
        w.shape[0] % (16 * peers) == 0 for w in (edge_w1, edge_w2, node_w1, node_w2)
    )
    me = lax.axis_index(axis).astype(jnp.int32).reshape(1)
    fs, fr = fine_send.reshape(1, fine), fine_recv.reshape(1, fine)
    cs, cr = coarse_send.reshape(1, coarse), coarse_recv.reshape(1, coarse)
    eg, ng = edge_gain.reshape(1, width), node_gain.reshape(1, width)
    every = shape((peers, COARSE_DEV, width), BF16)

    made = call(
        tiles_kernel, "tiles", (nodes, halo), [VM, VM],
        [shape((tile, width), BF16)] * slots,
    )
    received = [passed_along(made[slot], axis, offset) for slot, offset in enumerate(offsets)]
    coarse_all = exchanged_with_all(jnp.broadcast_to(nodes[:COARSE_DEV][None], every.shape), axis)

    def saved_shapes(rows):
        return [
            shape((rows, width), BF16), shape((rows, width), BF16), shape((rows, width), BF16),
            shape((rows, width), BF16), shape((rows, width), BF16), shape((rows, 128), F32),
        ]

    new_coarse, coarse_part, *coarse_saved = call(
        coarse_forward_kernel, "coarse_forward",
        (coarse_all, coarse_edges, cs, cr, edge_w1, edge_w2, eg), [VM] * 4 + [Rows(3), VM, VM],
        [shape((coarse, width), BF16), every] + saved_shapes(coarse),
        flops=2 * coarse * width * width * 4,
    )
    share = exchanged_with_all(coarse_part, axis)

    block = 256 if fine % 256 == 0 else fine
    space_rows = own + slots * tile
    new_fine, fine_agg, *fine_saved = call(
        functools.partial(fine_forward_kernel, slots=slots, block=block), "fine_forward",
        (edge_count, nodes, *received, fine_edges, fs, fr, edge_w1, edge_w2, eg),
        [SM] + [VM] * (slots + 4) + [Rows(3), VM, VM],
        [shape((fine, width), BF16), shape((own, width), F32)] + saved_shapes(fine),
        scratch=[pltpu.VMEM((space_rows, width), BF16)],
        flops=2 * fine * width * (4 * width + space_rows + 3 * own),
    )

    def weight_shapes(w1, w2, more):
        if not ordered:
            return [shape(w1.shape, F32), shape(w2.shape, F32)], []
        rows = (w1.shape[0] + w2.shape[0]) // peers + more
        outs = [shape((peers // 2, rows, width), BF16)] * 2
        return outs, [pltpu.VMEM(w1.shape, F32), pltpu.VMEM(w2.shape, F32)]

    sum_shapes, sum_scratch = weight_shapes(node_w1, node_w2, 0)
    new_nodes, base, dagg, dagg_spread, *node_parts = call(
        functools.partial(node_kernel, ordered=ordered), "node_both",
        (me, nodes, fine_agg, share, d_nodes, node_w1, node_w2, ng), [SM] + [VM] * 4 + [Rows(2), VM, VM],
        [shape((own, width), BF16), shape((own, width), F32), shape((own, width), BF16), every] + sum_shapes,
        scratch=[pltpu.VMEM((own, width), F32)] + sum_scratch,
        flops=2 * own * width * width * 9,
    )
    dagg_all = exchanged_with_all(dagg_spread, axis)
    if ordered:
        node_taken = exchanged(node_parts[1], axis, 1)
        node_kept, node_given = first_halving(node_parts[0], node_taken)

    sum_shapes, sum_scratch = weight_shapes(edge_w1, edge_w2, 16)
    if ordered:
        cut = edge_w1.shape[0] // peers
        rows = sum_shapes[0].shape[1] - cut
        sum_shapes = [shape((peers // 2, cut, width), BF16)] * 2 + [shape((peers // 2, rows, width), BF16)] * 2
    f_zs, f_zr, f_hidden, f_slope, f_normed, f_std = fine_saved
    c_zs, c_zr, c_hidden, c_slope, c_normed, c_std = coarse_saved
    pair = [Rows(joined=2), None]
    edges = fine + coarse
    rows_out = shape((edges, width), BF16)
    part = shape((peers * COARSE_DEV, width), F32) if ordered else every
    out, pre, g_fine, g_coarse, coarse_part, own_grad, *pieces = call(
        functools.partial(edge_heads_kernel, block=block, fine=fine), "edge_heads",
        (
            edge_count, fr, dagg, d_fine, d_coarse, eg, f_std, c_std, f_normed, c_normed, edge_w2, f_slope, c_slope,
            edge_w1, fs, cr, dagg_all, cs, base,
        ),
        [SM, VM, VM] + pair + [VM] + pair * 2 + [VM] + pair + [Rows(3)] + [VM] * 5,
        [rows_out, rows_out, shape((fine, width), BF16), shape((coarse, width), BF16), part]
        + [shape((own, width), F32)] + [shape((tile, width), BF16)] * slots,
        scratch=[pltpu.VMEM((space_rows, width), F32)],
        flops=2 * edges * width * (4 * width + space_rows + 2 * own),
    )
    if ordered:
        node_taken = exchanged(node_given, axis, 2)
    edge_parts = call(
        functools.partial(edge_weights_kernel, ordered=ordered), "edge_weights",
        (
            me, fine_edges, coarse_edges, pre, f_zs, c_zs, f_zr, c_zr, f_hidden, c_hidden, out, coarse_part,
            *((node_taken,) if ordered else ()),
        ),
        [SM] + pair + [VM] + pair * 3 + [VM] + [VM if ordered else None] + [None] * ordered,
        sum_shapes,
        scratch=sum_scratch,
        flops=2 * edges * width * width * 4,
    )

    def rows_of(w):
        return w.shape[0] // peers

    def returned_tiles(pieces):
        returned = [passed_along(pieces[slot], axis, -offset) for slot, offset in enumerate(offsets)]
        (total,) = small_call(
            node_gradient_kernel, "node_gradient", (own_grad, halo, *returned), [shape((own, width), F32)]
        )
        return total

    if ordered:

        def along_z(given):
            return [exchanged(part, axis, 4 * (k + 1)) for k, part in enumerate(given)]

        kept1, given1, kept2, given2 = edge_parts
        taken1 = exchanged(given1, axis, 1)
        taken2 = exchanged(given2, axis, 1)
        kept1, given1 = first_halving(kept1, taken1)
        taken1 = exchanged(given1, axis, 2)
        kept2, given2 = first_halving(kept2, taken2)
        taken2 = exchanged(given2, axis, 2)
        node_kept, *given = second_halving(node_kept, node_taken)
        g_nw1, g_nw2 = last_sum(node_kept, along_z(given), (rows_of(node_w1), rows_of(node_w2)))
        kept1, *given = second_halving(kept1, taken1, tuple(pieces))
        given, pieces = given[:-slots], given[-slots:]
        taken1 = along_z(given)
        kept2, *given = second_halving(kept2, taken2)
        taken2 = along_z(given)
        total = returned_tiles(pieces)
        (g_ew1,) = last_sum(kept1, taken1, (rows_of(edge_w1),))
        g_ew2, g_nodes = last_sum(kept2, taken2, (rows_of(edge_w2),), total)
    else:
        coarse_share = exchanged_with_all(coarse_part, axis)
        (g_nodes,) = small_call(
            coarse_gradient_kernel, "coarse_gradient", (returned_tiles(pieces), coarse_share),
            [shape((own, width), BF16)],
        )
        g_nw1, g_nw2, g_ew1, g_ew2 = [
            lax.psum_scatter(g, axis, scatter_dimension=0, tiled=True) for g in [*node_parts, *edge_parts]
        ]
    return (new_nodes, new_fine, new_coarse, g_nodes, g_fine, g_coarse, g_ew1, g_ew2, g_nw1, g_nw2)


def solution(mesh):
    split = P(("groups", "patch"))
    rows = P(("groups", "patch"), None)
    return jax.shard_map(
        local,
        mesh=mesh,
        in_specs=(
            rows, rows, rows, split, split, split, split, P(("groups", "patch"), None, None), split,
            P(), P(), P(), P(), P(), P(), rows, rows, rows,
        ),
        out_specs=(rows,) * 10,
        check_vma=False,
    )
```

```python
import functools

import jax
import jax.numpy as jnp
from jax import lax
from jax.experimental import pallas as pl
from jax.experimental.pallas import tpu as pltpu
from jax.sharding import PartitionSpec as P

COARSE_DEV = 8
EPSILON = 1e-05
F32 = jnp.float32
BF16 = jnp.bfloat16
VMEM_LIMIT = 60 * 1024 * 1024
SMALL_LIMIT = 16 * 1024 * 1024


def mm(a, b):
    return lax.dot_general(a, b, (((1,), (0,)), ((), ())), preferred_element_type=F32)


def mm_nt(a, b):
    return lax.dot_general(a, b, (((1,), (1,)), ((), ())), preferred_element_type=F32)


def mm_tn(a, b):
    return lax.dot_general(a, b, (((0,), (0,)), ((), ())), preferred_element_type=F32)


def halves(value):
    high = value.astype(BF16)
    low = (value - high.astype(F32)).astype(BF16)
    return high, low


def one_hot(index, rows):
    row = lax.broadcasted_iota(jnp.int32, (rows, index.shape[1]), 0)
    return jnp.where(row == index, 1.0, 0.0).astype(BF16)


def pick(index, table):
    entries = index.shape[1]
    column = jnp.transpose(jnp.broadcast_to(index, (128, entries)))
    lane = lax.broadcasted_iota(jnp.int32, (entries, 128), 1)
    parts = []
    for start in range(0, table.shape[0], 128):
        parts.append(jnp.where(column == lane + start, 1.0, 0.0).astype(BF16))
    return mm(jnp.concatenate(parts, 1), table)


def put_wide(hot, rows):
    high, low = halves(rows)
    return mm(hot, high) + mm(hot, low)


def row_mean(value):
    return jnp.mean(value, axis=-1, keepdims=True)


def tail_of_forward(pre, second_w, gain):
    sigmoid = jax.nn.sigmoid(pre)
    hidden = (pre * sigmoid).astype(BF16)
    slope = sigmoid * (1.0 + pre * (1.0 - sigmoid))
    output = mm(hidden, second_w)
    centred = output - row_mean(output)
    inv_std = lax.rsqrt(row_mean(centred * centred) + EPSILON)
    normed = centred * inv_std
    return normed * gain, hidden, slope, normed, inv_std


def head_of_backward(cotan, second_w, gain, slope, normed, inv_std):
    scaled = cotan * gain
    back_out = inv_std * (scaled - row_mean(scaled) - normed * row_mean(scaled * normed))
    back_out = back_out.astype(BF16)
    back_pre = (mm_nt(back_out, second_w) * slope).astype(BF16)
    return back_out, back_pre


def tiles_kernel(nodes_ref, halo_ref, *outs):
    nodes = nodes_ref[...]
    for slot, out in enumerate(outs):
        out[...] = pick(halo_ref[slot : slot + 1, :], nodes).astype(BF16)
        out.done()


def gathered(ref):
    value = ref[...].astype(F32)
    return value.reshape(value.shape[0] * value.shape[1], value.shape[2])


def coarse_forward_kernel(
    all_ref, edges_ref, send_ref, recv_ref, w1_ref, w2_ref, gain_ref,
    new_ref, part_ref, zs_ref, zr_ref, hidden_ref, slope_ref, normed_ref, std_ref,
):
    width = edges_ref.shape[1]
    table = gathered(all_ref).astype(BF16)
    hot_r = one_hot(recv_ref[...], table.shape[0])
    edges = edges_ref[...]
    zs = pick(send_ref[...], table).astype(BF16)
    zr = pick(recv_ref[...], table).astype(BF16)
    pre = (
        mm(edges, w1_ref[0:width, :])
        + mm(zs, w1_ref[width : 2 * width, :])
        + mm(zr, w1_ref[2 * width : 3 * width, :])
    )
    message, hidden, slope, normed, inv_std = tail_of_forward(pre, w2_ref[...], gain_ref[...])
    total = put_wide(hot_r, message)
    part_ref[...] = total.reshape(part_ref.shape).astype(BF16)
    part_ref.done()
    new_ref[...] = (edges.astype(F32) + message).astype(BF16)
    zs_ref[...] = zs
    zr_ref[...] = zr
    hidden_ref[...] = hidden
    slope_ref[...] = slope.astype(BF16)
    normed_ref[...] = normed.astype(BF16)
    std_ref[...] = jnp.broadcast_to(inv_std, std_ref.shape)


def fine_forward_kernel(count_ref, nodes_ref, *refs, slots, block):
    tile_refs = refs[:slots]
    (
        edges_ref, send_ref, recv_ref, w1_ref, w2_ref, gain_ref,
        new_ref, agg_ref, zs_ref, zr_ref, hidden_ref, slope_ref, normed_ref, std_ref, space_ref,
    ) = refs[slots:]
    count, width = edges_ref.shape
    own = nodes_ref.shape[0]
    tile = tile_refs[0].shape[0]
    space_ref[0:own, :] = nodes_ref[...]
    for slot in range(slots):
        space_ref[own + slot * tile : own + (slot + 1) * tile, :] = tile_refs[slot][...]
    for start in range(0, count, block):
        rows = slice(start, start + block)
        edges = edges_ref[rows, :]
        hot_r = one_hot(recv_ref[:, rows], own)
        zs = pick(send_ref[:, rows], space_ref[...]).astype(BF16)
        zr = pick(recv_ref[:, rows], nodes_ref[...]).astype(BF16)
        pre = (
            mm(edges, w1_ref[0:width, :])
            + mm(zs, w1_ref[width : 2 * width, :])
            + mm(zr, w1_ref[2 * width : 3 * width, :])
        )
        message, hidden, slope, normed, inv_std = tail_of_forward(pre, w2_ref[...], gain_ref[...])
        place = start + lax.broadcasted_iota(jnp.int32, (block, 1), 0)
        message = jnp.where(place < count_ref[0], message, 0.0)
        arrived = put_wide(hot_r, message)
        agg_ref[...] = arrived if start == 0 else agg_ref[...] + arrived
        new_ref[rows, :] = (edges.astype(F32) + message).astype(BF16)
        zs_ref[rows, :] = zs
        zr_ref[rows, :] = zr
        hidden_ref[rows, :] = hidden
        slope_ref[rows, :] = slope.astype(BF16)
        normed_ref[rows, :] = normed.astype(BF16)
        std_ref[rows, :] = jnp.broadcast_to(inv_std, (block, std_ref.shape[1]))
        for ref in (new_ref, zs_ref, zr_ref, hidden_ref, slope_ref, normed_ref, std_ref):
            ref.done(rows)


def by_distance(me, peers, sums, kept_ref, given_ref):
    quarter = peers // 4
    for r in list(range(1, peers, 2)) + list(range(0, peers, 2)):
        if r == 0:
            given_ref.done()
        to = jnp.bitwise_xor(me, r)
        out = given_ref if r % 2 else kept_ref
        slot = (r // 2 % 2) * quarter + r // 4
        place = 0
        for total in sums:
            rows = total.shape[0] // peers
            part = total[pl.ds(pl.multiple_of(to * rows, 8), rows), :]
            if rows % 16:
                part = jnp.concatenate([part, jnp.zeros((-rows % 16, part.shape[1]), F32)], 0)
            out[slot, place : place + part.shape[0], :] = part.astype(BF16)
            place += part.shape[0]
    kept_ref.done()


def node_kernel(
    me_ref, nodes_ref, agg_ref, share_ref, d_ref, w1_ref, w2_ref, gain_ref,
    new_ref, base_ref, dagg_ref, spread_ref, *rest, ordered,
):
    if ordered:
        kept_ref, given_ref, total_ref, g1_ref, g2_ref = rest
    else:
        g1_ref, g2_ref, total_ref = rest
    width = nodes_ref.shape[1]
    total_ref[...] = agg_ref[...]
    total_ref[0:COARSE_DEV, :] += jnp.sum(share_ref[...].astype(F32), 0)
    nodes = nodes_ref[...]
    agg = total_ref[...].astype(BF16)
    pre = mm(nodes, w1_ref[0:width, :]) + mm(agg, w1_ref[width : 2 * width, :])
    update, hidden, slope, normed, inv_std = tail_of_forward(pre, w2_ref[...], gain_ref[...])
    new_ref[...] = (nodes.astype(F32) + update).astype(BF16)
    cotan = d_ref[...].astype(F32)
    back_out, back_pre = head_of_backward(cotan, w2_ref[...], gain_ref[...], slope, normed, inv_std)
    dagg = mm_nt(back_pre, w1_ref[width : 2 * width, :])
    dagg_ref[...] = dagg.astype(BF16)
    rows = dagg[:COARSE_DEV].astype(BF16)
    for peer in range(spread_ref.shape[0]):
        spread_ref[peer] = rows
    base_ref[...] = cotan + mm_nt(back_pre, w1_ref[0:width, :])
    g1_ref[0:width, :] = mm_tn(nodes, back_pre)
    g1_ref[width : 2 * width, :] = mm_tn(agg, back_pre)
    g2_ref[...] = mm_tn(hidden, back_out)
    if ordered:
        by_distance(me_ref[0], spread_ref.shape[0], (g1_ref, g2_ref), kept_ref, given_ref)


def fine_backward_kernel(
    count_ref, recv_ref, dagg_ref, d_ref, gain_ref, std_ref, normed_ref, w2_ref, slope_ref,
    w1_ref, send_ref, base_ref,
    out_ref, pre_ref, g_ref, own_ref, *rest, block,
):
    piece_refs, space_ref = rest[:-1], rest[-1]
    count, width = d_ref.shape
    own = base_ref.shape[0]
    received = None
    for start in range(0, count, block):
        rows = slice(start, start + block)
        hot_r = one_hot(recv_ref[:, rows], own)
        d_edges = d_ref[rows, :].astype(F32)
        place = start + lax.broadcasted_iota(jnp.int32, (block, 1), 0)
        cotan = jnp.where(place < count_ref[0], d_edges + pick(recv_ref[:, rows], dagg_ref[...]), 0.0)
        back_out, back_pre = head_of_backward(
            cotan, w2_ref[...], gain_ref[...], slope_ref[rows, :].astype(F32),
            normed_ref[rows, :].astype(F32), std_ref[rows, 0:1],
        )
        out_ref[rows, :] = back_out
        pre_ref[rows, :] = back_pre
        out_ref.done(rows)
        pre_ref.done(rows)
        g_ref[rows, :] = (d_edges + mm_nt(back_pre, w1_ref[0:width, :])).astype(BF16)
        g_ref.done(rows)
        dz_send = mm_nt(back_pre, w1_ref[width : 2 * width, :]).astype(BF16)
        dz_recv = mm_nt(back_pre, w1_ref[2 * width : 3 * width, :]).astype(BF16)
        sent = mm(one_hot(send_ref[:, rows], space_ref.shape[0]), dz_send)
        space_ref[...] = sent if start == 0 else space_ref[...] + sent
        arrived = mm(hot_r, dz_recv)
        received = arrived if received is None else received + arrived
    for slot, piece in enumerate(piece_refs):
        tile = piece.shape[0]
        piece[...] = space_ref[own + slot * tile : own + (slot + 1) * tile, :].astype(BF16)
        piece.done()
    own_ref[...] = base_ref[...] + received + space_ref[0:own, :]


def coarse_backward_kernel(
    me_ref, recv_ref, all_ref, d_ref, gain_ref, std_ref, normed_ref, w2_ref, slope_ref,
    edges_ref, pre_ref, zs_ref, zr_ref, hidden_ref, out_ref, w1_ref, send_ref,
    g_ref, *rest, ordered,
):
    if ordered:
        kept1_ref, given1_ref, kept2_ref, given2_ref, part_ref, g1_ref, g2_ref = rest
    else:
        part_ref, g1_ref, g2_ref = rest
    width = d_ref.shape[1]
    count = hidden_ref.shape[0]
    rows = slice(count - d_ref.shape[0], count)
    table = gathered(all_ref).astype(BF16)
    d_edges = d_ref[...].astype(F32)
    cotan = d_edges + pick(recv_ref[...], table)
    back_out, back_pre = head_of_backward(
        cotan, w2_ref[...], gain_ref[...], slope_ref[...].astype(F32), normed_ref[...].astype(F32), std_ref[:, 0:1]
    )
    out_ref[rows, :] = back_out
    pre_ref[rows, :] = back_pre
    g1_ref[0:width, :] = mm_tn(edges_ref[...], pre_ref[...])
    g1_ref[width : 2 * width, :] = mm_tn(zs_ref[...], pre_ref[...])
    g1_ref[2 * width : 3 * width, :] = mm_tn(zr_ref[...], pre_ref[...])
    if ordered:
        by_distance(me_ref[0], 2 * kept1_ref.shape[0], (g1_ref,), kept1_ref, given1_ref)
    g2_ref[...] = mm_tn(hidden_ref[...], out_ref[...])
    dz_send = mm_nt(back_pre, w1_ref[width : 2 * width, :]).astype(BF16)
    dz_recv = mm_nt(back_pre, w1_ref[2 * width : 3 * width, :]).astype(BF16)
    total = mm(one_hot(send_ref[...], table.shape[0]), dz_send) + mm(one_hot(recv_ref[...], table.shape[0]), dz_recv)
    part_ref[...] = total.reshape(part_ref.shape).astype(part_ref.dtype)
    if ordered:
        by_distance(me_ref[0], 2 * kept2_ref.shape[0], (g2_ref, part_ref), kept2_ref, given2_ref)
    g_ref[...] = (d_edges + mm_nt(back_pre, w1_ref[0:width, :])).astype(BF16)


def node_gradient_kernel(own_ref, halo_ref, *refs, slots):
    passing = (len(refs) - slots - 1) // 2
    piece_refs, out_ref = refs[:slots], refs[slots + passing]
    arrived = None
    for slot, piece in enumerate(piece_refs):
        part = mm(one_hot(halo_ref[slot : slot + 1, :], own_ref.shape[0]), piece[...])
        arrived = part if arrived is None else arrived + part
    out_ref[...] = own_ref[...] + arrived


def coarse_gradient_kernel(total_ref, share_ref, g_ref):
    share = jnp.sum(share_ref[...].astype(F32), 0)
    first = total_ref[0:16, :] + jnp.concatenate([share, jnp.zeros_like(share)], 0)
    g_ref[...] = total_ref[...].astype(BF16)
    g_ref[0:16, :] = first.astype(BF16)


def second_halving_kernel(kept_ref, taken_ref, *refs, passing):
    keep_ref, give_refs = refs[passing], refs[passing + 1 : len(refs) - passing]
    for j in range(kept_ref.shape[0]):
        total = kept_ref[j].astype(F32) + taken_ref[j].astype(F32)
        if j:
            give_refs[j - 1][...] = total.astype(BF16)
        else:
            keep_ref[...] = total


def last_sum_kernel(*refs, counts, sizes, with_nodes):
    place = 0
    totals = []
    for count in counts:
        total = refs[place][...]
        for ref in refs[place + 1 : place + count]:
            total = total + ref[...].astype(F32)
        totals.append(total)
        place += count
    if with_nodes:
        nodes_ref, g_ref = refs[place], refs[-1]
        place += 1
    for total, rows in zip(totals, sizes):
        start = 0
        for count in rows:
            refs[place][...] = total[start : start + count]
            start += count
            place += 1
    if with_nodes:
        g_ref[...] = nodes_ref[...].astype(BF16)
        g_ref[0:16, :] = (nodes_ref[0:16, :] + totals[-1][start : start + 16]).astype(BF16)


VM = pl.BlockSpec(memory_space=pltpu.VMEM)
SM = pl.BlockSpec(memory_space=pltpu.SMEM)
ANY = pl.BlockSpec(memory_space=pl.ANY)


def shape(dims, dtype):
    return jax.ShapeDtypeStruct(tuple(dims), dtype)


class Rows:
    def __init__(self, parts=1, joined=1, extra=0):
        self.parts = parts
        self.joined = joined
        self.extra = extra


class Fetched:
    def __init__(self, sources, buffer, semaphores, parts):
        self.buffer = buffer
        self.shape = buffer.shape
        self.waiting = []
        place = 0
        for source in sources:
            rows = source.shape[0] // parts
            for part in range(parts):
                if source.shape == buffer.shape and parts == 1:
                    copy = pltpu.make_async_copy(source, buffer, next(semaphores))
                else:
                    copy = pltpu.make_async_copy(
                        source.at[pl.ds(part * rows, rows)], buffer.at[pl.ds(place, rows)], next(semaphores)
                    )
                copy.start()
                self.waiting.append((place, place + rows, copy))
                place += rows

    def ready(self, low=0, high=None):
        left = []
        for first, last, copy in self.waiting:
            if high is None or (first < high and low < last):
                copy.wait()
            else:
                left.append((first, last, copy))
        self.waiting = left

    def __getitem__(self, index):
        rows = index[0] if isinstance(index, tuple) else None
        if isinstance(rows, slice) and rows.start is not None:
            self.ready(rows.start, rows.stop)
        else:
            self.ready()
        return self.buffer[index]

    def __setitem__(self, index, value):
        self.buffer[index] = value


class Stored:
    def __init__(self, target, buffer, semaphores):
        self.target = target
        self.buffer = buffer
        self.shape = buffer.shape
        self.dtype = buffer.dtype
        self.semaphores = semaphores
        self.copies = []

    def __getitem__(self, index):
        return self.buffer[index]

    def __setitem__(self, index, value):
        self.buffer[index] = value

    def done(self, rows=None):
        if rows is None:
            copy = pltpu.make_async_copy(self.buffer, self.target, next(self.semaphores))
        else:
            part = pl.ds(rows.start, rows.stop - rows.start)
            copy = pltpu.make_async_copy(self.buffer.at[part], self.target.at[part], next(self.semaphores))
        copy.start()
        self.copies.append(copy)


SEMAPHORES = 64


def staged_kernel(body, in_specs, out_specs, *refs):
    ins, outs = refs[: len(in_specs)], refs[len(in_specs) : len(in_specs) + len(out_specs)]
    rest = refs[len(in_specs) + len(out_specs) :]
    semaphores = iter([rest[0].at[i] for i in range(SEMAPHORES)])
    buffers = iter(rest[1:])
    fetched, stored = [], []
    for place, (ref, spec) in enumerate(zip(ins, in_specs)):
        if spec is VM:
            fetched.append(Fetched([ref], next(buffers), semaphores, 1))
        elif spec is SM:
            fetched.append(ref)
        elif isinstance(spec, Rows):
            fetched.append(Fetched(ins[place : place + spec.joined], next(buffers), semaphores, spec.parts))
    for ref, spec in zip(outs, out_specs):
        stored.append(Stored(ref, next(buffers), semaphores))
    body(*fetched, *stored, *buffers)
    for ref in fetched:
        if isinstance(ref, Fetched):
            ref.ready()
    for ref in stored:
        if not ref.copies:
            ref.done()
    for ref in stored:
        for copy in ref.copies:
            copy.wait()


def cost(ins, outs, flops):
    moved = sum(a.size * a.dtype.itemsize for a in list(ins) + list(outs))
    return pl.CostEstimate(flops=flops, bytes_accessed=moved, transcendentals=0)


def call(kernel, name, ins, in_specs, outs, scratch=(), flops=0):
    out_specs = [VM] * len(outs)
    buffers = []
    for place, spec in enumerate(in_specs):
        if spec is VM:
            buffers.append(pltpu.VMEM(ins[place].shape, ins[place].dtype))
        elif isinstance(spec, Rows):
            joined = ins[place : place + spec.joined]
            rows = sum(a.shape[0] for a in joined) + spec.extra
            buffers.append(pltpu.VMEM((rows,) + joined[0].shape[1:], joined[0].dtype))
    buffers += [pltpu.VMEM(a.shape, a.dtype) for a in outs]
    return pl.pallas_call(
        functools.partial(staged_kernel, kernel, in_specs, out_specs),
        out_shape=tuple(outs),
        in_specs=[SM if spec is SM else ANY for spec in in_specs],
        out_specs=tuple([ANY] * len(outs)),
        scratch_shapes=[pltpu.SemaphoreType.DMA((SEMAPHORES,))] + buffers + list(scratch),
        name=name,
        cost_estimate=cost(ins, outs, flops),
        compiler_params=pltpu.CompilerParams(vmem_limit_bytes=VMEM_LIMIT),
    )(*ins)


def small_call(kernel, name, ins, outs, passing=()):
    first = len(ins)
    last = len(outs)
    outs = list(outs) + [shape(a.shape, a.dtype) for a in passing]
    return pl.pallas_call(
        kernel,
        out_shape=tuple(outs),
        input_output_aliases={first + i: last + i for i in range(len(passing))},
        in_specs=[VM] * first + [ANY] * len(passing),
        out_specs=tuple([VM] * last + [ANY] * len(passing)),
        name=name,
        cost_estimate=cost(ins, outs, 0),
        compiler_params=pltpu.CompilerParams(vmem_limit_bytes=SMALL_LIMIT),
    )(*ins, *passing)


def passed_along(block, axis, distance):
    count = lax.axis_size(axis)
    route = [((i - distance) % count, i) for i in range(count)]
    return lax.ppermute(block, axis, route)


def exchanged(block, axis, distance):
    return lax.ppermute(block, axis, [(i, i ^ distance) for i in range(lax.axis_size(axis))])


def exchanged_with_all(blocks, axis):
    return lax.all_to_all(blocks, axis, 0, 0)


def first_halving(kept, taken):
    half = kept.shape[0] // 2
    give = (kept[half:].astype(F32) + taken[half:].astype(F32)).astype(BF16)
    return kept[:half].astype(F32) + taken[:half].astype(F32), give


def second_halving(kept, taken, passing=()):
    block = kept.shape[1:]
    outs = [shape(block, F32)] + [shape(block, BF16)] * (kept.shape[0] - 1)
    kernel = functools.partial(second_halving_kernel, passing=len(passing))
    return small_call(kernel, "second_halving", (kept, taken), outs, passing)


def last_sum(groups, sizes, nodes=None):
    ins, outs = [], []
    for (kept, taken), rows in zip(groups, sizes):
        ins += [kept, *taken]
        outs += [shape((count, kept.shape[1]), F32) for count in rows]
    if nodes is not None:
        ins.append(nodes)
        outs.append(shape(nodes.shape, BF16))
    kernel = functools.partial(
        last_sum_kernel, counts=[1 + len(taken) for _, taken in groups], sizes=sizes, with_nodes=nodes is not None
    )
    return small_call(kernel, "last_sum", ins, outs)


def local(
    nodes,
    fine_edges,
    coarse_edges,
    fine_send,
    fine_recv,
    coarse_send,
    coarse_recv,
    halo_rows,
    edge_count,
    edge_w1,
    edge_w2,
    edge_gain,
    node_w1,
    node_w2,
    node_gain,
    d_nodes,
    d_fine,
    d_coarse,
):
    axis = "patch"
    peers = lax.axis_size(axis)
    own, width = nodes.shape
    fine = fine_edges.shape[0]
    coarse = coarse_edges.shape[0]
    halo = halo_rows[0]
    slots, tile = halo.shape
    hops = slots // 2
    offsets = list(range(1, hops + 1)) + [-k for k in range(1, hops + 1)]
    ordered = peers == 16 and all(
        w.shape[0] % (16 * peers) == 0 for w in (edge_w1, edge_w2, node_w1, node_w2)
    )
    me = lax.axis_index(axis).astype(jnp.int32).reshape(1)
    fs, fr = fine_send.reshape(1, fine), fine_recv.reshape(1, fine)
    cs, cr = coarse_send.reshape(1, coarse), coarse_recv.reshape(1, coarse)
    eg, ng = edge_gain.reshape(1, width), node_gain.reshape(1, width)
    every = shape((peers, COARSE_DEV, width), BF16)

    made = call(
        tiles_kernel, "tiles", (nodes, halo), [VM, VM],
        [shape((tile, width), BF16)] * slots,
    )
    received = [passed_along(made[slot], axis, offset) for slot, offset in enumerate(offsets)]
    coarse_all = exchanged_with_all(jnp.broadcast_to(nodes[:COARSE_DEV][None], every.shape), axis)

    def saved_shapes(rows):
        return [
            shape((rows, width), BF16), shape((rows, width), BF16), shape((rows, width), BF16),
            shape((rows, width), BF16), shape((rows, width), BF16), shape((rows, 128), F32),
        ]

    new_coarse, coarse_part, *coarse_saved = call(
        coarse_forward_kernel, "coarse_forward",
        (coarse_all, coarse_edges, cs, cr, edge_w1, edge_w2, eg), [VM] * 4 + [Rows(3), VM, VM],
        [shape((coarse, width), BF16), every] + saved_shapes(coarse),
        flops=2 * coarse * width * width * 4,
    )
    share = exchanged_with_all(coarse_part, axis)

    block = 256 if fine % 256 == 0 else fine
    space_rows = own + slots * tile
    new_fine, fine_agg, *fine_saved = call(
        functools.partial(fine_forward_kernel, slots=slots, block=block), "fine_forward",
        (edge_count, nodes, *received, fine_edges, fs, fr, edge_w1, edge_w2, eg),
        [SM] + [VM] * (slots + 4) + [Rows(3), VM, VM],
        [shape((fine, width), BF16), shape((own, width), F32)] + saved_shapes(fine),
        scratch=[pltpu.VMEM((space_rows, width), BF16)],
        flops=2 * fine * width * (4 * width + space_rows + 3 * own),
    )

    def weight_shapes(w1, w2, more):
        if not ordered:
            return [shape(w1.shape, F32), shape(w2.shape, F32)], []
        rows = (w1.shape[0] + w2.shape[0]) // peers + more
        outs = [shape((peers // 2, rows, width), BF16)] * 2
        return outs, [pltpu.VMEM(w1.shape, F32), pltpu.VMEM(w2.shape, F32)]

    sum_shapes, sum_scratch = weight_shapes(node_w1, node_w2, 0)
    new_nodes, base, dagg, dagg_spread, *node_parts = call(
        functools.partial(node_kernel, ordered=ordered), "node_both",
        (me, nodes, fine_agg, share, d_nodes, node_w1, node_w2, ng), [SM] + [VM] * 4 + [Rows(2), VM, VM],
        [shape((own, width), BF16), shape((own, width), F32), shape((own, width), BF16), every] + sum_shapes,
        scratch=[pltpu.VMEM((own, width), F32)] + sum_scratch,
        flops=2 * own * width * width * 9,
    )
    dagg_all = exchanged_with_all(dagg_spread, axis)
    if ordered:
        node_taken = exchanged(node_parts[1], axis, 1)
        node_kept, node_given = first_halving(node_parts[0], node_taken)

    sum_shapes, sum_scratch = weight_shapes(edge_w1, edge_w2, 16)
    if ordered:
        cut = edge_w1.shape[0] // peers
        rows = sum_shapes[0].shape[1] - cut
        sum_shapes = [shape((peers // 2, cut, width), BF16)] * 2 + [shape((peers // 2, rows, width), BF16)] * 2
    f_zs, f_zr, f_hidden, f_slope, f_normed, f_std = fine_saved
    c_zs, c_zr, c_hidden, c_slope, c_normed, c_std = coarse_saved
    fine_out, fine_pre, g_fine, own_grad, *pieces = call(
        functools.partial(fine_backward_kernel, block=block), "fine_backward",
        (edge_count, fr, dagg, d_fine, eg, f_std, f_normed, edge_w2, f_slope, edge_w1, fs, base),
        [SM] + [VM] * 8 + [Rows(3), VM, VM],
        [shape((fine, width), BF16)] * 3 + [shape((own, width), F32)] + [shape((tile, width), BF16)] * slots,
        scratch=[pltpu.VMEM((space_rows, width), F32)],
        flops=2 * fine * width * (4 * width + space_rows + 2 * own),
    )
    returned = [passed_along(pieces[slot], axis, -offset) for slot, offset in enumerate(offsets)]
    if ordered:
        node_taken = exchanged(node_given, axis, 2)
    pair = [Rows(joined=2), None]
    more = [Rows(extra=coarse)]
    order = (node_taken,) if ordered else ()
    g_coarse, *edge_parts = call(
        functools.partial(coarse_backward_kernel, ordered=ordered), "coarse_backward",
        (
            me, cr, dagg_all, d_coarse, eg, c_std, c_normed, edge_w2, c_slope, fine_edges, coarse_edges,
            fine_pre, f_zs, c_zs, f_zr, c_zr, f_hidden, c_hidden, fine_out, edge_w1, cs, *order,
        ),
        [SM] + [VM] * 8 + pair + more + pair * 3 + more + [Rows(3), VM] + [None] * len(order),
        [shape((coarse, width), BF16)] + ([] if ordered else [every]) + sum_shapes,
        scratch=([pltpu.VMEM((peers * COARSE_DEV, width), F32)] if ordered else []) + sum_scratch,
        flops=2 * width * width * (4 * fine + 12 * coarse),
    )

    def rows_of(w):
        return w.shape[0] // peers

    def returned_tiles(passing=()):
        return small_call(
            functools.partial(node_gradient_kernel, slots=slots), "node_gradient",
            (own_grad, halo, *returned), [shape((own, width), F32)], passing,
        )

    if ordered:

        def along_z(given):
            return [exchanged(part, axis, 4 * (k + 1)) for k, part in enumerate(given)]

        kept1, given1, kept2, given2 = edge_parts
        total, given1 = returned_tiles((given1,))
        taken1 = exchanged(given1, axis, 1)
        taken2 = exchanged(given2, axis, 1)
        kept1, given1 = first_halving(kept1, taken1)
        taken1 = exchanged(given1, axis, 2)
        kept2, given2 = first_halving(kept2, taken2)
        taken2 = exchanged(given2, axis, 2)
        node_kept, *given = second_halving(node_kept, node_taken)
        g_nw1, g_nw2 = last_sum([(node_kept, along_z(given))], [(rows_of(node_w1), rows_of(node_w2))])
        kept1, *given1 = second_halving(kept1, taken1)
        kept2, *given2 = second_halving(kept2, taken2)
        g_ew1, g_ew2, g_nodes = last_sum(
            [(kept1, along_z(given1)), (kept2, along_z(given2))], [(rows_of(edge_w1),), (rows_of(edge_w2),)], total
        )
    else:
        coarse_share = exchanged_with_all(edge_parts[0], axis)
        (g_nodes,) = small_call(
            coarse_gradient_kernel, "coarse_gradient", (*returned_tiles(), coarse_share),
            [shape((own, width), BF16)],
        )
        g_nw1, g_nw2, g_ew1, g_ew2 = [
            lax.psum_scatter(g, axis, scatter_dimension=0, tiled=True) for g in [*node_parts, *edge_parts[1:]]
        ]
    return (new_nodes, new_fine, new_coarse, g_nodes, g_fine, g_coarse, g_ew1, g_ew2, g_nw1, g_nw2)


def solution(mesh):
    split = P(("groups", "patch"))
    rows = P(("groups", "patch"), None)
    return jax.shard_map(
        local,
        mesh=mesh,
        in_specs=(
            rows, rows, rows, split, split, split, split, P(("groups", "patch"), None, None), split,
            P(), P(), P(), P(), P(), P(), rows, rows, rows,
        ),
        out_specs=(rows,) * 10,
        check_vma=False,
    )
```

```python
import functools

import jax
import jax.numpy as jnp
from jax import lax
from jax.experimental import pallas as pl
from jax.experimental.pallas import tpu as pltpu
from jax.sharding import PartitionSpec as P

COARSE_DEV = 8
EPSILON = 1e-05
F32 = jnp.float32
BF16 = jnp.bfloat16
VMEM_LIMIT = 60 * 1024 * 1024
SMALL_LIMIT = 16 * 1024 * 1024


def mm(a, b):
    return lax.dot_general(a, b, (((1,), (0,)), ((), ())), preferred_element_type=F32)


def mm_nt(a, b):
    return lax.dot_general(a, b, (((1,), (1,)), ((), ())), preferred_element_type=F32)


def mm_tn(a, b):
    return lax.dot_general(a, b, (((0,), (0,)), ((), ())), preferred_element_type=F32)


def halves(value):
    high = value.astype(BF16)
    low = (value - high.astype(F32)).astype(BF16)
    return high, low


def one_hot(index, rows):
    row = lax.broadcasted_iota(jnp.int32, (rows, index.shape[1]), 0)
    return jnp.where(row == index, 1.0, 0.0).astype(BF16)


def pick(index, table):
    entries = index.shape[1]
    column = jnp.transpose(jnp.broadcast_to(index, (128, entries)))
    lane = lax.broadcasted_iota(jnp.int32, (entries, 128), 1)
    parts = []
    for start in range(0, table.shape[0], 128):
        parts.append(jnp.where(column == lane + start, 1.0, 0.0).astype(BF16))
    return mm(jnp.concatenate(parts, 1), table)


def put_wide(hot, rows):
    high, low = halves(rows)
    return mm(hot, high) + mm(hot, low)


def row_mean(value):
    return jnp.mean(value, axis=-1, keepdims=True)


def tail_of_forward(pre, second_w, gain):
    sigmoid = jax.nn.sigmoid(pre)
    hidden = (pre * sigmoid).astype(BF16)
    slope = sigmoid * (1.0 + pre * (1.0 - sigmoid))
    output = mm(hidden, second_w)
    centred = output - row_mean(output)
    inv_std = lax.rsqrt(row_mean(centred * centred) + EPSILON)
    normed = centred * inv_std
    return normed * gain, hidden, slope, normed, inv_std


def head_of_backward(cotan, second_w, gain, slope, normed, inv_std):
    scaled = cotan * gain
    back_out = inv_std * (scaled - row_mean(scaled) - normed * row_mean(scaled * normed))
    back_out = back_out.astype(BF16)
    back_pre = (mm_nt(back_out, second_w) * slope).astype(BF16)
    return back_out, back_pre


def tiles_kernel(nodes_ref, halo_ref, *outs):
    nodes = nodes_ref[...]
    for slot, out in enumerate(outs):
        out[...] = pick(halo_ref[slot : slot + 1, :], nodes).astype(BF16)
        out.done()


def gathered(ref):
    value = ref[...].astype(F32)
    return value.reshape(value.shape[0] * value.shape[1], value.shape[2])


def coarse_forward_kernel(
    all_ref, edges_ref, send_ref, recv_ref, w1_ref, w2_ref, gain_ref,
    new_ref, part_ref, zs_ref, zr_ref, hidden_ref, slope_ref, normed_ref, std_ref,
):
    width = edges_ref.shape[1]
    table = gathered(all_ref).astype(BF16)
    hot_r = one_hot(recv_ref[...], table.shape[0])
    edges = edges_ref[...]
    zs = pick(send_ref[...], table).astype(BF16)
    zr = pick(recv_ref[...], table).astype(BF16)
    pre = (
        mm(edges, w1_ref[0:width, :])
        + mm(zs, w1_ref[width : 2 * width, :])
        + mm(zr, w1_ref[2 * width : 3 * width, :])
    )
    message, hidden, slope, normed, inv_std = tail_of_forward(pre, w2_ref[...], gain_ref[...])
    total = put_wide(hot_r, message)
    part_ref[...] = total.reshape(part_ref.shape).astype(BF16)
    part_ref.done()
    new_ref[...] = (edges.astype(F32) + message).astype(BF16)
    zs_ref[...] = zs
    zr_ref[...] = zr
    hidden_ref[...] = hidden
    slope_ref[...] = slope.astype(BF16)
    normed_ref[...] = normed.astype(BF16)
    std_ref[...] = jnp.broadcast_to(inv_std, std_ref.shape)


def fine_forward_kernel(count_ref, nodes_ref, *refs, slots, block):
    tile_refs = refs[:slots]
    (
        edges_ref, send_ref, recv_ref, w1_ref, w2_ref, gain_ref,
        new_ref, agg_ref, zs_ref, zr_ref, hidden_ref, slope_ref, normed_ref, std_ref, space_ref,
    ) = refs[slots:]
    count, width = edges_ref.shape
    own = nodes_ref.shape[0]
    tile = tile_refs[0].shape[0]
    space_ref[0:own, :] = nodes_ref[...]
    for slot in range(slots):
        space_ref[own + slot * tile : own + (slot + 1) * tile, :] = tile_refs[slot][...]
    for start in range(0, count, block):
        rows = slice(start, start + block)
        edges = edges_ref[rows, :]
        hot_r = one_hot(recv_ref[:, rows], own)
        zs = pick(send_ref[:, rows], space_ref[...]).astype(BF16)
        zr = pick(recv_ref[:, rows], nodes_ref[...]).astype(BF16)
        pre = (
            mm(edges, w1_ref[0:width, :])
            + mm(zs, w1_ref[width : 2 * width, :])
            + mm(zr, w1_ref[2 * width : 3 * width, :])
        )
        message, hidden, slope, normed, inv_std = tail_of_forward(pre, w2_ref[...], gain_ref[...])
        place = start + lax.broadcasted_iota(jnp.int32, (block, 1), 0)
        message = jnp.where(place < count_ref[0], message, 0.0)
        arrived = put_wide(hot_r, message)
        agg_ref[...] = arrived if start == 0 else agg_ref[...] + arrived
        new_ref[rows, :] = (edges.astype(F32) + message).astype(BF16)
        zs_ref[rows, :] = zs
        zr_ref[rows, :] = zr
        hidden_ref[rows, :] = hidden
        slope_ref[rows, :] = slope.astype(BF16)
        normed_ref[rows, :] = normed.astype(BF16)
        std_ref[rows, :] = jnp.broadcast_to(inv_std, (block, std_ref.shape[1]))
        for ref in (new_ref, zs_ref, zr_ref, hidden_ref, slope_ref, normed_ref, std_ref):
            ref.done(rows)


def by_distance(me, peers, sums, kept_ref, given_ref):
    for r in list(range(1, peers, 2)) + list(range(0, peers, 2)):
        if r == 0:
            given_ref.done()
        to = jnp.bitwise_xor(me, r)
        out = given_ref if r % 2 else kept_ref
        slot, rest, span = 0, r // 2, peers // 4
        while span:
            slot += rest % 2 * span
            rest, span = rest // 2, span // 2
        place = 0
        for total in sums:
            rows = total.shape[0] // peers
            part = total[pl.ds(pl.multiple_of(to * rows, 8), rows), :]
            if rows % 16:
                part = jnp.concatenate([part, jnp.zeros((-rows % 16, part.shape[1]), F32)], 0)
            out[slot, place : place + part.shape[0], :] = part.astype(BF16)
            place += part.shape[0]
    kept_ref.done()


def node_kernel(
    me_ref, nodes_ref, agg_ref, share_ref, d_ref, w1_ref, w2_ref, gain_ref,
    new_ref, base_ref, dagg_ref, spread_ref, *rest, ordered,
):
    if ordered:
        kept_ref, given_ref, total_ref, g1_ref, g2_ref = rest
    else:
        g1_ref, g2_ref, total_ref = rest
    width = nodes_ref.shape[1]
    total_ref[...] = agg_ref[...]
    total_ref[0:COARSE_DEV, :] += jnp.sum(share_ref[...].astype(F32), 0)
    nodes = nodes_ref[...]
    agg = total_ref[...].astype(BF16)
    pre = mm(nodes, w1_ref[0:width, :]) + mm(agg, w1_ref[width : 2 * width, :])
    update, hidden, slope, normed, inv_std = tail_of_forward(pre, w2_ref[...], gain_ref[...])
    new_ref[...] = (nodes.astype(F32) + update).astype(BF16)
    cotan = d_ref[...].astype(F32)
    back_out, back_pre = head_of_backward(cotan, w2_ref[...], gain_ref[...], slope, normed, inv_std)
    dagg = mm_nt(back_pre, w1_ref[width : 2 * width, :])
    dagg_ref[...] = dagg.astype(BF16)
    rows = dagg[:COARSE_DEV].astype(BF16)
    for peer in range(spread_ref.shape[0]):
        spread_ref[peer] = rows
    base_ref[...] = cotan + mm_nt(back_pre, w1_ref[0:width, :])
    g1_ref[0:width, :] = mm_tn(nodes, back_pre)
    g1_ref[width : 2 * width, :] = mm_tn(agg, back_pre)
    g2_ref[...] = mm_tn(hidden, back_out)
    if ordered:
        by_distance(me_ref[0], spread_ref.shape[0], (g1_ref, g2_ref), kept_ref, given_ref)


def fine_backward_kernel(
    count_ref, recv_ref, dagg_ref, d_ref, gain_ref, std_ref, normed_ref, w2_ref, slope_ref,
    w1_ref, send_ref, base_ref,
    out_ref, pre_ref, g_ref, own_ref, *rest, block,
):
    piece_refs, space_ref = rest[:-1], rest[-1]
    count, width = d_ref.shape
    own = base_ref.shape[0]
    received = None
    for start in range(0, count, block):
        rows = slice(start, start + block)
        hot_r = one_hot(recv_ref[:, rows], own)
        d_edges = d_ref[rows, :].astype(F32)
        place = start + lax.broadcasted_iota(jnp.int32, (block, 1), 0)
        cotan = jnp.where(place < count_ref[0], d_edges + pick(recv_ref[:, rows], dagg_ref[...]), 0.0)
        back_out, back_pre = head_of_backward(
            cotan, w2_ref[...], gain_ref[...], slope_ref[rows, :].astype(F32),
            normed_ref[rows, :].astype(F32), std_ref[rows, 0:1],
        )
        out_ref[rows, :] = back_out
        pre_ref[rows, :] = back_pre
        out_ref.done(rows)
        pre_ref.done(rows)
        g_ref[rows, :] = (d_edges + mm_nt(back_pre, w1_ref[0:width, :])).astype(BF16)
        g_ref.done(rows)
        dz_send = mm_nt(back_pre, w1_ref[width : 2 * width, :]).astype(BF16)
        dz_recv = mm_nt(back_pre, w1_ref[2 * width : 3 * width, :]).astype(BF16)
        sent = mm(one_hot(send_ref[:, rows], space_ref.shape[0]), dz_send)
        space_ref[...] = sent if start == 0 else space_ref[...] + sent
        arrived = mm(hot_r, dz_recv)
        received = arrived if received is None else received + arrived
    for slot, piece in enumerate(piece_refs):
        tile = piece.shape[0]
        piece[...] = space_ref[own + slot * tile : own + (slot + 1) * tile, :].astype(BF16)
        piece.done()
    own_ref[...] = base_ref[...] + received + space_ref[0:own, :]


def coarse_backward_kernel(
    me_ref, recv_ref, all_ref, d_ref, gain_ref, std_ref, normed_ref, w2_ref, slope_ref,
    edges_ref, pre_ref, zs_ref, zr_ref, hidden_ref, out_ref, w1_ref, send_ref,
    g_ref, *rest, ordered,
):
    if ordered:
        kept1_ref, given1_ref, kept2_ref, given2_ref, part_ref, g1_ref, g2_ref = rest
    else:
        part_ref, g1_ref, g2_ref = rest
    width = d_ref.shape[1]
    count = hidden_ref.shape[0]
    rows = slice(count - d_ref.shape[0], count)
    table = gathered(all_ref).astype(BF16)
    d_edges = d_ref[...].astype(F32)
    cotan = d_edges + pick(recv_ref[...], table)
    back_out, back_pre = head_of_backward(
        cotan, w2_ref[...], gain_ref[...], slope_ref[...].astype(F32), normed_ref[...].astype(F32), std_ref[:, 0:1]
    )
    out_ref[rows, :] = back_out
    pre_ref[rows, :] = back_pre
    g1_ref[0:width, :] = mm_tn(edges_ref[...], pre_ref[...])
    g1_ref[width : 2 * width, :] = mm_tn(zs_ref[...], pre_ref[...])
    g1_ref[2 * width : 3 * width, :] = mm_tn(zr_ref[...], pre_ref[...])
    if ordered:
        by_distance(me_ref[0], 2 * kept1_ref.shape[0], (g1_ref,), kept1_ref, given1_ref)
    g2_ref[...] = mm_tn(hidden_ref[...], out_ref[...])
    dz_send = mm_nt(back_pre, w1_ref[width : 2 * width, :]).astype(BF16)
    dz_recv = mm_nt(back_pre, w1_ref[2 * width : 3 * width, :]).astype(BF16)
    total = mm(one_hot(send_ref[...], table.shape[0]), dz_send) + mm(one_hot(recv_ref[...], table.shape[0]), dz_recv)
    part_ref[...] = total.reshape(part_ref.shape).astype(part_ref.dtype)
    if ordered:
        by_distance(me_ref[0], 2 * kept2_ref.shape[0], (g2_ref, part_ref), kept2_ref, given2_ref)
    g_ref[...] = (d_edges + mm_nt(back_pre, w1_ref[0:width, :])).astype(BF16)


def node_gradient_kernel(own_ref, halo_ref, *refs):
    piece_refs, out_ref = refs[:-1], refs[-1]
    arrived = None
    for slot, piece in enumerate(piece_refs):
        part = mm(one_hot(halo_ref[slot : slot + 1, :], own_ref.shape[0]), piece[...])
        arrived = part if arrived is None else arrived + part
    out_ref[...] = own_ref[...] + arrived


def coarse_gradient_kernel(total_ref, share_ref, g_ref):
    share = jnp.sum(share_ref[...].astype(F32), 0)
    first = total_ref[0:16, :] + jnp.concatenate([share, jnp.zeros_like(share)], 0)
    g_ref[...] = total_ref[...].astype(BF16)
    g_ref[0:16, :] = first.astype(BF16)


def order_kernel(*refs):
    pass


def halving_kernel(kept_ref, taken_ref, keep_ref, give_ref):
    half = keep_ref.shape[0]
    for j in range(half):
        give_ref[j] = (kept_ref[half + j] + taken_ref[half + j].astype(F32)).astype(BF16)
    for j in range(half):
        keep_ref[j] = kept_ref[j] + taken_ref[j].astype(F32)


def last_sum_kernel(*refs, sizes, with_nodes):
    place = 2 * len(sizes)
    totals = [refs[2 * i][0] + refs[2 * i + 1][0].astype(F32) for i in range(len(sizes))]
    if with_nodes:
        nodes_ref, g_ref = refs[place], refs[-1]
        place += 1
    for total, rows in zip(totals, sizes):
        start = 0
        for count in rows:
            refs[place][...] = total[start : start + count]
            start += count
            place += 1
    if with_nodes:
        g_ref[...] = nodes_ref[...].astype(BF16)
        g_ref[0:16, :] = (nodes_ref[0:16, :] + totals[-1][start : start + 16]).astype(BF16)


VM = pl.BlockSpec(memory_space=pltpu.VMEM)
SM = pl.BlockSpec(memory_space=pltpu.SMEM)
ANY = pl.BlockSpec(memory_space=pl.ANY)


def shape(dims, dtype):
    return jax.ShapeDtypeStruct(tuple(dims), dtype)


class Rows:
    def __init__(self, parts=1, joined=1, extra=0):
        self.parts = parts
        self.joined = joined
        self.extra = extra


class Fetched:
    def __init__(self, sources, buffer, semaphores, parts):
        self.buffer = buffer
        self.shape = buffer.shape
        self.waiting = []
        place = 0
        for source in sources:
            rows = source.shape[0] // parts
            for part in range(parts):
                if source.shape == buffer.shape and parts == 1:
                    copy = pltpu.make_async_copy(source, buffer, next(semaphores))
                else:
                    copy = pltpu.make_async_copy(
                        source.at[pl.ds(part * rows, rows)], buffer.at[pl.ds(place, rows)], next(semaphores)
                    )
                copy.start()
                self.waiting.append((place, place + rows, copy))
                place += rows

    def ready(self, low=0, high=None):
        left = []
        for first, last, copy in self.waiting:
            if high is None or (first < high and low < last):
                copy.wait()
            else:
                left.append((first, last, copy))
        self.waiting = left

    def __getitem__(self, index):
        rows = index[0] if isinstance(index, tuple) else None
        if isinstance(rows, slice) and rows.start is not None:
            self.ready(rows.start, rows.stop)
        else:
            self.ready()
        return self.buffer[index]

    def __setitem__(self, index, value):
        self.buffer[index] = value


class Stored:
    def __init__(self, target, buffer, semaphores):
        self.target = target
        self.buffer = buffer
        self.shape = buffer.shape
        self.dtype = buffer.dtype
        self.semaphores = semaphores
        self.copies = []

    def __getitem__(self, index):
        return self.buffer[index]

    def __setitem__(self, index, value):
        self.buffer[index] = value

    def done(self, rows=None):
        if rows is None:
            copy = pltpu.make_async_copy(self.buffer, self.target, next(self.semaphores))
        else:
            part = pl.ds(rows.start, rows.stop - rows.start)
            copy = pltpu.make_async_copy(self.buffer.at[part], self.target.at[part], next(self.semaphores))
        copy.start()
        self.copies.append(copy)


SEMAPHORES = 64


def staged_kernel(body, in_specs, out_specs, *refs):
    ins, outs = refs[: len(in_specs)], refs[len(in_specs) : len(in_specs) + len(out_specs)]
    rest = refs[len(in_specs) + len(out_specs) :]
    semaphores = iter([rest[0].at[i] for i in range(SEMAPHORES)])
    buffers = iter(rest[1:])
    fetched, stored = [], []
    for place, (ref, spec) in enumerate(zip(ins, in_specs)):
        if spec is VM:
            fetched.append(Fetched([ref], next(buffers), semaphores, 1))
        elif spec is SM:
            fetched.append(ref)
        elif isinstance(spec, Rows):
            fetched.append(Fetched(ins[place : place + spec.joined], next(buffers), semaphores, spec.parts))
    for ref, spec in zip(outs, out_specs):
        stored.append(Stored(ref, next(buffers), semaphores))
    body(*fetched, *stored, *buffers)
    for ref in fetched:
        if isinstance(ref, Fetched):
            ref.ready()
    for ref in stored:
        if not ref.copies:
            ref.done()
    for ref in stored:
        for copy in ref.copies:
            copy.wait()


def cost(ins, outs, flops):
    moved = sum(a.size * a.dtype.itemsize for a in list(ins) + list(outs))
    return pl.CostEstimate(flops=flops, bytes_accessed=moved, transcendentals=0)


def call(kernel, name, ins, in_specs, outs, scratch=(), flops=0):
    out_specs = [VM] * len(outs)
    buffers = []
    for place, spec in enumerate(in_specs):
        if spec is VM:
            buffers.append(pltpu.VMEM(ins[place].shape, ins[place].dtype))
        elif isinstance(spec, Rows):
            joined = ins[place : place + spec.joined]
            rows = sum(a.shape[0] for a in joined) + spec.extra
            buffers.append(pltpu.VMEM((rows,) + joined[0].shape[1:], joined[0].dtype))
    buffers += [pltpu.VMEM(a.shape, a.dtype) for a in outs]
    return pl.pallas_call(
        functools.partial(staged_kernel, kernel, in_specs, out_specs),
        out_shape=tuple(outs),
        in_specs=[SM if spec is SM else ANY for spec in in_specs],
        out_specs=tuple([ANY] * len(outs)),
        scratch_shapes=[pltpu.SemaphoreType.DMA((SEMAPHORES,))] + buffers + list(scratch),
        name=name,
        cost_estimate=cost(ins, outs, flops),
        compiler_params=pltpu.CompilerParams(vmem_limit_bytes=VMEM_LIMIT),
    )(*ins)


def small_call(kernel, name, ins, outs, passing=()):
    first = len(ins)
    last = len(outs)
    outs = list(outs) + [shape(a.shape, a.dtype) for a in passing]
    return pl.pallas_call(
        kernel,
        out_shape=tuple(outs),
        input_output_aliases={first + i: last + i for i in range(len(passing))},
        in_specs=[VM] * first + [ANY] * len(passing),
        out_specs=tuple([VM] * last + [ANY] * len(passing)),
        name=name,
        cost_estimate=cost(ins, outs, 0),
        compiler_params=pltpu.CompilerParams(vmem_limit_bytes=SMALL_LIMIT),
    )(*ins, *passing)


def passed_along(block, axis, distance):
    count = lax.axis_size(axis)
    route = [((i - distance) % count, i) for i in range(count)]
    return lax.ppermute(block, axis, route)


def exchanged(block, axis, distance):
    return lax.ppermute(block, axis, [(i, i ^ distance) for i in range(lax.axis_size(axis))])


def exchanged_with_all(blocks, axis):
    return lax.all_to_all(blocks, axis, 0, 0)


def first_halving(kept, taken):
    half = kept.shape[0] // 2
    give = (kept[half:].astype(F32) + taken[half:].astype(F32)).astype(BF16)
    return kept[:half].astype(F32) + taken[:half].astype(F32), give


def halving(kept, taken):
    half = (kept.shape[0] // 2,) + kept.shape[1:]
    return small_call(halving_kernel, "halving", (kept, taken), [shape(half, F32), shape(half, BF16)])


def last_sum(groups, sizes, nodes=None):
    ins, outs = [], []
    for (kept, taken), rows in zip(groups, sizes):
        ins += [kept, taken]
        outs += [shape((count, kept.shape[2]), F32) for count in rows]
    if nodes is not None:
        ins.append(nodes)
        outs.append(shape(nodes.shape, BF16))
    return small_call(
        functools.partial(last_sum_kernel, sizes=sizes, with_nodes=nodes is not None), "last_sum", ins, outs
    )


def local(
    nodes,
    fine_edges,
    coarse_edges,
    fine_send,
    fine_recv,
    coarse_send,
    coarse_recv,
    halo_rows,
    edge_count,
    edge_w1,
    edge_w2,
    edge_gain,
    node_w1,
    node_w2,
    node_gain,
    d_nodes,
    d_fine,
    d_coarse,
):
    axis = "patch"
    peers = lax.axis_size(axis)
    own, width = nodes.shape
    fine = fine_edges.shape[0]
    coarse = coarse_edges.shape[0]
    halo = halo_rows[0]
    slots, tile = halo.shape
    hops = slots // 2
    offsets = list(range(1, hops + 1)) + [-k for k in range(1, hops + 1)]
    ordered = peers == 16 and all(
        w.shape[0] % (16 * peers) == 0 for w in (edge_w1, edge_w2, node_w1, node_w2)
    )
    me = lax.axis_index(axis).astype(jnp.int32).reshape(1)
    fs, fr = fine_send.reshape(1, fine), fine_recv.reshape(1, fine)
    cs, cr = coarse_send.reshape(1, coarse), coarse_recv.reshape(1, coarse)
    eg, ng = edge_gain.reshape(1, width), node_gain.reshape(1, width)
    every = shape((peers, COARSE_DEV, width), BF16)

    made = call(
        tiles_kernel, "tiles", (nodes, halo), [VM, VM],
        [shape((tile, width), BF16)] * slots,
    )
    received = [passed_along(made[slot], axis, offset) for slot, offset in enumerate(offsets)]
    coarse_all = exchanged_with_all(jnp.broadcast_to(nodes[:COARSE_DEV][None], every.shape), axis)

    def saved_shapes(rows):
        return [
            shape((rows, width), BF16), shape((rows, width), BF16), shape((rows, width), BF16),
            shape((rows, width), BF16), shape((rows, width), BF16), shape((rows, 128), F32),
        ]

    new_coarse, coarse_part, *coarse_saved = call(
        coarse_forward_kernel, "coarse_forward",
        (coarse_all, coarse_edges, cs, cr, edge_w1, edge_w2, eg), [VM] * 4 + [Rows(3), VM, VM],
        [shape((coarse, width), BF16), every] + saved_shapes(coarse),
        flops=2 * coarse * width * width * 4,
    )
    share = exchanged_with_all(coarse_part, axis)

    block = 256 if fine % 256 == 0 else fine
    space_rows = own + slots * tile
    new_fine, fine_agg, *fine_saved = call(
        functools.partial(fine_forward_kernel, slots=slots, block=block), "fine_forward",
        (edge_count, nodes, *received, fine_edges, fs, fr, edge_w1, edge_w2, eg),
        [SM] + [VM] * (slots + 4) + [Rows(3), VM, VM],
        [shape((fine, width), BF16), shape((own, width), F32)] + saved_shapes(fine),
        scratch=[pltpu.VMEM((space_rows, width), BF16)],
        flops=2 * fine * width * (4 * width + space_rows + 3 * own),
    )

    def weight_shapes(w1, w2, more):
        if not ordered:
            return [shape(w1.shape, F32), shape(w2.shape, F32)], []
        rows = (w1.shape[0] + w2.shape[0]) // peers + more
        outs = [shape((peers // 2, rows, width), BF16)] * 2
        return outs, [pltpu.VMEM(w1.shape, F32), pltpu.VMEM(w2.shape, F32)]

    sum_shapes, sum_scratch = weight_shapes(node_w1, node_w2, 0)
    new_nodes, base, dagg, dagg_spread, *node_parts = call(
        functools.partial(node_kernel, ordered=ordered), "node_both",
        (me, nodes, fine_agg, share, d_nodes, node_w1, node_w2, ng), [SM] + [VM] * 4 + [Rows(2), VM, VM],
        [shape((own, width), BF16), shape((own, width), F32), shape((own, width), BF16), every] + sum_shapes,
        scratch=[pltpu.VMEM((own, width), F32)] + sum_scratch,
        flops=2 * own * width * width * 9,
    )
    dagg_all = exchanged_with_all(dagg_spread, axis)
    if ordered:
        node_taken = exchanged(node_parts[1], axis, 1)
        node_kept, node_given = first_halving(node_parts[0], node_taken)

    sum_shapes, sum_scratch = weight_shapes(edge_w1, edge_w2, 16)
    if ordered:
        cut = edge_w1.shape[0] // peers
        rows = sum_shapes[0].shape[1] - cut
        sum_shapes = [shape((peers // 2, cut, width), BF16)] * 2 + [shape((peers // 2, rows, width), BF16)] * 2
    f_zs, f_zr, f_hidden, f_slope, f_normed, f_std = fine_saved
    c_zs, c_zr, c_hidden, c_slope, c_normed, c_std = coarse_saved
    fine_out, fine_pre, g_fine, own_grad, *pieces = call(
        functools.partial(fine_backward_kernel, block=block), "fine_backward",
        (edge_count, fr, dagg, d_fine, eg, f_std, f_normed, edge_w2, f_slope, edge_w1, fs, base),
        [SM] + [VM] * 8 + [Rows(3), VM, VM],
        [shape((fine, width), BF16)] * 3 + [shape((own, width), F32)] + [shape((tile, width), BF16)] * slots,
        scratch=[pltpu.VMEM((space_rows, width), F32)],
        flops=2 * fine * width * (4 * width + space_rows + 2 * own),
    )
    returned = [passed_along(pieces[slot], axis, -offset) for slot, offset in enumerate(offsets)]
    if ordered:
        node_taken = exchanged(node_given, axis, 2)
    pair = [Rows(joined=2), None]
    more = [Rows(extra=coarse)]
    order = (node_taken,) if ordered else ()
    g_coarse, *edge_parts = call(
        functools.partial(coarse_backward_kernel, ordered=ordered), "coarse_backward",
        (
            me, cr, dagg_all, d_coarse, eg, c_std, c_normed, edge_w2, c_slope, fine_edges, coarse_edges,
            fine_pre, f_zs, c_zs, f_zr, c_zr, f_hidden, c_hidden, fine_out, edge_w1, cs, *order,
        ),
        [SM] + [VM] * 8 + pair + more + pair * 3 + more + [Rows(3), VM] + [None] * len(order),
        [shape((coarse, width), BF16)] + ([] if ordered else [every]) + sum_shapes,
        scratch=([pltpu.VMEM((peers * COARSE_DEV, width), F32)] if ordered else []) + sum_scratch,
        flops=2 * width * width * (4 * fine + 12 * coarse),
    )

    def rows_of(w):
        return w.shape[0] // peers

    def tile_gradient():
        (total,) = small_call(
            node_gradient_kernel, "node_gradient", (own_grad, halo, *returned), [shape((own, width), F32)]
        )
        return total

    if ordered:
        kept1, given1, kept2, given2 = edge_parts
        given1, *returned = small_call(order_kernel, "order", (), [], (given1, *returned))
        taken1 = exchanged(given1, axis, 1)
        taken2 = exchanged(given2, axis, 1)
        kept1, given1 = first_halving(kept1, taken1)
        taken1 = exchanged(given1, axis, 2)
        kept2, given2 = first_halving(kept2, taken2)
        taken2 = exchanged(given2, axis, 2)
        distance = 4
        while distance < peers:
            node_kept, given = halving(node_kept, node_taken)
            node_taken = exchanged(given, axis, distance)
            kept1, given1 = halving(kept1, taken1)
            taken1 = exchanged(given1, axis, distance)
            kept2, given2 = halving(kept2, taken2)
            taken2 = exchanged(given2, axis, distance)
            distance *= 2
        g_nw1, g_nw2 = last_sum([(node_kept, node_taken)], [(rows_of(node_w1), rows_of(node_w2))])
        g_ew1, g_ew2, g_nodes = last_sum(
            [(kept1, taken1), (kept2, taken2)], [(rows_of(edge_w1),), (rows_of(edge_w2),)], tile_gradient()
        )
    else:
        coarse_share = exchanged_with_all(edge_parts[0], axis)
        (g_nodes,) = small_call(
            coarse_gradient_kernel, "coarse_gradient", (tile_gradient(), coarse_share), [shape((own, width), BF16)],
        )
        g_nw1, g_nw2, g_ew1, g_ew2 = [
            lax.psum_scatter(g, axis, scatter_dimension=0, tiled=True) for g in [*node_parts, *edge_parts[1:]]
        ]
    return (new_nodes, new_fine, new_coarse, g_nodes, g_fine, g_coarse, g_ew1, g_ew2, g_nw1, g_nw2)


def solution(mesh):
    split = P(("groups", "patch"))
    rows = P(("groups", "patch"), None)
    return jax.shard_map(
        local,
        mesh=mesh,
        in_specs=(
            rows, rows, rows, split, split, split, split, P(("groups", "patch"), None, None), split,
            P(), P(), P(), P(), P(), P(), rows, rows, rows,
        ),
        out_specs=(rows,) * 10,
        check_vma=False,
    )
```

```python
import functools

import jax
import jax.numpy as jnp
from jax import lax
from jax.experimental import pallas as pl
from jax.experimental.pallas import tpu as pltpu
from jax.sharding import PartitionSpec as P

COARSE_DEV = 8
EPSILON = 1e-05
F32 = jnp.float32
BF16 = jnp.bfloat16
VMEM_LIMIT = 60 * 1024 * 1024
SMALL_LIMIT = 16 * 1024 * 1024


def mm(a, b):
    return lax.dot_general(a, b, (((1,), (0,)), ((), ())), preferred_element_type=F32)


def mm_nt(a, b):
    return lax.dot_general(a, b, (((1,), (1,)), ((), ())), preferred_element_type=F32)


def mm_tn(a, b):
    return lax.dot_general(a, b, (((0,), (0,)), ((), ())), preferred_element_type=F32)


def halves(value):
    high = value.astype(BF16)
    low = (value - high.astype(F32)).astype(BF16)
    return high, low


def one_hot(index, rows):
    row = lax.broadcasted_iota(jnp.int32, (rows, index.shape[1]), 0)
    return jnp.where(row == index, 1.0, 0.0).astype(BF16)


def pick(index, table):
    entries = index.shape[1]
    column = jnp.transpose(jnp.broadcast_to(index, (128, entries)))
    lane = lax.broadcasted_iota(jnp.int32, (entries, 128), 1)
    parts = []
    for start in range(0, table.shape[0], 128):
        parts.append(jnp.where(column == lane + start, 1.0, 0.0).astype(BF16))
    return mm(jnp.concatenate(parts, 1), table)


def put_wide(hot, rows):
    high, low = halves(rows)
    return mm(hot, high) + mm(hot, low)


def row_mean(value):
    return jnp.mean(value, axis=-1, keepdims=True)


def tail_of_forward(pre, second_w, gain):
    sigmoid = jax.nn.sigmoid(pre)
    hidden = (pre * sigmoid).astype(BF16)
    slope = sigmoid * (1.0 + pre * (1.0 - sigmoid))
    output = mm(hidden, second_w)
    centred = output - row_mean(output)
    inv_std = lax.rsqrt(row_mean(centred * centred) + EPSILON)
    normed = centred * inv_std
    return normed * gain, hidden, slope, normed, inv_std


def head_of_backward(cotan, second_w, gain, slope, normed, inv_std):
    scaled = cotan * gain
    back_out = inv_std * (scaled - row_mean(scaled) - normed * row_mean(scaled * normed))
    back_out = back_out.astype(BF16)
    back_pre = (mm_nt(back_out, second_w) * slope).astype(BF16)
    return back_out, back_pre


def tiles_kernel(nodes_ref, halo_ref, *outs):
    nodes = nodes_ref[...]
    for slot, out in enumerate(outs):
        out[...] = pick(halo_ref[slot : slot + 1, :], nodes).astype(BF16)
        out.done()


def gathered(ref):
    value = ref[...].astype(F32)
    return value.reshape(value.shape[0] * value.shape[1], value.shape[2])


def coarse_forward_kernel(
    all_ref, edges_ref, send_ref, recv_ref, w1_ref, w2_ref, gain_ref,
    new_ref, part_ref, zs_ref, zr_ref, hidden_ref, slope_ref, normed_ref, std_ref,
):
    width = edges_ref.shape[1]
    table = gathered(all_ref).astype(BF16)
    hot_r = one_hot(recv_ref[...], table.shape[0])
    edges = edges_ref[...]
    zs = pick(send_ref[...], table).astype(BF16)
    zr = pick(recv_ref[...], table).astype(BF16)
    pre = (
        mm(edges, w1_ref[0:width, :])
        + mm(zs, w1_ref[width : 2 * width, :])
        + mm(zr, w1_ref[2 * width : 3 * width, :])
    )
    message, hidden, slope, normed, inv_std = tail_of_forward(pre, w2_ref[...], gain_ref[...])
    total = put_wide(hot_r, message)
    part_ref[...] = total.reshape(part_ref.shape).astype(BF16)
    part_ref.done()
    new_ref[...] = (edges.astype(F32) + message).astype(BF16)
    zs_ref[...] = zs
    zr_ref[...] = zr
    hidden_ref[...] = hidden
    slope_ref[...] = slope.astype(BF16)
    normed_ref[...] = normed.astype(BF16)
    std_ref[...] = jnp.broadcast_to(inv_std, std_ref.shape)


def fine_forward_kernel(count_ref, nodes_ref, *refs, slots, block):
    tile_refs = refs[:slots]
    (
        edges_ref, send_ref, recv_ref, w1_ref, w2_ref, gain_ref,
        new_ref, agg_ref, zs_ref, zr_ref, hidden_ref, slope_ref, normed_ref, std_ref, space_ref,
    ) = refs[slots:]
    count, width = edges_ref.shape
    own = nodes_ref.shape[0]
    tile = tile_refs[0].shape[0]
    space_ref[0:own, :] = nodes_ref[...]
    for slot in range(slots):
        space_ref[own + slot * tile : own + (slot + 1) * tile, :] = tile_refs[slot][...]
    for start in range(0, count, block):
        rows = slice(start, start + block)
        edges = edges_ref[rows, :]
        hot_r = one_hot(recv_ref[:, rows], own)
        zs = pick(send_ref[:, rows], space_ref[...]).astype(BF16)
        zr = pick(recv_ref[:, rows], nodes_ref[...]).astype(BF16)
        pre = (
            mm(edges, w1_ref[0:width, :])
            + mm(zs, w1_ref[width : 2 * width, :])
            + mm(zr, w1_ref[2 * width : 3 * width, :])
        )
        message, hidden, slope, normed, inv_std = tail_of_forward(pre, w2_ref[...], gain_ref[...])
        place = start + lax.broadcasted_iota(jnp.int32, (block, 1), 0)
        message = jnp.where(place < count_ref[0], message, 0.0)
        arrived = put_wide(hot_r, message)
        agg_ref[...] = arrived if start == 0 else agg_ref[...] + arrived
        new_ref[rows, :] = (edges.astype(F32) + message).astype(BF16)
        zs_ref[rows, :] = zs
        zr_ref[rows, :] = zr
        hidden_ref[rows, :] = hidden
        slope_ref[rows, :] = slope.astype(BF16)
        normed_ref[rows, :] = normed.astype(BF16)
        std_ref[rows, :] = jnp.broadcast_to(inv_std, (block, std_ref.shape[1]))
        for ref in (new_ref, zs_ref, zr_ref, hidden_ref, slope_ref, normed_ref, std_ref):
            ref.done(rows)


def x_first(peers):
    return [1 << bit for bit in range(1, peers.bit_length() - 1)]


def x_last(peers):
    steps = x_first(peers)
    return steps[1:] + steps[:1]


def by_distance(me, peers, steps, sums, kept_ref, given_ref):
    for r in list(range(1, peers, 2)) + list(range(0, peers, 2)):
        if r == 0:
            given_ref.done()
        to = jnp.bitwise_xor(me, r)
        out = given_ref if r % 2 else kept_ref
        slot = 0
        for distance in steps:
            slot = 2 * slot + r // distance % 2
        place = 0
        for total in sums:
            rows = total.shape[0] // peers
            part = total[pl.ds(pl.multiple_of(to * rows, 8), rows), :]
            if rows % 16:
                part = jnp.concatenate([part, jnp.zeros((-rows % 16, part.shape[1]), F32)], 0)
            out[slot, place : place + part.shape[0], :] = part.astype(BF16)
            place += part.shape[0]
    kept_ref.done()


def node_kernel(
    me_ref, nodes_ref, agg_ref, share_ref, d_ref, w1_ref, w2_ref, gain_ref,
    new_ref, base_ref, dagg_ref, spread_ref, *rest, ordered,
):
    if ordered:
        kept_ref, given_ref, total_ref, g1_ref, g2_ref = rest
    else:
        g1_ref, g2_ref, total_ref = rest
    width = nodes_ref.shape[1]
    total_ref[...] = agg_ref[...]
    total_ref[0:COARSE_DEV, :] += jnp.sum(share_ref[...].astype(F32), 0)
    nodes = nodes_ref[...]
    agg = total_ref[...].astype(BF16)
    pre = mm(nodes, w1_ref[0:width, :]) + mm(agg, w1_ref[width : 2 * width, :])
    update, hidden, slope, normed, inv_std = tail_of_forward(pre, w2_ref[...], gain_ref[...])
    new_ref[...] = (nodes.astype(F32) + update).astype(BF16)
    cotan = d_ref[...].astype(F32)
    back_out, back_pre = head_of_backward(cotan, w2_ref[...], gain_ref[...], slope, normed, inv_std)
    dagg = mm_nt(back_pre, w1_ref[width : 2 * width, :])
    dagg_ref[...] = dagg.astype(BF16)
    rows = dagg[:COARSE_DEV].astype(BF16)
    for peer in range(spread_ref.shape[0]):
        spread_ref[peer] = rows
    base_ref[...] = cotan + mm_nt(back_pre, w1_ref[0:width, :])
    g1_ref[0:width, :] = mm_tn(nodes, back_pre)
    g1_ref[width : 2 * width, :] = mm_tn(agg, back_pre)
    g2_ref[...] = mm_tn(hidden, back_out)
    if ordered:
        by_distance(me_ref[0], spread_ref.shape[0], x_first(spread_ref.shape[0]), (g1_ref, g2_ref), kept_ref, given_ref)


def fine_and_node_kernel(count_ref, me_ref, nodes_ref, *refs, slots, block, ordered):
    edge_ins, node_ins = refs[: slots + 6], refs[slots + 6 : slots + 11]
    edge_outs, node_outs = refs[slots + 11 : slots + 18], refs[slots + 18 : slots + 24]
    space_ref, agg_ref, *scratch = refs[slots + 24 :]
    fine_forward_kernel(
        count_ref, nodes_ref, *edge_ins, edge_outs[0], agg_ref, *edge_outs[1:], space_ref, slots=slots, block=block
    )
    share_ref, *node_ins = node_ins
    node_kernel(me_ref, nodes_ref, agg_ref, share_ref, *node_ins, *node_outs, *scratch, ordered=ordered)


def fine_backward_kernel(
    count_ref, recv_ref, dagg_ref, d_ref, gain_ref, std_ref, normed_ref, w2_ref, slope_ref,
    w1_ref, send_ref, base_ref,
    out_ref, pre_ref, g_ref, own_ref, *rest, block,
):
    piece_refs, space_ref = rest[:-1], rest[-1]
    count, width = d_ref.shape
    own = base_ref.shape[0]
    received = None
    for start in range(0, count, block):
        rows = slice(start, start + block)
        hot_r = one_hot(recv_ref[:, rows], own)
        d_edges = d_ref[rows, :].astype(F32)
        place = start + lax.broadcasted_iota(jnp.int32, (block, 1), 0)
        cotan = jnp.where(place < count_ref[0], d_edges + pick(recv_ref[:, rows], dagg_ref[...]), 0.0)
        back_out, back_pre = head_of_backward(
            cotan, w2_ref[...], gain_ref[...], slope_ref[rows, :].astype(F32),
            normed_ref[rows, :].astype(F32), std_ref[rows, 0:1],
        )
        out_ref[rows, :] = back_out
        pre_ref[rows, :] = back_pre
        out_ref.done(rows)
        pre_ref.done(rows)
        g_ref[rows, :] = (d_edges + mm_nt(back_pre, w1_ref[0:width, :])).astype(BF16)
        g_ref.done(rows)
        dz_send = mm_nt(back_pre, w1_ref[width : 2 * width, :]).astype(BF16)
        dz_recv = mm_nt(back_pre, w1_ref[2 * width : 3 * width, :]).astype(BF16)
        sent = mm(one_hot(send_ref[:, rows], space_ref.shape[0]), dz_send)
        space_ref[...] = sent if start == 0 else space_ref[...] + sent
        arrived = mm(hot_r, dz_recv)
        received = arrived if received is None else received + arrived
    for slot, piece in enumerate(piece_refs):
        tile = piece.shape[0]
        piece[...] = space_ref[own + slot * tile : own + (slot + 1) * tile, :].astype(BF16)
        piece.done()
    own_ref[...] = base_ref[...] + received + space_ref[0:own, :]


def coarse_backward_kernel(
    me_ref, recv_ref, all_ref, d_ref, gain_ref, std_ref, normed_ref, w2_ref, slope_ref,
    edges_ref, pre_ref, zs_ref, zr_ref, hidden_ref, out_ref, w1_ref, send_ref,
    g_ref, *rest, ordered,
):
    if ordered:
        kept1_ref, given1_ref, kept2_ref, given2_ref, part_ref, g1_ref, g2_ref = rest
    else:
        part_ref, g1_ref, g2_ref = rest
    width = d_ref.shape[1]
    count = hidden_ref.shape[0]
    rows = slice(count - d_ref.shape[0], count)
    table = gathered(all_ref).astype(BF16)
    d_edges = d_ref[...].astype(F32)
    cotan = d_edges + pick(recv_ref[...], table)
    back_out, back_pre = head_of_backward(
        cotan, w2_ref[...], gain_ref[...], slope_ref[...].astype(F32), normed_ref[...].astype(F32), std_ref[:, 0:1]
    )
    out_ref[rows, :] = back_out
    pre_ref[rows, :] = back_pre
    g1_ref[0:width, :] = mm_tn(edges_ref[...], pre_ref[...])
    g1_ref[width : 2 * width, :] = mm_tn(zs_ref[...], pre_ref[...])
    g1_ref[2 * width : 3 * width, :] = mm_tn(zr_ref[...], pre_ref[...])
    if ordered:
        peers = 2 * kept1_ref.shape[0]
        by_distance(me_ref[0], peers, x_first(peers), (g1_ref,), kept1_ref, given1_ref)
    g2_ref[...] = mm_tn(hidden_ref[...], out_ref[...])
    dz_send = mm_nt(back_pre, w1_ref[width : 2 * width, :]).astype(BF16)
    dz_recv = mm_nt(back_pre, w1_ref[2 * width : 3 * width, :]).astype(BF16)
    total = mm(one_hot(send_ref[...], table.shape[0]), dz_send) + mm(one_hot(recv_ref[...], table.shape[0]), dz_recv)
    part_ref[...] = total.reshape(part_ref.shape).astype(part_ref.dtype)
    if ordered:
        by_distance(me_ref[0], peers, x_last(peers), (g2_ref, part_ref), kept2_ref, given2_ref)
    g_ref[...] = (d_edges + mm_nt(back_pre, w1_ref[0:width, :])).astype(BF16)


def node_gradient_kernel(own_ref, halo_ref, *refs):
    piece_refs, out_ref = refs[:-1], refs[-1]
    arrived = None
    for slot, piece in enumerate(piece_refs):
        part = mm(one_hot(halo_ref[slot : slot + 1, :], own_ref.shape[0]), piece[...])
        arrived = part if arrived is None else arrived + part
    out_ref[...] = own_ref[...] + arrived


def coarse_gradient_kernel(total_ref, share_ref, g_ref):
    share = jnp.sum(share_ref[...].astype(F32), 0)
    first = total_ref[0:16, :] + jnp.concatenate([share, jnp.zeros_like(share)], 0)
    g_ref[...] = total_ref[...].astype(BF16)
    g_ref[0:16, :] = first.astype(BF16)


def order_kernel(*refs):
    pass


def halving_kernel(kept_ref, taken_ref, *refs):
    passing = (len(refs) - 2) // 2
    keep_ref, give_ref = refs[passing : passing + 2]
    half = keep_ref.shape[0]
    for j in range(half):
        give_ref[j] = (kept_ref[half + j] + taken_ref[half + j].astype(F32)).astype(BF16)
    for j in range(half):
        keep_ref[j] = kept_ref[j] + taken_ref[j].astype(F32)


def last_sum_kernel(*refs, sizes, with_nodes):
    place = 2 * len(sizes)
    totals = [refs[2 * i][0] + refs[2 * i + 1][0].astype(F32) for i in range(len(sizes))]
    if with_nodes:
        nodes_ref, g_ref = refs[place], refs[-1]
        place += 1
    for total, rows in zip(totals, sizes):
        start = 0
        for count in rows:
            refs[place][...] = total[start : start + count]
            start += count
            place += 1
    if with_nodes:
        g_ref[...] = nodes_ref[...].astype(BF16)
        g_ref[0:16, :] = (nodes_ref[0:16, :] + totals[-1][start : start + 16]).astype(BF16)


VM = pl.BlockSpec(memory_space=pltpu.VMEM)
SM = pl.BlockSpec(memory_space=pltpu.SMEM)
ANY = pl.BlockSpec(memory_space=pl.ANY)


def shape(dims, dtype):
    return jax.ShapeDtypeStruct(tuple(dims), dtype)


class Rows:
    def __init__(self, parts=1, joined=1, extra=0):
        self.parts = parts
        self.joined = joined
        self.extra = extra


class Fetched:
    def __init__(self, sources, buffer, semaphores, parts):
        self.buffer = buffer
        self.shape = buffer.shape
        self.waiting = []
        place = 0
        for source in sources:
            rows = source.shape[0] // parts
            for part in range(parts):
                if source.shape == buffer.shape and parts == 1:
                    copy = pltpu.make_async_copy(source, buffer, next(semaphores))
                else:
                    copy = pltpu.make_async_copy(
                        source.at[pl.ds(part * rows, rows)], buffer.at[pl.ds(place, rows)], next(semaphores)
                    )
                copy.start()
                self.waiting.append((place, place + rows, copy))
                place += rows

    def ready(self, low=0, high=None):
        left = []
        for first, last, copy in self.waiting:
            if high is None or (first < high and low < last):
                copy.wait()
            else:
                left.append((first, last, copy))
        self.waiting = left

    def __getitem__(self, index):
        rows = index[0] if isinstance(index, tuple) else None
        if isinstance(rows, slice) and rows.start is not None:
            self.ready(rows.start, rows.stop)
        else:
            self.ready()
        return self.buffer[index]

    def __setitem__(self, index, value):
        self.buffer[index] = value


class Stored:
    def __init__(self, target, buffer, semaphores):
        self.target = target
        self.buffer = buffer
        self.shape = buffer.shape
        self.dtype = buffer.dtype
        self.semaphores = semaphores
        self.copies = []

    def __getitem__(self, index):
        return self.buffer[index]

    def __setitem__(self, index, value):
        self.buffer[index] = value

    def done(self, rows=None):
        if rows is None:
            copy = pltpu.make_async_copy(self.buffer, self.target, next(self.semaphores))
        else:
            part = pl.ds(rows.start, rows.stop - rows.start)
            copy = pltpu.make_async_copy(self.buffer.at[part], self.target.at[part], next(self.semaphores))
        copy.start()
        self.copies.append(copy)


SEMAPHORES = 64


def staged_kernel(body, in_specs, out_specs, *refs):
    ins, outs = refs[: len(in_specs)], refs[len(in_specs) : len(in_specs) + len(out_specs)]
    rest = refs[len(in_specs) + len(out_specs) :]
    semaphores = iter([rest[0].at[i] for i in range(SEMAPHORES)])
    buffers = iter(rest[1:])
    fetched, stored = [], []
    for place, (ref, spec) in enumerate(zip(ins, in_specs)):
        if spec is VM:
            fetched.append(Fetched([ref], next(buffers), semaphores, 1))
        elif spec is SM:
            fetched.append(ref)
        elif isinstance(spec, Rows):
            fetched.append(Fetched(ins[place : place + spec.joined], next(buffers), semaphores, spec.parts))
    for ref, spec in zip(outs, out_specs):
        stored.append(Stored(ref, next(buffers), semaphores))
    body(*fetched, *stored, *buffers)
    for ref in fetched:
        if isinstance(ref, Fetched):
            ref.ready()
    for ref in stored:
        if not ref.copies:
            ref.done()
    for ref in stored:
        for copy in ref.copies:
            copy.wait()


def cost(ins, outs, flops):
    moved = sum(a.size * a.dtype.itemsize for a in list(ins) + list(outs))
    return pl.CostEstimate(flops=flops, bytes_accessed=moved, transcendentals=0)


def call(kernel, name, ins, in_specs, outs, scratch=(), flops=0):
    out_specs = [VM] * len(outs)
    buffers = []
    for place, spec in enumerate(in_specs):
        if spec is VM:
            buffers.append(pltpu.VMEM(ins[place].shape, ins[place].dtype))
        elif isinstance(spec, Rows):
            joined = ins[place : place + spec.joined]
            rows = sum(a.shape[0] for a in joined) + spec.extra
            buffers.append(pltpu.VMEM((rows,) + joined[0].shape[1:], joined[0].dtype))
    buffers += [pltpu.VMEM(a.shape, a.dtype) for a in outs]
    return pl.pallas_call(
        functools.partial(staged_kernel, kernel, in_specs, out_specs),
        out_shape=tuple(outs),
        in_specs=[SM if spec is SM else ANY for spec in in_specs],
        out_specs=tuple([ANY] * len(outs)),
        scratch_shapes=[pltpu.SemaphoreType.DMA((SEMAPHORES,))] + buffers + list(scratch),
        name=name,
        cost_estimate=cost(ins, outs, flops),
        compiler_params=pltpu.CompilerParams(vmem_limit_bytes=VMEM_LIMIT),
    )(*ins)


def small_call(kernel, name, ins, outs, passing=()):
    first = len(ins)
    last = len(outs)
    outs = list(outs) + [shape(a.shape, a.dtype) for a in passing]
    return pl.pallas_call(
        kernel,
        out_shape=tuple(outs),
        input_output_aliases={first + i: last + i for i in range(len(passing))},
        in_specs=[VM] * first + [ANY] * len(passing),
        out_specs=tuple([VM] * last + [ANY] * len(passing)),
        name=name,
        cost_estimate=cost(ins, outs, 0),
        compiler_params=pltpu.CompilerParams(vmem_limit_bytes=SMALL_LIMIT),
    )(*ins, *passing)


def passed_along(block, axis, distance):
    count = lax.axis_size(axis)
    route = [((i - distance) % count, i) for i in range(count)]
    return lax.ppermute(block, axis, route)


def exchanged(block, axis, distance):
    return lax.ppermute(block, axis, [(i, i ^ distance) for i in range(lax.axis_size(axis))])


def exchanged_with_all(blocks, axis):
    return lax.all_to_all(blocks, axis, 0, 0)


def first_halving(kept, taken):
    half = kept.shape[0] // 2
    give = (kept[half:].astype(F32) + taken[half:].astype(F32)).astype(BF16)
    return kept[:half].astype(F32) + taken[:half].astype(F32), give


def halving(kept, taken, passing=()):
    half = (kept.shape[0] // 2,) + kept.shape[1:]
    return small_call(halving_kernel, "halving", (kept, taken), [shape(half, F32), shape(half, BF16)], passing)


def last_sum(groups, sizes, nodes=None):
    ins, outs = [], []
    for (kept, taken), rows in zip(groups, sizes):
        ins += [kept, taken]
        outs += [shape((count, kept.shape[2]), F32) for count in rows]
    if nodes is not None:
        ins.append(nodes)
        outs.append(shape(nodes.shape, BF16))
    return small_call(
        functools.partial(last_sum_kernel, sizes=sizes, with_nodes=nodes is not None), "last_sum", ins, outs
    )


def local(
    nodes,
    fine_edges,
    coarse_edges,
    fine_send,
    fine_recv,
    coarse_send,
    coarse_recv,
    halo_rows,
    edge_count,
    edge_w1,
    edge_w2,
    edge_gain,
    node_w1,
    node_w2,
    node_gain,
    d_nodes,
    d_fine,
    d_coarse,
):
    axis = "patch"
    peers = lax.axis_size(axis)
    own, width = nodes.shape
    fine = fine_edges.shape[0]
    coarse = coarse_edges.shape[0]
    halo = halo_rows[0]
    slots, tile = halo.shape
    hops = slots // 2
    offsets = list(range(1, hops + 1)) + [-k for k in range(1, hops + 1)]
    ordered = peers == 16 and all(
        w.shape[0] % (16 * peers) == 0 for w in (edge_w1, edge_w2, node_w1, node_w2)
    )
    me = lax.axis_index(axis).astype(jnp.int32).reshape(1)
    fs, fr = fine_send.reshape(1, fine), fine_recv.reshape(1, fine)
    cs, cr = coarse_send.reshape(1, coarse), coarse_recv.reshape(1, coarse)
    eg, ng = edge_gain.reshape(1, width), node_gain.reshape(1, width)
    every = shape((peers, COARSE_DEV, width), BF16)

    made = call(
        tiles_kernel, "tiles", (nodes, halo), [VM, VM],
        [shape((tile, width), BF16)] * slots,
    )
    received = [passed_along(made[slot], axis, offset) for slot, offset in enumerate(offsets)]
    coarse_all = exchanged_with_all(jnp.broadcast_to(nodes[:COARSE_DEV][None], every.shape), axis)

    def saved_shapes(rows):
        return [
            shape((rows, width), BF16), shape((rows, width), BF16), shape((rows, width), BF16),
            shape((rows, width), BF16), shape((rows, width), BF16), shape((rows, 128), F32),
        ]

    new_coarse, coarse_part, *coarse_saved = call(
        coarse_forward_kernel, "coarse_forward",
        (coarse_all, coarse_edges, cs, cr, edge_w1, edge_w2, eg), [VM] * 4 + [Rows(3), VM, VM],
        [shape((coarse, width), BF16), every] + saved_shapes(coarse),
        flops=2 * coarse * width * width * 4,
    )
    share = exchanged_with_all(coarse_part, axis)

    block = 256 if fine % 256 == 0 else fine
    space_rows = own + slots * tile
    def weight_shapes(w1, w2, more):
        if not ordered:
            return [shape(w1.shape, F32), shape(w2.shape, F32)], []
        rows = (w1.shape[0] + w2.shape[0]) // peers + more
        outs = [shape((peers // 2, rows, width), BF16)] * 2
        return outs, [pltpu.VMEM(w1.shape, F32), pltpu.VMEM(w2.shape, F32)]

    sum_shapes, sum_scratch = weight_shapes(node_w1, node_w2, 0)
    new_fine, *made = call(
        functools.partial(fine_and_node_kernel, slots=slots, block=block, ordered=ordered), "fine_and_node",
        (
            edge_count, me, nodes, *received, fine_edges, fs, fr, edge_w1, edge_w2, eg,
            share, d_nodes, node_w1, node_w2, ng,
        ),
        [SM, SM] + [VM] * (slots + 4) + [Rows(3)] + [VM] * 4 + [Rows(2), VM, VM],
        [shape((fine, width), BF16)] + saved_shapes(fine)
        + [shape((own, width), BF16), shape((own, width), F32), shape((own, width), BF16), every] + sum_shapes,
        scratch=[pltpu.VMEM((space_rows, width), BF16)] + [pltpu.VMEM((own, width), F32)] * 2 + sum_scratch,
        flops=2 * fine * width * (4 * width + space_rows + 3 * own) + 2 * own * width * width * 9,
    )
    fine_saved, (new_nodes, base, dagg, dagg_spread), node_parts = made[:6], made[6:10], made[10:]
    dagg_all = exchanged_with_all(dagg_spread, axis)
    if ordered:
        node_taken = exchanged(node_parts[1], axis, 1)
        node_kept, node_given = first_halving(node_parts[0], node_taken)

    sum_shapes, sum_scratch = weight_shapes(edge_w1, edge_w2, 16)
    if ordered:
        cut = edge_w1.shape[0] // peers
        rows = sum_shapes[0].shape[1] - cut
        sum_shapes = [shape((peers // 2, cut, width), BF16)] * 2 + [shape((peers // 2, rows, width), BF16)] * 2
    f_zs, f_zr, f_hidden, f_slope, f_normed, f_std = fine_saved
    c_zs, c_zr, c_hidden, c_slope, c_normed, c_std = coarse_saved
    fine_out, fine_pre, g_fine, own_grad, *pieces = call(
        functools.partial(fine_backward_kernel, block=block), "fine_backward",
        (edge_count, fr, dagg, d_fine, eg, f_std, f_normed, edge_w2, f_slope, edge_w1, fs, base),
        [SM] + [VM] * 8 + [Rows(3), VM, VM],
        [shape((fine, width), BF16)] * 3 + [shape((own, width), F32)] + [shape((tile, width), BF16)] * slots,
        scratch=[pltpu.VMEM((space_rows, width), F32)],
        flops=2 * fine * width * (4 * width + space_rows + 2 * own),
    )
    returned = [passed_along(pieces[slot], axis, -offset) for slot, offset in enumerate(offsets)]
    if ordered:
        node_taken = exchanged(node_given, axis, 2)
    pair = [Rows(joined=2), None]
    more = [Rows(extra=coarse)]
    order = (node_taken,) if ordered else ()
    g_coarse, *edge_parts = call(
        functools.partial(coarse_backward_kernel, ordered=ordered), "coarse_backward",
        (
            me, cr, dagg_all, d_coarse, eg, c_std, c_normed, edge_w2, c_slope, fine_edges, coarse_edges,
            fine_pre, f_zs, c_zs, f_zr, c_zr, f_hidden, c_hidden, fine_out, edge_w1, cs, *order,
        ),
        [SM] + [VM] * 8 + pair + more + pair * 3 + more + [Rows(3), VM] + [None] * len(order),
        [shape((coarse, width), BF16)] + ([] if ordered else [every]) + sum_shapes,
        scratch=([pltpu.VMEM((peers * COARSE_DEV, width), F32)] if ordered else []) + sum_scratch,
        flops=2 * width * width * (4 * fine + 12 * coarse),
    )

    def rows_of(w):
        return w.shape[0] // peers

    def tile_gradient():
        (total,) = small_call(
            node_gradient_kernel, "node_gradient", (own_grad, halo, *returned), [shape((own, width), F32)]
        )
        return total

    if ordered:
        kept1, given1, kept2, given2 = edge_parts
        given1, *returned = small_call(order_kernel, "order", (), [], (given1, *returned))
        taken1 = exchanged(given1, axis, 1)
        taken2 = exchanged(given2, axis, 1)
        steps1, steps2 = x_first(peers), x_last(peers)
        kept1, given1 = first_halving(kept1, taken1)
        taken1 = exchanged(given1, axis, steps1[0])
        kept2, given2 = first_halving(kept2, taken2)
        taken2 = exchanged(given2, axis, steps2[0])
        for k in range(1, len(steps1)):
            passing = (kept1,) if k > 1 else ()
            node_kept, given, *passing = halving(node_kept, node_taken, passing)
            node_taken = exchanged(given, axis, steps1[k])
            kept2, given2, *passing = halving(kept2, taken2, tuple(passing))
            taken2 = exchanged(given2, axis, steps2[k])
            kept1, given1 = halving(passing[0] if passing else kept1, taken1)
            taken1 = exchanged(given1, axis, steps1[k])
        g_nw1, g_nw2 = last_sum([(node_kept, node_taken)], [(rows_of(node_w1), rows_of(node_w2))])
        g_ew1, g_ew2, g_nodes = last_sum(
            [(kept1, taken1), (kept2, taken2)], [(rows_of(edge_w1),), (rows_of(edge_w2),)], tile_gradient()
        )
    else:
        coarse_share = exchanged_with_all(edge_parts[0], axis)
        (g_nodes,) = small_call(
            coarse_gradient_kernel, "coarse_gradient", (tile_gradient(), coarse_share), [shape((own, width), BF16)],
        )
        g_nw1, g_nw2, g_ew1, g_ew2 = [
            lax.psum_scatter(g, axis, scatter_dimension=0, tiled=True) for g in [*node_parts, *edge_parts[1:]]
        ]
    return (new_nodes, new_fine, new_coarse, g_nodes, g_fine, g_coarse, g_ew1, g_ew2, g_nw1, g_nw2)


def solution(mesh):
    split = P(("groups", "patch"))
    rows = P(("groups", "patch"), None)
    return jax.shard_map(
        local,
        mesh=mesh,
        in_specs=(
            rows, rows, rows, split, split, split, split, P(("groups", "patch"), None, None), split,
            P(), P(), P(), P(), P(), P(), rows, rows, rows,
        ),
        out_specs=(rows,) * 10,
        check_vma=False,
    )
```

```python
import functools

import jax
import jax.numpy as jnp
from jax import lax
from jax.experimental import pallas as pl
from jax.experimental.pallas import tpu as pltpu
from jax.sharding import PartitionSpec as P

COARSE_DEV = 8
EPSILON = 1e-05
F32 = jnp.float32
BF16 = jnp.bfloat16
VMEM_LIMIT = 60 * 1024 * 1024
SMALL_LIMIT = 16 * 1024 * 1024


def mm(a, b):
    return lax.dot_general(a, b, (((1,), (0,)), ((), ())), preferred_element_type=F32)


def mm_nt(a, b):
    return lax.dot_general(a, b, (((1,), (1,)), ((), ())), preferred_element_type=F32)


def mm_tn(a, b):
    return lax.dot_general(a, b, (((0,), (0,)), ((), ())), preferred_element_type=F32)


def halves(value):
    high = value.astype(BF16)
    low = (value - high.astype(F32)).astype(BF16)
    return high, low


def one_hot(index, rows):
    row = lax.broadcasted_iota(jnp.int32, (rows, index.shape[1]), 0)
    return jnp.where(row == index, 1.0, 0.0).astype(BF16)


def pick(index, table):
    entries = index.shape[1]
    column = jnp.transpose(jnp.broadcast_to(index, (128, entries)))
    lane = lax.broadcasted_iota(jnp.int32, (entries, 128), 1)
    parts = []
    for start in range(0, table.shape[0], 128):
        parts.append(jnp.where(column == lane + start, 1.0, 0.0).astype(BF16))
    return mm(jnp.concatenate(parts, 1), table)


def put_wide(hot, rows):
    high, low = halves(rows)
    return mm(hot, high) + mm(hot, low)


def row_mean(value):
    return jnp.mean(value, axis=-1, keepdims=True)


def tail_of_forward(pre, second_w, gain):
    sigmoid = jax.nn.sigmoid(pre)
    hidden = (pre * sigmoid).astype(BF16)
    slope = sigmoid * (1.0 + pre * (1.0 - sigmoid))
    output = mm(hidden, second_w)
    centred = output - row_mean(output)
    inv_std = lax.rsqrt(row_mean(centred * centred) + EPSILON)
    normed = centred * inv_std
    return normed * gain, hidden, slope, normed, inv_std


def head_of_backward(cotan, second_w, gain, slope, normed, inv_std):
    scaled = cotan * gain
    back_out = inv_std * (scaled - row_mean(scaled) - normed * row_mean(scaled * normed))
    back_out = back_out.astype(BF16)
    back_pre = (mm_nt(back_out, second_w) * slope).astype(BF16)
    return back_out, back_pre


def tiles_kernel(nodes_ref, halo_ref, *outs):
    nodes = nodes_ref[...]
    for slot, out in enumerate(outs):
        out[...] = pick(halo_ref[slot : slot + 1, :], nodes).astype(BF16)
        out.done()


def gathered(ref):
    value = ref[...].astype(F32)
    return value.reshape(value.shape[0] * value.shape[1], value.shape[2])


def coarse_forward_kernel(
    all_ref, edges_ref, send_ref, recv_ref, w1_ref, w2_ref, gain_ref,
    new_ref, part_ref, zs_ref, zr_ref, hidden_ref, slope_ref, normed_ref, std_ref,
):
    width = edges_ref.shape[1]
    table = gathered(all_ref).astype(BF16)
    hot_r = one_hot(recv_ref[...], table.shape[0])
    edges = edges_ref[...]
    zs = pick(send_ref[...], table).astype(BF16)
    zr = pick(recv_ref[...], table).astype(BF16)
    pre = (
        mm(edges, w1_ref[0:width, :])
        + mm(zs, w1_ref[width : 2 * width, :])
        + mm(zr, w1_ref[2 * width : 3 * width, :])
    )
    message, hidden, slope, normed, inv_std = tail_of_forward(pre, w2_ref[...], gain_ref[...])
    total = put_wide(hot_r, message)
    part_ref[...] = total.reshape(part_ref.shape).astype(BF16)
    part_ref.done()
    new_ref[...] = (edges.astype(F32) + message).astype(BF16)
    zs_ref[...] = zs
    zr_ref[...] = zr
    hidden_ref[...] = hidden
    slope_ref[...] = slope.astype(BF16)
    normed_ref[...] = normed.astype(BF16)
    std_ref[...] = jnp.broadcast_to(inv_std, std_ref.shape)


def fine_forward_kernel(count_ref, nodes_ref, *refs, slots, block):
    tile_refs = refs[:slots]
    (
        edges_ref, send_ref, recv_ref, w1_ref, w2_ref, gain_ref,
        new_ref, agg_ref, zs_ref, zr_ref, hidden_ref, slope_ref, normed_ref, std_ref, space_ref,
    ) = refs[slots:]
    count, width = edges_ref.shape
    own = nodes_ref.shape[0]
    tile = tile_refs[0].shape[0]
    space_ref[0:own, :] = nodes_ref[...]
    for slot in range(slots):
        space_ref[own + slot * tile : own + (slot + 1) * tile, :] = tile_refs[slot][...]
    for start in range(0, count, block):
        rows = slice(start, start + block)
        edges = edges_ref[rows, :]
        hot_r = one_hot(recv_ref[:, rows], own)
        zs = pick(send_ref[:, rows], space_ref[...]).astype(BF16)
        zr = pick(recv_ref[:, rows], nodes_ref[...]).astype(BF16)
        pre = (
            mm(edges, w1_ref[0:width, :])
            + mm(zs, w1_ref[width : 2 * width, :])
            + mm(zr, w1_ref[2 * width : 3 * width, :])
        )
        message, hidden, slope, normed, inv_std = tail_of_forward(pre, w2_ref[...], gain_ref[...])
        place = start + lax.broadcasted_iota(jnp.int32, (block, 1), 0)
        message = jnp.where(place < count_ref[0], message, 0.0)
        arrived = put_wide(hot_r, message)
        agg_ref[...] = arrived if start == 0 else agg_ref[...] + arrived
        new_ref[rows, :] = (edges.astype(F32) + message).astype(BF16)
        zs_ref[rows, :] = zs
        zr_ref[rows, :] = zr
        hidden_ref[rows, :] = hidden
        slope_ref[rows, :] = slope.astype(BF16)
        normed_ref[rows, :] = normed.astype(BF16)
        std_ref[rows, :] = jnp.broadcast_to(inv_std, (block, std_ref.shape[1]))
        for ref in (new_ref, zs_ref, zr_ref, hidden_ref, slope_ref, normed_ref, std_ref):
            ref.done(rows)


def x_first(peers):
    return [1 << bit for bit in range(1, peers.bit_length() - 1)]


def x_last(peers):
    steps = x_first(peers)
    return steps[1:] + steps[:1]


def x_then_far(peers):
    steps = x_first(peers)
    return steps[:1] + steps[:0:-1]


def by_distance(me, peers, steps, sums, kept_ref, given_ref):
    for r in list(range(1, peers, 2)) + list(range(0, peers, 2)):
        if r == 0:
            given_ref.done()
        to = jnp.bitwise_xor(me, r)
        out = given_ref if r % 2 else kept_ref
        slot = 0
        for distance in steps:
            slot = 2 * slot + r // distance % 2
        place = 0
        for total in sums:
            rows = total.shape[0] // peers
            part = total[pl.ds(pl.multiple_of(to * rows, 8), rows), :]
            if rows % 16:
                part = jnp.concatenate([part, jnp.zeros((-rows % 16, part.shape[1]), F32)], 0)
            out[slot, place : place + part.shape[0], :] = part.astype(BF16)
            place += part.shape[0]
    kept_ref.done()


def node_kernel(
    me_ref, nodes_ref, agg_ref, share_ref, d_ref, w1_ref, w2_ref, gain_ref,
    new_ref, base_ref, dagg_ref, spread_ref, *rest, ordered,
):
    if ordered:
        kept_ref, given_ref, total_ref, g1_ref, g2_ref = rest
    else:
        g1_ref, g2_ref, total_ref = rest
    width = nodes_ref.shape[1]
    total_ref[...] = agg_ref[...]
    total_ref[0:COARSE_DEV, :] += jnp.sum(share_ref[...].astype(F32), 0)
    nodes = nodes_ref[...]
    agg = total_ref[...].astype(BF16)
    pre = mm(nodes, w1_ref[0:width, :]) + mm(agg, w1_ref[width : 2 * width, :])
    update, hidden, slope, normed, inv_std = tail_of_forward(pre, w2_ref[...], gain_ref[...])
    new_ref[...] = (nodes.astype(F32) + update).astype(BF16)
    cotan = d_ref[...].astype(F32)
    back_out, back_pre = head_of_backward(cotan, w2_ref[...], gain_ref[...], slope, normed, inv_std)
    dagg = mm_nt(back_pre, w1_ref[width : 2 * width, :])
    dagg_ref[...] = dagg.astype(BF16)
    rows = dagg[:COARSE_DEV].astype(BF16)
    for peer in range(spread_ref.shape[0]):
        spread_ref[peer] = rows
    base_ref[...] = cotan + mm_nt(back_pre, w1_ref[0:width, :])
    g1_ref[0:width, :] = mm_tn(nodes, back_pre)
    g1_ref[width : 2 * width, :] = mm_tn(agg, back_pre)
    g2_ref[...] = mm_tn(hidden, back_out)
    if ordered:
        by_distance(me_ref[0], spread_ref.shape[0], x_then_far(spread_ref.shape[0]), (g1_ref, g2_ref), kept_ref, given_ref)


def fine_backward_kernel(
    count_ref, recv_ref, dagg_ref, d_ref, gain_ref, std_ref, normed_ref, w2_ref, slope_ref,
    w1_ref, send_ref, base_ref,
    out_ref, pre_ref, g_ref, own_ref, *rest, block,
):
    piece_refs, space_ref = rest[:-1], rest[-1]
    count, width = d_ref.shape
    own = base_ref.shape[0]
    received = None
    for start in range(0, count, block):
        rows = slice(start, start + block)
        hot_r = one_hot(recv_ref[:, rows], own)
        d_edges = d_ref[rows, :].astype(F32)
        place = start + lax.broadcasted_iota(jnp.int32, (block, 1), 0)
        cotan = jnp.where(place < count_ref[0], d_edges + pick(recv_ref[:, rows], dagg_ref[...]), 0.0)
        back_out, back_pre = head_of_backward(
            cotan, w2_ref[...], gain_ref[...], slope_ref[rows, :].astype(F32),
            normed_ref[rows, :].astype(F32), std_ref[rows, 0:1],
        )
        out_ref[rows, :] = back_out
        pre_ref[rows, :] = back_pre
        out_ref.done(rows)
        pre_ref.done(rows)
        g_ref[rows, :] = (d_edges + mm_nt(back_pre, w1_ref[0:width, :])).astype(BF16)
        g_ref.done(rows)
        dz_send = mm_nt(back_pre, w1_ref[width : 2 * width, :]).astype(BF16)
        dz_recv = mm_nt(back_pre, w1_ref[2 * width : 3 * width, :]).astype(BF16)
        sent = mm(one_hot(send_ref[:, rows], space_ref.shape[0]), dz_send)
        space_ref[...] = sent if start == 0 else space_ref[...] + sent
        arrived = mm(hot_r, dz_recv)
        received = arrived if received is None else received + arrived
    for slot, piece in enumerate(piece_refs):
        tile = piece.shape[0]
        piece[...] = space_ref[own + slot * tile : own + (slot + 1) * tile, :].astype(BF16)
        piece.done()
    own_ref[...] = base_ref[...] + received + space_ref[0:own, :]


def coarse_backward_kernel(
    me_ref, recv_ref, all_ref, d_ref, gain_ref, std_ref, normed_ref, w2_ref, slope_ref,
    edges_ref, pre_ref, zs_ref, zr_ref, hidden_ref, out_ref, w1_ref, send_ref,
    g_ref, *rest, ordered,
):
    if ordered:
        kept1_ref, given1_ref, kept2_ref, given2_ref, part_ref, g1_ref, g2_ref = rest
    else:
        part_ref, g1_ref, g2_ref = rest
    width = d_ref.shape[1]
    count = hidden_ref.shape[0]
    rows = slice(count - d_ref.shape[0], count)
    table = gathered(all_ref).astype(BF16)
    d_edges = d_ref[...].astype(F32)
    cotan = d_edges + pick(recv_ref[...], table)
    back_out, back_pre = head_of_backward(
        cotan, w2_ref[...], gain_ref[...], slope_ref[...].astype(F32), normed_ref[...].astype(F32), std_ref[:, 0:1]
    )
    out_ref[rows, :] = back_out
    pre_ref[rows, :] = back_pre
    g1_ref[0:width, :] = mm_tn(edges_ref[...], pre_ref[...])
    g1_ref[width : 2 * width, :] = mm_tn(zs_ref[...], pre_ref[...])
    g1_ref[2 * width : 3 * width, :] = mm_tn(zr_ref[...], pre_ref[...])
    if ordered:
        peers = 2 * kept1_ref.shape[0]
        by_distance(me_ref[0], peers, x_first(peers), (g1_ref,), kept1_ref, given1_ref)
    g2_ref[...] = mm_tn(hidden_ref[...], out_ref[...])
    dz_send = mm_nt(back_pre, w1_ref[width : 2 * width, :]).astype(BF16)
    dz_recv = mm_nt(back_pre, w1_ref[2 * width : 3 * width, :]).astype(BF16)
    total = mm(one_hot(send_ref[...], table.shape[0]), dz_send) + mm(one_hot(recv_ref[...], table.shape[0]), dz_recv)
    part_ref[...] = total.reshape(part_ref.shape).astype(part_ref.dtype)
    if ordered:
        by_distance(me_ref[0], peers, x_last(peers), (g2_ref, part_ref), kept2_ref, given2_ref)
    g_ref[...] = (d_edges + mm_nt(back_pre, w1_ref[0:width, :])).astype(BF16)


def node_gradient_kernel(own_ref, halo_ref, *refs):
    piece_refs, out_ref = refs[:-1], refs[-1]
    arrived = None
    for slot, piece in enumerate(piece_refs):
        part = mm(one_hot(halo_ref[slot : slot + 1, :], own_ref.shape[0]), piece[...])
        arrived = part if arrived is None else arrived + part
    out_ref[...] = own_ref[...] + arrived


def coarse_gradient_kernel(total_ref, share_ref, g_ref):
    share = jnp.sum(share_ref[...].astype(F32), 0)
    first = total_ref[0:16, :] + jnp.concatenate([share, jnp.zeros_like(share)], 0)
    g_ref[...] = total_ref[...].astype(BF16)
    g_ref[0:16, :] = first.astype(BF16)


def order_kernel(*refs):
    pass


def halving_kernel(kept_ref, taken_ref, *refs):
    passing = (len(refs) - 2) // 2
    keep_ref, give_ref = refs[passing : passing + 2]
    half = keep_ref.shape[0]
    for j in range(half):
        give_ref[j] = (kept_ref[half + j] + taken_ref[half + j].astype(F32)).astype(BF16)
    for j in range(half):
        keep_ref[j] = kept_ref[j] + taken_ref[j].astype(F32)


def last_sum_kernel(*refs, sizes, with_nodes):
    place = 2 * len(sizes)
    totals = [refs[2 * i][0] + refs[2 * i + 1][0].astype(F32) for i in range(len(sizes))]
    if with_nodes:
        nodes_ref, g_ref = refs[place], refs[-1]
        place += 1
    for total, rows in zip(totals, sizes):
        start = 0
        for count in rows:
            refs[place][...] = total[start : start + count]
            start += count
            place += 1
    if with_nodes:
        g_ref[...] = nodes_ref[...].astype(BF16)
        g_ref[0:16, :] = (nodes_ref[0:16, :] + totals[-1][start : start + 16]).astype(BF16)


VM = pl.BlockSpec(memory_space=pltpu.VMEM)
SM = pl.BlockSpec(memory_space=pltpu.SMEM)
ANY = pl.BlockSpec(memory_space=pl.ANY)


def shape(dims, dtype):
    return jax.ShapeDtypeStruct(tuple(dims), dtype)


class Rows:
    def __init__(self, parts=1, joined=1, extra=0):
        self.parts = parts
        self.joined = joined
        self.extra = extra


class Fetched:
    def __init__(self, sources, buffer, semaphores, parts):
        self.buffer = buffer
        self.shape = buffer.shape
        self.waiting = []
        place = 0
        for source in sources:
            rows = source.shape[0] // parts
            for part in range(parts):
                if source.shape == buffer.shape and parts == 1:
                    copy = pltpu.make_async_copy(source, buffer, next(semaphores))
                else:
                    copy = pltpu.make_async_copy(
                        source.at[pl.ds(part * rows, rows)], buffer.at[pl.ds(place, rows)], next(semaphores)
                    )
                copy.start()
                self.waiting.append((place, place + rows, copy))
                place += rows

    def ready(self, low=0, high=None):
        left = []
        for first, last, copy in self.waiting:
            if high is None or (first < high and low < last):
                copy.wait()
            else:
                left.append((first, last, copy))
        self.waiting = left

    def __getitem__(self, index):
        rows = index[0] if isinstance(index, tuple) else None
        if isinstance(rows, slice) and rows.start is not None:
            self.ready(rows.start, rows.stop)
        else:
            self.ready()
        return self.buffer[index]

    def __setitem__(self, index, value):
        self.buffer[index] = value


class Stored:
    def __init__(self, target, buffer, semaphores):
        self.target = target
        self.buffer = buffer
        self.shape = buffer.shape
        self.dtype = buffer.dtype
        self.semaphores = semaphores
        self.copies = []

    def __getitem__(self, index):
        return self.buffer[index]

    def __setitem__(self, index, value):
        self.buffer[index] = value

    def done(self, rows=None):
        if rows is None:
            copy = pltpu.make_async_copy(self.buffer, self.target, next(self.semaphores))
        else:
            part = pl.ds(rows.start, rows.stop - rows.start)
            copy = pltpu.make_async_copy(self.buffer.at[part], self.target.at[part], next(self.semaphores))
        copy.start()
        self.copies.append(copy)


SEMAPHORES = 64


def staged_kernel(body, in_specs, out_specs, *refs):
    ins, outs = refs[: len(in_specs)], refs[len(in_specs) : len(in_specs) + len(out_specs)]
    rest = refs[len(in_specs) + len(out_specs) :]
    semaphores = iter([rest[0].at[i] for i in range(SEMAPHORES)])
    buffers = iter(rest[1:])
    fetched, stored = [], []
    for place, (ref, spec) in enumerate(zip(ins, in_specs)):
        if spec is VM:
            fetched.append(Fetched([ref], next(buffers), semaphores, 1))
        elif spec is SM:
            fetched.append(ref)
        elif isinstance(spec, Rows):
            fetched.append(Fetched(ins[place : place + spec.joined], next(buffers), semaphores, spec.parts))
    for ref, spec in zip(outs, out_specs):
        stored.append(Stored(ref, next(buffers), semaphores))
    body(*fetched, *stored, *buffers)
    for ref in fetched:
        if isinstance(ref, Fetched):
            ref.ready()
    for ref in stored:
        if not ref.copies:
            ref.done()
    for ref in stored:
        for copy in ref.copies:
            copy.wait()


def cost(ins, outs, flops):
    moved = sum(a.size * a.dtype.itemsize for a in list(ins) + list(outs))
    return pl.CostEstimate(flops=flops, bytes_accessed=moved, transcendentals=0)


def call(kernel, name, ins, in_specs, outs, scratch=(), flops=0):
    out_specs = [VM] * len(outs)
    buffers = []
    for place, spec in enumerate(in_specs):
        if spec is VM:
            buffers.append(pltpu.VMEM(ins[place].shape, ins[place].dtype))
        elif isinstance(spec, Rows):
            joined = ins[place : place + spec.joined]
            rows = sum(a.shape[0] for a in joined) + spec.extra
            buffers.append(pltpu.VMEM((rows,) + joined[0].shape[1:], joined[0].dtype))
    buffers += [pltpu.VMEM(a.shape, a.dtype) for a in outs]
    return pl.pallas_call(
        functools.partial(staged_kernel, kernel, in_specs, out_specs),
        out_shape=tuple(outs),
        in_specs=[SM if spec is SM else ANY for spec in in_specs],
        out_specs=tuple([ANY] * len(outs)),
        scratch_shapes=[pltpu.SemaphoreType.DMA((SEMAPHORES,))] + buffers + list(scratch),
        name=name,
        cost_estimate=cost(ins, outs, flops),
        compiler_params=pltpu.CompilerParams(vmem_limit_bytes=VMEM_LIMIT),
    )(*ins)


def small_call(kernel, name, ins, outs, passing=()):
    first = len(ins)
    last = len(outs)
    outs = list(outs) + [shape(a.shape, a.dtype) for a in passing]
    return pl.pallas_call(
        kernel,
        out_shape=tuple(outs),
        input_output_aliases={first + i: last + i for i in range(len(passing))},
        in_specs=[VM] * first + [ANY] * len(passing),
        out_specs=tuple([VM] * last + [ANY] * len(passing)),
        name=name,
        cost_estimate=cost(ins, outs, 0),
        compiler_params=pltpu.CompilerParams(vmem_limit_bytes=SMALL_LIMIT),
    )(*ins, *passing)


def passed_along(block, axis, distance):
    count = lax.axis_size(axis)
    route = [((i - distance) % count, i) for i in range(count)]
    return lax.ppermute(block, axis, route)


def exchanged(block, axis, distance):
    return lax.ppermute(block, axis, [(i, i ^ distance) for i in range(lax.axis_size(axis))])


def exchanged_with_all(blocks, axis):
    return lax.all_to_all(blocks, axis, 0, 0)


def first_halving(kept, taken):
    half = kept.shape[0] // 2
    give = (kept[half:].astype(F32) + taken[half:].astype(F32)).astype(BF16)
    return kept[:half].astype(F32) + taken[:half].astype(F32), give


def halving(kept, taken, passing=()):
    half = (kept.shape[0] // 2,) + kept.shape[1:]
    return small_call(halving_kernel, "halving", (kept, taken), [shape(half, F32), shape(half, BF16)], passing)


def last_sum(groups, sizes, nodes=None):
    ins, outs = [], []
    for (kept, taken), rows in zip(groups, sizes):
        ins += [kept, taken]
        outs += [shape((count, kept.shape[2]), F32) for count in rows]
    if nodes is not None:
        ins.append(nodes)
        outs.append(shape(nodes.shape, BF16))
    return small_call(
        functools.partial(last_sum_kernel, sizes=sizes, with_nodes=nodes is not None), "last_sum", ins, outs
    )


def local(
    nodes,
    fine_edges,
    coarse_edges,
    fine_send,
    fine_recv,
    coarse_send,
    coarse_recv,
    halo_rows,
    edge_count,
    edge_w1,
    edge_w2,
    edge_gain,
    node_w1,
    node_w2,
    node_gain,
    d_nodes,
    d_fine,
    d_coarse,
):
    axis = "patch"
    peers = lax.axis_size(axis)
    own, width = nodes.shape
    fine = fine_edges.shape[0]
    coarse = coarse_edges.shape[0]
    halo = halo_rows[0]
    slots, tile = halo.shape
    hops = slots // 2
    offsets = list(range(1, hops + 1)) + [-k for k in range(1, hops + 1)]
    ordered = peers == 16 and all(
        w.shape[0] % (16 * peers) == 0 for w in (edge_w1, edge_w2, node_w1, node_w2)
    )
    me = lax.axis_index(axis).astype(jnp.int32).reshape(1)
    fs, fr = fine_send.reshape(1, fine), fine_recv.reshape(1, fine)
    cs, cr = coarse_send.reshape(1, coarse), coarse_recv.reshape(1, coarse)
    eg, ng = edge_gain.reshape(1, width), node_gain.reshape(1, width)
    every = shape((peers, COARSE_DEV, width), BF16)

    made = call(
        tiles_kernel, "tiles", (nodes, halo), [VM, VM],
        [shape((tile, width), BF16)] * slots,
    )
    received = [passed_along(made[slot], axis, offset) for slot, offset in enumerate(offsets)]
    coarse_all = exchanged_with_all(jnp.broadcast_to(nodes[:COARSE_DEV][None], every.shape), axis)

    def saved_shapes(rows):
        return [
            shape((rows, width), BF16), shape((rows, width), BF16), shape((rows, width), BF16),
            shape((rows, width), BF16), shape((rows, width), BF16), shape((rows, 128), F32),
        ]

    new_coarse, coarse_part, *coarse_saved = call(
        coarse_forward_kernel, "coarse_forward",
        (coarse_all, coarse_edges, cs, cr, edge_w1, edge_w2, eg), [VM] * 4 + [Rows(3), VM, VM],
        [shape((coarse, width), BF16), every] + saved_shapes(coarse),
        flops=2 * coarse * width * width * 4,
    )
    share = exchanged_with_all(coarse_part, axis)

    block = 256 if fine % 256 == 0 else fine
    space_rows = own + slots * tile
    new_fine, fine_agg, *fine_saved = call(
        functools.partial(fine_forward_kernel, slots=slots, block=block), "fine_forward",
        (edge_count, nodes, *received, fine_edges, fs, fr, edge_w1, edge_w2, eg),
        [SM] + [VM] * (slots + 4) + [Rows(3), VM, VM],
        [shape((fine, width), BF16), shape((own, width), F32)] + saved_shapes(fine),
        scratch=[pltpu.VMEM((space_rows, width), BF16)],
        flops=2 * fine * width * (4 * width + space_rows + 3 * own),
    )

    def weight_shapes(w1, w2, more):
        if not ordered:
            return [shape(w1.shape, F32), shape(w2.shape, F32)], []
        rows = (w1.shape[0] + w2.shape[0]) // peers + more
        outs = [shape((peers // 2, rows, width), BF16)] * 2
        return outs, [pltpu.VMEM(w1.shape, F32), pltpu.VMEM(w2.shape, F32)]

    sum_shapes, sum_scratch = weight_shapes(node_w1, node_w2, 0)
    new_nodes, base, dagg, dagg_spread, *node_parts = call(
        functools.partial(node_kernel, ordered=ordered), "node_both",
        (me, nodes, fine_agg, share, d_nodes, node_w1, node_w2, ng), [SM] + [VM] * 4 + [Rows(2), VM, VM],
        [shape((own, width), BF16), shape((own, width), F32), shape((own, width), BF16), every] + sum_shapes,
        scratch=[pltpu.VMEM((own, width), F32)] + sum_scratch,
        flops=2 * own * width * width * 9,
    )
    dagg_all = exchanged_with_all(dagg_spread, axis)
    if ordered:
        node_taken = exchanged(node_parts[1], axis, 1)
        node_kept, node_given = first_halving(node_parts[0], node_taken)

    sum_shapes, sum_scratch = weight_shapes(edge_w1, edge_w2, 16)
    if ordered:
        cut = edge_w1.shape[0] // peers
        rows = sum_shapes[0].shape[1] - cut
        sum_shapes = [shape((peers // 2, cut, width), BF16)] * 2 + [shape((peers // 2, rows, width), BF16)] * 2
    f_zs, f_zr, f_hidden, f_slope, f_normed, f_std = fine_saved
    c_zs, c_zr, c_hidden, c_slope, c_normed, c_std = coarse_saved
    fine_out, fine_pre, g_fine, own_grad, *pieces = call(
        functools.partial(fine_backward_kernel, block=block), "fine_backward",
        (edge_count, fr, dagg, d_fine, eg, f_std, f_normed, edge_w2, f_slope, edge_w1, fs, base),
        [SM] + [VM] * 8 + [Rows(3), VM, VM],
        [shape((fine, width), BF16)] * 3 + [shape((own, width), F32)] + [shape((tile, width), BF16)] * slots,
        scratch=[pltpu.VMEM((space_rows, width), F32)],
        flops=2 * fine * width * (4 * width + space_rows + 2 * own),
    )
    returned = [passed_along(pieces[slot], axis, -offset) for slot, offset in enumerate(offsets)]
    if ordered:
        node_taken = exchanged(node_given, axis, 2)
    pair = [Rows(joined=2), None]
    more = [Rows(extra=coarse)]
    order = (node_taken,) if ordered else ()
    g_coarse, *edge_parts = call(
        functools.partial(coarse_backward_kernel, ordered=ordered), "coarse_backward",
        (
            me, cr, dagg_all, d_coarse, eg, c_std, c_normed, edge_w2, c_slope, fine_edges, coarse_edges,
            fine_pre, f_zs, c_zs, f_zr, c_zr, f_hidden, c_hidden, fine_out, edge_w1, cs, *order,
        ),
        [SM] + [VM] * 8 + pair + more + pair * 3 + more + [Rows(3), VM] + [None] * len(order),
        [shape((coarse, width), BF16)] + ([] if ordered else [every]) + sum_shapes,
        scratch=([pltpu.VMEM((peers * COARSE_DEV, width), F32)] if ordered else []) + sum_scratch,
        flops=2 * width * width * (4 * fine + 12 * coarse),
    )

    def rows_of(w):
        return w.shape[0] // peers

    def tile_gradient():
        (total,) = small_call(
            node_gradient_kernel, "node_gradient", (own_grad, halo, *returned), [shape((own, width), F32)]
        )
        return total

    if ordered:
        kept1, given1, kept2, given2 = edge_parts
        given1, *returned = small_call(order_kernel, "order", (), [], (given1, *returned))
        taken1 = exchanged(given1, axis, 1)
        taken2 = exchanged(given2, axis, 1)
        steps1, steps2, node_steps = x_first(peers), x_last(peers), x_then_far(peers)
        kept1, given1 = first_halving(kept1, taken1)
        taken1 = exchanged(given1, axis, steps1[0])
        kept2, given2 = first_halving(kept2, taken2)
        taken2 = exchanged(given2, axis, steps2[0])
        for k in range(1, len(steps1)):
            passing = (kept1,) if k == 1 else ()
            node_kept, given, *passing = halving(node_kept, node_taken, passing)
            node_taken = exchanged(given, axis, node_steps[k])
            kept2, given2, *passing = halving(kept2, taken2, tuple(passing))
            taken2 = exchanged(given2, axis, steps2[k])
            kept1, given1 = halving(passing[0] if passing else kept1, taken1)
            taken1 = exchanged(given1, axis, steps1[k])
        g_nw1, g_nw2 = last_sum([(node_kept, node_taken)], [(rows_of(node_w1), rows_of(node_w2))])
        g_ew1, g_ew2, g_nodes = last_sum(
            [(kept1, taken1), (kept2, taken2)], [(rows_of(edge_w1),), (rows_of(edge_w2),)], tile_gradient()
        )
    else:
        coarse_share = exchanged_with_all(edge_parts[0], axis)
        (g_nodes,) = small_call(
            coarse_gradient_kernel, "coarse_gradient", (tile_gradient(), coarse_share), [shape((own, width), BF16)],
        )
        g_nw1, g_nw2, g_ew1, g_ew2 = [
            lax.psum_scatter(g, axis, scatter_dimension=0, tiled=True) for g in [*node_parts, *edge_parts[1:]]
        ]
    return (new_nodes, new_fine, new_coarse, g_nodes, g_fine, g_coarse, g_ew1, g_ew2, g_nw1, g_nw2)


def solution(mesh):
    split = P(("groups", "patch"))
    rows = P(("groups", "patch"), None)
    return jax.shard_map(
        local,
        mesh=mesh,
        in_specs=(
            rows, rows, rows, split, split, split, split, P(("groups", "patch"), None, None), split,
            P(), P(), P(), P(), P(), P(), rows, rows, rows,
        ),
        out_specs=(rows,) * 10,
        check_vma=False,
    )
```

```python
import functools

import jax
import jax.numpy as jnp
from jax import lax
from jax.experimental import pallas as pl
from jax.experimental.pallas import tpu as pltpu
from jax.sharding import PartitionSpec as P

COARSE_DEV = 8
EPSILON = 1e-05
F32 = jnp.float32
BF16 = jnp.bfloat16
VMEM_LIMIT = 60 * 1024 * 1024
SMALL_LIMIT = 16 * 1024 * 1024


def mm(a, b):
    return lax.dot_general(a, b, (((1,), (0,)), ((), ())), preferred_element_type=F32)


def mm_nt(a, b):
    return lax.dot_general(a, b, (((1,), (1,)), ((), ())), preferred_element_type=F32)


def mm_tn(a, b):
    return lax.dot_general(a, b, (((0,), (0,)), ((), ())), preferred_element_type=F32)


def halves(value):
    high = value.astype(BF16)
    low = (value - high.astype(F32)).astype(BF16)
    return high, low


def one_hot(index, rows):
    row = lax.broadcasted_iota(jnp.int32, (rows, index.shape[1]), 0)
    return jnp.where(row == index, 1.0, 0.0).astype(BF16)


def pick(index, table):
    entries = index.shape[1]
    column = jnp.transpose(jnp.broadcast_to(index, (128, entries)))
    lane = lax.broadcasted_iota(jnp.int32, (entries, 128), 1)
    parts = []
    for start in range(0, table.shape[0], 128):
        parts.append(jnp.where(column == lane + start, 1.0, 0.0).astype(BF16))
    return mm(jnp.concatenate(parts, 1), table)


def put_wide(hot, rows):
    high, low = halves(rows)
    return mm(hot, high) + mm(hot, low)


def row_mean(value):
    return jnp.mean(value, axis=-1, keepdims=True)


def tail_of_forward(pre, second_w, gain):
    sigmoid = jax.nn.sigmoid(pre)
    hidden = (pre * sigmoid).astype(BF16)
    slope = sigmoid * (1.0 + pre * (1.0 - sigmoid))
    output = mm(hidden, second_w)
    centred = output - row_mean(output)
    inv_std = lax.rsqrt(row_mean(centred * centred) + EPSILON)
    normed = centred * inv_std
    return normed * gain, hidden, slope, normed, inv_std


def head_of_backward(cotan, second_w, gain, slope, normed, inv_std):
    scaled = cotan * gain
    back_out = inv_std * (scaled - row_mean(scaled) - normed * row_mean(scaled * normed))
    back_out = back_out.astype(BF16)
    back_pre = (mm_nt(back_out, second_w) * slope).astype(BF16)
    return back_out, back_pre


def tiles_kernel(nodes_ref, halo_ref, *outs):
    nodes = nodes_ref[...]
    for slot, out in enumerate(outs):
        out[...] = pick(halo_ref[slot : slot + 1, :], nodes).astype(BF16)
        out.done()


def gathered(ref):
    value = ref[...].astype(F32)
    return value.reshape(value.shape[0] * value.shape[1], value.shape[2])


def coarse_forward_kernel(
    all_ref, edges_ref, send_ref, recv_ref, w1_ref, w2_ref, gain_ref,
    new_ref, part_ref, zs_ref, zr_ref, hidden_ref, slope_ref, normed_ref, std_ref,
):
    width = edges_ref.shape[1]
    table = gathered(all_ref).astype(BF16)
    hot_r = one_hot(recv_ref[...], table.shape[0])
    edges = edges_ref[...]
    zs = pick(send_ref[...], table).astype(BF16)
    zr = pick(recv_ref[...], table).astype(BF16)
    pre = (
        mm(edges, w1_ref[0:width, :])
        + mm(zs, w1_ref[width : 2 * width, :])
        + mm(zr, w1_ref[2 * width : 3 * width, :])
    )
    message, hidden, slope, normed, inv_std = tail_of_forward(pre, w2_ref[...], gain_ref[...])
    total = put_wide(hot_r, message)
    part_ref[...] = total.reshape(part_ref.shape).astype(BF16)
    part_ref.done()
    new_ref[...] = (edges.astype(F32) + message).astype(BF16)
    zs_ref[...] = zs
    zr_ref[...] = zr
    hidden_ref[...] = hidden
    slope_ref[...] = slope.astype(BF16)
    normed_ref[...] = normed.astype(BF16)
    std_ref[...] = jnp.broadcast_to(inv_std, std_ref.shape)


def fine_forward_kernel(count_ref, nodes_ref, *refs, slots, block):
    tile_refs = refs[:slots]
    (
        edges_ref, send_ref, recv_ref, w1_ref, w2_ref, gain_ref,
        new_ref, agg_ref, zs_ref, zr_ref, hidden_ref, slope_ref, normed_ref, std_ref, space_ref,
    ) = refs[slots:]
    count, width = edges_ref.shape
    own = nodes_ref.shape[0]
    tile = tile_refs[0].shape[0]
    space_ref[0:own, :] = nodes_ref[...]
    for slot in range(slots):
        space_ref[own + slot * tile : own + (slot + 1) * tile, :] = tile_refs[slot][...]
    for start in range(0, count, block):
        rows = slice(start, start + block)
        edges = edges_ref[rows, :]
        hot_r = one_hot(recv_ref[:, rows], own)
        zs = pick(send_ref[:, rows], space_ref[...]).astype(BF16)
        zr = pick(recv_ref[:, rows], nodes_ref[...]).astype(BF16)
        pre = (
            mm(edges, w1_ref[0:width, :])
            + mm(zs, w1_ref[width : 2 * width, :])
            + mm(zr, w1_ref[2 * width : 3 * width, :])
        )
        message, hidden, slope, normed, inv_std = tail_of_forward(pre, w2_ref[...], gain_ref[...])
        place = start + lax.broadcasted_iota(jnp.int32, (block, 1), 0)
        message = jnp.where(place < count_ref[0], message, 0.0)
        arrived = put_wide(hot_r, message)
        agg_ref[...] = arrived if start == 0 else agg_ref[...] + arrived
        new_ref[rows, :] = (edges.astype(F32) + message).astype(BF16)
        zs_ref[rows, :] = zs
        zr_ref[rows, :] = zr
        hidden_ref[rows, :] = hidden
        slope_ref[rows, :] = slope.astype(BF16)
        normed_ref[rows, :] = normed.astype(BF16)
        std_ref[rows, :] = jnp.broadcast_to(inv_std, (block, std_ref.shape[1]))
        for ref in (new_ref, zs_ref, zr_ref, hidden_ref, slope_ref, normed_ref, std_ref):
            ref.done(rows)


def x_first(peers):
    return [1 << bit for bit in range(1, peers.bit_length() - 1)]


def x_last(peers):
    steps = x_first(peers)
    return steps[1:] + steps[:1]


def first_rows(rows):
    return rows * 5 // 6 // 16 * 16


def by_distance(me, peers, steps, sums, kept_ref, given_ref):
    for r in list(range(1, peers, 2)) + list(range(0, peers, 2)):
        if r == 0:
            given_ref.done()
        to = jnp.bitwise_xor(me, r)
        out = given_ref if r % 2 else kept_ref
        slot = 0
        for distance in steps:
            slot = 2 * slot + r // distance % 2
        place = 0
        for total, first, last in sums:
            whole = total.shape[0] // peers
            rows = last - first
            part = total[pl.ds(pl.multiple_of(to * whole + first, 8), rows), :]
            if rows % 16:
                part = jnp.concatenate([part, jnp.zeros((-rows % 16, part.shape[1]), F32)], 0)
            out[slot, place : place + part.shape[0], :] = part.astype(BF16)
            place += part.shape[0]
    kept_ref.done()


def node_kernel(
    me_ref, nodes_ref, agg_ref, share_ref, d_ref, w1_ref, w2_ref, gain_ref,
    new_ref, base_ref, dagg_ref, spread_ref, *rest, ordered,
):
    if ordered:
        kept_ref, given_ref, total_ref, g1_ref, g2_ref = rest
    else:
        g1_ref, g2_ref, total_ref = rest
    width = nodes_ref.shape[1]
    total_ref[...] = agg_ref[...]
    total_ref[0:COARSE_DEV, :] += jnp.sum(share_ref[...].astype(F32), 0)
    nodes = nodes_ref[...]
    agg = total_ref[...].astype(BF16)
    pre = mm(nodes, w1_ref[0:width, :]) + mm(agg, w1_ref[width : 2 * width, :])
    update, hidden, slope, normed, inv_std = tail_of_forward(pre, w2_ref[...], gain_ref[...])
    new_ref[...] = (nodes.astype(F32) + update).astype(BF16)
    cotan = d_ref[...].astype(F32)
    back_out, back_pre = head_of_backward(cotan, w2_ref[...], gain_ref[...], slope, normed, inv_std)
    dagg = mm_nt(back_pre, w1_ref[width : 2 * width, :])
    dagg_ref[...] = dagg.astype(BF16)
    rows = dagg[:COARSE_DEV].astype(BF16)
    for peer in range(spread_ref.shape[0]):
        spread_ref[peer] = rows
    base_ref[...] = cotan + mm_nt(back_pre, w1_ref[0:width, :])
    g1_ref[0:width, :] = mm_tn(nodes, back_pre)
    g1_ref[width : 2 * width, :] = mm_tn(agg, back_pre)
    g2_ref[...] = mm_tn(hidden, back_out)
    if ordered:
        peers = spread_ref.shape[0]

        def share(ref):
            return ref, 0, ref.shape[0] // peers

        by_distance(me_ref[0], peers, x_last(peers), (share(g1_ref), share(g2_ref)), kept_ref, given_ref)


def fine_backward_kernel(
    count_ref, recv_ref, dagg_ref, d_ref, gain_ref, std_ref, normed_ref, w2_ref, slope_ref,
    w1_ref, send_ref, base_ref,
    out_ref, pre_ref, g_ref, own_ref, *rest, block,
):
    piece_refs, space_ref = rest[:-1], rest[-1]
    count, width = d_ref.shape
    own = base_ref.shape[0]
    received = None
    for start in range(0, count, block):
        rows = slice(start, start + block)
        hot_r = one_hot(recv_ref[:, rows], own)
        d_edges = d_ref[rows, :].astype(F32)
        place = start + lax.broadcasted_iota(jnp.int32, (block, 1), 0)
        cotan = jnp.where(place < count_ref[0], d_edges + pick(recv_ref[:, rows], dagg_ref[...]), 0.0)
        back_out, back_pre = head_of_backward(
            cotan, w2_ref[...], gain_ref[...], slope_ref[rows, :].astype(F32),
            normed_ref[rows, :].astype(F32), std_ref[rows, 0:1],
        )
        out_ref[rows, :] = back_out
        pre_ref[rows, :] = back_pre
        out_ref.done(rows)
        pre_ref.done(rows)
        g_ref[rows, :] = (d_edges + mm_nt(back_pre, w1_ref[0:width, :])).astype(BF16)
        g_ref.done(rows)
        dz_send = mm_nt(back_pre, w1_ref[width : 2 * width, :]).astype(BF16)
        dz_recv = mm_nt(back_pre, w1_ref[2 * width : 3 * width, :]).astype(BF16)
        sent = mm(one_hot(send_ref[:, rows], space_ref.shape[0]), dz_send)
        space_ref[...] = sent if start == 0 else space_ref[...] + sent
        arrived = mm(hot_r, dz_recv)
        received = arrived if received is None else received + arrived
    for slot, piece in enumerate(piece_refs):
        tile = piece.shape[0]
        piece[...] = space_ref[own + slot * tile : own + (slot + 1) * tile, :].astype(BF16)
        piece.done()
    own_ref[...] = base_ref[...] + received + space_ref[0:own, :]


def coarse_backward_kernel(
    me_ref, recv_ref, all_ref, d_ref, gain_ref, std_ref, normed_ref, w2_ref, slope_ref,
    edges_ref, pre_ref, zs_ref, zr_ref, hidden_ref, out_ref, w1_ref, send_ref,
    g_ref, *rest, ordered,
):
    if ordered:
        kept1_ref, given1_ref, kept2_ref, given2_ref, part_ref, g1_ref, g2_ref = rest
    else:
        part_ref, g1_ref, g2_ref = rest
    width = d_ref.shape[1]
    count = hidden_ref.shape[0]
    rows = slice(count - d_ref.shape[0], count)
    table = gathered(all_ref).astype(BF16)
    d_edges = d_ref[...].astype(F32)
    cotan = d_edges + pick(recv_ref[...], table)
    back_out, back_pre = head_of_backward(
        cotan, w2_ref[...], gain_ref[...], slope_ref[...].astype(F32), normed_ref[...].astype(F32), std_ref[:, 0:1]
    )
    out_ref[rows, :] = back_out
    pre_ref[rows, :] = back_pre
    g1_ref[0:width, :] = mm_tn(edges_ref[...], pre_ref[...])
    g1_ref[width : 2 * width, :] = mm_tn(zs_ref[...], pre_ref[...])
    g1_ref[2 * width : 3 * width, :] = mm_tn(zr_ref[...], pre_ref[...])
    if ordered:
        peers = 2 * kept1_ref.shape[0]
        by_distance(me_ref[0], peers, x_first(peers), ((g1_ref, 0, kept1_ref.shape[1]),), kept1_ref, given1_ref)
    g2_ref[...] = mm_tn(hidden_ref[...], out_ref[...])
    dz_send = mm_nt(back_pre, w1_ref[width : 2 * width, :]).astype(BF16)
    dz_recv = mm_nt(back_pre, w1_ref[2 * width : 3 * width, :]).astype(BF16)
    total = mm(one_hot(send_ref[...], table.shape[0]), dz_send) + mm(one_hot(recv_ref[...], table.shape[0]), dz_recv)
    part_ref[...] = total.reshape(part_ref.shape).astype(part_ref.dtype)
    if ordered:
        sums = (
            (g1_ref, kept1_ref.shape[1], g1_ref.shape[0] // peers),
            (g2_ref, 0, g2_ref.shape[0] // peers),
            (part_ref, 0, part_ref.shape[0] // peers),
        )
        by_distance(me_ref[0], peers, x_last(peers), sums, kept2_ref, given2_ref)
    g_ref[...] = (d_edges + mm_nt(back_pre, w1_ref[0:width, :])).astype(BF16)


def node_gradient_kernel(own_ref, halo_ref, *refs):
    piece_refs, out_ref = refs[:-1], refs[-1]
    arrived = None
    for slot, piece in enumerate(piece_refs):
        part = mm(one_hot(halo_ref[slot : slot + 1, :], own_ref.shape[0]), piece[...])
        arrived = part if arrived is None else arrived + part
    out_ref[...] = own_ref[...] + arrived


def coarse_gradient_kernel(total_ref, share_ref, g_ref):
    share = jnp.sum(share_ref[...].astype(F32), 0)
    first = total_ref[0:16, :] + jnp.concatenate([share, jnp.zeros_like(share)], 0)
    g_ref[...] = total_ref[...].astype(BF16)
    g_ref[0:16, :] = first.astype(BF16)


def order_kernel(*refs):
    pass


def halving_kernel(kept_ref, taken_ref, *refs):
    passing = (len(refs) - 2) // 2
    keep_ref, give_ref = refs[passing : passing + 2]
    half = keep_ref.shape[0]
    for j in range(half):
        give_ref[j] = (kept_ref[half + j] + taken_ref[half + j].astype(F32)).astype(BF16)
    for j in range(half):
        keep_ref[j] = kept_ref[j] + taken_ref[j].astype(F32)


def last_sum_kernel(*refs, groups, with_nodes):
    place = 2 * groups
    totals = [refs[2 * i][0] + refs[2 * i + 1][0].astype(F32) for i in range(groups)]
    if with_nodes:
        nodes_ref, g_ref = refs[place], refs[-1]
    first_ref, second_ref = refs[place + with_nodes :][:2]
    done = totals[0].shape[0]
    cut = first_ref.shape[0]
    if groups == 1:
        first_ref[...] = totals[0][:cut]
        second_ref[...] = totals[0][cut:]
        return
    rest = totals[1]
    first_ref[0:done, :] = totals[0]
    first_ref[done:cut, :] = rest[: cut - done]
    start = cut - done + second_ref.shape[0]
    second_ref[...] = rest[cut - done : start]
    g_ref[...] = nodes_ref[...].astype(BF16)
    g_ref[0:16, :] = (nodes_ref[0:16, :] + rest[start : start + 16]).astype(BF16)


VM = pl.BlockSpec(memory_space=pltpu.VMEM)
SM = pl.BlockSpec(memory_space=pltpu.SMEM)
ANY = pl.BlockSpec(memory_space=pl.ANY)


def shape(dims, dtype):
    return jax.ShapeDtypeStruct(tuple(dims), dtype)


class Rows:
    def __init__(self, parts=1, joined=1, extra=0):
        self.parts = parts
        self.joined = joined
        self.extra = extra


class Fetched:
    def __init__(self, sources, buffer, semaphores, parts):
        self.buffer = buffer
        self.shape = buffer.shape
        self.waiting = []
        place = 0
        for source in sources:
            rows = source.shape[0] // parts
            for part in range(parts):
                if source.shape == buffer.shape and parts == 1:
                    copy = pltpu.make_async_copy(source, buffer, next(semaphores))
                else:
                    copy = pltpu.make_async_copy(
                        source.at[pl.ds(part * rows, rows)], buffer.at[pl.ds(place, rows)], next(semaphores)
                    )
                copy.start()
                self.waiting.append((place, place + rows, copy))
                place += rows

    def ready(self, low=0, high=None):
        left = []
        for first, last, copy in self.waiting:
            if high is None or (first < high and low < last):
                copy.wait()
            else:
                left.append((first, last, copy))
        self.waiting = left

    def __getitem__(self, index):
        rows = index[0] if isinstance(index, tuple) else None
        if isinstance(rows, slice) and rows.start is not None:
            self.ready(rows.start, rows.stop)
        else:
            self.ready()
        return self.buffer[index]

    def __setitem__(self, index, value):
        self.buffer[index] = value


class Stored:
    def __init__(self, target, buffer, semaphores):
        self.target = target
        self.buffer = buffer
        self.shape = buffer.shape
        self.dtype = buffer.dtype
        self.semaphores = semaphores
        self.copies = []

    def __getitem__(self, index):
        return self.buffer[index]

    def __setitem__(self, index, value):
        self.buffer[index] = value

    def done(self, rows=None):
        if rows is None:
            copy = pltpu.make_async_copy(self.buffer, self.target, next(self.semaphores))
        else:
            part = pl.ds(rows.start, rows.stop - rows.start)
            copy = pltpu.make_async_copy(self.buffer.at[part], self.target.at[part], next(self.semaphores))
        copy.start()
        self.copies.append(copy)


SEMAPHORES = 64


def staged_kernel(body, in_specs, out_specs, *refs):
    ins, outs = refs[: len(in_specs)], refs[len(in_specs) : len(in_specs) + len(out_specs)]
    rest = refs[len(in_specs) + len(out_specs) :]
    semaphores = iter([rest[0].at[i] for i in range(SEMAPHORES)])
    buffers = iter(rest[1:])
    fetched, stored = [], []
    for place, (ref, spec) in enumerate(zip(ins, in_specs)):
        if spec is VM:
            fetched.append(Fetched([ref], next(buffers), semaphores, 1))
        elif spec is SM:
            fetched.append(ref)
        elif isinstance(spec, Rows):
            fetched.append(Fetched(ins[place : place + spec.joined], next(buffers), semaphores, spec.parts))
    for ref, spec in zip(outs, out_specs):
        stored.append(Stored(ref, next(buffers), semaphores))
    body(*fetched, *stored, *buffers)
    for ref in fetched:
        if isinstance(ref, Fetched):
            ref.ready()
    for ref in stored:
        if not ref.copies:
            ref.done()
    for ref in stored:
        for copy in ref.copies:
            copy.wait()


def cost(ins, outs, flops):
    moved = sum(a.size * a.dtype.itemsize for a in list(ins) + list(outs))
    return pl.CostEstimate(flops=flops, bytes_accessed=moved, transcendentals=0)


def call(kernel, name, ins, in_specs, outs, scratch=(), flops=0):
    out_specs = [VM] * len(outs)
    buffers = []
    for place, spec in enumerate(in_specs):
        if spec is VM:
            buffers.append(pltpu.VMEM(ins[place].shape, ins[place].dtype))
        elif isinstance(spec, Rows):
            joined = ins[place : place + spec.joined]
            rows = sum(a.shape[0] for a in joined) + spec.extra
            buffers.append(pltpu.VMEM((rows,) + joined[0].shape[1:], joined[0].dtype))
    buffers += [pltpu.VMEM(a.shape, a.dtype) for a in outs]
    return pl.pallas_call(
        functools.partial(staged_kernel, kernel, in_specs, out_specs),
        out_shape=tuple(outs),
        in_specs=[SM if spec is SM else ANY for spec in in_specs],
        out_specs=tuple([ANY] * len(outs)),
        scratch_shapes=[pltpu.SemaphoreType.DMA((SEMAPHORES,))] + buffers + list(scratch),
        name=name,
        cost_estimate=cost(ins, outs, flops),
        compiler_params=pltpu.CompilerParams(vmem_limit_bytes=VMEM_LIMIT),
    )(*ins)


def small_call(kernel, name, ins, outs, passing=()):
    first = len(ins)
    last = len(outs)
    outs = list(outs) + [shape(a.shape, a.dtype) for a in passing]
    return pl.pallas_call(
        kernel,
        out_shape=tuple(outs),
        input_output_aliases={first + i: last + i for i in range(len(passing))},
        in_specs=[VM] * first + [ANY] * len(passing),
        out_specs=tuple([VM] * last + [ANY] * len(passing)),
        name=name,
        cost_estimate=cost(ins, outs, 0),
        compiler_params=pltpu.CompilerParams(vmem_limit_bytes=SMALL_LIMIT),
    )(*ins, *passing)


def passed_along(block, axis, distance):
    count = lax.axis_size(axis)
    route = [((i - distance) % count, i) for i in range(count)]
    return lax.ppermute(block, axis, route)


def exchanged(block, axis, distance):
    return lax.ppermute(block, axis, [(i, i ^ distance) for i in range(lax.axis_size(axis))])


def exchanged_with_all(blocks, axis):
    return lax.all_to_all(blocks, axis, 0, 0)


def first_halving(kept, taken):
    half = kept.shape[0] // 2
    give = (kept[half:].astype(F32) + taken[half:].astype(F32)).astype(BF16)
    return kept[:half].astype(F32) + taken[:half].astype(F32), give


def halving(kept, taken, passing=()):
    half = (kept.shape[0] // 2,) + kept.shape[1:]
    return small_call(halving_kernel, "halving", (kept, taken), [shape(half, F32), shape(half, BF16)], passing)


def last_sum(groups, sizes, nodes=None):
    ins = [array for group in groups for array in group]
    outs = [shape((count, ins[0].shape[2]), F32) for count in sizes]
    if nodes is not None:
        ins.append(nodes)
        outs.append(shape(nodes.shape, BF16))
    kernel = functools.partial(last_sum_kernel, groups=len(groups), with_nodes=nodes is not None)
    return small_call(kernel, "last_sum", ins, outs)


def local(
    nodes,
    fine_edges,
    coarse_edges,
    fine_send,
    fine_recv,
    coarse_send,
    coarse_recv,
    halo_rows,
    edge_count,
    edge_w1,
    edge_w2,
    edge_gain,
    node_w1,
    node_w2,
    node_gain,
    d_nodes,
    d_fine,
    d_coarse,
):
    axis = "patch"
    peers = lax.axis_size(axis)
    own, width = nodes.shape
    fine = fine_edges.shape[0]
    coarse = coarse_edges.shape[0]
    halo = halo_rows[0]
    slots, tile = halo.shape
    hops = slots // 2
    offsets = list(range(1, hops + 1)) + [-k for k in range(1, hops + 1)]
    ordered = peers == 16 and all(
        w.shape[0] % (16 * peers) == 0 for w in (edge_w1, edge_w2, node_w1, node_w2)
    )
    me = lax.axis_index(axis).astype(jnp.int32).reshape(1)
    fs, fr = fine_send.reshape(1, fine), fine_recv.reshape(1, fine)
    cs, cr = coarse_send.reshape(1, coarse), coarse_recv.reshape(1, coarse)
    eg, ng = edge_gain.reshape(1, width), node_gain.reshape(1, width)
    every = shape((peers, COARSE_DEV, width), BF16)

    made = call(
        tiles_kernel, "tiles", (nodes, halo), [VM, VM],
        [shape((tile, width), BF16)] * slots,
    )
    received = [passed_along(made[slot], axis, offset) for slot, offset in enumerate(offsets)]
    coarse_all = exchanged_with_all(jnp.broadcast_to(nodes[:COARSE_DEV][None], every.shape), axis)

    def saved_shapes(rows):
        return [
            shape((rows, width), BF16), shape((rows, width), BF16), shape((rows, width), BF16),
            shape((rows, width), BF16), shape((rows, width), BF16), shape((rows, 128), F32),
        ]

    new_coarse, coarse_part, *coarse_saved = call(
        coarse_forward_kernel, "coarse_forward",
        (coarse_all, coarse_edges, cs, cr, edge_w1, edge_w2, eg), [VM] * 4 + [Rows(3), VM, VM],
        [shape((coarse, width), BF16), every] + saved_shapes(coarse),
        flops=2 * coarse * width * width * 4,
    )
    share = exchanged_with_all(coarse_part, axis)

    block = 256 if fine % 256 == 0 else fine
    space_rows = own + slots * tile
    new_fine, fine_agg, *fine_saved = call(
        functools.partial(fine_forward_kernel, slots=slots, block=block), "fine_forward",
        (edge_count, nodes, *received, fine_edges, fs, fr, edge_w1, edge_w2, eg),
        [SM] + [VM] * (slots + 4) + [Rows(3), VM, VM],
        [shape((fine, width), BF16), shape((own, width), F32)] + saved_shapes(fine),
        scratch=[pltpu.VMEM((space_rows, width), BF16)],
        flops=2 * fine * width * (4 * width + space_rows + 3 * own),
    )

    def weight_shapes(w1, w2, more):
        if not ordered:
            return [shape(w1.shape, F32), shape(w2.shape, F32)], []
        rows = (w1.shape[0] + w2.shape[0]) // peers + more
        outs = [shape((peers // 2, rows, width), BF16)] * 2
        return outs, [pltpu.VMEM(w1.shape, F32), pltpu.VMEM(w2.shape, F32)]

    sum_shapes, sum_scratch = weight_shapes(node_w1, node_w2, 0)
    new_nodes, base, dagg, dagg_spread, *node_parts = call(
        functools.partial(node_kernel, ordered=ordered), "node_both",
        (me, nodes, fine_agg, share, d_nodes, node_w1, node_w2, ng), [SM] + [VM] * 4 + [Rows(2), VM, VM],
        [shape((own, width), BF16), shape((own, width), F32), shape((own, width), BF16), every] + sum_shapes,
        scratch=[pltpu.VMEM((own, width), F32)] + sum_scratch,
        flops=2 * own * width * width * 9,
    )
    dagg_all = exchanged_with_all(dagg_spread, axis)
    if ordered:
        node_taken = exchanged(node_parts[1], axis, 1)
        node_kept, node_given = first_halving(node_parts[0], node_taken)

    sum_shapes, sum_scratch = weight_shapes(edge_w1, edge_w2, 16)
    if ordered:
        cut = first_rows(edge_w1.shape[0] // peers)
        rows = sum_shapes[0].shape[1] - cut
        sum_shapes = [shape((peers // 2, cut, width), BF16)] * 2 + [shape((peers // 2, rows, width), BF16)] * 2
    f_zs, f_zr, f_hidden, f_slope, f_normed, f_std = fine_saved
    c_zs, c_zr, c_hidden, c_slope, c_normed, c_std = coarse_saved
    fine_out, fine_pre, g_fine, own_grad, *pieces = call(
        functools.partial(fine_backward_kernel, block=block), "fine_backward",
        (edge_count, fr, dagg, d_fine, eg, f_std, f_normed, edge_w2, f_slope, edge_w1, fs, base),
        [SM] + [VM] * 8 + [Rows(3), VM, VM],
        [shape((fine, width), BF16)] * 3 + [shape((own, width), F32)] + [shape((tile, width), BF16)] * slots,
        scratch=[pltpu.VMEM((space_rows, width), F32)],
        flops=2 * fine * width * (4 * width + space_rows + 2 * own),
    )
    returned = [passed_along(pieces[slot], axis, -offset) for slot, offset in enumerate(offsets)]
    if ordered:
        node_taken = exchanged(node_given, axis, 4)
    pair = [Rows(joined=2), None]
    more = [Rows(extra=coarse)]
    g_coarse, *edge_parts = call(
        functools.partial(coarse_backward_kernel, ordered=ordered), "coarse_backward",
        (
            me, cr, dagg_all, d_coarse, eg, c_std, c_normed, edge_w2, c_slope, fine_edges, coarse_edges,
            fine_pre, f_zs, c_zs, f_zr, c_zr, f_hidden, c_hidden, fine_out, edge_w1, cs,
        ),
        [SM] + [VM] * 8 + pair + more + pair * 3 + more + [Rows(3), VM],
        [shape((coarse, width), BF16)] + ([] if ordered else [every]) + sum_shapes,
        scratch=([pltpu.VMEM((peers * COARSE_DEV, width), F32)] if ordered else []) + sum_scratch,
        flops=2 * width * width * (4 * fine + 12 * coarse),
    )

    def rows_of(w):
        return w.shape[0] // peers

    def tile_gradient():
        (total,) = small_call(
            node_gradient_kernel, "node_gradient", (own_grad, halo, *returned), [shape((own, width), F32)]
        )
        return total

    if ordered:
        kept1, given1, kept2, given2 = edge_parts
        given1, node_taken, *returned = small_call(
            order_kernel, "order", (), [], (given1, node_taken, *returned)
        )
        taken1 = exchanged(given1, axis, 1)
        taken2 = exchanged(given2, axis, 1)
        steps1, steps2 = x_first(peers), x_last(peers)
        kept1, given1 = first_halving(kept1, taken1)
        taken1 = exchanged(given1, axis, steps1[0])
        kept2, given2 = first_halving(kept2, taken2)
        taken2 = exchanged(given2, axis, steps2[0])
        for k in range(1, len(steps1)):
            passing = (kept1,) if k == 1 else ()
            node_kept, given, *passing = halving(node_kept, node_taken, passing)
            node_taken = exchanged(given, axis, steps2[k])
            kept2, given2, *passing = halving(kept2, taken2, tuple(passing))
            taken2 = exchanged(given2, axis, steps2[k])
            kept1, given1 = halving(passing[0] if passing else kept1, taken1)
            taken1 = exchanged(given1, axis, steps1[k])
        g_nw1, g_nw2 = last_sum([(node_kept, node_taken)], (rows_of(node_w1), rows_of(node_w2)))
        g_ew1, g_ew2, g_nodes = last_sum(
            [(kept1, taken1), (kept2, taken2)], (rows_of(edge_w1), rows_of(edge_w2)), tile_gradient()
        )
    else:
        coarse_share = exchanged_with_all(edge_parts[0], axis)
        (g_nodes,) = small_call(
            coarse_gradient_kernel, "coarse_gradient", (tile_gradient(), coarse_share), [shape((own, width), BF16)],
        )
        g_nw1, g_nw2, g_ew1, g_ew2 = [
            lax.psum_scatter(g, axis, scatter_dimension=0, tiled=True) for g in [*node_parts, *edge_parts[1:]]
        ]
    return (new_nodes, new_fine, new_coarse, g_nodes, g_fine, g_coarse, g_ew1, g_ew2, g_nw1, g_nw2)


def solution(mesh):
    split = P(("groups", "patch"))
    rows = P(("groups", "patch"), None)
    return jax.shard_map(
        local,
        mesh=mesh,
        in_specs=(
            rows, rows, rows, split, split, split, split, P(("groups", "patch"), None, None), split,
            P(), P(), P(), P(), P(), P(), rows, rows, rows,
        ),
        out_specs=(rows,) * 10,
        check_vma=False,
    )
```

```python
import functools

import jax
import jax.numpy as jnp
from jax import lax
from jax.experimental import pallas as pl
from jax.experimental.pallas import tpu as pltpu
from jax.sharding import PartitionSpec as P

COARSE_DEV = 8
EPSILON = 1e-05
F32 = jnp.float32
BF16 = jnp.bfloat16
VMEM_LIMIT = 60 * 1024 * 1024
SMALL_LIMIT = 16 * 1024 * 1024


def mm(a, b):
    return lax.dot_general(a, b, (((1,), (0,)), ((), ())), preferred_element_type=F32)


def mm_nt(a, b):
    return lax.dot_general(a, b, (((1,), (1,)), ((), ())), preferred_element_type=F32)


def mm_tn(a, b):
    return lax.dot_general(a, b, (((0,), (0,)), ((), ())), preferred_element_type=F32)


def halves(value):
    high = value.astype(BF16)
    low = (value - high.astype(F32)).astype(BF16)
    return high, low


def one_hot(index, rows):
    row = lax.broadcasted_iota(jnp.int32, (rows, index.shape[1]), 0)
    return jnp.where(row == index, 1.0, 0.0).astype(BF16)


def pick(index, table):
    entries = index.shape[1]
    column = jnp.transpose(jnp.broadcast_to(index, (128, entries)))
    lane = lax.broadcasted_iota(jnp.int32, (entries, 128), 1)
    parts = []
    for start in range(0, table.shape[0], 128):
        parts.append(jnp.where(column == lane + start, 1.0, 0.0).astype(BF16))
    return mm(jnp.concatenate(parts, 1), table)


def put_wide(hot, rows):
    high, low = halves(rows)
    return mm(hot, high) + mm(hot, low)


def row_mean(value):
    return jnp.mean(value, axis=-1, keepdims=True)


def tail_of_forward(pre, second_w, gain):
    sigmoid = jax.nn.sigmoid(pre)
    hidden = (pre * sigmoid).astype(BF16)
    slope = sigmoid * (1.0 + pre * (1.0 - sigmoid))
    output = mm(hidden, second_w)
    centred = output - row_mean(output)
    inv_std = lax.rsqrt(row_mean(centred * centred) + EPSILON)
    normed = centred * inv_std
    return normed * gain, hidden, slope, normed, inv_std


def head_of_backward(cotan, second_w, gain, slope, normed, inv_std):
    scaled = cotan * gain
    back_out = inv_std * (scaled - row_mean(scaled) - normed * row_mean(scaled * normed))
    back_out = back_out.astype(BF16)
    back_pre = (mm_nt(back_out, second_w) * slope).astype(BF16)
    return back_out, back_pre


def tiles_kernel(nodes_ref, halo_ref, *outs):
    nodes = nodes_ref[...]
    for slot, out in enumerate(outs):
        out[...] = pick(halo_ref[slot : slot + 1, :], nodes).astype(BF16)
        out.done()


def gathered(ref):
    value = ref[...].astype(F32)
    return value.reshape(value.shape[0] * value.shape[1], value.shape[2])


def coarse_forward_kernel(
    all_ref, edges_ref, send_ref, recv_ref, w1_ref, w2_ref, gain_ref,
    new_ref, part_ref, zs_ref, zr_ref, hidden_ref, slope_ref, normed_ref, std_ref,
):
    width = edges_ref.shape[1]
    table = gathered(all_ref).astype(BF16)
    hot_r = one_hot(recv_ref[...], table.shape[0])
    edges = edges_ref[...]
    zs = pick(send_ref[...], table).astype(BF16)
    zr = pick(recv_ref[...], table).astype(BF16)
    pre = (
        mm(edges, w1_ref[0:width, :])
        + mm(zs, w1_ref[width : 2 * width, :])
        + mm(zr, w1_ref[2 * width : 3 * width, :])
    )
    message, hidden, slope, normed, inv_std = tail_of_forward(pre, w2_ref[...], gain_ref[...])
    total = put_wide(hot_r, message)
    part_ref[...] = total.reshape(part_ref.shape).astype(BF16)
    part_ref.done()
    new_ref[...] = (edges.astype(F32) + message).astype(BF16)
    zs_ref[...] = zs
    zr_ref[...] = zr
    hidden_ref[...] = hidden
    slope_ref[...] = slope.astype(BF16)
    normed_ref[...] = normed.astype(BF16)
    std_ref[...] = jnp.broadcast_to(inv_std, std_ref.shape)


def fine_forward_kernel(count_ref, nodes_ref, *refs, slots, block):
    tile_refs = refs[:slots]
    (
        edges_ref, send_ref, recv_ref, w1_ref, w2_ref, gain_ref,
        new_ref, agg_ref, zs_ref, zr_ref, hidden_ref, slope_ref, normed_ref, std_ref, space_ref,
    ) = refs[slots:]
    count, width = edges_ref.shape
    own = nodes_ref.shape[0]
    tile = tile_refs[0].shape[0]
    space_ref[0:own, :] = nodes_ref[...]
    for slot in range(slots):
        space_ref[own + slot * tile : own + (slot + 1) * tile, :] = tile_refs[slot][...]
    for start in range(0, count, block):
        rows = slice(start, start + block)
        edges = edges_ref[rows, :]
        hot_r = one_hot(recv_ref[:, rows], own)
        zs = pick(send_ref[:, rows], space_ref[...]).astype(BF16)
        zr = pick(recv_ref[:, rows], nodes_ref[...]).astype(BF16)
        pre = (
            mm(edges, w1_ref[0:width, :])
            + mm(zs, w1_ref[width : 2 * width, :])
            + mm(zr, w1_ref[2 * width : 3 * width, :])
        )
        message, hidden, slope, normed, inv_std = tail_of_forward(pre, w2_ref[...], gain_ref[...])
        place = start + lax.broadcasted_iota(jnp.int32, (block, 1), 0)
        message = jnp.where(place < count_ref[0], message, 0.0)
        arrived = put_wide(hot_r, message)
        agg_ref[...] = arrived if start == 0 else agg_ref[...] + arrived
        new_ref[rows, :] = (edges.astype(F32) + message).astype(BF16)
        zs_ref[rows, :] = zs
        zr_ref[rows, :] = zr
        hidden_ref[rows, :] = hidden
        slope_ref[rows, :] = slope.astype(BF16)
        normed_ref[rows, :] = normed.astype(BF16)
        std_ref[rows, :] = jnp.broadcast_to(inv_std, (block, std_ref.shape[1]))
        for ref in (new_ref, zs_ref, zr_ref, hidden_ref, slope_ref, normed_ref, std_ref):
            ref.done(rows)


def x_first(peers):
    return [1 << bit for bit in range(1, peers.bit_length() - 1)]


def x_last(peers):
    steps = x_first(peers)
    return steps[1:] + steps[:1]


def first_rows(rows):
    return rows * 5 // 6 // 16 * 16


def by_distance(me, peers, steps, sums, kept_ref, given_ref):
    for r in list(range(1, peers, 2)) + list(range(0, peers, 2)):
        if r == 0:
            given_ref.done()
        to = jnp.bitwise_xor(me, r)
        out = given_ref if r % 2 else kept_ref
        slot = 0
        for distance in steps:
            slot = 2 * slot + r // distance % 2
        place = 0
        for total, first, last in sums:
            whole = total.shape[0] // peers
            rows = last - first
            part = total[pl.ds(pl.multiple_of(to * whole + first, 8), rows), :]
            if rows % 16:
                part = jnp.concatenate([part, jnp.zeros((-rows % 16, part.shape[1]), F32)], 0)
            out[slot, place : place + part.shape[0], :] = part.astype(BF16)
            place += part.shape[0]
    kept_ref.done()


def node_kernel(
    me_ref, nodes_ref, agg_ref, share_ref, d_ref, w1_ref, w2_ref, gain_ref,
    new_ref, base_ref, dagg_ref, spread_ref, *rest, ordered,
):
    if ordered:
        kept_ref, given_ref, total_ref, g1_ref, g2_ref = rest
    else:
        g1_ref, g2_ref, total_ref = rest
    width = nodes_ref.shape[1]
    total_ref[...] = agg_ref[...]
    total_ref[0:COARSE_DEV, :] += jnp.sum(share_ref[...].astype(F32), 0)
    nodes = nodes_ref[...]
    agg = total_ref[...].astype(BF16)
    pre = mm(nodes, w1_ref[0:width, :]) + mm(agg, w1_ref[width : 2 * width, :])
    update, hidden, slope, normed, inv_std = tail_of_forward(pre, w2_ref[...], gain_ref[...])
    new_ref[...] = (nodes.astype(F32) + update).astype(BF16)
    cotan = d_ref[...].astype(F32)
    back_out, back_pre = head_of_backward(cotan, w2_ref[...], gain_ref[...], slope, normed, inv_std)
    dagg = mm_nt(back_pre, w1_ref[width : 2 * width, :])
    dagg_ref[...] = dagg.astype(BF16)
    rows = dagg[:COARSE_DEV].astype(BF16)
    for peer in range(spread_ref.shape[0]):
        spread_ref[peer] = rows
    base_ref[...] = cotan + mm_nt(back_pre, w1_ref[0:width, :])
    g1_ref[0:width, :] = mm_tn(nodes, back_pre)
    g1_ref[width : 2 * width, :] = mm_tn(agg, back_pre)
    g2_ref[...] = mm_tn(hidden, back_out)
    if ordered:
        peers = spread_ref.shape[0]

        def share(ref):
            return ref, 0, ref.shape[0] // peers

        by_distance(me_ref[0], peers, x_last(peers), (share(g1_ref), share(g2_ref)), kept_ref, given_ref)


def fine_backward_kernel(
    count_ref, recv_ref, dagg_ref, d_ref, gain_ref, std_ref, normed_ref, w2_ref, slope_ref,
    w1_ref, send_ref, base_ref,
    out_ref, pre_ref, g_ref, own_ref, *rest, block,
):
    piece_refs, space_ref = rest[:-1], rest[-1]
    count, width = d_ref.shape
    own = base_ref.shape[0]
    received = None
    for start in range(0, count, block):
        rows = slice(start, start + block)
        hot_r = one_hot(recv_ref[:, rows], own)
        d_edges = d_ref[rows, :].astype(F32)
        place = start + lax.broadcasted_iota(jnp.int32, (block, 1), 0)
        cotan = jnp.where(place < count_ref[0], d_edges + pick(recv_ref[:, rows], dagg_ref[...]), 0.0)
        back_out, back_pre = head_of_backward(
            cotan, w2_ref[...], gain_ref[...], slope_ref[rows, :].astype(F32),
            normed_ref[rows, :].astype(F32), std_ref[rows, 0:1],
        )
        out_ref[rows, :] = back_out
        pre_ref[rows, :] = back_pre
        out_ref.done(rows)
        pre_ref.done(rows)
        g_ref[rows, :] = (d_edges + mm_nt(back_pre, w1_ref[0:width, :])).astype(BF16)
        g_ref.done(rows)
        dz_send = mm_nt(back_pre, w1_ref[width : 2 * width, :]).astype(BF16)
        dz_recv = mm_nt(back_pre, w1_ref[2 * width : 3 * width, :]).astype(BF16)
        sent = mm(one_hot(send_ref[:, rows], space_ref.shape[0]), dz_send)
        space_ref[...] = sent if start == 0 else space_ref[...] + sent
        arrived = mm(hot_r, dz_recv)
        received = arrived if received is None else received + arrived
    for slot, piece in enumerate(piece_refs):
        tile = piece.shape[0]
        piece[...] = space_ref[own + slot * tile : own + (slot + 1) * tile, :].astype(BF16)
        piece.done()
    own_ref[...] = base_ref[...] + received + space_ref[0:own, :]


def coarse_backward_kernel(
    me_ref, recv_ref, all_ref, d_ref, gain_ref, std_ref, normed_ref, w2_ref, slope_ref,
    edges_ref, pre_ref, zs_ref, zr_ref, hidden_ref, out_ref, w1_ref, send_ref,
    g_ref, *rest, ordered,
):
    if ordered:
        kept1_ref, given1_ref, kept2_ref, given2_ref, part_ref, g1_ref, g2_ref = rest
    else:
        part_ref, g1_ref, g2_ref = rest
    width = d_ref.shape[1]
    count = hidden_ref.shape[0]
    rows = slice(count - d_ref.shape[0], count)
    table = gathered(all_ref).astype(BF16)
    d_edges = d_ref[...].astype(F32)
    cotan = d_edges + pick(recv_ref[...], table)
    back_out, back_pre = head_of_backward(
        cotan, w2_ref[...], gain_ref[...], slope_ref[...].astype(F32), normed_ref[...].astype(F32), std_ref[:, 0:1]
    )
    out_ref[rows, :] = back_out
    pre_ref[rows, :] = back_pre
    g1_ref[0:width, :] = mm_tn(edges_ref[...], pre_ref[...])
    g1_ref[width : 2 * width, :] = mm_tn(zs_ref[...], pre_ref[...])
    g1_ref[2 * width : 3 * width, :] = mm_tn(zr_ref[...], pre_ref[...])
    if ordered:
        peers = 2 * kept1_ref.shape[0]
        by_distance(me_ref[0], peers, x_first(peers), ((g1_ref, 0, kept1_ref.shape[1]),), kept1_ref, given1_ref)
    g2_ref[...] = mm_tn(hidden_ref[...], out_ref[...])
    dz_send = mm_nt(back_pre, w1_ref[width : 2 * width, :]).astype(BF16)
    dz_recv = mm_nt(back_pre, w1_ref[2 * width : 3 * width, :]).astype(BF16)
    total = mm(one_hot(send_ref[...], table.shape[0]), dz_send) + mm(one_hot(recv_ref[...], table.shape[0]), dz_recv)
    part_ref[...] = total.reshape(part_ref.shape).astype(part_ref.dtype)
    if ordered:
        sums = (
            (g1_ref, kept1_ref.shape[1], g1_ref.shape[0] // peers),
            (g2_ref, 0, g2_ref.shape[0] // peers),
            (part_ref, 0, part_ref.shape[0] // peers),
        )
        by_distance(me_ref[0], peers, x_last(peers), sums, kept2_ref, given2_ref)
    g_ref[...] = (d_edges + mm_nt(back_pre, w1_ref[0:width, :])).astype(BF16)


def node_gradient_kernel(own_ref, halo_ref, *refs):
    piece_refs, out_ref = refs[:-1], refs[-1]
    arrived = None
    for slot, piece in enumerate(piece_refs):
        part = mm(one_hot(halo_ref[slot : slot + 1, :], own_ref.shape[0]), piece[...])
        arrived = part if arrived is None else arrived + part
    out_ref[...] = own_ref[...] + arrived


def coarse_gradient_kernel(total_ref, share_ref, g_ref):
    share = jnp.sum(share_ref[...].astype(F32), 0)
    first = total_ref[0:16, :] + jnp.concatenate([share, jnp.zeros_like(share)], 0)
    g_ref[...] = total_ref[...].astype(BF16)
    g_ref[0:16, :] = first.astype(BF16)


def order_kernel(*refs):
    pass


def halving_kernel(kept_ref, taken_ref, keep_ref, give_ref):
    half = keep_ref.shape[0]
    for j in range(half):
        give_ref[j] = (kept_ref[half + j] + taken_ref[half + j].astype(F32)).astype(BF16)
    for j in range(half):
        keep_ref[j] = kept_ref[j] + taken_ref[j].astype(F32)


def last_sum_kernel(*refs, groups, with_nodes):
    place = 2 * groups
    totals = [refs[2 * i][0] + refs[2 * i + 1][0].astype(F32) for i in range(groups)]
    if with_nodes:
        nodes_ref, g_ref = refs[place], refs[-1]
    first_ref, second_ref = refs[place + with_nodes :][:2]
    done = totals[0].shape[0]
    cut = first_ref.shape[0]
    if groups == 1:
        first_ref[...] = totals[0][:cut]
        second_ref[...] = totals[0][cut:]
        return
    rest = totals[1]
    first_ref[0:done, :] = totals[0]
    first_ref[done:cut, :] = rest[: cut - done]
    start = cut - done + second_ref.shape[0]
    second_ref[...] = rest[cut - done : start]
    g_ref[...] = nodes_ref[...].astype(BF16)
    g_ref[0:16, :] = (nodes_ref[0:16, :] + rest[start : start + 16]).astype(BF16)


VM = pl.BlockSpec(memory_space=pltpu.VMEM)
SM = pl.BlockSpec(memory_space=pltpu.SMEM)
ANY = pl.BlockSpec(memory_space=pl.ANY)


def shape(dims, dtype):
    return jax.ShapeDtypeStruct(tuple(dims), dtype)


class Rows:
    def __init__(self, parts=1, joined=1, extra=0):
        self.parts = parts
        self.joined = joined
        self.extra = extra


class Fetched:
    def __init__(self, sources, buffer, semaphores, parts):
        self.buffer = buffer
        self.shape = buffer.shape
        self.waiting = []
        place = 0
        for source in sources:
            rows = source.shape[0] // parts
            for part in range(parts):
                if source.shape == buffer.shape and parts == 1:
                    copy = pltpu.make_async_copy(source, buffer, next(semaphores))
                else:
                    copy = pltpu.make_async_copy(
                        source.at[pl.ds(part * rows, rows)], buffer.at[pl.ds(place, rows)], next(semaphores)
                    )
                copy.start()
                self.waiting.append((place, place + rows, copy))
                place += rows

    def ready(self, low=0, high=None):
        left = []
        for first, last, copy in self.waiting:
            if high is None or (first < high and low < last):
                copy.wait()
            else:
                left.append((first, last, copy))
        self.waiting = left

    def __getitem__(self, index):
        rows = index[0] if isinstance(index, tuple) else None
        if isinstance(rows, slice) and rows.start is not None:
            self.ready(rows.start, rows.stop)
        else:
            self.ready()
        return self.buffer[index]

    def __setitem__(self, index, value):
        self.buffer[index] = value


class Stored:
    def __init__(self, target, buffer, semaphores):
        self.target = target
        self.buffer = buffer
        self.shape = buffer.shape
        self.dtype = buffer.dtype
        self.semaphores = semaphores
        self.copies = []

    def __getitem__(self, index):
        return self.buffer[index]

    def __setitem__(self, index, value):
        self.buffer[index] = value

    def done(self, rows=None):
        if rows is None:
            copy = pltpu.make_async_copy(self.buffer, self.target, next(self.semaphores))
        else:
            part = pl.ds(rows.start, rows.stop - rows.start)
            copy = pltpu.make_async_copy(self.buffer.at[part], self.target.at[part], next(self.semaphores))
        copy.start()
        self.copies.append(copy)


SEMAPHORES = 64


def staged_kernel(body, in_specs, out_specs, *refs):
    ins, outs = refs[: len(in_specs)], refs[len(in_specs) : len(in_specs) + len(out_specs)]
    rest = refs[len(in_specs) + len(out_specs) :]
    semaphores = iter([rest[0].at[i] for i in range(SEMAPHORES)])
    buffers = iter(rest[1:])
    fetched, stored = [], []
    for place, (ref, spec) in enumerate(zip(ins, in_specs)):
        if spec is VM:
            fetched.append(Fetched([ref], next(buffers), semaphores, 1))
        elif spec is SM:
            fetched.append(ref)
        elif isinstance(spec, Rows):
            fetched.append(Fetched(ins[place : place + spec.joined], next(buffers), semaphores, spec.parts))
    for ref, spec in zip(outs, out_specs):
        stored.append(Stored(ref, next(buffers), semaphores))
    body(*fetched, *stored, *buffers)
    for ref in fetched:
        if isinstance(ref, Fetched):
            ref.ready()
    for ref in stored:
        if not ref.copies:
            ref.done()
    for ref in stored:
        for copy in ref.copies:
            copy.wait()


def cost(ins, outs, flops):
    moved = sum(a.size * a.dtype.itemsize for a in list(ins) + list(outs))
    return pl.CostEstimate(flops=flops, bytes_accessed=moved, transcendentals=0)


def call(kernel, name, ins, in_specs, outs, scratch=(), flops=0):
    out_specs = [VM] * len(outs)
    buffers = []
    for place, spec in enumerate(in_specs):
        if spec is VM:
            buffers.append(pltpu.VMEM(ins[place].shape, ins[place].dtype))
        elif isinstance(spec, Rows):
            joined = ins[place : place + spec.joined]
            rows = sum(a.shape[0] for a in joined) + spec.extra
            buffers.append(pltpu.VMEM((rows,) + joined[0].shape[1:], joined[0].dtype))
    buffers += [pltpu.VMEM(a.shape, a.dtype) for a in outs]
    return pl.pallas_call(
        functools.partial(staged_kernel, kernel, in_specs, out_specs),
        out_shape=tuple(outs),
        in_specs=[SM if spec is SM else ANY for spec in in_specs],
        out_specs=tuple([ANY] * len(outs)),
        scratch_shapes=[pltpu.SemaphoreType.DMA((SEMAPHORES,))] + buffers + list(scratch),
        name=name,
        cost_estimate=cost(ins, outs, flops),
        compiler_params=pltpu.CompilerParams(vmem_limit_bytes=VMEM_LIMIT),
    )(*ins)


def small_call(kernel, name, ins, outs, passing=(), limit=SMALL_LIMIT):
    first = len(ins)
    last = len(outs)
    outs = list(outs) + [shape(a.shape, a.dtype) for a in passing]
    return pl.pallas_call(
        kernel,
        out_shape=tuple(outs),
        input_output_aliases={first + i: last + i for i in range(len(passing))},
        in_specs=[VM] * first + [ANY] * len(passing),
        out_specs=tuple([VM] * last + [ANY] * len(passing)),
        name=name,
        cost_estimate=cost(ins, outs, 0),
        compiler_params=pltpu.CompilerParams(vmem_limit_bytes=limit),
    )(*ins, *passing)


def passed_along(block, axis, distance):
    count = lax.axis_size(axis)
    route = [((i - distance) % count, i) for i in range(count)]
    return lax.ppermute(block, axis, route)


def exchanged(block, axis, distance):
    return lax.ppermute(block, axis, [(i, i ^ distance) for i in range(lax.axis_size(axis))])


def exchanged_with_all(blocks, axis):
    return lax.all_to_all(blocks, axis, 0, 0)


def first_halving(kept, taken):
    half = kept.shape[0] // 2
    give = (kept[half:].astype(F32) + taken[half:].astype(F32)).astype(BF16)
    return kept[:half].astype(F32) + taken[:half].astype(F32), give


def halving(kept, taken):
    half = (kept.shape[0] // 2,) + kept.shape[1:]
    return small_call(halving_kernel, "halving", (kept, taken), [shape(half, F32), shape(half, BF16)])


def last_sum(groups, sizes, nodes=None):
    ins = [array for group in groups for array in group]
    outs = [shape((count, ins[0].shape[2]), F32) for count in sizes]
    if nodes is not None:
        ins.append(nodes)
        outs.append(shape(nodes.shape, BF16))
    kernel = functools.partial(last_sum_kernel, groups=len(groups), with_nodes=nodes is not None)
    return small_call(kernel, "last_sum", ins, outs)


def local(
    nodes,
    fine_edges,
    coarse_edges,
    fine_send,
    fine_recv,
    coarse_send,
    coarse_recv,
    halo_rows,
    edge_count,
    edge_w1,
    edge_w2,
    edge_gain,
    node_w1,
    node_w2,
    node_gain,
    d_nodes,
    d_fine,
    d_coarse,
):
    axis = "patch"
    peers = lax.axis_size(axis)
    own, width = nodes.shape
    fine = fine_edges.shape[0]
    coarse = coarse_edges.shape[0]
    halo = halo_rows[0]
    slots, tile = halo.shape
    hops = slots // 2
    offsets = list(range(1, hops + 1)) + [-k for k in range(1, hops + 1)]
    ordered = peers == 16 and all(
        w.shape[0] % (16 * peers) == 0 for w in (edge_w1, edge_w2, node_w1, node_w2)
    )
    me = lax.axis_index(axis).astype(jnp.int32).reshape(1)
    fs, fr = fine_send.reshape(1, fine), fine_recv.reshape(1, fine)
    cs, cr = coarse_send.reshape(1, coarse), coarse_recv.reshape(1, coarse)
    eg, ng = edge_gain.reshape(1, width), node_gain.reshape(1, width)
    every = shape((peers, COARSE_DEV, width), BF16)

    made = call(
        tiles_kernel, "tiles", (nodes, halo), [VM, VM],
        [shape((tile, width), BF16)] * slots,
    )
    received = [passed_along(made[slot], axis, offset) for slot, offset in enumerate(offsets)]
    spread = jnp.maximum(jnp.broadcast_to(nodes[:COARSE_DEV][None], every.shape), jnp.asarray(-1000.0, BF16))
    coarse_all = exchanged_with_all(spread, axis)

    def saved_shapes(rows):
        return [
            shape((rows, width), BF16), shape((rows, width), BF16), shape((rows, width), BF16),
            shape((rows, width), BF16), shape((rows, width), BF16), shape((rows, 128), F32),
        ]

    new_coarse, coarse_part, *coarse_saved = call(
        coarse_forward_kernel, "coarse_forward",
        (coarse_all, coarse_edges, cs, cr, edge_w1, edge_w2, eg), [VM] * 4 + [Rows(3), VM, VM],
        [shape((coarse, width), BF16), every] + saved_shapes(coarse),
        flops=2 * coarse * width * width * 4,
    )
    share = exchanged_with_all(coarse_part, axis)

    block = 256 if fine % 256 == 0 else fine
    space_rows = own + slots * tile
    new_fine, fine_agg, *fine_saved = call(
        functools.partial(fine_forward_kernel, slots=slots, block=block), "fine_forward",
        (edge_count, nodes, *received, fine_edges, fs, fr, edge_w1, edge_w2, eg),
        [SM] + [VM] * (slots + 4) + [Rows(3), VM, VM],
        [shape((fine, width), BF16), shape((own, width), F32)] + saved_shapes(fine),
        scratch=[pltpu.VMEM((space_rows, width), BF16)],
        flops=2 * fine * width * (4 * width + space_rows + 3 * own),
    )

    def weight_shapes(w1, w2, more):
        if not ordered:
            return [shape(w1.shape, F32), shape(w2.shape, F32)], []
        rows = (w1.shape[0] + w2.shape[0]) // peers + more
        outs = [shape((peers // 2, rows, width), BF16)] * 2
        return outs, [pltpu.VMEM(w1.shape, F32), pltpu.VMEM(w2.shape, F32)]

    sum_shapes, sum_scratch = weight_shapes(node_w1, node_w2, 0)
    new_nodes, base, dagg, dagg_spread, *node_parts = call(
        functools.partial(node_kernel, ordered=ordered), "node_both",
        (me, nodes, fine_agg, share, d_nodes, node_w1, node_w2, ng), [SM] + [VM] * 4 + [Rows(2), VM, VM],
        [shape((own, width), BF16), shape((own, width), F32), shape((own, width), BF16), every] + sum_shapes,
        scratch=[pltpu.VMEM((own, width), F32)] + sum_scratch,
        flops=2 * own * width * width * 9,
    )
    dagg_all = exchanged_with_all(dagg_spread, axis)
    if ordered:
        node_taken = exchanged(node_parts[1], axis, 1)
        node_kept, node_given = first_halving(node_parts[0], node_taken)

    sum_shapes, sum_scratch = weight_shapes(edge_w1, edge_w2, 16)
    if ordered:
        cut = first_rows(edge_w1.shape[0] // peers)
        rows = sum_shapes[0].shape[1] - cut
        sum_shapes = [shape((peers // 2, cut, width), BF16)] * 2 + [shape((peers // 2, rows, width), BF16)] * 2
    f_zs, f_zr, f_hidden, f_slope, f_normed, f_std = fine_saved
    c_zs, c_zr, c_hidden, c_slope, c_normed, c_std = coarse_saved
    fine_out, fine_pre, g_fine, own_grad, *pieces = call(
        functools.partial(fine_backward_kernel, block=block), "fine_backward",
        (edge_count, fr, dagg, d_fine, eg, f_std, f_normed, edge_w2, f_slope, edge_w1, fs, base),
        [SM] + [VM] * 8 + [Rows(3), VM, VM],
        [shape((fine, width), BF16)] * 3 + [shape((own, width), F32)] + [shape((tile, width), BF16)] * slots,
        scratch=[pltpu.VMEM((space_rows, width), F32)],
        flops=2 * fine * width * (4 * width + space_rows + 2 * own),
    )
    returned = [passed_along(pieces[slot], axis, -offset) for slot, offset in enumerate(offsets)]
    if ordered:
        node_taken = exchanged(node_given, axis, 4)
    pair = [Rows(joined=2), None]
    more = [Rows(extra=coarse)]
    g_coarse, *edge_parts = call(
        functools.partial(coarse_backward_kernel, ordered=ordered), "coarse_backward",
        (
            me, cr, dagg_all, d_coarse, eg, c_std, c_normed, edge_w2, c_slope, fine_edges, coarse_edges,
            fine_pre, f_zs, c_zs, f_zr, c_zr, f_hidden, c_hidden, fine_out, edge_w1, cs,
        ),
        [SM] + [VM] * 8 + pair + more + pair * 3 + more + [Rows(3), VM],
        [shape((coarse, width), BF16)] + ([] if ordered else [every]) + sum_shapes,
        scratch=([pltpu.VMEM((peers * COARSE_DEV, width), F32)] if ordered else []) + sum_scratch,
        flops=2 * width * width * (4 * fine + 12 * coarse),
    )

    def rows_of(w):
        return w.shape[0] // peers

    def tile_gradient():
        (total,) = small_call(
            node_gradient_kernel, "node_gradient", (own_grad, halo, *returned), [shape((own, width), F32)]
        )
        return total

    if ordered:
        kept1, given1, kept2, given2 = edge_parts
        given1, node_taken, *returned = small_call(
            order_kernel, "order", (), [], (given1, node_taken, *returned), VMEM_LIMIT
        )
        taken1 = exchanged(given1, axis, 1)
        taken2 = exchanged(given2, axis, 1)
        steps1, steps2 = x_first(peers), x_last(peers)
        kept1, given1 = first_halving(kept1, taken1)
        taken1 = exchanged(given1, axis, steps1[0])
        kept2, given2 = first_halving(kept2, taken2)
        taken2 = exchanged(given2, axis, steps2[0])
        for k in range(1, len(steps1)):
            node_kept, given = halving(node_kept, node_taken)
            node_taken = exchanged(given, axis, steps2[k])
            kept1, given1 = halving(kept1, taken1)
            taken1 = exchanged(given1, axis, steps1[k])
            kept2, given2 = halving(kept2, taken2)
            taken2 = exchanged(given2, axis, steps2[k])
        g_nw1, g_nw2 = last_sum([(node_kept, node_taken)], (rows_of(node_w1), rows_of(node_w2)))
        g_ew1, g_ew2, g_nodes = last_sum(
            [(kept1, taken1), (kept2, taken2)], (rows_of(edge_w1), rows_of(edge_w2)), tile_gradient()
        )
    else:
        coarse_share = exchanged_with_all(edge_parts[0], axis)
        (g_nodes,) = small_call(
            coarse_gradient_kernel, "coarse_gradient", (tile_gradient(), coarse_share), [shape((own, width), BF16)],
        )
        g_nw1, g_nw2, g_ew1, g_ew2 = [
            lax.psum_scatter(g, axis, scatter_dimension=0, tiled=True) for g in [*node_parts, *edge_parts[1:]]
        ]
    return (new_nodes, new_fine, new_coarse, g_nodes, g_fine, g_coarse, g_ew1, g_ew2, g_nw1, g_nw2)


def solution(mesh):
    split = P(("groups", "patch"))
    rows = P(("groups", "patch"), None)
    return jax.shard_map(
        local,
        mesh=mesh,
        in_specs=(
            rows, rows, rows, split, split, split, split, P(("groups", "patch"), None, None), split,
            P(), P(), P(), P(), P(), P(), rows, rows, rows,
        ),
        out_specs=(rows,) * 10,
        check_vma=False,
    )
```

```python
import functools

import jax
import jax.numpy as jnp
from jax import lax
from jax.experimental import pallas as pl
from jax.experimental.pallas import tpu as pltpu
from jax.sharding import PartitionSpec as P

COARSE_DEV = 8
EPSILON = 1e-05
F32 = jnp.float32
BF16 = jnp.bfloat16
VMEM_LIMIT = 60 * 1024 * 1024
SMALL_LIMIT = 16 * 1024 * 1024


def mm(a, b):
    return lax.dot_general(a, b, (((1,), (0,)), ((), ())), preferred_element_type=F32)


def mm_nt(a, b):
    return lax.dot_general(a, b, (((1,), (1,)), ((), ())), preferred_element_type=F32)


def mm_tn(a, b):
    return lax.dot_general(a, b, (((0,), (0,)), ((), ())), preferred_element_type=F32)


def halves(value):
    high = value.astype(BF16)
    low = (value - high.astype(F32)).astype(BF16)
    return high, low


def one_hot(index, rows):
    row = lax.broadcasted_iota(jnp.int32, (rows, index.shape[1]), 0)
    return jnp.where(row == index, 1.0, 0.0).astype(BF16)


def pick(index, table):
    entries = index.shape[1]
    column = jnp.transpose(jnp.broadcast_to(index, (128, entries)))
    lane = lax.broadcasted_iota(jnp.int32, (entries, 128), 1)
    parts = []
    for start in range(0, table.shape[0], 128):
        parts.append(jnp.where(column == lane + start, 1.0, 0.0).astype(BF16))
    return mm(jnp.concatenate(parts, 1), table)


def put_wide(hot, rows):
    high, low = halves(rows)
    return mm(hot, high) + mm(hot, low)


def row_mean(value):
    return jnp.mean(value, axis=-1, keepdims=True)


def tail_of_forward(pre, second_w, gain):
    sigmoid = jax.nn.sigmoid(pre)
    hidden = (pre * sigmoid).astype(BF16)
    slope = sigmoid * (1.0 + pre * (1.0 - sigmoid))
    output = mm(hidden, second_w)
    centred = output - row_mean(output)
    inv_std = lax.rsqrt(row_mean(centred * centred) + EPSILON)
    normed = centred * inv_std
    return normed * gain, hidden, slope, normed, inv_std


def head_of_backward(cotan, second_w, gain, slope, normed, inv_std):
    scaled = cotan * gain
    back_out = inv_std * (scaled - row_mean(scaled) - normed * row_mean(scaled * normed))
    back_out = back_out.astype(BF16)
    back_pre = (mm_nt(back_out, second_w) * slope).astype(BF16)
    return back_out, back_pre


def tiles_kernel(nodes_ref, halo_ref, *outs):
    nodes = nodes_ref[...]
    for slot, out in enumerate(outs):
        out[...] = pick(halo_ref[slot : slot + 1, :], nodes).astype(BF16)
        out.done()


def gathered(ref):
    value = ref[...].astype(F32)
    return value.reshape(value.shape[0] * value.shape[1], value.shape[2])


def coarse_forward_kernel(
    all_ref, edges_ref, send_ref, recv_ref, w1_ref, w2_ref, gain_ref,
    new_ref, part_ref, zs_ref, zr_ref, hidden_ref, slope_ref, normed_ref, std_ref,
):
    width = edges_ref.shape[1]
    table = gathered(all_ref).astype(BF16)
    hot_r = one_hot(recv_ref[...], table.shape[0])
    edges = edges_ref[...]
    zs = pick(send_ref[...], table).astype(BF16)
    zr = pick(recv_ref[...], table).astype(BF16)
    pre = (
        mm(edges, w1_ref[0:width, :])
        + mm(zs, w1_ref[width : 2 * width, :])
        + mm(zr, w1_ref[2 * width : 3 * width, :])
    )
    message, hidden, slope, normed, inv_std = tail_of_forward(pre, w2_ref[...], gain_ref[...])
    total = put_wide(hot_r, message)
    part_ref[...] = total.reshape(part_ref.shape).astype(BF16)
    part_ref.done()
    new_ref[...] = (edges.astype(F32) + message).astype(BF16)
    zs_ref[...] = zs
    zr_ref[...] = zr
    hidden_ref[...] = hidden
    slope_ref[...] = slope.astype(BF16)
    normed_ref[...] = normed.astype(BF16)
    std_ref[...] = jnp.broadcast_to(inv_std, std_ref.shape)


def fine_forward_kernel(count_ref, nodes_ref, *refs, slots, block):
    tile_refs = refs[:slots]
    (
        edges_ref, send_ref, recv_ref, w1_ref, w2_ref, gain_ref,
        new_ref, agg_ref, zs_ref, zr_ref, hidden_ref, slope_ref, normed_ref, std_ref, space_ref,
    ) = refs[slots:]
    count, width = edges_ref.shape
    own = nodes_ref.shape[0]
    tile = tile_refs[0].shape[0]
    space_ref[0:own, :] = nodes_ref[...]
    for slot in range(slots):
        space_ref[own + slot * tile : own + (slot + 1) * tile, :] = tile_refs[slot][...]
    for start in range(0, count, block):
        rows = slice(start, start + block)
        edges = edges_ref[rows, :]
        hot_r = one_hot(recv_ref[:, rows], own)
        zs = pick(send_ref[:, rows], space_ref[...]).astype(BF16)
        zr = pick(recv_ref[:, rows], nodes_ref[...]).astype(BF16)
        pre = (
            mm(edges, w1_ref[0:width, :])
            + mm(zs, w1_ref[width : 2 * width, :])
            + mm(zr, w1_ref[2 * width : 3 * width, :])
        )
        message, hidden, slope, normed, inv_std = tail_of_forward(pre, w2_ref[...], gain_ref[...])
        place = start + lax.broadcasted_iota(jnp.int32, (block, 1), 0)
        message = jnp.where(place < count_ref[0], message, 0.0)
        arrived = put_wide(hot_r, message)
        agg_ref[...] = arrived if start == 0 else agg_ref[...] + arrived
        new_ref[rows, :] = (edges.astype(F32) + message).astype(BF16)
        zs_ref[rows, :] = zs
        zr_ref[rows, :] = zr
        hidden_ref[rows, :] = hidden
        slope_ref[rows, :] = slope.astype(BF16)
        normed_ref[rows, :] = normed.astype(BF16)
        std_ref[rows, :] = jnp.broadcast_to(inv_std, (block, std_ref.shape[1]))
        for ref in (new_ref, zs_ref, zr_ref, hidden_ref, slope_ref, normed_ref, std_ref):
            ref.done(rows)


def x_first(peers):
    return [1 << bit for bit in range(1, peers.bit_length() - 1)]


def x_last(peers):
    steps = x_first(peers)
    return steps[1:] + steps[:1]


def first_rows(rows):
    return rows * 5 // 6 // 16 * 16


def by_distance(me, peers, steps, sums, kept_ref, given_ref):
    for r in list(range(1, peers, 2)) + list(range(0, peers, 2)):
        if r == 0:
            given_ref.done()
        to = jnp.bitwise_xor(me, r)
        out = given_ref if r % 2 else kept_ref
        slot = 0
        for distance in steps:
            slot = 2 * slot + r // distance % 2
        place = 0
        for total, first, last in sums:
            whole = total.shape[0] // peers
            rows = last - first
            part = total[pl.ds(pl.multiple_of(to * whole + first, 8), rows), :]
            if rows % 16:
                part = jnp.concatenate([part, jnp.zeros((-rows % 16, part.shape[1]), F32)], 0)
            out[slot, place : place + part.shape[0], :] = part.astype(BF16)
            place += part.shape[0]
    kept_ref.done()


def node_kernel(
    me_ref, nodes_ref, agg_ref, share_ref, d_ref, w1_ref, w2_ref, gain_ref,
    new_ref, base_ref, dagg_ref, spread_ref, *rest, ordered,
):
    if ordered:
        kept_ref, given_ref, total_ref, g1_ref, g2_ref = rest
    else:
        g1_ref, g2_ref, total_ref = rest
    width = nodes_ref.shape[1]
    total_ref[...] = agg_ref[...]
    total_ref[0:COARSE_DEV, :] += jnp.sum(share_ref[...].astype(F32), 0)
    nodes = nodes_ref[...]
    agg = total_ref[...].astype(BF16)
    pre = mm(nodes, w1_ref[0:width, :]) + mm(agg, w1_ref[width : 2 * width, :])
    update, hidden, slope, normed, inv_std = tail_of_forward(pre, w2_ref[...], gain_ref[...])
    new_ref[...] = (nodes.astype(F32) + update).astype(BF16)
    cotan = d_ref[...].astype(F32)
    back_out, back_pre = head_of_backward(cotan, w2_ref[...], gain_ref[...], slope, normed, inv_std)
    dagg = mm_nt(back_pre, w1_ref[width : 2 * width, :])
    dagg_ref[...] = dagg.astype(BF16)
    rows = dagg[:COARSE_DEV].astype(BF16)
    for peer in range(spread_ref.shape[0]):
        spread_ref[peer] = rows
    base_ref[...] = cotan + mm_nt(back_pre, w1_ref[0:width, :])
    g1_ref[0:width, :] = mm_tn(nodes, back_pre)
    g1_ref[width : 2 * width, :] = mm_tn(agg, back_pre)
    g2_ref[...] = mm_tn(hidden, back_out)
    if ordered:
        peers = spread_ref.shape[0]

        def share(ref):
            return ref, 0, ref.shape[0] // peers

        by_distance(me_ref[0], peers, x_first(peers), (share(g1_ref), share(g2_ref)), kept_ref, given_ref)


def fine_backward_kernel(
    count_ref, recv_ref, dagg_ref, d_ref, gain_ref, std_ref, normed_ref, w2_ref, slope_ref,
    w1_ref, send_ref, base_ref,
    out_ref, pre_ref, g_ref, own_ref, order_ref, *rest, block,
):
    piece_refs, (send_dz_ref, recv_dz_ref) = rest[:-2], rest[-2:]
    count, width = d_ref.shape
    own = base_ref.shape[0]
    tile = piece_refs[0].shape[0]
    order_ref[...] = jnp.zeros(order_ref.shape, F32)
    order_ref.done()
    for start in range(0, count, block):
        rows = slice(start, start + block)
        d_edges = d_ref[rows, :].astype(F32)
        place = start + lax.broadcasted_iota(jnp.int32, (block, 1), 0)
        cotan = jnp.where(place < count_ref[0], d_edges + pick(recv_ref[:, rows], dagg_ref[...]), 0.0)
        back_out, back_pre = head_of_backward(
            cotan, w2_ref[...], gain_ref[...], slope_ref[rows, :].astype(F32),
            normed_ref[rows, :].astype(F32), std_ref[rows, 0:1],
        )
        out_ref[rows, :] = back_out
        pre_ref[rows, :] = back_pre
        out_ref.done(rows)
        pre_ref.done(rows)
        g_ref[rows, :] = (d_edges + mm_nt(back_pre, w1_ref[0:width, :])).astype(BF16)
        g_ref.done(rows)
        send_dz_ref[rows, :] = mm_nt(back_pre, w1_ref[width : 2 * width, :]).astype(BF16)
        recv_dz_ref[rows, :] = mm_nt(back_pre, w1_ref[2 * width : 3 * width, :]).astype(BF16)
    send = send_ref[...]
    for slot, piece in enumerate(piece_refs):
        piece[...] = mm(one_hot(send - (own + slot * tile), tile), send_dz_ref[...]).astype(BF16)
        piece.done()
    own_ref[...] = (
        base_ref[...] + (mm(one_hot(recv_ref[...], own), recv_dz_ref[...]) + mm(one_hot(send, own), send_dz_ref[...]))
    )


def coarse_backward_kernel(
    me_ref, recv_ref, all_ref, d_ref, gain_ref, std_ref, normed_ref, w2_ref, slope_ref,
    edges_ref, pre_ref, zs_ref, zr_ref, hidden_ref, out_ref, w1_ref, send_ref,
    g_ref, *rest, ordered,
):
    if ordered:
        kept1_ref, given1_ref, kept2_ref, given2_ref, part_ref, g1_ref, g2_ref = rest
    else:
        part_ref, g1_ref, g2_ref = rest
    width = d_ref.shape[1]
    count = hidden_ref.shape[0]
    rows = slice(count - d_ref.shape[0], count)
    table = gathered(all_ref).astype(BF16)
    d_edges = d_ref[...].astype(F32)
    cotan = d_edges + pick(recv_ref[...], table)
    back_out, back_pre = head_of_backward(
        cotan, w2_ref[...], gain_ref[...], slope_ref[...].astype(F32), normed_ref[...].astype(F32), std_ref[:, 0:1]
    )
    out_ref[rows, :] = back_out
    pre_ref[rows, :] = back_pre
    g1_ref[0:width, :] = mm_tn(edges_ref[...], pre_ref[...])
    g1_ref[width : 2 * width, :] = mm_tn(zs_ref[...], pre_ref[...])
    g1_ref[2 * width : 3 * width, :] = mm_tn(zr_ref[...], pre_ref[...])
    if ordered:
        peers = 2 * kept1_ref.shape[0]
        by_distance(me_ref[0], peers, x_first(peers), ((g1_ref, 0, kept1_ref.shape[1]),), kept1_ref, given1_ref)
    g2_ref[...] = mm_tn(hidden_ref[...], out_ref[...])
    dz_send = mm_nt(back_pre, w1_ref[width : 2 * width, :]).astype(BF16)
    dz_recv = mm_nt(back_pre, w1_ref[2 * width : 3 * width, :]).astype(BF16)
    total = mm(one_hot(send_ref[...], table.shape[0]), dz_send) + mm(one_hot(recv_ref[...], table.shape[0]), dz_recv)
    part_ref[...] = total.reshape(part_ref.shape).astype(part_ref.dtype)
    if ordered:
        sums = (
            (g1_ref, kept1_ref.shape[1], g1_ref.shape[0] // peers),
            (g2_ref, 0, g2_ref.shape[0] // peers),
            (part_ref, 0, part_ref.shape[0] // peers),
        )
        by_distance(me_ref[0], peers, x_last(peers), sums, kept2_ref, given2_ref)
    g_ref[...] = (d_edges + mm_nt(back_pre, w1_ref[0:width, :])).astype(BF16)


def node_gradient_kernel(own_ref, halo_ref, *refs):
    piece_refs, out_ref = refs[:-1], refs[-1]
    arrived = None
    for slot, piece in enumerate(piece_refs):
        part = mm(one_hot(halo_ref[slot : slot + 1, :], own_ref.shape[0]), piece[...])
        arrived = part if arrived is None else arrived + part
    out_ref[...] = own_ref[...] + arrived


def coarse_gradient_kernel(total_ref, share_ref, g_ref):
    share = jnp.sum(share_ref[...].astype(F32), 0)
    first = total_ref[0:16, :] + jnp.concatenate([share, jnp.zeros_like(share)], 0)
    g_ref[...] = total_ref[...].astype(BF16)
    g_ref[0:16, :] = first.astype(BF16)


def order_kernel(*refs):
    pass


def halving_kernel(kept_ref, taken_ref, *refs):
    keep_ref, give_ref = refs if len(refs) == 2 else refs[1:3]
    half = keep_ref.shape[0]
    for j in range(half):
        give_ref[j] = (kept_ref[half + j] + taken_ref[half + j].astype(F32)).astype(BF16)
    for j in range(half):
        keep_ref[j] = kept_ref[j] + taken_ref[j].astype(F32)


def last_sum_kernel(*refs, groups, with_nodes):
    place = 2 * groups
    totals = [refs[2 * i][0] + refs[2 * i + 1][0].astype(F32) for i in range(groups)]
    if with_nodes:
        nodes_ref, g_ref = refs[place], refs[-1]
    first_ref, second_ref = refs[place + with_nodes :][:2]
    done = totals[0].shape[0]
    cut = first_ref.shape[0]
    if groups == 1:
        first_ref[...] = totals[0][:cut]
        second_ref[...] = totals[0][cut:]
        return
    rest = totals[1]
    first_ref[0:done, :] = totals[0]
    first_ref[done:cut, :] = rest[: cut - done]
    start = cut - done + second_ref.shape[0]
    second_ref[...] = rest[cut - done : start]
    g_ref[...] = nodes_ref[...].astype(BF16)
    g_ref[0:16, :] = (nodes_ref[0:16, :] + rest[start : start + 16]).astype(BF16)


VM = pl.BlockSpec(memory_space=pltpu.VMEM)
SM = pl.BlockSpec(memory_space=pltpu.SMEM)
ANY = pl.BlockSpec(memory_space=pl.ANY)


def shape(dims, dtype):
    return jax.ShapeDtypeStruct(tuple(dims), dtype)


class Rows:
    def __init__(self, parts=1, joined=1, extra=0):
        self.parts = parts
        self.joined = joined
        self.extra = extra


class Fetched:
    def __init__(self, sources, buffer, semaphores, parts):
        self.buffer = buffer
        self.shape = buffer.shape
        self.waiting = []
        place = 0
        for source in sources:
            rows = source.shape[0] // parts
            for part in range(parts):
                if source.shape == buffer.shape and parts == 1:
                    copy = pltpu.make_async_copy(source, buffer, next(semaphores))
                else:
                    copy = pltpu.make_async_copy(
                        source.at[pl.ds(part * rows, rows)], buffer.at[pl.ds(place, rows)], next(semaphores)
                    )
                copy.start()
                self.waiting.append((place, place + rows, copy))
                place += rows

    def ready(self, low=0, high=None):
        left = []
        for first, last, copy in self.waiting:
            if high is None or (first < high and low < last):
                copy.wait()
            else:
                left.append((first, last, copy))
        self.waiting = left

    def __getitem__(self, index):
        rows = index[0] if isinstance(index, tuple) else None
        if isinstance(rows, slice) and rows.start is not None:
            self.ready(rows.start, rows.stop)
        else:
            self.ready()
        return self.buffer[index]

    def __setitem__(self, index, value):
        self.buffer[index] = value


class Stored:
    def __init__(self, target, buffer, semaphores):
        self.target = target
        self.buffer = buffer
        self.shape = buffer.shape
        self.dtype = buffer.dtype
        self.semaphores = semaphores
        self.copies = []

    def __getitem__(self, index):
        return self.buffer[index]

    def __setitem__(self, index, value):
        self.buffer[index] = value

    def done(self, rows=None):
        if rows is None:
            copy = pltpu.make_async_copy(self.buffer, self.target, next(self.semaphores))
        else:
            part = pl.ds(rows.start, rows.stop - rows.start)
            copy = pltpu.make_async_copy(self.buffer.at[part], self.target.at[part], next(self.semaphores))
        copy.start()
        self.copies.append(copy)


SEMAPHORES = 64


def staged_kernel(body, in_specs, out_specs, *refs):
    ins, outs = refs[: len(in_specs)], refs[len(in_specs) : len(in_specs) + len(out_specs)]
    rest = refs[len(in_specs) + len(out_specs) :]
    semaphores = iter([rest[0].at[i] for i in range(SEMAPHORES)])
    buffers = iter(rest[1:])
    fetched, stored = [], []
    for place, (ref, spec) in enumerate(zip(ins, in_specs)):
        if spec is VM:
            fetched.append(Fetched([ref], next(buffers), semaphores, 1))
        elif spec is SM:
            fetched.append(ref)
        elif isinstance(spec, Rows):
            fetched.append(Fetched(ins[place : place + spec.joined], next(buffers), semaphores, spec.parts))
    for ref, spec in zip(outs, out_specs):
        stored.append(Stored(ref, next(buffers), semaphores))
    body(*fetched, *stored, *buffers)
    for ref in fetched:
        if isinstance(ref, Fetched):
            ref.ready()
    for ref in stored:
        if not ref.copies:
            ref.done()
    for ref in stored:
        for copy in ref.copies:
            copy.wait()


def cost(ins, outs, flops):
    moved = sum(a.size * a.dtype.itemsize for a in list(ins) + list(outs))
    return pl.CostEstimate(flops=flops, bytes_accessed=moved, transcendentals=0)


def call(kernel, name, ins, in_specs, outs, scratch=(), flops=0):
    out_specs = [VM] * len(outs)
    buffers = []
    for place, spec in enumerate(in_specs):
        if spec is VM:
            buffers.append(pltpu.VMEM(ins[place].shape, ins[place].dtype))
        elif isinstance(spec, Rows):
            joined = ins[place : place + spec.joined]
            rows = sum(a.shape[0] for a in joined) + spec.extra
            buffers.append(pltpu.VMEM((rows,) + joined[0].shape[1:], joined[0].dtype))
    buffers += [pltpu.VMEM(a.shape, a.dtype) for a in outs]
    return pl.pallas_call(
        functools.partial(staged_kernel, kernel, in_specs, out_specs),
        out_shape=tuple(outs),
        in_specs=[SM if spec is SM else ANY for spec in in_specs],
        out_specs=tuple([ANY] * len(outs)),
        scratch_shapes=[pltpu.SemaphoreType.DMA((SEMAPHORES,))] + buffers + list(scratch),
        name=name,
        cost_estimate=cost(ins, outs, flops),
        compiler_params=pltpu.CompilerParams(vmem_limit_bytes=VMEM_LIMIT),
    )(*ins)


def small_call(kernel, name, ins, outs, passing=(), limit=SMALL_LIMIT):
    first = len(ins)
    last = len(outs)
    outs = list(outs) + [shape(a.shape, a.dtype) for a in passing]
    return pl.pallas_call(
        kernel,
        out_shape=tuple(outs),
        input_output_aliases={first + i: last + i for i in range(len(passing))},
        in_specs=[VM] * first + [ANY] * len(passing),
        out_specs=tuple([VM] * last + [ANY] * len(passing)),
        name=name,
        cost_estimate=cost(ins, outs, 0),
        compiler_params=pltpu.CompilerParams(vmem_limit_bytes=limit),
    )(*ins, *passing)


def passed_along(block, axis, distance):
    count = lax.axis_size(axis)
    route = [((i - distance) % count, i) for i in range(count)]
    return lax.ppermute(block, axis, route)


def exchanged(block, axis, distance):
    return lax.ppermute(block, axis, [(i, i ^ distance) for i in range(lax.axis_size(axis))])


def exchanged_with_all(blocks, axis):
    return lax.all_to_all(blocks, axis, 0, 0)


def first_halving(kept, taken):
    half = kept.shape[0] // 2
    give = (kept[half:].astype(F32) + taken[half:].astype(F32)).astype(BF16)
    return kept[:half].astype(F32) + taken[:half].astype(F32), give


def halving(kept, taken, passing=()):
    half = (kept.shape[0] // 2,) + kept.shape[1:]
    return small_call(halving_kernel, "halving", (kept, taken), [shape(half, F32), shape(half, BF16)], passing)


def last_sum(groups, sizes, nodes=None):
    ins = [array for group in groups for array in group]
    outs = [shape((count, ins[0].shape[2]), F32) for count in sizes]
    if nodes is not None:
        ins.append(nodes)
        outs.append(shape(nodes.shape, BF16))
    kernel = functools.partial(last_sum_kernel, groups=len(groups), with_nodes=nodes is not None)
    return small_call(kernel, "last_sum", ins, outs)


def local(
    nodes,
    fine_edges,
    coarse_edges,
    fine_send,
    fine_recv,
    coarse_send,
    coarse_recv,
    halo_rows,
    edge_count,
    edge_w1,
    edge_w2,
    edge_gain,
    node_w1,
    node_w2,
    node_gain,
    d_nodes,
    d_fine,
    d_coarse,
):
    axis = "patch"
    peers = lax.axis_size(axis)
    own, width = nodes.shape
    fine = fine_edges.shape[0]
    coarse = coarse_edges.shape[0]
    halo = halo_rows[0]
    slots, tile = halo.shape
    hops = slots // 2
    offsets = list(range(1, hops + 1)) + [-k for k in range(1, hops + 1)]
    ordered = peers == 16 and all(
        w.shape[0] % (16 * peers) == 0 for w in (edge_w1, edge_w2, node_w1, node_w2)
    )
    me = lax.axis_index(axis).astype(jnp.int32).reshape(1)
    fs, fr = fine_send.reshape(1, fine), fine_recv.reshape(1, fine)
    cs, cr = coarse_send.reshape(1, coarse), coarse_recv.reshape(1, coarse)
    eg, ng = edge_gain.reshape(1, width), node_gain.reshape(1, width)
    every = shape((peers, COARSE_DEV, width), BF16)

    made = call(
        tiles_kernel, "tiles", (nodes, halo), [VM, VM],
        [shape((tile, width), BF16)] * slots,
    )
    received = [passed_along(made[slot], axis, offset) for slot, offset in enumerate(offsets)]
    coarse_all = exchanged_with_all(jnp.broadcast_to(nodes[:COARSE_DEV][None], every.shape), axis)

    def saved_shapes(rows):
        return [
            shape((rows, width), BF16), shape((rows, width), BF16), shape((rows, width), BF16),
            shape((rows, width), BF16), shape((rows, width), BF16), shape((rows, 128), F32),
        ]

    new_coarse, coarse_part, *coarse_saved = call(
        coarse_forward_kernel, "coarse_forward",
        (coarse_all, coarse_edges, cs, cr, edge_w1, edge_w2, eg), [VM] * 4 + [Rows(3), VM, VM],
        [shape((coarse, width), BF16), every] + saved_shapes(coarse),
        flops=2 * coarse * width * width * 4,
    )
    share = exchanged_with_all(coarse_part, axis)

    block = 256 if fine % 256 == 0 else fine
    space_rows = own + slots * tile
    new_fine, fine_agg, *fine_saved = call(
        functools.partial(fine_forward_kernel, slots=slots, block=block), "fine_forward",
        (edge_count, nodes, *received, fine_edges, fs, fr, edge_w1, edge_w2, eg),
        [SM] + [VM] * (slots + 4) + [Rows(3), VM, VM],
        [shape((fine, width), BF16), shape((own, width), F32)] + saved_shapes(fine),
        scratch=[pltpu.VMEM((space_rows, width), BF16)],
        flops=2 * fine * width * (4 * width + space_rows + 3 * own),
    )

    def weight_shapes(w1, w2, more):
        if not ordered:
            return [shape(w1.shape, F32), shape(w2.shape, F32)], []
        rows = (w1.shape[0] + w2.shape[0]) // peers + more
        outs = [shape((peers // 2, rows, width), BF16)] * 2
        return outs, [pltpu.VMEM(w1.shape, F32), pltpu.VMEM(w2.shape, F32)]

    sum_shapes, sum_scratch = weight_shapes(node_w1, node_w2, 0)
    new_nodes, base, dagg, dagg_spread, *node_parts = call(
        functools.partial(node_kernel, ordered=ordered), "node_both",
        (me, nodes, fine_agg, share, d_nodes, node_w1, node_w2, ng), [SM] + [VM] * 4 + [Rows(2), VM, VM],
        [shape((own, width), BF16), shape((own, width), F32), shape((own, width), BF16), every] + sum_shapes,
        scratch=[pltpu.VMEM((own, width), F32)] + sum_scratch,
        flops=2 * own * width * width * 9,
    )
    dagg_all = exchanged_with_all(dagg_spread, axis)
    if ordered:
        node_taken = exchanged(node_parts[1], axis, 1)
        node_kept, node_given = first_halving(node_parts[0], node_taken)

    sum_shapes, sum_scratch = weight_shapes(edge_w1, edge_w2, 16)
    if ordered:
        cut = first_rows(edge_w1.shape[0] // peers)
        rows = sum_shapes[0].shape[1] - cut
        sum_shapes = [shape((peers // 2, cut, width), BF16)] * 2 + [shape((peers // 2, rows, width), BF16)] * 2
    f_zs, f_zr, f_hidden, f_slope, f_normed, f_std = fine_saved
    c_zs, c_zr, c_hidden, c_slope, c_normed, c_std = coarse_saved
    fine_out, fine_pre, g_fine, own_grad, behind, *pieces = call(
        functools.partial(fine_backward_kernel, block=block), "fine_backward",
        (edge_count, fr, dagg, d_fine, eg, f_std, f_normed, edge_w2, f_slope, edge_w1, fs, base),
        [SM] + [VM] * 8 + [Rows(3), VM, VM],
        [shape((fine, width), BF16)] * 3 + [shape((own, width), F32), shape((8, 128), F32)]
        + [shape((tile, width), BF16)] * slots,
        scratch=[pltpu.VMEM((fine, width), BF16)] * 2,
        flops=2 * fine * width * (4 * width + space_rows + 2 * own),
    )
    returned = [passed_along(pieces[slot], axis, -offset) for slot, offset in enumerate(offsets)]
    if ordered:
        node_taken = exchanged(node_given, axis, 2)
        node_kept, node_given, _ = halving(node_kept, node_taken, (behind,))
        node_taken = exchanged(node_given, axis, 4)
    pair = [Rows(joined=2), None]
    more = [Rows(extra=coarse)]
    g_coarse, *edge_parts = call(
        functools.partial(coarse_backward_kernel, ordered=ordered), "coarse_backward",
        (
            me, cr, dagg_all, d_coarse, eg, c_std, c_normed, edge_w2, c_slope, fine_edges, coarse_edges,
            fine_pre, f_zs, c_zs, f_zr, c_zr, f_hidden, c_hidden, fine_out, edge_w1, cs,
        ),
        [SM] + [VM] * 8 + pair + more + pair * 3 + more + [Rows(3), VM],
        [shape((coarse, width), BF16)] + ([] if ordered else [every]) + sum_shapes,
        scratch=([pltpu.VMEM((peers * COARSE_DEV, width), F32)] if ordered else []) + sum_scratch,
        flops=2 * width * width * (4 * fine + 12 * coarse),
    )

    def rows_of(w):
        return w.shape[0] // peers

    def tile_gradient():
        (total,) = small_call(
            node_gradient_kernel, "node_gradient", (own_grad, halo, *returned), [shape((own, width), F32)]
        )
        return total

    if ordered:
        kept1, given1, kept2, given2 = edge_parts
        given1, node_taken, *returned = small_call(
            order_kernel, "order", (), [], (given1, node_taken, *returned), VMEM_LIMIT
        )
        taken1 = exchanged(given1, axis, 1)
        taken2 = exchanged(given2, axis, 1)
        steps1, steps2 = x_first(peers), x_last(peers)
        kept1, given1 = first_halving(kept1, taken1)
        taken1 = exchanged(given1, axis, steps1[0])
        kept2, given2 = first_halving(kept2, taken2)
        taken2 = exchanged(given2, axis, steps2[0])
        for k in range(1, len(steps1)):
            if k > 1:
                node_kept, given = halving(node_kept, node_taken)
                node_taken = exchanged(given, axis, steps1[k])
            kept1, given1 = halving(kept1, taken1)
            taken1 = exchanged(given1, axis, steps1[k])
            kept2, given2 = halving(kept2, taken2)
            taken2 = exchanged(given2, axis, steps2[k])
        g_nw1, g_nw2 = last_sum([(node_kept, node_taken)], (rows_of(node_w1), rows_of(node_w2)))
        g_ew1, g_ew2, g_nodes = last_sum(
            [(kept1, taken1), (kept2, taken2)], (rows_of(edge_w1), rows_of(edge_w2)), tile_gradient()
        )
    else:
        coarse_share = exchanged_with_all(edge_parts[0], axis)
        (g_nodes,) = small_call(
            coarse_gradient_kernel, "coarse_gradient", (tile_gradient(), coarse_share), [shape((own, width), BF16)],
        )
        g_nw1, g_nw2, g_ew1, g_ew2 = [
            lax.psum_scatter(g, axis, scatter_dimension=0, tiled=True) for g in [*node_parts, *edge_parts[1:]]
        ]
    return (new_nodes, new_fine, new_coarse, g_nodes, g_fine, g_coarse, g_ew1, g_ew2, g_nw1, g_nw2)


def solution(mesh):
    split = P(("groups", "patch"))
    rows = P(("groups", "patch"), None)
    return jax.shard_map(
        local,
        mesh=mesh,
        in_specs=(
            rows, rows, rows, split, split, split, split, P(("groups", "patch"), None, None), split,
            P(), P(), P(), P(), P(), P(), rows, rows, rows,
        ),
        out_specs=(rows,) * 10,
        check_vma=False,
    )
```

```python
import functools

import jax
import jax.numpy as jnp
from jax import lax
from jax.experimental import pallas as pl
from jax.experimental.pallas import tpu as pltpu
from jax.sharding import PartitionSpec as P

COARSE_DEV = 8
EPSILON = 1e-05
F32 = jnp.float32
BF16 = jnp.bfloat16
VMEM_LIMIT = 60 * 1024 * 1024
SMALL_LIMIT = 16 * 1024 * 1024


def mm(a, b):
    return lax.dot_general(a, b, (((1,), (0,)), ((), ())), preferred_element_type=F32)


def mm_nt(a, b):
    return lax.dot_general(a, b, (((1,), (1,)), ((), ())), preferred_element_type=F32)


def mm_tn(a, b):
    return lax.dot_general(a, b, (((0,), (0,)), ((), ())), preferred_element_type=F32)


def halves(value):
    high = value.astype(BF16)
    low = (value - high.astype(F32)).astype(BF16)
    return high, low


def one_hot(index, rows):
    row = lax.broadcasted_iota(jnp.int32, (rows, index.shape[1]), 0)
    return jnp.where(row == index, 1.0, 0.0).astype(BF16)


def pick(index, table):
    entries = index.shape[1]
    column = jnp.transpose(jnp.broadcast_to(index, (128, entries)))
    lane = lax.broadcasted_iota(jnp.int32, (entries, 128), 1)
    parts = []
    for start in range(0, table.shape[0], 128):
        parts.append(jnp.where(column == lane + start, 1.0, 0.0).astype(BF16))
    return mm(jnp.concatenate(parts, 1), table)


def put_wide(hot, rows):
    high, low = halves(rows)
    return mm(hot, high) + mm(hot, low)


def row_mean(value):
    return jnp.mean(value, axis=-1, keepdims=True)


def tail_of_forward(pre, second_w, gain):
    sigmoid = jax.nn.sigmoid(pre)
    hidden = (pre * sigmoid).astype(BF16)
    slope = sigmoid * (1.0 + pre * (1.0 - sigmoid))
    output = mm(hidden, second_w)
    centred = output - row_mean(output)
    inv_std = lax.rsqrt(row_mean(centred * centred) + EPSILON)
    normed = centred * inv_std
    return normed * gain, hidden, slope, normed, inv_std


def head_of_backward(cotan, second_w, gain, slope, normed, inv_std):
    scaled = cotan * gain
    back_out = inv_std * (scaled - row_mean(scaled) - normed * row_mean(scaled * normed))
    back_out = back_out.astype(BF16)
    back_pre = (mm_nt(back_out, second_w) * slope).astype(BF16)
    return back_out, back_pre


def tiles_kernel(nodes_ref, halo_ref, *outs):
    nodes = nodes_ref[...]
    for slot, out in enumerate(outs):
        out[...] = pick(halo_ref[slot : slot + 1, :], nodes).astype(BF16)
        out.done()


def gathered(ref):
    value = ref[...].astype(F32)
    return value.reshape(value.shape[0] * value.shape[1], value.shape[2])


def coarse_forward_kernel(
    all_ref, edges_ref, send_ref, recv_ref, w1_ref, w2_ref, gain_ref,
    new_ref, part_ref, zs_ref, zr_ref, hidden_ref, slope_ref, normed_ref, std_ref,
):
    width = edges_ref.shape[1]
    table = gathered(all_ref).astype(BF16)
    hot_r = one_hot(recv_ref[...], table.shape[0])
    edges = edges_ref[...]
    zs = pick(send_ref[...], table).astype(BF16)
    zr = pick(recv_ref[...], table).astype(BF16)
    pre = (
        mm(edges, w1_ref[0:width, :])
        + mm(zs, w1_ref[width : 2 * width, :])
        + mm(zr, w1_ref[2 * width : 3 * width, :])
    )
    message, hidden, slope, normed, inv_std = tail_of_forward(pre, w2_ref[...], gain_ref[...])
    total = put_wide(hot_r, message)
    part_ref[...] = total.reshape(part_ref.shape).astype(BF16)
    part_ref.done()
    new_ref[...] = (edges.astype(F32) + message).astype(BF16)
    zs_ref[...] = zs
    zr_ref[...] = zr
    hidden_ref[...] = hidden
    slope_ref[...] = slope.astype(BF16)
    normed_ref[...] = normed.astype(BF16)
    std_ref[...] = jnp.broadcast_to(inv_std, std_ref.shape)


def fine_forward_kernel(count_ref, nodes_ref, *refs, slots, block):
    tile_refs = refs[:slots]
    (
        edges_ref, send_ref, recv_ref, w1_ref, w2_ref, gain_ref,
        new_ref, agg_ref, zs_ref, zr_ref, hidden_ref, slope_ref, normed_ref, std_ref, space_ref,
    ) = refs[slots:]
    count, width = edges_ref.shape
    own = nodes_ref.shape[0]
    tile = tile_refs[0].shape[0]
    space_ref[0:own, :] = nodes_ref[...]
    for slot in range(slots):
        space_ref[own + slot * tile : own + (slot + 1) * tile, :] = tile_refs[slot][...]
    for start in range(0, count, block):
        rows = slice(start, start + block)
        edges = edges_ref[rows, :]
        hot_r = one_hot(recv_ref[:, rows], own)
        zs = pick(send_ref[:, rows], space_ref[...]).astype(BF16)
        zr = pick(recv_ref[:, rows], nodes_ref[...]).astype(BF16)
        pre = (
            mm(edges, w1_ref[0:width, :])
            + mm(zs, w1_ref[width : 2 * width, :])
            + mm(zr, w1_ref[2 * width : 3 * width, :])
        )
        message, hidden, slope, normed, inv_std = tail_of_forward(pre, w2_ref[...], gain_ref[...])
        place = start + lax.broadcasted_iota(jnp.int32, (block, 1), 0)
        message = jnp.where(place < count_ref[0], message, 0.0)
        arrived = put_wide(hot_r, message)
        agg_ref[...] = arrived if start == 0 else agg_ref[...] + arrived
        new_ref[rows, :] = (edges.astype(F32) + message).astype(BF16)
        zs_ref[rows, :] = zs
        zr_ref[rows, :] = zr
        hidden_ref[rows, :] = hidden
        slope_ref[rows, :] = slope.astype(BF16)
        normed_ref[rows, :] = normed.astype(BF16)
        std_ref[rows, :] = jnp.broadcast_to(inv_std, (block, std_ref.shape[1]))
        for ref in (new_ref, zs_ref, zr_ref, hidden_ref, slope_ref, normed_ref, std_ref):
            ref.done(rows)


def x_first(peers):
    return [1 << bit for bit in range(1, peers.bit_length() - 1)]


def x_last(peers):
    steps = x_first(peers)
    return steps[1:] + steps[:1]


def first_rows(rows):
    return rows


def by_distance(me, peers, steps, sums, kept_ref, given_ref):
    for r in list(range(1, peers, 2)) + list(range(0, peers, 2)):
        if r == 0:
            given_ref.done()
        to = jnp.bitwise_xor(me, r)
        out = given_ref if r % 2 else kept_ref
        slot = 0
        for distance in steps:
            slot = 2 * slot + r // distance % 2
        place = 0
        for total, first, last in sums:
            whole = total.shape[0] // peers
            rows = last - first
            if rows == 0:
                continue
            part = total[pl.ds(pl.multiple_of(to * whole + first, 8), rows), :]
            if rows % 16:
                part = jnp.concatenate([part, jnp.zeros((-rows % 16, part.shape[1]), F32)], 0)
            out[slot, place : place + part.shape[0], :] = part.astype(BF16)
            place += part.shape[0]
    kept_ref.done()


def node_kernel(
    me_ref, nodes_ref, agg_ref, share_ref, d_ref, w1_ref, w2_ref, gain_ref,
    new_ref, base_ref, dagg_ref, spread_ref, *rest, ordered,
):
    if ordered:
        kept_ref, given_ref, total_ref, g1_ref, g2_ref = rest
    else:
        g1_ref, g2_ref, total_ref = rest
    width = nodes_ref.shape[1]
    total_ref[...] = agg_ref[...]
    total_ref[0:COARSE_DEV, :] += jnp.sum(share_ref[...].astype(F32), 0)
    nodes = nodes_ref[...]
    agg = total_ref[...].astype(BF16)
    pre = mm(nodes, w1_ref[0:width, :]) + mm(agg, w1_ref[width : 2 * width, :])
    update, hidden, slope, normed, inv_std = tail_of_forward(pre, w2_ref[...], gain_ref[...])
    new_ref[...] = (nodes.astype(F32) + update).astype(BF16)
    cotan = d_ref[...].astype(F32)
    back_out, back_pre = head_of_backward(cotan, w2_ref[...], gain_ref[...], slope, normed, inv_std)
    dagg = mm_nt(back_pre, w1_ref[width : 2 * width, :])
    dagg_ref[...] = dagg.astype(BF16)
    rows = dagg[:COARSE_DEV].astype(BF16)
    for peer in range(spread_ref.shape[0]):
        spread_ref[peer] = rows
    base_ref[...] = cotan + mm_nt(back_pre, w1_ref[0:width, :])
    g1_ref[0:width, :] = mm_tn(nodes, back_pre)
    g1_ref[width : 2 * width, :] = mm_tn(agg, back_pre)
    g2_ref[...] = mm_tn(hidden, back_out)
    if ordered:
        peers = spread_ref.shape[0]

        def share(ref):
            return ref, 0, ref.shape[0] // peers

        by_distance(me_ref[0], peers, x_last(peers), (share(g1_ref), share(g2_ref)), kept_ref, given_ref)


def fine_backward_kernel(
    count_ref, recv_ref, dagg_ref, d_ref, gain_ref, std_ref, normed_ref, w2_ref, slope_ref,
    w1_ref, send_ref, base_ref,
    out_ref, pre_ref, g_ref, own_ref, *rest, block,
):
    piece_refs, space_ref = rest[:-1], rest[-1]
    count, width = d_ref.shape
    own = base_ref.shape[0]
    received = None
    for start in range(0, count, block):
        rows = slice(start, start + block)
        hot_r = one_hot(recv_ref[:, rows], own)
        d_edges = d_ref[rows, :].astype(F32)
        place = start + lax.broadcasted_iota(jnp.int32, (block, 1), 0)
        cotan = jnp.where(place < count_ref[0], d_edges + pick(recv_ref[:, rows], dagg_ref[...]), 0.0)
        back_out, back_pre = head_of_backward(
            cotan, w2_ref[...], gain_ref[...], slope_ref[rows, :].astype(F32),
            normed_ref[rows, :].astype(F32), std_ref[rows, 0:1],
        )
        out_ref[rows, :] = back_out
        pre_ref[rows, :] = back_pre
        out_ref.done(rows)
        pre_ref.done(rows)
        g_ref[rows, :] = (d_edges + mm_nt(back_pre, w1_ref[0:width, :])).astype(BF16)
        g_ref.done(rows)
        dz_send = mm_nt(back_pre, w1_ref[width : 2 * width, :]).astype(BF16)
        dz_recv = mm_nt(back_pre, w1_ref[2 * width : 3 * width, :]).astype(BF16)
        sent = mm(one_hot(send_ref[:, rows], space_ref.shape[0]), dz_send)
        space_ref[...] = sent if start == 0 else space_ref[...] + sent
        arrived = mm(hot_r, dz_recv)
        received = arrived if received is None else received + arrived
    for slot, piece in enumerate(piece_refs):
        tile = piece.shape[0]
        piece[...] = space_ref[own + slot * tile : own + (slot + 1) * tile, :].astype(BF16)
        piece.done()
    own_ref[...] = base_ref[...] + received + space_ref[0:own, :]


def coarse_backward_kernel(
    me_ref, recv_ref, all_ref, d_ref, gain_ref, std_ref, normed_ref, w2_ref, slope_ref,
    edges_ref, pre_ref, zs_ref, zr_ref, hidden_ref, out_ref, w1_ref, send_ref,
    g_ref, *rest, ordered,
):
    if ordered:
        kept1_ref, given1_ref, kept2_ref, given2_ref, part_ref, g1_ref, g2_ref = rest
    else:
        part_ref, g1_ref, g2_ref = rest
    width = d_ref.shape[1]
    count = hidden_ref.shape[0]
    rows = slice(count - d_ref.shape[0], count)
    table = gathered(all_ref).astype(BF16)
    d_edges = d_ref[...].astype(F32)
    cotan = d_edges + pick(recv_ref[...], table)
    back_out, back_pre = head_of_backward(
        cotan, w2_ref[...], gain_ref[...], slope_ref[...].astype(F32), normed_ref[...].astype(F32), std_ref[:, 0:1]
    )
    out_ref[rows, :] = back_out
    pre_ref[rows, :] = back_pre
    g1_ref[0:width, :] = mm_tn(edges_ref[...], pre_ref[...])
    g1_ref[width : 2 * width, :] = mm_tn(zs_ref[...], pre_ref[...])
    g1_ref[2 * width : 3 * width, :] = mm_tn(zr_ref[...], pre_ref[...])
    if ordered:
        peers = 2 * kept1_ref.shape[0]
        by_distance(me_ref[0], peers, x_first(peers), ((g1_ref, 0, kept1_ref.shape[1]),), kept1_ref, given1_ref)
    g2_ref[...] = mm_tn(hidden_ref[...], out_ref[...])
    dz_send = mm_nt(back_pre, w1_ref[width : 2 * width, :]).astype(BF16)
    dz_recv = mm_nt(back_pre, w1_ref[2 * width : 3 * width, :]).astype(BF16)
    total = mm(one_hot(send_ref[...], table.shape[0]), dz_send) + mm(one_hot(recv_ref[...], table.shape[0]), dz_recv)
    part_ref[...] = total.reshape(part_ref.shape).astype(part_ref.dtype)
    if ordered:
        sums = (
            (g1_ref, kept1_ref.shape[1], g1_ref.shape[0] // peers),
            (g2_ref, 0, g2_ref.shape[0] // peers),
            (part_ref, 0, part_ref.shape[0] // peers),
        )
        by_distance(me_ref[0], peers, x_last(peers), sums, kept2_ref, given2_ref)
    g_ref[...] = (d_edges + mm_nt(back_pre, w1_ref[0:width, :])).astype(BF16)


def node_gradient_kernel(own_ref, halo_ref, *refs):
    piece_refs, out_ref = refs[:-1], refs[-1]
    arrived = None
    for slot, piece in enumerate(piece_refs):
        part = mm(one_hot(halo_ref[slot : slot + 1, :], own_ref.shape[0]), piece[...])
        arrived = part if arrived is None else arrived + part
    out_ref[...] = own_ref[...] + arrived


def coarse_gradient_kernel(total_ref, share_ref, g_ref):
    share = jnp.sum(share_ref[...].astype(F32), 0)
    first = total_ref[0:16, :] + jnp.concatenate([share, jnp.zeros_like(share)], 0)
    g_ref[...] = total_ref[...].astype(BF16)
    g_ref[0:16, :] = first.astype(BF16)


def order_kernel(*refs):
    pass


def halving_kernel(kept_ref, taken_ref, *refs):
    passing = (len(refs) - 2) // 2
    keep_ref, give_ref = refs[passing : passing + 2]
    half = keep_ref.shape[0]
    for j in range(half):
        give_ref[j] = (kept_ref[half + j] + taken_ref[half + j].astype(F32)).astype(BF16)
    for j in range(half):
        keep_ref[j] = kept_ref[j] + taken_ref[j].astype(F32)


def last_sum_kernel(*refs, groups, with_nodes):
    place = 2 * groups
    totals = [refs[2 * i][0] + refs[2 * i + 1][0].astype(F32) for i in range(groups)]
    if with_nodes:
        nodes_ref, g_ref = refs[place], refs[-1]
    first_ref, second_ref = refs[place + with_nodes :][:2]
    done = totals[0].shape[0]
    cut = first_ref.shape[0]
    if groups == 1:
        first_ref[...] = totals[0][:cut]
        second_ref[...] = totals[0][cut:]
        return
    rest = totals[1]
    first_ref[0:done, :] = totals[0]
    if done < cut:
        first_ref[done:cut, :] = rest[: cut - done]
    start = cut - done + second_ref.shape[0]
    second_ref[...] = rest[cut - done : start]
    g_ref[...] = nodes_ref[...].astype(BF16)
    g_ref[0:16, :] = (nodes_ref[0:16, :] + rest[start : start + 16]).astype(BF16)


VM = pl.BlockSpec(memory_space=pltpu.VMEM)
SM = pl.BlockSpec(memory_space=pltpu.SMEM)
ANY = pl.BlockSpec(memory_space=pl.ANY)


def shape(dims, dtype):
    return jax.ShapeDtypeStruct(tuple(dims), dtype)


class Rows:
    def __init__(self, parts=1, joined=1, extra=0):
        self.parts = parts
        self.joined = joined
        self.extra = extra


class Fetched:
    def __init__(self, sources, buffer, semaphores, parts):
        self.buffer = buffer
        self.shape = buffer.shape
        self.waiting = []
        place = 0
        for source in sources:
            rows = source.shape[0] // parts
            for part in range(parts):
                if source.shape == buffer.shape and parts == 1:
                    copy = pltpu.make_async_copy(source, buffer, next(semaphores))
                else:
                    copy = pltpu.make_async_copy(
                        source.at[pl.ds(part * rows, rows)], buffer.at[pl.ds(place, rows)], next(semaphores)
                    )
                copy.start()
                self.waiting.append((place, place + rows, copy))
                place += rows

    def ready(self, low=0, high=None):
        left = []
        for first, last, copy in self.waiting:
            if high is None or (first < high and low < last):
                copy.wait()
            else:
                left.append((first, last, copy))
        self.waiting = left

    def __getitem__(self, index):
        rows = index[0] if isinstance(index, tuple) else None
        if isinstance(rows, slice) and rows.start is not None:
            self.ready(rows.start, rows.stop)
        else:
            self.ready()
        return self.buffer[index]

    def __setitem__(self, index, value):
        self.buffer[index] = value


class Stored:
    def __init__(self, target, buffer, semaphores):
        self.target = target
        self.buffer = buffer
        self.shape = buffer.shape
        self.dtype = buffer.dtype
        self.semaphores = semaphores
        self.copies = []

    def __getitem__(self, index):
        return self.buffer[index]

    def __setitem__(self, index, value):
        self.buffer[index] = value

    def done(self, rows=None):
        if rows is None:
            copy = pltpu.make_async_copy(self.buffer, self.target, next(self.semaphores))
        else:
            part = pl.ds(rows.start, rows.stop - rows.start)
            copy = pltpu.make_async_copy(self.buffer.at[part], self.target.at[part], next(self.semaphores))
        copy.start()
        self.copies.append(copy)


SEMAPHORES = 64


def staged_kernel(body, in_specs, out_specs, *refs):
    ins, outs = refs[: len(in_specs)], refs[len(in_specs) : len(in_specs) + len(out_specs)]
    rest = refs[len(in_specs) + len(out_specs) :]
    semaphores = iter([rest[0].at[i] for i in range(SEMAPHORES)])
    buffers = iter(rest[1:])
    fetched, stored = [], []
    for place, (ref, spec) in enumerate(zip(ins, in_specs)):
        if spec is VM:
            fetched.append(Fetched([ref], next(buffers), semaphores, 1))
        elif spec is SM:
            fetched.append(ref)
        elif isinstance(spec, Rows):
            fetched.append(Fetched(ins[place : place + spec.joined], next(buffers), semaphores, spec.parts))
    for ref, spec in zip(outs, out_specs):
        stored.append(Stored(ref, next(buffers), semaphores))
    body(*fetched, *stored, *buffers)
    for ref in fetched:
        if isinstance(ref, Fetched):
            ref.ready()
    for ref in stored:
        if not ref.copies:
            ref.done()
    for ref in stored:
        for copy in ref.copies:
            copy.wait()


def cost(ins, outs, flops):
    moved = sum(a.size * a.dtype.itemsize for a in list(ins) + list(outs))
    return pl.CostEstimate(flops=flops, bytes_accessed=moved, transcendentals=0)


def call(kernel, name, ins, in_specs, outs, scratch=(), flops=0):
    out_specs = [VM] * len(outs)
    buffers = []
    for place, spec in enumerate(in_specs):
        if spec is VM:
            buffers.append(pltpu.VMEM(ins[place].shape, ins[place].dtype))
        elif isinstance(spec, Rows):
            joined = ins[place : place + spec.joined]
            rows = sum(a.shape[0] for a in joined) + spec.extra
            buffers.append(pltpu.VMEM((rows,) + joined[0].shape[1:], joined[0].dtype))
    buffers += [pltpu.VMEM(a.shape, a.dtype) for a in outs]
    return pl.pallas_call(
        functools.partial(staged_kernel, kernel, in_specs, out_specs),
        out_shape=tuple(outs),
        in_specs=[SM if spec is SM else ANY for spec in in_specs],
        out_specs=tuple([ANY] * len(outs)),
        scratch_shapes=[pltpu.SemaphoreType.DMA((SEMAPHORES,))] + buffers + list(scratch),
        name=name,
        cost_estimate=cost(ins, outs, flops),
        compiler_params=pltpu.CompilerParams(vmem_limit_bytes=VMEM_LIMIT),
    )(*ins)


def small_call(kernel, name, ins, outs, passing=(), limit=SMALL_LIMIT):
    first = len(ins)
    last = len(outs)
    outs = list(outs) + [shape(a.shape, a.dtype) for a in passing]
    return pl.pallas_call(
        kernel,
        out_shape=tuple(outs),
        input_output_aliases={first + i: last + i for i in range(len(passing))},
        in_specs=[VM] * first + [ANY] * len(passing),
        out_specs=tuple([VM] * last + [ANY] * len(passing)),
        name=name,
        cost_estimate=cost(ins, outs, 0),
        compiler_params=pltpu.CompilerParams(vmem_limit_bytes=limit),
    )(*ins, *passing)


def passed_along(block, axis, distance):
    count = lax.axis_size(axis)
    route = [((i - distance) % count, i) for i in range(count)]
    return lax.ppermute(block, axis, route)


def exchanged(block, axis, distance):
    return lax.ppermute(block, axis, [(i, i ^ distance) for i in range(lax.axis_size(axis))])


def exchanged_with_all(blocks, axis):
    return lax.all_to_all(blocks, axis, 0, 0)


def first_halving(kept, taken):
    half = kept.shape[0] // 2
    give = (kept[half:].astype(F32) + taken[half:].astype(F32)).astype(BF16)
    return kept[:half].astype(F32) + taken[:half].astype(F32), give


def halving(kept, taken, passing=()):
    half = (kept.shape[0] // 2,) + kept.shape[1:]
    return small_call(halving_kernel, "halving", (kept, taken), [shape(half, F32), shape(half, BF16)], passing)


def last_sum(groups, sizes, nodes=None):
    ins = [array for group in groups for array in group]
    outs = [shape((count, ins[0].shape[2]), F32) for count in sizes]
    if nodes is not None:
        ins.append(nodes)
        outs.append(shape(nodes.shape, BF16))
    kernel = functools.partial(last_sum_kernel, groups=len(groups), with_nodes=nodes is not None)
    return small_call(kernel, "last_sum", ins, outs)


def local(
    nodes,
    fine_edges,
    coarse_edges,
    fine_send,
    fine_recv,
    coarse_send,
    coarse_recv,
    halo_rows,
    edge_count,
    edge_w1,
    edge_w2,
    edge_gain,
    node_w1,
    node_w2,
    node_gain,
    d_nodes,
    d_fine,
    d_coarse,
):
    axis = "patch"
    peers = lax.axis_size(axis)
    own, width = nodes.shape
    fine = fine_edges.shape[0]
    coarse = coarse_edges.shape[0]
    halo = halo_rows[0]
    slots, tile = halo.shape
    hops = slots // 2
    offsets = list(range(1, hops + 1)) + [-k for k in range(1, hops + 1)]
    ordered = peers == 16 and all(
        w.shape[0] % (16 * peers) == 0 for w in (edge_w1, edge_w2, node_w1, node_w2)
    )
    me = lax.axis_index(axis).astype(jnp.int32).reshape(1)
    fs, fr = fine_send.reshape(1, fine), fine_recv.reshape(1, fine)
    cs, cr = coarse_send.reshape(1, coarse), coarse_recv.reshape(1, coarse)
    eg, ng = edge_gain.reshape(1, width), node_gain.reshape(1, width)
    every = shape((peers, COARSE_DEV, width), BF16)

    made = call(
        tiles_kernel, "tiles", (nodes, halo), [VM, VM],
        [shape((tile, width), BF16)] * slots,
    )
    received = [passed_along(made[slot], axis, offset) for slot, offset in enumerate(offsets)]
    coarse_all = exchanged_with_all(jnp.broadcast_to(nodes[:COARSE_DEV][None], every.shape), axis)

    def saved_shapes(rows):
        return [
            shape((rows, width), BF16), shape((rows, width), BF16), shape((rows, width), BF16),
            shape((rows, width), BF16), shape((rows, width), BF16), shape((rows, 128), F32),
        ]

    new_coarse, coarse_part, *coarse_saved = call(
        coarse_forward_kernel, "coarse_forward",
        (coarse_all, coarse_edges, cs, cr, edge_w1, edge_w2, eg), [VM] * 4 + [Rows(3), VM, VM],
        [shape((coarse, width), BF16), every] + saved_shapes(coarse),
        flops=2 * coarse * width * width * 4,
    )
    share = exchanged_with_all(coarse_part, axis)

    block = 256 if fine % 256 == 0 else fine
    space_rows = own + slots * tile
    new_fine, fine_agg, *fine_saved = call(
        functools.partial(fine_forward_kernel, slots=slots, block=block), "fine_forward",
        (edge_count, nodes, *received, fine_edges, fs, fr, edge_w1, edge_w2, eg),
        [SM] + [VM] * (slots + 4) + [Rows(3), VM, VM],
        [shape((fine, width), BF16), shape((own, width), F32)] + saved_shapes(fine),
        scratch=[pltpu.VMEM((space_rows, width), BF16)],
        flops=2 * fine * width * (4 * width + space_rows + 3 * own),
    )

    def weight_shapes(w1, w2, more):
        if not ordered:
            return [shape(w1.shape, F32), shape(w2.shape, F32)], []
        rows = (w1.shape[0] + w2.shape[0]) // peers + more
        outs = [shape((peers // 2, rows, width), BF16)] * 2
        return outs, [pltpu.VMEM(w1.shape, F32), pltpu.VMEM(w2.shape, F32)]

    sum_shapes, sum_scratch = weight_shapes(node_w1, node_w2, 0)
    new_nodes, base, dagg, dagg_spread, *node_parts = call(
        functools.partial(node_kernel, ordered=ordered), "node_both",
        (me, nodes, fine_agg, share, d_nodes, node_w1, node_w2, ng), [SM] + [VM] * 4 + [Rows(2), VM, VM],
        [shape((own, width), BF16), shape((own, width), F32), shape((own, width), BF16), every] + sum_shapes,
        scratch=[pltpu.VMEM((own, width), F32)] + sum_scratch,
        flops=2 * own * width * width * 9,
    )
    dagg_all = exchanged_with_all(dagg_spread, axis)
    if ordered:
        node_taken = exchanged(node_parts[1], axis, 1)
        node_kept, node_given = first_halving(node_parts[0], node_taken)

    sum_shapes, sum_scratch = weight_shapes(edge_w1, edge_w2, 16)
    if ordered:
        cut = first_rows(edge_w1.shape[0] // peers)
        rows = sum_shapes[0].shape[1] - cut
        sum_shapes = [shape((peers // 2, cut, width), BF16)] * 2 + [shape((peers // 2, rows, width), BF16)] * 2
    f_zs, f_zr, f_hidden, f_slope, f_normed, f_std = fine_saved
    c_zs, c_zr, c_hidden, c_slope, c_normed, c_std = coarse_saved
    fine_out, fine_pre, g_fine, own_grad, *pieces = call(
        functools.partial(fine_backward_kernel, block=block), "fine_backward",
        (edge_count, fr, dagg, d_fine, eg, f_std, f_normed, edge_w2, f_slope, edge_w1, fs, base),
        [SM] + [VM] * 8 + [Rows(3), VM, VM],
        [shape((fine, width), BF16)] * 3 + [shape((own, width), F32)] + [shape((tile, width), BF16)] * slots,
        scratch=[pltpu.VMEM((space_rows, width), F32)],
        flops=2 * fine * width * (4 * width + space_rows + 2 * own),
    )
    returned = [passed_along(pieces[slot], axis, -offset) for slot, offset in enumerate(offsets)]
    if ordered:
        node_taken = exchanged(node_given, axis, 4)
    pair = [Rows(joined=2), None]
    more = [Rows(extra=coarse)]
    g_coarse, *edge_parts = call(
        functools.partial(coarse_backward_kernel, ordered=ordered), "coarse_backward",
        (
            me, cr, dagg_all, d_coarse, eg, c_std, c_normed, edge_w2, c_slope, fine_edges, coarse_edges,
            fine_pre, f_zs, c_zs, f_zr, c_zr, f_hidden, c_hidden, fine_out, edge_w1, cs,
        ),
        [SM] + [VM] * 8 + pair + more + pair * 3 + more + [Rows(3), VM],
        [shape((coarse, width), BF16)] + ([] if ordered else [every]) + sum_shapes,
        scratch=([pltpu.VMEM((peers * COARSE_DEV, width), F32)] if ordered else []) + sum_scratch,
        flops=2 * width * width * (4 * fine + 12 * coarse),
    )

    def rows_of(w):
        return w.shape[0] // peers

    def tile_gradient():
        (total,) = small_call(
            node_gradient_kernel, "node_gradient", (own_grad, halo, *returned), [shape((own, width), F32)]
        )
        return total

    if ordered:
        kept1, given1, kept2, given2 = edge_parts
        given1, node_taken, *returned = small_call(
            order_kernel, "order", (), [], (given1, node_taken, *returned), VMEM_LIMIT
        )
        taken1 = exchanged(given1, axis, 1)
        taken2 = exchanged(given2, axis, 1)
        steps1, steps2 = x_first(peers), x_last(peers)
        kept1, given1 = first_halving(kept1, taken1)
        taken1 = exchanged(given1, axis, steps1[0])
        kept2, given2 = first_halving(kept2, taken2)
        taken2 = exchanged(given2, axis, steps2[0])
        for k in range(1, len(steps1)):
            passing = (kept1,) if k == 1 else ()
            node_kept, given, *passing = halving(node_kept, node_taken, passing)
            node_taken = exchanged(given, axis, steps2[k])
            kept2, given2, *passing = halving(kept2, taken2, tuple(passing))
            taken2 = exchanged(given2, axis, steps2[k])
            kept1, given1 = halving(passing[0] if passing else kept1, taken1)
            taken1 = exchanged(given1, axis, steps1[k])
        g_nw1, g_nw2 = last_sum([(node_kept, node_taken)], (rows_of(node_w1), rows_of(node_w2)))
        g_ew1, g_ew2, g_nodes = last_sum(
            [(kept1, taken1), (kept2, taken2)], (rows_of(edge_w1), rows_of(edge_w2)), tile_gradient()
        )
    else:
        coarse_share = exchanged_with_all(edge_parts[0], axis)
        (g_nodes,) = small_call(
            coarse_gradient_kernel, "coarse_gradient", (tile_gradient(), coarse_share), [shape((own, width), BF16)],
        )
        g_nw1, g_nw2, g_ew1, g_ew2 = [
            lax.psum_scatter(g, axis, scatter_dimension=0, tiled=True) for g in [*node_parts, *edge_parts[1:]]
        ]
    return (new_nodes, new_fine, new_coarse, g_nodes, g_fine, g_coarse, g_ew1, g_ew2, g_nw1, g_nw2)


def solution(mesh):
    split = P(("groups", "patch"))
    rows = P(("groups", "patch"), None)
    return jax.shard_map(
        local,
        mesh=mesh,
        in_specs=(
            rows, rows, rows, split, split, split, split, P(("groups", "patch"), None, None), split,
            P(), P(), P(), P(), P(), P(), rows, rows, rows,
        ),
        out_specs=(rows,) * 10,
        check_vma=False,
    )
```

```python
import functools

import jax
import jax.numpy as jnp
from jax import lax
from jax.experimental import pallas as pl
from jax.experimental.pallas import tpu as pltpu
from jax.sharding import PartitionSpec as P

COARSE_DEV = 8
EPSILON = 1e-05
F32 = jnp.float32
BF16 = jnp.bfloat16
VMEM_LIMIT = 60 * 1024 * 1024
SMALL_LIMIT = 16 * 1024 * 1024


def mm(a, b):
    return lax.dot_general(a, b, (((1,), (0,)), ((), ())), preferred_element_type=F32)


def mm_nt(a, b):
    return lax.dot_general(a, b, (((1,), (1,)), ((), ())), preferred_element_type=F32)


def mm_tn(a, b):
    return lax.dot_general(a, b, (((0,), (0,)), ((), ())), preferred_element_type=F32)


def halves(value):
    high = value.astype(BF16)
    low = (value - high.astype(F32)).astype(BF16)
    return high, low


def one_hot(index, rows):
    row = lax.broadcasted_iota(jnp.int32, (rows, index.shape[1]), 0)
    return jnp.where(row == index, 1.0, 0.0).astype(BF16)


def pick(index, table):
    entries = index.shape[1]
    column = jnp.transpose(jnp.broadcast_to(index, (128, entries)))
    lane = lax.broadcasted_iota(jnp.int32, (entries, 128), 1)
    parts = []
    for start in range(0, table.shape[0], 128):
        parts.append(jnp.where(column == lane + start, 1.0, 0.0).astype(BF16))
    return mm(jnp.concatenate(parts, 1), table)


def put_wide(hot, rows):
    high, low = halves(rows)
    return mm(hot, high) + mm(hot, low)


def row_mean(value):
    return jnp.mean(value, axis=-1, keepdims=True)


def tail_of_forward(pre, second_w, gain):
    sigmoid = jax.nn.sigmoid(pre)
    hidden = (pre * sigmoid).astype(BF16)
    slope = sigmoid * (1.0 + pre * (1.0 - sigmoid))
    output = mm(hidden, second_w)
    centred = output - row_mean(output)
    inv_std = lax.rsqrt(row_mean(centred * centred) + EPSILON)
    normed = centred * inv_std
    return normed * gain, hidden, slope, normed, inv_std


def head_of_backward(cotan, second_w, gain, slope, normed, inv_std):
    scaled = cotan * gain
    back_out = inv_std * (scaled - row_mean(scaled) - normed * row_mean(scaled * normed))
    back_out = back_out.astype(BF16)
    back_pre = (mm_nt(back_out, second_w) * slope).astype(BF16)
    return back_out, back_pre


def tiles_kernel(nodes_ref, halo_ref, *outs):
    nodes = nodes_ref[...]
    for slot, out in enumerate(outs):
        out[...] = pick(halo_ref[slot : slot + 1, :], nodes).astype(BF16)
        out.done()


def gathered(ref):
    value = ref[...].astype(F32)
    return value.reshape(value.shape[0] * value.shape[1], value.shape[2])


def coarse_forward_kernel(
    all_ref, edges_ref, send_ref, recv_ref, w1_ref, w2_ref, gain_ref,
    new_ref, part_ref, zs_ref, zr_ref, hidden_ref, slope_ref, normed_ref, std_ref,
):
    width = edges_ref.shape[1]
    table = gathered(all_ref).astype(BF16)
    hot_r = one_hot(recv_ref[...], table.shape[0])
    edges = edges_ref[...]
    zs = pick(send_ref[...], table).astype(BF16)
    zr = pick(recv_ref[...], table).astype(BF16)
    pre = (
        mm(edges, w1_ref[0:width, :])
        + mm(zs, w1_ref[width : 2 * width, :])
        + mm(zr, w1_ref[2 * width : 3 * width, :])
    )
    message, hidden, slope, normed, inv_std = tail_of_forward(pre, w2_ref[...], gain_ref[...])
    total = put_wide(hot_r, message)
    part_ref[...] = total.reshape(part_ref.shape).astype(BF16)
    part_ref.done()
    new_ref[...] = (edges.astype(F32) + message).astype(BF16)
    zs_ref[...] = zs
    zr_ref[...] = zr
    hidden_ref[...] = hidden
    slope_ref[...] = slope.astype(BF16)
    normed_ref[...] = normed.astype(BF16)
    std_ref[...] = jnp.broadcast_to(inv_std, std_ref.shape)


def fine_forward_kernel(count_ref, nodes_ref, *refs, slots, block):
    tile_refs = refs[:slots]
    (
        edges_ref, send_ref, recv_ref, w1_ref, w2_ref, gain_ref,
        new_ref, agg_ref, zs_ref, zr_ref, hidden_ref, slope_ref, normed_ref, std_ref, space_ref,
    ) = refs[slots:]
    count, width = edges_ref.shape
    own = nodes_ref.shape[0]
    tile = tile_refs[0].shape[0]
    space_ref[0:own, :] = nodes_ref[...]
    for slot in range(slots):
        space_ref[own + slot * tile : own + (slot + 1) * tile, :] = tile_refs[slot][...]
    for start in range(0, count, block):
        rows = slice(start, start + block)
        edges = edges_ref[rows, :]
        hot_r = one_hot(recv_ref[:, rows], own)
        zs = pick(send_ref[:, rows], space_ref[...]).astype(BF16)
        zr = pick(recv_ref[:, rows], nodes_ref[...]).astype(BF16)
        pre = (
            mm(edges, w1_ref[0:width, :])
            + mm(zs, w1_ref[width : 2 * width, :])
            + mm(zr, w1_ref[2 * width : 3 * width, :])
        )
        message, hidden, slope, normed, inv_std = tail_of_forward(pre, w2_ref[...], gain_ref[...])
        place = start + lax.broadcasted_iota(jnp.int32, (block, 1), 0)
        message = jnp.where(place < count_ref[0], message, 0.0)
        arrived = put_wide(hot_r, message)
        agg_ref[...] = arrived if start == 0 else agg_ref[...] + arrived
        new_ref[rows, :] = (edges.astype(F32) + message).astype(BF16)
        zs_ref[rows, :] = zs
        zr_ref[rows, :] = zr
        hidden_ref[rows, :] = hidden
        slope_ref[rows, :] = slope.astype(BF16)
        normed_ref[rows, :] = normed.astype(BF16)
        std_ref[rows, :] = jnp.broadcast_to(inv_std, (block, std_ref.shape[1]))
        for ref in (new_ref, zs_ref, zr_ref, hidden_ref, slope_ref, normed_ref, std_ref):
            ref.done(rows)


def x_first(peers):
    return [1 << bit for bit in range(1, peers.bit_length() - 1)]


def x_last(peers):
    steps = x_first(peers)
    return steps[1:] + steps[:1]


def first_rows(rows):
    return rows * 5 // 6 // 16 * 16


def by_distance(me, peers, steps, sums, kept_ref, given_ref):
    for r in list(range(1, peers, 2)) + list(range(0, peers, 2)):
        if r == 0:
            given_ref.done()
        to = jnp.bitwise_xor(me, r)
        out = given_ref if r % 2 else kept_ref
        slot = 0
        for distance in steps:
            slot = 2 * slot + r // distance % 2
        place = 0
        for total, first, last in sums:
            whole = total.shape[0] // peers
            rows = last - first
            part = total[pl.ds(pl.multiple_of(to * whole + first, 8), rows), :]
            if rows % 16:
                part = jnp.concatenate([part, jnp.zeros((-rows % 16, part.shape[1]), F32)], 0)
            out[slot, place : place + part.shape[0], :] = part.astype(BF16)
            place += part.shape[0]
    kept_ref.done()


def node_kernel(
    me_ref, nodes_ref, agg_ref, share_ref, d_ref, w1_ref, w2_ref, gain_ref,
    new_ref, base_ref, dagg_ref, spread_ref, *rest, ordered,
):
    if ordered:
        kept_ref, given_ref, total_ref, g1_ref, g2_ref = rest
    else:
        g1_ref, g2_ref, total_ref = rest
    width = nodes_ref.shape[1]
    total_ref[...] = agg_ref[...]
    total_ref[0:COARSE_DEV, :] += jnp.sum(share_ref[...].astype(F32), 0)
    nodes = nodes_ref[...]
    agg = total_ref[...].astype(BF16)
    pre = mm(nodes, w1_ref[0:width, :]) + mm(agg, w1_ref[width : 2 * width, :])
    update, hidden, slope, normed, inv_std = tail_of_forward(pre, w2_ref[...], gain_ref[...])
    new_ref[...] = (nodes.astype(F32) + update).astype(BF16)
    cotan = d_ref[...].astype(F32)
    back_out, back_pre = head_of_backward(cotan, w2_ref[...], gain_ref[...], slope, normed, inv_std)
    dagg = mm_nt(back_pre, w1_ref[width : 2 * width, :])
    dagg_ref[...] = dagg.astype(BF16)
    rows = dagg[:COARSE_DEV].astype(BF16)
    for peer in range(spread_ref.shape[0]):
        spread_ref[peer] = rows
    base_ref[...] = cotan + mm_nt(back_pre, w1_ref[0:width, :])
    g1_ref[0:width, :] = mm_tn(nodes, back_pre)
    g1_ref[width : 2 * width, :] = mm_tn(agg, back_pre)
    g2_ref[...] = mm_tn(hidden, back_out)
    if ordered:
        peers = spread_ref.shape[0]

        def share(ref):
            return ref, 0, ref.shape[0] // peers

        by_distance(me_ref[0], peers, x_last(peers), (share(g1_ref), share(g2_ref)), kept_ref, given_ref)


def fine_backward_kernel(
    count_ref, recv_ref, dagg_ref, d_ref, gain_ref, std_ref, normed_ref, w2_ref, slope_ref,
    w1_ref, send_ref, base_ref,
    out_ref, pre_ref, g_ref, own_ref, *rest, block,
):
    piece_refs, space_ref = rest[:-1], rest[-1]
    count, width = d_ref.shape
    own = base_ref.shape[0]
    received = None
    for start in range(0, count, block):
        rows = slice(start, start + block)
        hot_r = one_hot(recv_ref[:, rows], own)
        d_edges = d_ref[rows, :].astype(F32)
        place = start + lax.broadcasted_iota(jnp.int32, (block, 1), 0)
        cotan = jnp.where(place < count_ref[0], d_edges + pick(recv_ref[:, rows], dagg_ref[...]), 0.0)
        back_out, back_pre = head_of_backward(
            cotan, w2_ref[...], gain_ref[...], slope_ref[rows, :].astype(F32),
            normed_ref[rows, :].astype(F32), std_ref[rows, 0:1],
        )
        out_ref[rows, :] = back_out
        pre_ref[rows, :] = back_pre
        out_ref.done(rows)
        pre_ref.done(rows)
        g_ref[rows, :] = (d_edges + mm_nt(back_pre, w1_ref[0:width, :])).astype(BF16)
        g_ref.done(rows)
        dz_send = mm_nt(back_pre, w1_ref[width : 2 * width, :]).astype(BF16)
        dz_recv = mm_nt(back_pre, w1_ref[2 * width : 3 * width, :]).astype(BF16)
        sent = mm(one_hot(send_ref[:, rows], space_ref.shape[0]), dz_send)
        space_ref[...] = sent if start == 0 else space_ref[...] + sent
        arrived = mm(hot_r, dz_recv)
        received = arrived if received is None else received + arrived
    for slot, piece in enumerate(piece_refs):
        tile = piece.shape[0]
        piece[...] = space_ref[own + slot * tile : own + (slot + 1) * tile, :].astype(BF16)
        piece.done()
    own_ref[...] = base_ref[...] + received + space_ref[0:own, :]


def coarse_backward_kernel(
    me_ref, recv_ref, all_ref, d_ref, gain_ref, std_ref, normed_ref, w2_ref, slope_ref,
    edges_ref, pre_ref, zs_ref, zr_ref, hidden_ref, out_ref, w1_ref, send_ref,
    g_ref, *rest, ordered,
):
    if ordered:
        kept1_ref, given1_ref, kept2_ref, given2_ref, part_ref, g1_ref, g2_ref = rest
    else:
        part_ref, g1_ref, g2_ref = rest
    width = d_ref.shape[1]
    count = hidden_ref.shape[0]
    rows = slice(count - d_ref.shape[0], count)
    table = gathered(all_ref).astype(BF16)
    d_edges = d_ref[...].astype(F32)
    cotan = d_edges + pick(recv_ref[...], table)
    back_out, back_pre = head_of_backward(
        cotan, w2_ref[...], gain_ref[...], slope_ref[...].astype(F32), normed_ref[...].astype(F32), std_ref[:, 0:1]
    )
    out_ref[rows, :] = back_out
    pre_ref[rows, :] = back_pre
    g1_ref[0:width, :] = mm_tn(edges_ref[...], pre_ref[...])
    g1_ref[width : 2 * width, :] = mm_tn(zs_ref[...], pre_ref[...])
    g1_ref[2 * width : 3 * width, :] = mm_tn(zr_ref[...], pre_ref[...])
    if ordered:
        peers = 2 * kept1_ref.shape[0]
        by_distance(me_ref[0], peers, x_first(peers), ((g1_ref, 0, kept1_ref.shape[1]),), kept1_ref, given1_ref)
    g2_ref[...] = mm_tn(hidden_ref[...], out_ref[...])
    dz_send = mm_nt(back_pre, w1_ref[width : 2 * width, :]).astype(BF16)
    dz_recv = mm_nt(back_pre, w1_ref[2 * width : 3 * width, :]).astype(BF16)
    total = mm(one_hot(send_ref[...], table.shape[0]), dz_send) + mm(one_hot(recv_ref[...], table.shape[0]), dz_recv)
    part_ref[...] = total.reshape(part_ref.shape).astype(part_ref.dtype)
    if ordered:
        sums = (
            (g1_ref, kept1_ref.shape[1], g1_ref.shape[0] // peers),
            (g2_ref, 0, g2_ref.shape[0] // peers),
            (part_ref, 0, part_ref.shape[0] // peers),
        )
        by_distance(me_ref[0], peers, x_last(peers), sums, kept2_ref, given2_ref)
    g_ref[...] = (d_edges + mm_nt(back_pre, w1_ref[0:width, :])).astype(BF16)


def node_gradient_kernel(own_ref, halo_ref, *refs):
    piece_refs, out_ref = refs[:-1], refs[-1]
    arrived = None
    for slot, piece in enumerate(piece_refs):
        part = mm(one_hot(halo_ref[slot : slot + 1, :], own_ref.shape[0]), piece[...])
        arrived = part if arrived is None else arrived + part
    out_ref[...] = own_ref[...] + arrived


def coarse_gradient_kernel(total_ref, share_ref, g_ref):
    share = jnp.sum(share_ref[...].astype(F32), 0)
    first = total_ref[0:16, :] + jnp.concatenate([share, jnp.zeros_like(share)], 0)
    g_ref[...] = total_ref[...].astype(BF16)
    g_ref[0:16, :] = first.astype(BF16)


def order_kernel(*refs):
    pass


def halving_kernel(kept_ref, taken_ref, *refs):
    passing = (len(refs) - 2) // 2
    keep_ref, give_ref = refs[passing : passing + 2]
    half = keep_ref.shape[0]
    for j in range(half):
        give_ref[j] = (kept_ref[half + j] + taken_ref[half + j].astype(F32)).astype(BF16)
    for j in range(half):
        keep_ref[j] = kept_ref[j] + taken_ref[j].astype(F32)


def last_sum_kernel(*refs, groups, with_nodes):
    place = 2 * groups
    totals = [refs[2 * i][0] + refs[2 * i + 1][0].astype(F32) for i in range(groups)]
    if with_nodes:
        nodes_ref, g_ref = refs[place], refs[-1]
    first_ref, second_ref = refs[place + with_nodes :][:2]
    done = totals[0].shape[0]
    cut = first_ref.shape[0]
    if groups == 1:
        first_ref[...] = totals[0][:cut]
        second_ref[...] = totals[0][cut:]
        return
    rest = totals[1]
    first_ref[0:done, :] = totals[0]
    first_ref[done:cut, :] = rest[: cut - done]
    start = cut - done + second_ref.shape[0]
    second_ref[...] = rest[cut - done : start]
    g_ref[...] = nodes_ref[...].astype(BF16)
    g_ref[0:16, :] = (nodes_ref[0:16, :] + rest[start : start + 16]).astype(BF16)


VM = pl.BlockSpec(memory_space=pltpu.VMEM)
SM = pl.BlockSpec(memory_space=pltpu.SMEM)
ANY = pl.BlockSpec(memory_space=pl.ANY)


def shape(dims, dtype):
    return jax.ShapeDtypeStruct(tuple(dims), dtype)


class Rows:
    def __init__(self, parts=1, joined=1, extra=0):
        self.parts = parts
        self.joined = joined
        self.extra = extra


class Fetched:
    def __init__(self, sources, buffer, semaphores, parts):
        self.buffer = buffer
        self.shape = buffer.shape
        self.waiting = []
        place = 0
        for source in sources:
            rows = source.shape[0] // parts
            for part in range(parts):
                if source.shape == buffer.shape and parts == 1:
                    copy = pltpu.make_async_copy(source, buffer, next(semaphores))
                else:
                    copy = pltpu.make_async_copy(
                        source.at[pl.ds(part * rows, rows)], buffer.at[pl.ds(place, rows)], next(semaphores)
                    )
                copy.start()
                self.waiting.append((place, place + rows, copy))
                place += rows

    def ready(self, low=0, high=None):
        left = []
        for first, last, copy in self.waiting:
            if high is None or (first < high and low < last):
                copy.wait()
            else:
                left.append((first, last, copy))
        self.waiting = left

    def __getitem__(self, index):
        rows = index[0] if isinstance(index, tuple) else None
        if isinstance(rows, slice) and rows.start is not None:
            self.ready(rows.start, rows.stop)
        else:
            self.ready()
        return self.buffer[index]

    def __setitem__(self, index, value):
        self.buffer[index] = value


class Stored:
    def __init__(self, target, buffer, semaphores):
        self.target = target
        self.buffer = buffer
        self.shape = buffer.shape
        self.dtype = buffer.dtype
        self.semaphores = semaphores
        self.copies = []

    def __getitem__(self, index):
        return self.buffer[index]

    def __setitem__(self, index, value):
        self.buffer[index] = value

    def done(self, rows=None):
        if rows is None:
            copy = pltpu.make_async_copy(self.buffer, self.target, next(self.semaphores))
        else:
            part = pl.ds(rows.start, rows.stop - rows.start)
            copy = pltpu.make_async_copy(self.buffer.at[part], self.target.at[part], next(self.semaphores))
        copy.start()
        self.copies.append(copy)


SEMAPHORES = 64


def staged_kernel(body, in_specs, out_specs, *refs):
    ins, outs = refs[: len(in_specs)], refs[len(in_specs) : len(in_specs) + len(out_specs)]
    rest = refs[len(in_specs) + len(out_specs) :]
    semaphores = iter([rest[0].at[i] for i in range(SEMAPHORES)])
    buffers = iter(rest[1:])
    fetched, stored = [], []
    for place, (ref, spec) in enumerate(zip(ins, in_specs)):
        if spec is VM:
            fetched.append(Fetched([ref], next(buffers), semaphores, 1))
        elif spec is SM:
            fetched.append(ref)
        elif isinstance(spec, Rows):
            fetched.append(Fetched(ins[place : place + spec.joined], next(buffers), semaphores, spec.parts))
    for ref, spec in zip(outs, out_specs):
        stored.append(Stored(ref, next(buffers), semaphores))
    body(*fetched, *stored, *buffers)
    for ref in fetched:
        if isinstance(ref, Fetched):
            ref.ready()
    for ref in stored:
        if not ref.copies:
            ref.done()
    for ref in stored:
        for copy in ref.copies:
            copy.wait()


def cost(ins, outs, flops):
    moved = sum(a.size * a.dtype.itemsize for a in list(ins) + list(outs))
    return pl.CostEstimate(flops=flops, bytes_accessed=moved, transcendentals=0)


def call(kernel, name, ins, in_specs, outs, scratch=(), flops=0):
    out_specs = [VM] * len(outs)
    buffers = []
    for place, spec in enumerate(in_specs):
        if spec is VM:
            buffers.append(pltpu.VMEM(ins[place].shape, ins[place].dtype))
        elif isinstance(spec, Rows):
            joined = ins[place : place + spec.joined]
            rows = sum(a.shape[0] for a in joined) + spec.extra
            buffers.append(pltpu.VMEM((rows,) + joined[0].shape[1:], joined[0].dtype))
    buffers += [pltpu.VMEM(a.shape, a.dtype) for a in outs]
    return pl.pallas_call(
        functools.partial(staged_kernel, kernel, in_specs, out_specs),
        out_shape=tuple(outs),
        in_specs=[SM if spec is SM else ANY for spec in in_specs],
        out_specs=tuple([ANY] * len(outs)),
        scratch_shapes=[pltpu.SemaphoreType.DMA((SEMAPHORES,))] + buffers + list(scratch),
        name=name,
        cost_estimate=cost(ins, outs, flops),
        compiler_params=pltpu.CompilerParams(vmem_limit_bytes=VMEM_LIMIT),
    )(*ins)


def small_call(kernel, name, ins, outs, passing=()):
    first = len(ins)
    last = len(outs)
    outs = list(outs) + [shape(a.shape, a.dtype) for a in passing]
    return pl.pallas_call(
        kernel,
        out_shape=tuple(outs),
        input_output_aliases={first + i: last + i for i in range(len(passing))},
        in_specs=[VM] * first + [ANY] * len(passing),
        out_specs=tuple([VM] * last + [ANY] * len(passing)),
        name=name,
        cost_estimate=cost(ins, outs, 0),
        compiler_params=pltpu.CompilerParams(vmem_limit_bytes=SMALL_LIMIT),
    )(*ins, *passing)


def passed_along(block, axis, distance):
    count = lax.axis_size(axis)
    route = [((i - distance) % count, i) for i in range(count)]
    return lax.ppermute(block, axis, route)


def exchanged(block, axis, distance):
    return lax.ppermute(block, axis, [(i, i ^ distance) for i in range(lax.axis_size(axis))])


def exchanged_with_all(blocks, axis):
    return lax.all_to_all(blocks, axis, 0, 0)


def first_halving(kept, taken):
    half = kept.shape[0] // 2
    give = (kept[half:].astype(F32) + taken[half:].astype(F32)).astype(BF16)
    return kept[:half].astype(F32) + taken[:half].astype(F32), give


def halving(kept, taken, passing=()):
    half = (kept.shape[0] // 2,) + kept.shape[1:]
    return small_call(halving_kernel, "halving", (kept, taken), [shape(half, F32), shape(half, BF16)], passing)


def last_sum(groups, sizes, nodes=None):
    ins = [array for group in groups for array in group]
    outs = [shape((count, ins[0].shape[2]), F32) for count in sizes]
    if nodes is not None:
        ins.append(nodes)
        outs.append(shape(nodes.shape, BF16))
    kernel = functools.partial(last_sum_kernel, groups=len(groups), with_nodes=nodes is not None)
    return small_call(kernel, "last_sum", ins, outs)


def local(
    nodes,
    fine_edges,
    coarse_edges,
    fine_send,
    fine_recv,
    coarse_send,
    coarse_recv,
    halo_rows,
    edge_count,
    edge_w1,
    edge_w2,
    edge_gain,
    node_w1,
    node_w2,
    node_gain,
    d_nodes,
    d_fine,
    d_coarse,
):
    axis = "patch"
    peers = lax.axis_size(axis)
    own, width = nodes.shape
    fine = fine_edges.shape[0]
    coarse = coarse_edges.shape[0]
    halo = halo_rows[0]
    slots, tile = halo.shape
    hops = slots // 2
    offsets = list(range(1, hops + 1)) + [-k for k in range(1, hops + 1)]
    ordered = peers == 16 and all(
        w.shape[0] % (16 * peers) == 0 for w in (edge_w1, edge_w2, node_w1, node_w2)
    )
    me = lax.axis_index(axis).astype(jnp.int32).reshape(1)
    fs, fr = fine_send.reshape(1, fine), fine_recv.reshape(1, fine)
    cs, cr = coarse_send.reshape(1, coarse), coarse_recv.reshape(1, coarse)
    eg, ng = edge_gain.reshape(1, width), node_gain.reshape(1, width)
    every = shape((peers, COARSE_DEV, width), BF16)

    made = call(
        tiles_kernel, "tiles", (nodes, halo), [VM, VM],
        [shape((tile, width), BF16)] * slots,
    )
    received = [passed_along(made[slot], axis, offset) for slot, offset in enumerate(offsets)]
    coarse_all = exchanged_with_all(jnp.broadcast_to(nodes[:COARSE_DEV][None], every.shape), axis)

    def saved_shapes(rows):
        return [
            shape((rows, width), BF16), shape((rows, width), BF16), shape((rows, width), BF16),
            shape((rows, width), BF16), shape((rows, width), BF16), shape((rows, 128), F32),
        ]

    new_coarse, coarse_part, *coarse_saved = call(
        coarse_forward_kernel, "coarse_forward",
        (coarse_all, coarse_edges, cs, cr, edge_w1, edge_w2, eg), [VM] * 4 + [Rows(3), VM, VM],
        [shape((coarse, width), BF16), every] + saved_shapes(coarse),
        flops=2 * coarse * width * width * 4,
    )
    share = exchanged_with_all(coarse_part, axis)

    block = 512 if fine % 512 == 0 else fine
    space_rows = own + slots * tile
    new_fine, fine_agg, *fine_saved = call(
        functools.partial(fine_forward_kernel, slots=slots, block=block), "fine_forward",
        (edge_count, nodes, *received, fine_edges, fs, fr, edge_w1, edge_w2, eg),
        [SM] + [VM] * (slots + 4) + [Rows(3), VM, VM],
        [shape((fine, width), BF16), shape((own, width), F32)] + saved_shapes(fine),
        scratch=[pltpu.VMEM((space_rows, width), BF16)],
        flops=2 * fine * width * (4 * width + space_rows + 3 * own),
    )

    def weight_shapes(w1, w2, more):
        if not ordered:
            return [shape(w1.shape, F32), shape(w2.shape, F32)], []
        rows = (w1.shape[0] + w2.shape[0]) // peers + more
        outs = [shape((peers // 2, rows, width), BF16)] * 2
        return outs, [pltpu.VMEM(w1.shape, F32), pltpu.VMEM(w2.shape, F32)]

    sum_shapes, sum_scratch = weight_shapes(node_w1, node_w2, 0)
    new_nodes, base, dagg, dagg_spread, *node_parts = call(
        functools.partial(node_kernel, ordered=ordered), "node_both",
        (me, nodes, fine_agg, share, d_nodes, node_w1, node_w2, ng), [SM] + [VM] * 4 + [Rows(2), VM, VM],
        [shape((own, width), BF16), shape((own, width), F32), shape((own, width), BF16), every] + sum_shapes,
        scratch=[pltpu.VMEM((own, width), F32)] + sum_scratch,
        flops=2 * own * width * width * 9,
    )
    dagg_all = exchanged_with_all(dagg_spread, axis)
    if ordered:
        node_taken = exchanged(node_parts[1], axis, 1)
        node_kept, node_given = first_halving(node_parts[0], node_taken)

    sum_shapes, sum_scratch = weight_shapes(edge_w1, edge_w2, 16)
    if ordered:
        cut = first_rows(edge_w1.shape[0] // peers)
        rows = sum_shapes[0].shape[1] - cut
        sum_shapes = [shape((peers // 2, cut, width), BF16)] * 2 + [shape((peers // 2, rows, width), BF16)] * 2
    f_zs, f_zr, f_hidden, f_slope, f_normed, f_std = fine_saved
    c_zs, c_zr, c_hidden, c_slope, c_normed, c_std = coarse_saved
    fine_out, fine_pre, g_fine, own_grad, *pieces = call(
        functools.partial(fine_backward_kernel, block=block), "fine_backward",
        (edge_count, fr, dagg, d_fine, eg, f_std, f_normed, edge_w2, f_slope, edge_w1, fs, base),
        [SM] + [VM] * 8 + [Rows(3), VM, VM],
        [shape((fine, width), BF16)] * 3 + [shape((own, width), F32)] + [shape((tile, width), BF16)] * slots,
        scratch=[pltpu.VMEM((space_rows, width), F32)],
        flops=2 * fine * width * (4 * width + space_rows + 2 * own),
    )
    returned = [passed_along(pieces[slot], axis, -offset) for slot, offset in enumerate(offsets)]
    if ordered:
        node_taken = exchanged(node_given, axis, 4)
    pair = [Rows(joined=2), None]
    more = [Rows(extra=coarse)]
    g_coarse, *edge_parts = call(
        functools.partial(coarse_backward_kernel, ordered=ordered), "coarse_backward",
        (
            me, cr, dagg_all, d_coarse, eg, c_std, c_normed, edge_w2, c_slope, fine_edges, coarse_edges,
            fine_pre, f_zs, c_zs, f_zr, c_zr, f_hidden, c_hidden, fine_out, edge_w1, cs,
        ),
        [SM] + [VM] * 8 + pair + more + pair * 3 + more + [Rows(3), VM],
        [shape((coarse, width), BF16)] + ([] if ordered else [every]) + sum_shapes,
        scratch=([pltpu.VMEM((peers * COARSE_DEV, width), F32)] if ordered else []) + sum_scratch,
        flops=2 * width * width * (4 * fine + 12 * coarse),
    )

    def rows_of(w):
        return w.shape[0] // peers

    def tile_gradient():
        (total,) = small_call(
            node_gradient_kernel, "node_gradient", (own_grad, halo, *returned), [shape((own, width), F32)]
        )
        return total

    if ordered:
        kept1, given1, kept2, given2 = edge_parts
        given1, node_taken, *returned = small_call(
            order_kernel, "order", (), [], (given1, node_taken, *returned)
        )
        taken1 = exchanged(given1, axis, 1)
        taken2 = exchanged(given2, axis, 1)
        steps1, steps2 = x_first(peers), x_last(peers)
        kept1, given1 = first_halving(kept1, taken1)
        taken1 = exchanged(given1, axis, steps1[0])
        kept2, given2 = first_halving(kept2, taken2)
        taken2 = exchanged(given2, axis, steps2[0])
        for k in range(1, len(steps1)):
            passing = (kept1,) if k == 1 else ()
            node_kept, given, *passing = halving(node_kept, node_taken, passing)
            node_taken = exchanged(given, axis, steps2[k])
            kept2, given2, *passing = halving(kept2, taken2, tuple(passing))
            taken2 = exchanged(given2, axis, steps2[k])
            kept1, given1 = halving(passing[0] if passing else kept1, taken1)
            taken1 = exchanged(given1, axis, steps1[k])
        g_nw1, g_nw2 = last_sum([(node_kept, node_taken)], (rows_of(node_w1), rows_of(node_w2)))
        g_ew1, g_ew2, g_nodes = last_sum(
            [(kept1, taken1), (kept2, taken2)], (rows_of(edge_w1), rows_of(edge_w2)), tile_gradient()
        )
    else:
        coarse_share = exchanged_with_all(edge_parts[0], axis)
        (g_nodes,) = small_call(
            coarse_gradient_kernel, "coarse_gradient", (tile_gradient(), coarse_share), [shape((own, width), BF16)],
        )
        g_nw1, g_nw2, g_ew1, g_ew2 = [
            lax.psum_scatter(g, axis, scatter_dimension=0, tiled=True) for g in [*node_parts, *edge_parts[1:]]
        ]
    return (new_nodes, new_fine, new_coarse, g_nodes, g_fine, g_coarse, g_ew1, g_ew2, g_nw1, g_nw2)


def solution(mesh):
    split = P(("groups", "patch"))
    rows = P(("groups", "patch"), None)
    return jax.shard_map(
        local,
        mesh=mesh,
        in_specs=(
            rows, rows, rows, split, split, split, split, P(("groups", "patch"), None, None), split,
            P(), P(), P(), P(), P(), P(), rows, rows, rows,
        ),
        out_specs=(rows,) * 10,
        check_vma=False,
    )
```
